32 devices in a mesh: seq: 8 (over z, core), head: 4 (over y, x).
Axes of the slice: x: 2, y: 2, z: 4, core: 2. Of those that a mesh axis runs over, the one named last changes fastest.
Arguments:
- tokens: bfloat16 [8192, 4096], P('seq', 'head'), may hold values from -6 to 6
- w_qkv: bfloat16 [3, 4096, 4096], P(None, None, 'head'), may hold values from -0.09375 to 0.09375
- w_out: bfloat16 [4096, 4096], P('head'), may hold values from -0.125 to 0.125
- decay_rate: float32 [32, 8192], P('head', 'seq'), may hold values from 0 to 1, as said below
- prior_state: float32 [32, 128, 128], P('head'), may hold values from -256 to 256
Outputs:
- mixed: bfloat16 [8192, 4096], P('seq', 'head')
The draws below stay inside these ranges and needn't reach their ends.
Inputs may be any that keep to these rules, and one draw needn't show every extreme that they name: `decay_rate`: rates of each head for each position; every rate is positive.
All inputs are finite; a program needn't handle non-finite values.
Results may differ from the reference program's by a relative error of at most 0.02.
Values may be sent and summed in bfloat16 or wider, within the bound.
No kernel may reach another device: no remote copies, remote signals or barrier semaphores. Data moves between devices by JAX's collectives and lax.ppermute only.
A program may use at most 128 MiB of HBM per device.

```python
import math
import jax
import jax.numpy as jnp
from jax import lax

D = 4096
DECAY_CHANNELS = 32
DH = 128
TOK_DEV = 1024
SEGMENTS = 8
HEAD_GROUPS = 4
TOKENS = 8192
N_SEQ = 8


def draw_decay_rate(key, part):
    lookup_vectors = jax.random.split(jax.random.fold_in(key, 41), 7)
    timeline_count = TOKENS
    fast_count = 5
    fast_flag = jax.random.randint(lookup_vectors[0], (DECAY_CHANNELS, 1), 0, 10) < fast_count
    fast_rate = jnp.exp(jax.random.uniform(lookup_vectors[1], (DECAY_CHANNELS, 1), jnp.float32, math.log(1.0 / 50.0), math.log(1.0 / 30.0)))
    slow_rate = jnp.exp(jax.random.uniform(lookup_vectors[2], (DECAY_CHANNELS, 1), jnp.float32, math.log(0.05), math.log(0.3))) / timeline_count
    floor_frequency = jnp.where(fast_flag, fast_rate, slow_rate)
    position = jnp.arange(timeline_count, dtype=jnp.float32)[None, :]
    phase = jax.random.uniform(lookup_vectors[3], (DECAY_CHANNELS, 1), jnp.float32, 0.0, 2.0 * math.pi)
    cyclic_waveform = jnp.exp(0.7 * jnp.sin(2.0 * math.pi * 3.0 * position / timeline_count + phase))
    stochastic_jitter = jax.random.uniform(lookup_vectors[4], (DECAY_CHANNELS, timeline_count), jnp.float32, 0.5, 1.5)
    spike_location = jax.random.randint(lookup_vectors[5], (DECAY_CHANNELS, 3), 0, timeline_count)
    spike_duration = -jnp.log(jax.random.uniform(lookup_vectors[6], (DECAY_CHANNELS, 3), jnp.float32, 0.5, 0.8))
    entry_numbers = jnp.arange(timeline_count, dtype=jnp.int32)[None, None, :]
    spike_occurrences = jnp.max(jnp.where(entry_numbers == spike_location[:, :, None], spike_duration[:, :, None], 0.0), axis=1)
    return (floor_frequency * cyclic_waveform * stochastic_jitter + spike_occurrences).astype(jnp.float32)


def with_spikes(entries, rng, source, target, parts, factor):
    owner, partner = [(jnp.arange(entries.shape[dim]) // (entries.shape[dim] // parts)).reshape([-1 if axis == dim else 1 for axis in range(entries.ndim)]) for dim in (source, target)]
    chosen = jax.random.permutation(rng, parts)[partner]
    strong = (owner == chosen) | (owner == (partner + parts // 2) % parts)
    return jnp.where(strong, factor * entries, entries)


def shard_levels(key, shape, pieces, low, top_value):
    gain, own = 1.0, jax.random.fold_in(key, 6)
    for axis_at, parts in pieces:
        heights = jnp.exp(jax.random.uniform(jax.random.fold_in(own, axis_at), (parts,), jnp.float32, low / len(pieces), top_value / len(pieces)))
        gain = gain * jnp.repeat(heights, shape[axis_at] // parts).reshape([-1 if axis == axis_at else 1 for axis in range(len(shape))])
    return gain


def bell_draw(rng, shape, spread, limit, cuts=(), kind=jnp.bfloat16):
    array = spread * jax.random.normal(rng, shape, jnp.float32)
    if cuts:
        array = array * shard_levels(rng, shape, cuts, -0.22, 0.18)
    return jnp.clip(array, -limit, limit).astype(kind)


def bell_draw_with(stream_key, shape, scale, bound, shards, heavy, kind=jnp.bfloat16):
    drawn = scale * jax.random.normal(stream_key, shape, jnp.float32)
    if shards:
        drawn = drawn * shard_levels(stream_key, shape, shards, -0.22, 0.18)
    return jnp.clip(with_spikes(drawn, jax.random.fold_in(stream_key, 3), *heavy), -bound, bound).astype(kind)


def setup_inputs(seed: int = 0) -> dict:
    streams_of = jax.random.split(jax.random.key(seed), 6)
    return {
        "tokens": bell_draw(streams_of[0], (TOKENS, D), 1.0, 6.0, ((0, 8), (1, 4))),
        "w_qkv": bell_draw(streams_of[1], (3, D, DECAY_CHANNELS * DH), D ** -0.5, 0.09375, ((2, 4),)),
        "w_out": bell_draw_with(streams_of[2], (DECAY_CHANNELS * DH, D), (DECAY_CHANNELS * DH) ** -0.5, 0.125, ((0, 4),), (0, 1, 4, 2.0)),
        "decay_rate": draw_decay_rate(jax.random.fold_in(streams_of[5], 71), 0),
        "prior_state": bell_draw(streams_of[4], (DECAY_CHANNELS, DH, DH), (0.5 * (TOK_DEV * N_SEQ) ** 0.5), 256.0, ((0, 4),), jnp.float32),
    }


def segment_terms(operands):
    queries, keys_seg, values_seg, rates = operands
    cumulative = jnp.cumsum(rates, axis=1)
    query_f = queries.astype(jnp.float32)
    key_f = keys_seg.astype(jnp.float32)
    value_f = values_seg.astype(jnp.float32)
    scores = jnp.einsum('thd,uhd->htu', query_f, key_f, precision=lax.Precision.HIGHEST)
    decay_gap = cumulative[:, :, None] - cumulative[:, None, :]
    timeline_count = rates.shape[1]
    causal = lax.broadcasted_iota(jnp.int32, (timeline_count, timeline_count), 0) >= lax.broadcasted_iota(jnp.int32, (timeline_count, timeline_count), 1)
    weights = jnp.where(causal[None], scores * jnp.exp(-jnp.maximum(decay_gap, 0.0)), 0.0)
    weights = lax.optimization_barrier(weights.astype(jnp.bfloat16)).astype(jnp.float32)
    within = jnp.einsum('htu,uhd->thd', weights, value_f, precision=lax.Precision.HIGHEST)
    tail_sum = cumulative[:, -1:]
    scaled_keys = key_f * jnp.exp(cumulative - tail_sum).T[:, :, None]
    scaled_keys = lax.optimization_barrier(scaled_keys.astype(jnp.bfloat16)).astype(jnp.float32)
    end_state = jnp.einsum('thd,the->hde', scaled_keys, value_f, precision=lax.Precision.HIGHEST)
    return (within, end_state, jnp.exp(-tail_sum[:, 0]), cumulative)

def segment_output(operands):
    queries, entering_seg, cumulative, within = operands
    rounded = lax.optimization_barrier(entering_seg.astype(jnp.bfloat16)).astype(jnp.float32)
    from_state = jnp.einsum('thd,hde->the', queries.astype(jnp.float32), rounded, precision=lax.Precision.HIGHEST)
    from_state = from_state * jnp.exp(-cumulative).T[:, :, None]
    combined = within + from_state
    normed = combined * lax.rsqrt(lax.optimization_barrier(jnp.mean(combined * combined, axis=2, keepdims=True)) + 1e-06)
    return normed.astype(jnp.bfloat16).reshape(normed.shape[0], -1)

def reference(tokens, w_qkv, w_out, decay_rate, prior_state):
    projected = [jnp.dot(tokens, w_qkv[part_index], preferred_element_type=jnp.float32).astype(jnp.bfloat16) for part_index in range(3)]
    shaped = [member.reshape(SEGMENTS, TOK_DEV, DECAY_CHANNELS, DH) for member in projected]
    rate_seg = decay_rate.reshape(DECAY_CHANNELS, SEGMENTS, TOK_DEV).transpose(1, 0, 2)
    within, end_states, end_decays, cumulative = lax.map(segment_terms, (shaped[0], shaped[1], shaped[2], rate_seg))

    def advance(state_now, pair):
        decay_seg, end_seg = pair
        return (decay_seg[:, None, None] * state_now + end_seg, state_now)
    final_state, entering = lax.scan(advance, prior_state.astype(jnp.float32), (end_decays, end_states))
    normed_all = lax.map(segment_output, (shaped[0], entering, cumulative, within)).reshape(TOKENS, DECAY_CHANNELS * DH)
    width = DECAY_CHANNELS // HEAD_GROUPS * DH

    def add_group(group, running):
        columns = lax.dynamic_slice_in_dim(normed_all, group * width, width, 1)
        rows = lax.dynamic_slice_in_dim(w_out, group * width, width, 0)
        term = jnp.dot(columns, rows, preferred_element_type=jnp.float32)
        return running + lax.optimization_barrier(term.astype(jnp.bfloat16)).astype(jnp.float32)
    summed = lax.fori_loop(0, HEAD_GROUPS, add_group, jnp.zeros((TOKENS, D), jnp.float32))
    return summed.astype(jnp.bfloat16)
```

```python
import functools

import jax
import jax.numpy as jnp
from jax import lax
from jax.experimental import pallas as pl
from jax.experimental.pallas import tpu as pltpu
from jax.sharding import PartitionSpec as P

BF16, F32 = jnp.bfloat16, jnp.float32
VMEM_LIMIT = 40 * 1024 * 1024


def dot(a, b, contract=((1,), (0,))):
    return lax.dot_general(a, b, (contract, ((), ())), preferred_element_type=F32)


def rows_of(refs):
    if len(refs) == 1:
        return refs[0][...]
    return jnp.concatenate([ref[...] for ref in refs], axis=0)


def chunk_kernel(layout, offs, *refs):
    count = sum(layout)
    piece_refs, refs = refs[:count], refs[count:]
    w_ref, row_ref, col_ref, state_ref, q_ref, within_ref, state_out_ref = refs
    pieces, at = [], 0
    for parts in layout:
        pieces.append(piece_refs[at : at + parts])
        at += parts
    width = piece_refs[0].shape[1]
    rows = q_ref.shape[0]
    heads, size = state_ref.shape[0], state_ref.shape[1]

    def project(c):
        total = None
        for i, piece in enumerate(pieces):
            start = pl.multiple_of(offs[i], width)
            term = dot(rows_of(piece), w_ref[c, pl.ds(start, width), :])
            total = term if total is None else total + term
        return total.astype(BF16)

    q_all, k_all, v_all = project(0), project(1), project(2)
    q_ref[...] = q_all
    causal = lax.broadcasted_iota(jnp.int32, (rows, rows), 0) >= lax.broadcasted_iota(
        jnp.int32, (rows, rows), 1
    )
    for a in range(heads):
        lanes = slice(a * size, (a + 1) * size)
        q, k, v = q_all[:, lanes], k_all[:, lanes], v_all[:, lanes]
        along, down = row_ref[0, a : a + 1, :], col_ref[0, :, a : a + 1]
        decay = jnp.exp(jnp.minimum(along - down, 0.0))
        weights = jnp.where(causal, dot(q, k, ((1,), (1,))) * decay, 0.0).astype(BF16)
        state = state_ref[a]
        within = dot(weights, v) + dot(q, state.astype(BF16)) * jnp.exp(-down)
        within_ref[:, lanes] = within
        last = down[rows - 1 :, :]
        scaled = (k.astype(F32) * jnp.exp(down - last)).astype(BF16)
        state_out_ref[a] = jnp.exp(-last) * state + dot(scaled, v, ((0,), (0,)))


def chunk_call(offs, pieces, w_qkv, along, down, state):
    rows = pieces[0][0].shape[0] if len(pieces[0]) == 1 else sum(p.shape[0] for p in pieces[0])
    heads, size = state.shape[0], state.shape[1]
    group = along.shape[1]
    steps = heads // group
    cols = group * size
    flat = [p for piece in pieces for p in piece]
    depth = w_qkv.shape[1]
    whole = [pl.BlockSpec(p.shape, lambda j, o: (0, 0)) for p in flat]
    flops = 2 * rows * depth * 3 * heads * size + 4 * heads * rows * size * (rows + size)
    return pl.pallas_call(
        functools.partial(chunk_kernel, tuple(len(p) for p in pieces)),
        out_shape=(
            jax.ShapeDtypeStruct((rows, heads * size), BF16),
            jax.ShapeDtypeStruct((rows, heads * size), F32),
            jax.ShapeDtypeStruct(state.shape, F32),
        ),
        grid_spec=pltpu.PrefetchScalarGridSpec(
            num_scalar_prefetch=1,
            grid=(steps,),
            in_specs=whole
            + [
                pl.BlockSpec((3, depth, cols), lambda j, o: (0, 0, j)),
                pl.BlockSpec((1, group, rows), lambda j, o: (j, 0, 0)),
                pl.BlockSpec((1, rows, group), lambda j, o: (j, 0, 0)),
                pl.BlockSpec((group, size, size), lambda j, o: (j, 0, 0)),
            ],
            out_specs=[
                pl.BlockSpec((rows, cols), lambda j, o: (0, j)),
                pl.BlockSpec((rows, cols), lambda j, o: (0, j)),
                pl.BlockSpec((group, size, size), lambda j, o: (j, 0, 0)),
            ],
        ),
        compiler_params=pltpu.CompilerParams(vmem_limit_bytes=VMEM_LIMIT),
        cost_estimate=pl.CostEstimate(
            flops=flops, bytes_accessed=w_qkv.size * 2 + rows * depth * 2, transcendentals=0
        ),
        name="chunk",
    )(offs, *flat, w_qkv, along, down, state)


def head_kernel(block, q_ref, within_ref, entering_ref, down_ref, w_ref, normed_ref, out_ref):
    heads, size = entering_ref.shape[0], entering_ref.shape[1]
    fade = jnp.exp(-down_ref[...])
    for a in range(heads):
        lanes = slice(a * size, (a + 1) * size)
        combined = within_ref[:, lanes] + dot(q_ref[:, lanes], entering_ref[a]) * fade[:, a : a + 1]
        power = jnp.mean(combined * combined, axis=1, keepdims=True)
        normed_ref[:, lanes] = (combined * lax.rsqrt(power + 1e-06)).astype(BF16)
    out_ref[...] = dot(normed_ref[...], w_ref[...]).astype(BF16)


def head_call(block, q, within, entering, down, w_out, width):
    rows, cols = q.shape
    heads = entering.shape[0]
    tile = min(rows, 256)
    return pl.pallas_call(
        head_kernel,
        out_shape=(
            jax.ShapeDtypeStruct((rows, cols), BF16),
            jax.ShapeDtypeStruct((rows, width), BF16),
        ),
        grid_spec=pltpu.PrefetchScalarGridSpec(
            num_scalar_prefetch=1,
            grid=(rows // tile,),
            in_specs=[
                pl.BlockSpec((tile, cols), lambda i, b: (i, 0)),
                pl.BlockSpec((tile, cols), lambda i, b: (i, 0)),
                pl.BlockSpec(entering.shape, lambda i, b: (0, 0, 0)),
                pl.BlockSpec((tile, heads), lambda i, b: (i, 0)),
                pl.BlockSpec((cols, width), lambda i, b: (0, b[0])),
            ],
            out_specs=[
                pl.BlockSpec((tile, cols), lambda i, b: (i, 0)),
                pl.BlockSpec((tile, width), lambda i, b: (i, 0)),
            ],
        ),
        compiler_params=pltpu.CompilerParams(vmem_limit_bytes=VMEM_LIMIT),
        cost_estimate=pl.CostEstimate(
            flops=2 * rows * cols * (width + 128),
            bytes_accessed=cols * width * 2 + rows * cols * 8 + rows * width * 2,
            transcendentals=0,
        ),
        name="heads",
    )(block, q, within, entering, down, w_out)


def out_kernel(block, normed_ref, w_ref, *refs):
    total = dot(normed_ref[...], w_ref[...])
    for ref in refs[:-1]:
        total = total + ref[...].astype(F32)
    refs[-1][...] = total.astype(BF16)


def out_call(block, normed, w_out, width, *arrived):
    rows, cols = normed.shape
    tile = min(width, 256)
    per = width // tile
    return pl.pallas_call(
        out_kernel,
        out_shape=jax.ShapeDtypeStruct((rows, width), BF16),
        grid_spec=pltpu.PrefetchScalarGridSpec(
            num_scalar_prefetch=1,
            grid=(per,),
            in_specs=[
                pl.BlockSpec((rows, cols), lambda j, b: (0, 0)),
                pl.BlockSpec((cols, tile), lambda j, b: (0, b[0] * per + j)),
            ]
            + [pl.BlockSpec((rows, tile), lambda j, b: (0, j)) for _ in arrived],
            out_specs=pl.BlockSpec((rows, tile), lambda j, b: (0, j)),
        ),
        compiler_params=pltpu.CompilerParams(vmem_limit_bytes=VMEM_LIMIT),
        cost_estimate=pl.CostEstimate(
            flops=2 * rows * cols * width,
            bytes_accessed=cols * width * 2 + rows * (cols + width * (1 + len(arrived))) * 2,
            transcendentals=0,
        ),
        name="project_out",
    )(block, normed, w_out, *arrived)


def local(n_head, n_seq, tokens, w_qkv, w_out, decay_rate, prior_state):
    rows, width = tokens.shape
    heads, size = prior_state.shape[0], prior_state.shape[1]
    square = n_head == 4
    place = lax.axis_index("head")
    chunk = min(rows, 256)
    chunks = rows // chunk
    group = 2 if heads % 2 == 0 else 1

    over_x = functools.partial(lax.ppermute, axis_name="head", perm=[(i, i ^ 1) for i in range(n_head)])
    over_y = functools.partial(lax.ppermute, axis_name="head", perm=[(i, i ^ 2) for i in range(n_head)])

    pieces = []
    if square:
        offs = jnp.stack([place, place ^ 1, place ^ 2, place ^ 3]).astype(jnp.int32) * width
        half = chunk // 2
        for c in range(chunks):
            own = tokens[c * chunk : (c + 1) * chunk]
            from_x, from_y = over_x(own), over_y(own)
            far = (over_y(from_x[:half]), over_x(from_y[half:]))
            pieces.append(((own,), (from_x,), (from_y,), far))
    else:
        offs = jnp.zeros((1,), jnp.int32)
        for c in range(chunks):
            own = tokens[c * chunk : (c + 1) * chunk]
            pieces.append(((lax.all_gather(own, "head", axis=1, tiled=True),),))

    inside = jnp.cumsum(decay_rate.reshape(heads, chunks, chunk), axis=2)
    sums = inside[:, :, -1]
    before = jnp.cumsum(sums, axis=1) - sums
    cumulative = (inside + before[:, :, None]).reshape(heads, rows)
    down_all = cumulative.T
    tail = jnp.sum(sums, axis=1)
    along = inside.reshape(heads // group, group, chunks, chunk)

    pos = lax.axis_index("seq")
    core = pos % 2
    n_chips = n_seq // 2
    swap = functools.partial(lax.ppermute, axis_name="seq", perm=[(i, i ^ 1) for i in range(n_seq)])

    def later(x, step):
        return lax.ppermute(x, "seq", perm=[(i, i + 2 * step) for i in range(n_seq - 2 * step)])

    tail_other = swap(tail)
    tail_chip = tail + tail_other
    tails = [later(tail_chip, s) for s in range(1, n_chips)]

    state = jnp.zeros((heads, size, size), F32)
    queries, withins = [], []
    for c in range(chunks):
        q, within, state = chunk_call(
            offs,
            pieces[c],
            w_qkv,
            along[:, :, c, :],
            along[:, :, c, :].transpose(0, 2, 1),
            state,
        )
        queries.append(q)
        withins.append(within)

    other = swap(state.astype(BF16)).astype(F32)
    first = jnp.where(core == 0, state, other)
    second = jnp.where(core == 0, other, state)
    tail_first = jnp.where(core == 0, tail, tail_other)
    tail_second = jnp.where(core == 0, tail_other, tail)
    share = heads // 2

    def mine(x):
        return lax.dynamic_slice_in_dim(x, core * share, share, 0)

    chip_state = (
        jnp.exp(-mine(tail_second))[:, None, None] * mine(first) + mine(second)
    ).astype(BF16)
    gap = jnp.zeros((share,), F32)
    chip_entering = jnp.zeros((share, size, size), F32)
    for s in range(1, n_chips):
        chip_entering += jnp.exp(-gap)[:, None, None] * later(chip_state, s).astype(F32)
        gap += mine(tails[s - 1])
    chip_entering += jnp.exp(-gap)[:, None, None] * mine(prior_state)
    there = swap(chip_entering.astype(BF16)).astype(F32)
    entering = jnp.concatenate(
        [jnp.where(core == 0, chip_entering, there), jnp.where(core == 0, there, chip_entering)]
    )
    entering = jnp.where(
        core == 0, entering, jnp.exp(-tail_first)[:, None, None] * entering + first
    ).astype(BF16)

    def block(flip):
        return (place ^ flip).astype(jnp.int32).reshape(1)

    if not square:
        q, within = jnp.concatenate(queries), jnp.concatenate(withins)
        normed, _ = head_call(block(0), q, within, entering, down_all, w_out, width)
        partial = dot(normed, w_out).astype(BF16)
        return lax.psum_scatter(partial, "head", scatter_dimension=1, tiled=True)

    cut = rows // 2
    per = chunks // 2
    normed, far = [], []
    for r in range(2):
        q = jnp.concatenate(queries[r * per : (r + 1) * per])
        within = jnp.concatenate(withins[r * per : (r + 1) * per])
        down = down_all[r * cut : (r + 1) * cut]
        n, p = head_call(block(3), q, within, entering, down, w_out, width)
        normed.append(n)
        far.append(p)
    via_x, via_y = over_x(far[0]), over_y(far[1])
    near_x = over_x(out_call(block(1), normed[0], w_out, width))
    near_y = over_y(out_call(block(2), normed[1], w_out, width))
    sum_x = over_x(out_call(block(1), normed[1], w_out, width, via_y))
    sum_y = over_y(out_call(block(2), normed[0], w_out, width, via_x))
    own_a = out_call(block(0), normed[0], w_out, width, near_x)
    own_b = out_call(block(0), normed[1], w_out, width, near_y)
    return jnp.concatenate(
        [
            (own_a.astype(F32) + sum_y.astype(F32)).astype(BF16),
            (own_b.astype(F32) + sum_x.astype(F32)).astype(BF16),
        ]
    )


def solution(mesh):
    in_specs = (
        P("seq", "head"),
        P(None, None, "head"),
        P("head", None),
        P("head", "seq"),
        P("head", None, None),
    )
    body = functools.partial(local, mesh.shape["head"], mesh.shape["seq"])
    return jax.shard_map(
        body, mesh=mesh, in_specs=in_specs, out_specs=P("seq", "head"), check_vma=False
    )
```

```python
import functools

import jax
import jax.numpy as jnp
from jax import lax
from jax.experimental import pallas as pl
from jax.experimental.pallas import tpu as pltpu
from jax.sharding import PartitionSpec as P

BF16, F32 = jnp.bfloat16, jnp.float32
PARAMS = pltpu.CompilerParams(vmem_limit_bytes=40 * 1024 * 1024)


def dot(a, b, contract=((1,), (0,))):
    return lax.dot_general(a, b, (contract, ((), ())), preferred_element_type=F32)


def after(x, *earlier):
    return lax.optimization_barrier((x, *earlier))[0]


def struct(shape, dtype):
    return jax.ShapeDtypeStruct(shape, dtype)


def fixed(shape):
    return pl.BlockSpec(shape, lambda j, o: (0,) * len(shape))


def call(kernel, name, steps, scalars, ins, in_specs, outs, out_specs, flops, scratch=(), aliases=None, light=False):
    moved = sum(a.size * a.dtype.itemsize for a in ins) + sum(
        o.size * jnp.dtype(o.dtype).itemsize for o in outs
    )
    return pl.pallas_call(
        kernel,
        out_shape=tuple(outs),
        grid_spec=pltpu.PrefetchScalarGridSpec(
            num_scalar_prefetch=1,
            grid=(steps,),
            in_specs=in_specs,
            out_specs=out_specs,
            scratch_shapes=list(scratch),
        ),
        input_output_aliases=aliases or {},
        compiler_params=PARAMS,
        cost_estimate=pl.CostEstimate(
            flops=1 if light else flops, bytes_accessed=1 if light else moved, transcendentals=0
        ),
        name=name,
    )(scalars, *ins)


def decay_kernel(chunk, _, rate_ref, along_ref, inside_ref, down_ref, tail_ref):
    heads, rows = rate_ref.shape
    lane = lax.broadcasted_iota(jnp.int32, (heads, chunk), 1)
    base = jnp.zeros((heads, 1), F32)
    insides, wholes = [], []
    for c in range(rows // chunk):
        x = rate_ref[:, c * chunk : (c + 1) * chunk]
        step = 1
        while step < chunk:
            x = x + jnp.where(lane >= step, pltpu.roll(x, step, 1), 0.0)
            step *= 2
        insides.append(x)
        wholes.append(x + base)
        base = base + x[:, chunk - 1 :]
    inside = jnp.concatenate(insides, axis=1)
    along_ref[...] = inside
    inside_ref[...] = inside.T
    down_ref[...] = jnp.concatenate(wholes, axis=1).T
    tail_ref[...] = jnp.broadcast_to(base, tail_ref.shape)


def decay_call(rate, chunk):
    heads, rows = rate.shape
    return call(
        functools.partial(decay_kernel, chunk),
        "decay",
        1,
        jnp.zeros((1,), jnp.int32),
        (rate,),
        [fixed((heads, rows))],
        (
            struct((heads, rows), F32),
            struct((rows, heads), F32),
            struct((rows, heads), F32),
            struct((heads, 128), F32),
        ),
        [fixed((heads, rows)), fixed((rows, heads)), fixed((rows, heads)), fixed((heads, 128))],
        heads * rows * 16,
    )


def column(table, head):
    lane = lax.broadcasted_iota(jnp.int32, table.shape, 1)
    return jnp.sum(jnp.where(lane == head, table, 0.0), axis=1, keepdims=True)


def scores(q, k, v, along, down, state):
    rows = q.shape[0]
    causal = lax.broadcasted_iota(jnp.int32, (rows, rows), 0) >= lax.broadcasted_iota(
        jnp.int32, (rows, rows), 1
    )
    decay = jnp.exp(jnp.minimum(along - down, 0.0))
    weights = jnp.where(causal, dot(q, k, ((1,), (1,))) * decay, 0.0).astype(BF16)
    return dot(weights, v) + dot(q, state.astype(BF16)) * jnp.exp(-down)


def advance(k, v, down, state):
    last = down[down.shape[0] - 1 :, :]
    scaled = (k.astype(F32) * jnp.exp(down - last)).astype(BF16)
    return jnp.exp(-last) * state + dot(scaled, v, ((0,), (0,)))


def first_kernel(layout, chunk, group, size, _, *refs):
    count = sum(layout)
    x_refs, w_refs, refs = refs[:count], refs[count : count + len(layout)], refs[count + len(layout) :]
    along_ref, inside_ref, q_ref, within_ref, state_ref, held = refs
    j = pl.program_id(0)
    rows, depth = held.shape[1], held.shape[2]

    @pl.when(j == 0)
    def _():
        at = 0
        for i, parts in enumerate(layout):
            tall = rows // parts
            for p in range(parts):
                held[i, p * tall : (p + 1) * tall, :] = x_refs[at][...]
                at += 1

    def project(c):
        total = dot(held[0], w_refs[0][c])
        for i in range(1, len(layout)):
            total = total + dot(held[i], w_refs[i][c])
        return total.astype(BF16)

    q_all, k_all, v_all = project(0), project(1), project(2)
    q_ref[...] = q_all
    for a in range(group):
        head = j * group + a
        lanes = slice(a * size, (a + 1) * size)
        state = jnp.zeros((size, size), F32)
        for c in range(rows // chunk):
            here = slice(c * chunk, (c + 1) * chunk)
            q, k, v = q_all[here, lanes], k_all[here, lanes], v_all[here, lanes]
            down = column(inside_ref[here, :], head)
            along = along_ref[pl.ds(head, 1), here]
            within_ref[here, lanes] = scores(q, k, v, along, down, state)
            state = advance(k, v, down, state)
        state_ref[a] = state


def first_call(places, blocks, pieces, w_qkv, along, inside, rows, chunk, size, group):
    heads = along.shape[0]
    cols = group * size
    flat = [p for piece in pieces for p in piece]
    depth = flat[0].shape[1]

    def block(i):
        return pl.BlockSpec((3, depth, cols), lambda j, o: (0, o[blocks[i]] if blocks else 0, j))

    wide = pl.BlockSpec((rows, cols), lambda j, o: (0, j))
    return call(
        functools.partial(first_kernel, tuple(len(p) for p in pieces), chunk, group, size),
        "first",
        heads // group,
        places,
        (*flat, *[w_qkv] * len(pieces), along, inside),
        [
            pl.BlockSpec((rows // len(piece), depth), lambda j, o: (0, 0))
            for piece in pieces
            for _ in piece
        ]
        + [block(i) for i in range(len(pieces))]
        + [fixed((heads, rows)), fixed((rows, heads))],
        (
            struct((rows, heads * size), BF16),
            struct((rows, heads * size), F32),
            struct((heads, size, size), F32),
        ),
        [wide, wide, pl.BlockSpec((group, size, size), lambda j, o: (j, 0, 0))],
        2 * rows * w_qkv.size,
        scratch=[pltpu.VMEM((len(pieces), rows, depth), BF16)],
    )


def part_kernel(layout, added, _, *refs):
    count = sum(layout)
    x_refs, w_refs = refs[:count], refs[count : count + len(layout)]
    out_ref, held = refs[-2], refs[-1]
    rows = held.shape[1]

    @pl.when(pl.program_id(0) == 0)
    def _():
        at = 0
        for i, parts in enumerate(layout):
            tall = rows // parts
            for p in range(parts):
                held[i, p * tall : (p + 1) * tall, :] = x_refs[at][...]
                at += 1

    for c in range(3):
        total = dot(held[0], w_refs[0][c])
        for i in range(1, len(layout)):
            total = total + dot(held[i], w_refs[i][c])
        if added:
            total = total + refs[-3][c]
        out_ref[c] = total


def part_call(places, blocks, pieces, w_qkv, rows, row_block, cols, before=None):
    flat = [p for piece in pieces for p in piece]
    depth = flat[0].shape[1]
    width = w_qkv.shape[2]

    def block(i):
        return pl.BlockSpec((3, depth, cols), lambda j, o: (0, o[blocks[i]], j))

    acc = pl.BlockSpec((3, rows, cols), lambda j, o: (0, 0, j))
    ins = [*flat, *[w_qkv] * len(pieces)]
    specs = [
        pl.BlockSpec((rows // len(piece), depth), lambda j, o: (row_block, 0))
        for piece in pieces
        for _ in piece
    ] + [block(i) for i in range(len(pieces))]
    if before is not None:
        ins.append(before)
        specs.append(acc)
    (out,) = call(
        functools.partial(part_kernel, tuple(len(p) for p in pieces), before is not None),
        "part",
        width // cols,
        places,
        ins,
        specs,
        (struct((3, rows, width), F32),),
        [acc],
        2 * rows * depth * len(pieces) * width * 3,
        scratch=[pltpu.VMEM((len(pieces), rows, depth), BF16)],
        aliases=None if before is None else {len(ins): 0},
    )
    return out


def state_kernel(chunk, group, size, _, *refs):
    xa, xb, wk, wv, acc_k, acc_v, inside_ref, state_ref = refs[:8]
    k_ref, v_ref, mid_ref, end_ref, sent_ref, held = refs[8:]
    j = pl.program_id(0)
    rows = held.shape[0]

    @pl.when(j == 0)
    def _():
        held[: rows // 2, :] = xa[...]
        held[rows // 2 :, :] = xb[...]

    k_all = (acc_k[0] + dot(held[...], wk[0])).astype(BF16)
    v_all = (acc_v[0] + dot(held[...], wv[0])).astype(BF16)
    k_ref[...] = k_all
    v_ref[...] = v_all
    for a in range(group):
        head = j * group + a
        lanes = slice(a * size, (a + 1) * size)
        state = state_ref[a]
        for c in range(rows // chunk):
            here = slice(c * chunk, (c + 1) * chunk)
            mid_ref[c, a] = state
            state = advance(
                k_all[here, lanes], v_all[here, lanes], column(inside_ref[here, :], head), state
            )
        end_ref[a] = state
        sent_ref[a] = state.astype(BF16)


def state_call(places, far, w_qkv, acc, inside, state, chunk, group):
    _, rows, width = acc.shape
    heads, size = state.shape[0], state.shape[1]
    depth = far[0].shape[1]
    cols = group * size
    wide = pl.BlockSpec((rows, cols), lambda j, o: (0, j))
    small = pl.BlockSpec((group, size, size), lambda j, o: (j, 0, 0))
    chunks = rows // chunk
    return call(
        functools.partial(state_kernel, chunk, group, size),
        "states",
        heads // group,
        places,
        (*far, w_qkv, w_qkv, acc, acc, inside, state),
        [fixed(far[0].shape), fixed(far[1].shape)]
        + [pl.BlockSpec((1, depth, cols), lambda j, o, c=c: (c, o[3], j)) for c in (1, 2)]
        + [pl.BlockSpec((1, rows, cols), lambda j, o, c=c: (c, 0, j)) for c in (1, 2)]
        + [pl.BlockSpec((rows, heads), lambda j, o: (1, 0)), small],
        (
            struct((rows, width), BF16),
            struct((rows, width), BF16),
            struct((chunks, heads, size, size), F32),
            struct(state.shape, F32),
            struct(state.shape, BF16),
        ),
        [
            wide,
            wide,
            pl.BlockSpec((chunks, group, size, size), lambda j, o: (0, j, 0, 0)),
            small,
            small,
        ],
        4 * rows * depth * width,
        scratch=[pltpu.VMEM((rows, depth), BF16)],
    )


def later_kernel(chunk, group, size, _, *refs):
    xa, xb, wq, acc_q, k_ref, v_ref, along_ref, inside_ref, mid_ref, q_ref, within_ref, held = refs
    j = pl.program_id(0)
    rows = held.shape[0]

    @pl.when(j == 0)
    def _():
        held[: rows // 2, :] = xa[...]
        held[rows // 2 :, :] = xb[...]

    q_all = (acc_q[0] + dot(held[...], wq[0])).astype(BF16)
    q_ref[...] = q_all
    for a in range(group):
        head = j * group + a
        lanes = slice(a * size, (a + 1) * size)
        for c in range(rows // chunk):
            here = slice(c * chunk, (c + 1) * chunk)
            within_ref[here, lanes] = scores(
                q_all[here, lanes],
                k_ref[here, lanes],
                v_ref[here, lanes],
                along_ref[pl.ds(head, 1), here],
                column(inside_ref[here, :], head),
                mid_ref[c, a],
            )


def later_call(places, far, w_qkv, acc, k, v, along, inside, mid, group):
    _, rows, width = acc.shape
    chunks, heads, size = mid.shape[0], mid.shape[1], mid.shape[2]
    chunk = rows // chunks
    depth = far[0].shape[1]
    cols = group * size
    wide = pl.BlockSpec((rows, cols), lambda j, o: (0, j))
    return call(
        functools.partial(later_kernel, chunk, group, size),
        "later",
        heads // group,
        places,
        (*far, w_qkv, acc, k, v, along, inside, mid),
        [
            fixed(far[0].shape),
            fixed(far[1].shape),
            pl.BlockSpec((1, depth, cols), lambda j, o: (0, o[3], j)),
            pl.BlockSpec((1, rows, cols), lambda j, o: (0, 0, j)),
            wide,
            wide,
            pl.BlockSpec((heads, rows), lambda j, o: (0, 1)),
            pl.BlockSpec((rows, heads), lambda j, o: (1, 0)),
            pl.BlockSpec((chunks, group, size, size), lambda j, o: (0, j, 0, 0)),
        ],
        (struct((rows, width), BF16), struct((rows, width), F32)),
        [wide, wide],
        2 * rows * depth * width + 4 * rows * (chunk + size) * width,
        scratch=[pltpu.VMEM((rows, depth), BF16)],
    )


def normalise(rows, q_ref, within_ref, entering_ref, down_ref, normed_ref):
    heads, size = entering_ref.shape[0], entering_ref.shape[1]
    fade = jnp.exp(-down_ref[...])
    for a in range(heads):
        lanes = slice(a * size, (a + 1) * size)
        combined = within_ref[:, lanes] + dot(q_ref[:, lanes], entering_ref[a]) * fade[:, a : a + 1]
        power = jnp.mean(combined * combined, axis=1, keepdims=True)
        normed_ref[rows, lanes] = (combined * lax.rsqrt(power + 1e-06)).astype(BF16)


def head_kernel(_, q_ref, within_ref, entering_ref, down_ref, w_ref, normed_ref, *parts):
    tall = q_ref.shape[0]
    for p, part in enumerate(parts):

        @pl.when(pl.program_id(0) == p)
        def _(p=p, part=part):
            rows = slice(p * tall, (p + 1) * tall)
            normalise(rows, q_ref, within_ref, entering_ref, down_ref, normed_ref)
            part[...] = dot(normed_ref[rows, :], w_ref[...]).astype(BF16)


def head_call(places, block, q, within, entering, down, w_out, width, tile):
    rows, cols = q.shape
    heads = entering.shape[0]
    parts = rows // tile
    part = pl.BlockSpec((tile, cols), lambda i, o: (i, 0))
    return call(
        head_kernel,
        "heads",
        parts,
        places,
        (q, within, entering, down, w_out),
        [
            part,
            part,
            fixed(entering.shape),
            pl.BlockSpec((tile, heads), lambda i, o: (i, 0)),
            pl.BlockSpec((cols, width), lambda i, o: (0, o[block])),
        ],
        (struct((rows, cols), BF16), *[struct((tile, width), BF16)] * parts),
        [fixed((rows, cols))] + [fixed((tile, width))] * parts,
        2 * rows * cols * (width + 128),
        light=True,
    )


def near_kernel(
    _, q_ref, within_ref, entering_ref, down_ref, first_ref, w_ref, normed_ref, *out_refs
):
    far_refs, near_refs = out_refs[:2], out_refs[2:]
    tall = q_ref.shape[0]
    for p in range(2):
        rows = slice(p * tall, (p + 1) * tall)

        @pl.when(pl.program_id(0) == p)
        def _(p=p, rows=rows):
            normalise(rows, q_ref, within_ref, entering_ref, down_ref, normed_ref)
            far_refs[p][...] = dot(normed_ref[rows, :], w_ref[...]).astype(BF16)

        @pl.when(pl.program_id(0) == 2 + p)
        def _(p=p, rows=rows):
            near_refs[p][:tall, :] = dot(first_ref[rows, :], w_ref[...]).astype(BF16)
            near_refs[p][tall:, :] = dot(normed_ref[rows, :], w_ref[...]).astype(BF16)


def near_call(places, q, within, entering, down, first, w_out, width):
    rows, cols = q.shape
    tall = rows // 2
    heads = entering.shape[0]
    part = pl.BlockSpec((tall, cols), lambda i, o: (jnp.minimum(i, 1), 0))
    return call(
        near_kernel,
        "heads_near",
        4,
        places,
        (q, within, entering, down, first, w_out),
        [
            part,
            part,
            fixed(entering.shape),
            pl.BlockSpec((tall, heads), lambda i, o: (2 + jnp.minimum(i, 1), 0)),
            fixed((rows, cols)),
            pl.BlockSpec((cols, width), lambda i, o: (0, o[jnp.where(i < 2, 3, i - 1)])),
        ],
        (
            struct((rows, cols), BF16),
            struct((tall, width), BF16),
            struct((tall, width), BF16),
            struct((rows, width), BF16),
            struct((rows, width), BF16),
        ),
        [
            fixed((rows, cols)),
            fixed((tall, width)),
            fixed((tall, width)),
            fixed((rows, width)),
            fixed((rows, width)),
        ],
        2 * rows * cols * (3 * width + 128),
        light=True,
    )


def out_kernel(count, kept, _, *refs):
    w_ref, out_ref = refs[count], refs[-1]
    arrived = refs[count + 1 : -1]
    tall = refs[0].shape[0]
    for i in range(count):
        total = dot(refs[i][...], w_ref[...])
        for ref, which in zip(arrived, kept, strict=True):
            if i in which:
                at = which.index(i) * tall
                total = total + ref[at : at + tall, :].astype(F32)
        out_ref[i * tall : (i + 1) * tall, :] = total.astype(BF16)


def out_call(places, block, normed, tall, w_out, width, arrived=()):
    cols = normed[0][0].shape[1]
    rows = tall * len(normed)
    tile = min(width, 256)
    per = width // tile
    return call(
        functools.partial(out_kernel, len(normed), tuple(w for _, w in arrived)),
        "project_out",
        per,
        places,
        (*[n for n, _ in normed], w_out, *[a for a, _ in arrived]),
        [pl.BlockSpec((tall, cols), lambda j, o, at=at: (at, 0)) for _, at in normed]
        + [pl.BlockSpec((cols, tile), lambda j, o: (0, o[block] * per + j))]
        + [pl.BlockSpec((a.shape[0], tile), lambda j, o: (0, j)) for a, _ in arrived],
        (struct((rows, width), BF16),),
        [pl.BlockSpec((rows, tile), lambda j, o: (0, j))],
        2 * rows * cols * width,
        light=True,
    )[0]


def last_kernel(_, kept_ref, a_ref, b_ref, out_ref):
    tall = a_ref.shape[0]
    out_ref[:tall, :] = (kept_ref[:tall, :].astype(F32) + a_ref[...].astype(F32)).astype(BF16)
    out_ref[tall:, :] = (kept_ref[tall:, :].astype(F32) + b_ref[...].astype(F32)).astype(BF16)


def last_call(kept, a, b, half):
    rows, width = kept.shape
    tile = min(width, 256)
    pair = pl.BlockSpec((rows // 2, tile), lambda j, o: (half, j))
    quarter = pl.BlockSpec((rows // 4, tile), lambda j, o: (0, j))
    return call(
        last_kernel,
        "last_add",
        width // tile,
        jnp.zeros((1,), jnp.int32),
        (kept, a, b),
        [pair, quarter, quarter],
        (struct(kept.shape, BF16),),
        [pair],
        rows * width,
        aliases={1: 0},
    )[0]


def local(n_head, n_seq, tokens, w_qkv, w_out, decay_rate, prior_state):
    rows, width = tokens.shape
    heads, size = prior_state.shape[0], prior_state.shape[1]
    square = n_head == 4
    place = lax.axis_index("head").astype(jnp.int32)
    quarter = rows // 4
    group = 2 if heads % 2 == 0 else 1
    cols = group * size

    over_x = functools.partial(lax.ppermute, axis_name="head", perm=[(i, i ^ 1) for i in range(n_head)])
    over_y = functools.partial(lax.ppermute, axis_name="head", perm=[(i, i ^ 2) for i in range(n_head)])

    flips = (0, 1, 2, 3) if square else (0,)
    places = jnp.stack([place ^ f for f in flips])

    along, inside, down, tail = decay_call(decay_rate, quarter)
    tail = tail[:, 0]
    pos = lax.axis_index("seq")
    core = pos % 2
    n_chips = n_seq // 2
    swap = functools.partial(lax.ppermute, axis_name="seq", perm=[(i, i ^ 1) for i in range(n_seq)])

    def later(x, step):
        return lax.ppermute(x, "seq", perm=[(i, i + 2 * step) for i in range(n_seq - 2 * step)])

    tail_other = swap(tail)
    tail_chip = tail + tail_other
    tails = [later(tail_chip, s) for s in range(1, n_chips)]

    if square:
        q0, q1 = tokens[:quarter], tokens[quarter : 2 * quarter]
        x0, y1 = over_x(q0), over_y(q1)
        acc = part_call(places, (0,), [(tokens,)], w_qkv, 2 * quarter, 1, cols)
        rest = after(tokens, acc)
        q2, q3 = rest[2 * quarter : 3 * quarter], rest[3 * quarter :]
        x1, y0 = over_x(after(q1, acc)), over_y(after(q0, acc))
        fy0, fx1 = over_y(x0), over_x(y1)
        x2, y3 = over_x(after(q2, x1, y0, *tails)), over_y(after(q3, x1, y0, *tails))
        x3, y2 = over_x(after(q3, fy0, fx1)), over_y(after(q2, fy0, fx1))
        query_a, within_a, state = first_call(
            places,
            (0, 1, 2, 3),
            [(tokens,), (x0, x1), (y0, y1), (fy0, fx1)],
            w_qkv,
            along,
            inside,
            2 * quarter,
            quarter,
            size,
            group,
        )
        fy2, fx3 = over_y(after(x2, state)), over_x(after(y3, state))
        acc = part_call(
            places, (1, 2), [(x2, x3), (y2, y3)], w_qkv, 2 * quarter, 0, cols, before=acc
        )
        far = (fy2, fx3)
        k, v, mid, state, sent = state_call(
            places, far, w_qkv, acc, inside, state, quarter, group
        )
        query_b, within_b = later_call(
            places, far, w_qkv, acc, k, v, along, inside, mid, group
        )
    else:
        gathered = lax.all_gather(tokens, "head", axis=1, tiled=True)
        query, within, state = first_call(
            places,
            (),
            [(gathered,)],
            w_qkv,
            along,
            inside,
            rows,
            quarter,
            size,
            group,
        )
        sent = state.astype(BF16)

    other = swap(sent).astype(F32)
    first = jnp.where(core == 0, state, other)
    second = jnp.where(core == 0, other, state)
    tail_first = jnp.where(core == 0, tail, tail_other)
    tail_second = jnp.where(core == 0, tail_other, tail)
    share = heads // 2

    def mine(x):
        return lax.dynamic_slice_in_dim(x, core * share, share, 0)

    chip_state = (
        jnp.exp(-mine(tail_second))[:, None, None] * mine(first) + mine(second)
    ).astype(BF16)
    gap = jnp.zeros((share,), F32)
    chip_entering = jnp.zeros((share, size, size), F32)
    shifted = [later(chip_state, s) for s in range(1, n_chips)]
    if square:
        shifted = lax.optimization_barrier((*shifted, query_b, within_b))[: n_chips - 1]
    for s in range(1, n_chips):
        chip_entering += jnp.exp(-gap)[:, None, None] * shifted[s - 1].astype(F32)
        gap += mine(tails[s - 1])
    chip_entering += jnp.exp(-gap)[:, None, None] * mine(prior_state)
    there = swap(chip_entering.astype(BF16)).astype(F32)
    entering = jnp.concatenate(
        [jnp.where(core == 0, chip_entering, there), jnp.where(core == 0, there, chip_entering)]
    )
    entering = jnp.where(
        core == 0, entering, jnp.exp(-tail_first)[:, None, None] * entering + first
    ).astype(BF16)

    if not square:
        normed = head_call(places, 0, query, within, entering, down, w_out, width, quarter)[0]
        partial = dot(normed, w_out).astype(BF16)
        return lax.psum_scatter(partial, "head", scatter_dimension=1, tiled=True)

    na, far0, far1 = head_call(
        places, 3, query_a, within_a, entering, down, w_out, width, quarter
    )
    far0, far1 = over_x(far0), over_y(far1)
    nb, far2, far3, near_x, near_y = near_call(
        places, query_b, within_b, entering, down, na, w_out, width
    )
    far2, far3 = over_x(far2), over_y(far3)
    near_x, near_y = over_x(after(near_x, far0, far1)), over_y(after(near_y, far0, far1))

    def out(block, *parts, arrived=()):
        return out_call(places, block, parts, quarter, w_out, width, arrived)

    n0, n1, n2, n3 = (na, 0), (na, 1), (nb, 0), (nb, 1)
    sum_x1 = over_x(out(1, n1, arrived=[(far1, (0,))]))
    sum_y0 = over_y(out(2, n0, arrived=[(far0, (0,))]))
    sum_x3 = over_x(out(1, n3, arrived=[(far3, (0,))]))
    sum_y2 = over_y(out(2, n2, arrived=[(far2, (0,))]))
    kept = out(0, n0, n1, n2, n3, arrived=[(near_x, (0, 2)), (near_y, (1, 3))])
    kept = last_call(kept, sum_y0, sum_x1, 0)
    return last_call(kept, sum_y2, sum_x3, 1)


def solution(mesh):
    in_specs = (
        P("seq", "head"),
        P(None, None, "head"),
        P("head", None),
        P("head", "seq"),
        P("head", None, None),
    )
    body = functools.partial(local, mesh.shape["head"], mesh.shape["seq"])
    return jax.shard_map(
        body, mesh=mesh, in_specs=in_specs, out_specs=P("seq", "head"), check_vma=False
    )
```

```python
import functools

import jax
import jax.numpy as jnp
from jax import lax
from jax.experimental import pallas as pl
from jax.experimental.pallas import tpu as pltpu
from jax.sharding import PartitionSpec as P

BF16, F32 = jnp.bfloat16, jnp.float32
PARAMS = pltpu.CompilerParams(vmem_limit_bytes=60 * 1024 * 1024)


def dot(a, b, contract=((1,), (0,))):
    return lax.dot_general(a, b, (contract, ((), ())), preferred_element_type=F32)


def after(x, *earlier):
    return lax.optimization_barrier((x, *earlier))[0]


def struct(shape, dtype):
    return jax.ShapeDtypeStruct(shape, dtype)


def fixed(shape):
    return pl.BlockSpec(shape, lambda j, o: (0,) * len(shape))


def call(kernel, name, steps, scalars, ins, in_specs, outs, out_specs, flops, scratch=(), aliases=None, light=False):
    moved = sum(a.size * a.dtype.itemsize for a in ins) + sum(
        o.size * jnp.dtype(o.dtype).itemsize for o in outs
    )
    return pl.pallas_call(
        kernel,
        out_shape=tuple(outs),
        grid_spec=pltpu.PrefetchScalarGridSpec(
            num_scalar_prefetch=1,
            grid=(steps,),
            in_specs=in_specs,
            out_specs=out_specs,
            scratch_shapes=list(scratch),
        ),
        input_output_aliases=aliases or {},
        compiler_params=PARAMS,
        cost_estimate=pl.CostEstimate(
            flops=1 if light else flops, bytes_accessed=1 if light else moved, transcendentals=0
        ),
        name=name,
    )(scalars, *ins)


def cut_kernel(first, x_ref, a_ref, b_ref, sems):
    tall = a_ref.shape[0]
    copies = [
        pltpu.make_async_copy(x_ref.at[pl.ds((first + i) * tall, tall)], out, sems.at[i])
        for i, out in enumerate((a_ref, b_ref))
    ]
    for copy in copies:
        copy.start()
    for copy in copies:
        copy.wait()


def cut_call(x, first):
    rows, width = x.shape
    half = struct((rows // 4, width), x.dtype)
    return pl.pallas_call(
        functools.partial(cut_kernel, first),
        out_shape=(half, half),
        in_specs=[pl.BlockSpec(memory_space=pl.ANY)],
        out_specs=[pl.BlockSpec(memory_space=pl.ANY)] * 2,
        scratch_shapes=[pltpu.SemaphoreType.DMA((2,))],
        cost_estimate=pl.CostEstimate(flops=0, bytes_accessed=x.size * 2, transcendentals=0),
        name="cut",
    )(x)


def decay_kernel(chunk, _, rate_ref, along_ref, inside_ref, down_ref, tail_ref):
    heads, rows = rate_ref.shape
    lane = lax.broadcasted_iota(jnp.int32, (heads, chunk), 1)
    base = jnp.zeros((heads, 1), F32)
    insides, wholes = [], []
    for c in range(rows // chunk):
        x = rate_ref[:, c * chunk : (c + 1) * chunk]
        step = 1
        while step < chunk:
            x = x + jnp.where(lane >= step, pltpu.roll(x, step, 1), 0.0)
            step *= 2
        insides.append(x)
        wholes.append(x + base)
        base = base + x[:, chunk - 1 :]
    inside = jnp.concatenate(insides, axis=1)
    along_ref[...] = inside
    inside_ref[...] = inside.T
    down_ref[...] = jnp.concatenate(wholes, axis=1).T
    tail_ref[...] = jnp.broadcast_to(base, tail_ref.shape)


def decay_call(rate, chunk):
    heads, rows = rate.shape
    return call(
        functools.partial(decay_kernel, chunk),
        "decay",
        1,
        jnp.zeros((1,), jnp.int32),
        (rate,),
        [fixed((heads, rows))],
        (
            struct((heads, rows), F32),
            struct((rows, heads), F32),
            struct((rows, heads), F32),
            struct((heads, 128), F32),
        ),
        [fixed((heads, rows)), fixed((rows, heads)), fixed((rows, heads)), fixed((heads, 128))],
        heads * rows * 16,
    )


def column(table, head):
    lane = lax.broadcasted_iota(jnp.int32, table.shape, 1)
    return jnp.sum(jnp.where(lane == head, table, 0.0), axis=1, keepdims=True)


def scores(q, k, v, along, down, state):
    rows = q.shape[0]
    causal = lax.broadcasted_iota(jnp.int32, (rows, rows), 0) >= lax.broadcasted_iota(
        jnp.int32, (rows, rows), 1
    )
    decay = jnp.exp(jnp.minimum(along - down, 0.0))
    weights = jnp.where(causal, dot(q, k, ((1,), (1,))) * decay, 0.0).astype(BF16)
    return dot(weights, v) + dot(q, state.astype(BF16)) * jnp.exp(-down)


def advance(k, v, down, state):
    last = down[down.shape[0] - 1 :, :]
    scaled = (k.astype(F32) * jnp.exp(down - last)).astype(BF16)
    return jnp.exp(-last) * state + dot(scaled, v, ((0,), (0,)))


def first_kernel(layout, added, chunk, group, size, _, *refs):
    count = sum(layout)
    x_refs, w_refs, refs = refs[:count], refs[count : count + len(layout)], refs[count + len(layout) :]
    along_ref, inside_ref, q_ref, within_ref, state_ref, held = refs[-6:]
    j = pl.program_id(0)
    rows = held.shape[1]

    @pl.when(j == 0)
    def _():
        at = 0
        for i, parts in enumerate(layout):
            tall = rows // parts
            for p in range(parts):
                held[i, p * tall : (p + 1) * tall, :] = x_refs[at][...]
                at += 1

    def project(c):
        total = dot(held[0], w_refs[0][c])
        for i in range(1, len(layout)):
            total = total + dot(held[i], w_refs[i][c])
        if added:
            total = total + refs[0][c]
        return total.astype(BF16)

    q_all, k_all, v_all = project(0), project(1), project(2)
    q_ref[...] = q_all
    for a in range(group):
        head = j * group + a
        lanes = slice(a * size, (a + 1) * size)
        state = jnp.zeros((size, size), F32)
        for c in range(rows // chunk):
            here = slice(c * chunk, (c + 1) * chunk)
            q, k, v = q_all[here, lanes], k_all[here, lanes], v_all[here, lanes]
            down = column(inside_ref[here, :], head)
            along = along_ref[pl.ds(head, 1), here]
            within_ref[here, lanes] = scores(q, k, v, along, down, state)
            state = advance(k, v, down, state)
        state_ref[a] = state


def first_call(places, blocks, pieces, before, w_qkv, along, inside, rows, chunk, size, group):
    heads = along.shape[0]
    cols = group * size
    flat = [p for piece in pieces for p in piece]
    depth = flat[0].shape[1]

    def block(i):
        return pl.BlockSpec((3, depth, cols), lambda j, o: (0, o[blocks[i]] if blocks else 0, j))

    wide = pl.BlockSpec((rows, cols), lambda j, o: (0, j))
    return call(
        functools.partial(
            first_kernel, tuple(len(p) for p in pieces), bool(before), chunk, group, size
        ),
        "first",
        heads // group,
        places,
        (*flat, *[w_qkv] * len(pieces), *before, along, inside),
        [
            pl.BlockSpec((rows // len(piece), depth), lambda j, o: (0, 0))
            for piece in pieces
            for _ in piece
        ]
        + [block(i) for i in range(len(pieces))]
        + [pl.BlockSpec((3, rows, cols), lambda j, o: (0, 0, j)) for _ in before]
        + [fixed((heads, rows)), fixed((rows, heads))],
        (
            struct((rows, heads * size), BF16),
            struct((rows, heads * size), F32),
            struct((heads, size, size), F32),
        ),
        [wide, wide, pl.BlockSpec((group, size, size), lambda j, o: (j, 0, 0))],
        2 * rows * 3 * heads * size * depth * len(pieces),
        scratch=[pltpu.VMEM((len(pieces), rows, depth), BF16)],
    )


def part_kernel(layout, added, _, *refs):
    count = sum(layout)
    x_refs, w_refs = refs[:count], refs[count : count + len(layout)]
    out_ref, held = refs[-2], refs[-1]
    rows = held.shape[1]

    @pl.when(pl.program_id(0) == 0)
    def _():
        at = 0
        for i, parts in enumerate(layout):
            tall = rows // parts
            for p in range(parts):
                held[i, p * tall : (p + 1) * tall, :] = x_refs[at][...]
                at += 1

    for c in range(3):
        total = dot(held[0], w_refs[0][c])
        for i in range(1, len(layout)):
            total = total + dot(held[i], w_refs[i][c])
        if added:
            total = total + refs[-3][c]
        out_ref[c] = total


def part_call(places, blocks, pieces, w_qkv, rows, cols, before=None, at=0):
    flat = [p for piece in pieces for p in piece]
    depth = flat[0].shape[1]
    width = w_qkv.shape[2]

    def block(i):
        return pl.BlockSpec((3, depth, cols), lambda j, o: (0, o[blocks[i]], j))

    ins = [*flat, *[w_qkv] * len(pieces)]
    specs = [
        pl.BlockSpec((rows // len(piece), depth), lambda j, o: (0, 0)) for piece in pieces for _ in piece
    ] + [block(i) for i in range(len(pieces))]
    if before is not None:
        ins.append(before)
        specs.append(pl.BlockSpec((3, rows, cols), lambda j, o: (0, at, j)))
    return call(
        functools.partial(part_kernel, tuple(len(p) for p in pieces), before is not None),
        "part",
        width // cols,
        places,
        ins,
        specs,
        (struct((3, rows, width), F32),),
        [pl.BlockSpec((3, rows, cols), lambda j, o: (0, 0, j))],
        2 * rows * depth * len(pieces) * width * 3,
        scratch=[pltpu.VMEM((len(pieces), rows, depth), BF16)],
    )[0]


def state_kernel(chunk, group, size, _, *refs):
    xa, xb, wk, wv, acc_k, acc_v, inside_ref, state_ref = refs[:8]
    k_ref, v_ref, mid_ref, end_ref, sent_ref, held = refs[8:]
    j = pl.program_id(0)
    rows = held.shape[0]

    @pl.when(j == 0)
    def _():
        held[: rows // 2, :] = xa[...]
        held[rows // 2 :, :] = xb[...]

    k_all = (acc_k[0] + dot(held[...], wk[0])).astype(BF16)
    v_all = (acc_v[0] + dot(held[...], wv[0])).astype(BF16)
    k_ref[...] = k_all
    v_ref[...] = v_all
    for a in range(group):
        head = j * group + a
        lanes = slice(a * size, (a + 1) * size)
        state = state_ref[a]
        for c in range(rows // chunk):
            here = slice(c * chunk, (c + 1) * chunk)
            mid_ref[c, a] = state
            state = advance(
                k_all[here, lanes], v_all[here, lanes], column(inside_ref[here, :], head), state
            )
        end_ref[a] = state
        sent_ref[a] = state.astype(BF16)


def state_call(places, far, w_qkv, acc, inside, state, chunk, group):
    _, rows, width = acc.shape
    heads, size = state.shape[0], state.shape[1]
    depth = far[0].shape[1]
    cols = group * size
    wide = pl.BlockSpec((rows, cols), lambda j, o: (0, j))
    small = pl.BlockSpec((group, size, size), lambda j, o: (j, 0, 0))
    chunks = rows // chunk
    return call(
        functools.partial(state_kernel, chunk, group, size),
        "states",
        heads // group,
        places,
        (*far, w_qkv, w_qkv, acc, acc, inside, state),
        [fixed(far[0].shape), fixed(far[1].shape)]
        + [pl.BlockSpec((1, depth, cols), lambda j, o, c=c: (c, o[3], j)) for c in (1, 2)]
        + [pl.BlockSpec((1, rows, cols), lambda j, o, c=c: (c, 0, j)) for c in (1, 2)]
        + [pl.BlockSpec((rows, heads), lambda j, o: (1, 0)), small],
        (
            struct((rows, width), BF16),
            struct((rows, width), BF16),
            struct((chunks, heads, size, size), F32),
            struct(state.shape, F32),
            struct(state.shape, BF16),
        ),
        [
            wide,
            wide,
            pl.BlockSpec((chunks, group, size, size), lambda j, o: (0, j, 0, 0)),
            small,
            small,
        ],
        4 * rows * depth * width,
        scratch=[pltpu.VMEM((rows, depth), BF16)],
    )


def later_kernel(chunk, group, size, _, *refs):
    xa, xb, wq, acc_q, k_ref, v_ref, along_ref, inside_ref, mid_ref, q_ref, within_ref, held = refs
    j = pl.program_id(0)
    rows = held.shape[0]

    @pl.when(j == 0)
    def _():
        held[: rows // 2, :] = xa[...]
        held[rows // 2 :, :] = xb[...]

    q_all = (acc_q[0] + dot(held[...], wq[0])).astype(BF16)
    q_ref[...] = q_all
    for a in range(group):
        head = j * group + a
        lanes = slice(a * size, (a + 1) * size)
        for c in range(rows // chunk):
            here = slice(c * chunk, (c + 1) * chunk)
            within_ref[here, lanes] = scores(
                q_all[here, lanes],
                k_ref[here, lanes],
                v_ref[here, lanes],
                along_ref[pl.ds(head, 1), here],
                column(inside_ref[here, :], head),
                mid_ref[c, a],
            )


def later_call(places, far, w_qkv, acc, k, v, along, inside, mid, group):
    _, rows, width = acc.shape
    chunks, heads, size = mid.shape[0], mid.shape[1], mid.shape[2]
    chunk = rows // chunks
    depth = far[0].shape[1]
    cols = group * size
    wide = pl.BlockSpec((rows, cols), lambda j, o: (0, j))
    return call(
        functools.partial(later_kernel, chunk, group, size),
        "later",
        heads // group,
        places,
        (*far, w_qkv, acc, k, v, along, inside, mid),
        [
            fixed(far[0].shape),
            fixed(far[1].shape),
            pl.BlockSpec((1, depth, cols), lambda j, o: (0, o[3], j)),
            pl.BlockSpec((1, rows, cols), lambda j, o: (0, 0, j)),
            wide,
            wide,
            pl.BlockSpec((heads, rows), lambda j, o: (0, 1)),
            pl.BlockSpec((rows, heads), lambda j, o: (1, 0)),
            pl.BlockSpec((chunks, group, size, size), lambda j, o: (0, j, 0, 0)),
        ],
        (struct((rows, width), BF16), struct((rows, width), F32)),
        [wide, wide],
        2 * rows * depth * width + 4 * rows * (chunk + size) * width,
        scratch=[pltpu.VMEM((rows, depth), BF16)],
    )


def head_kernel(_, q_ref, within_ref, entering_ref, down_ref, w_ref, normed_ref, *out_refs):
    heads, size = entering_ref.shape[0], entering_ref.shape[1]
    tall = q_ref.shape[0]
    for p, out_ref in enumerate(out_refs):
        rows = slice(p * tall, (p + 1) * tall)

        @pl.when(pl.program_id(0) == p)
        def _(rows=rows, out_ref=out_ref):
            fade = jnp.exp(-down_ref[...])
            for a in range(heads):
                lanes = slice(a * size, (a + 1) * size)
                seen = dot(q_ref[:, lanes], entering_ref[a]) * fade[:, a : a + 1]
                combined = within_ref[:, lanes] + seen
                power = jnp.mean(combined * combined, axis=1, keepdims=True)
                normed_ref[rows, lanes] = (combined * lax.rsqrt(power + 1e-06)).astype(BF16)
            out_ref[...] = dot(normed_ref[rows, :], w_ref[...]).astype(BF16)


def head_call(places, block, q, within, entering, down, w_out, width, at):
    rows, cols = q.shape
    tall = rows // 2
    heads = entering.shape[0]
    part = pl.BlockSpec((tall, cols), lambda i, o: (i, 0))
    return call(
        head_kernel,
        "heads",
        2,
        places,
        (q, within, entering, down, w_out),
        [
            part,
            part,
            fixed(entering.shape),
            pl.BlockSpec((tall, heads), lambda i, o: (2 * at + i, 0)),
            pl.BlockSpec((cols, width), lambda i, o: (0, o[block])),
        ],
        (struct((rows, cols), BF16), *[struct((tall, width), BF16)] * 2),
        [fixed((rows, cols))] + [fixed((tall, width))] * 2,
        2 * rows * cols * (width + 128),
        light=True,
    )


def heads_near_kernel(_, q_ref, within_ref, entering_ref, down_ref, first_ref, w_ref, normed_ref, *out_refs):
    tall = q_ref.shape[0]
    head_kernel(_, q_ref, within_ref, entering_ref, down_ref, w_ref, normed_ref, *out_refs[:2])
    for p, out_ref in enumerate(out_refs[2:]):
        rows = slice(p * tall, (p + 1) * tall)

        @pl.when(pl.program_id(0) == 2 + p)
        def _(rows=rows, out_ref=out_ref):
            out_ref[:tall, :] = dot(first_ref[rows, :], w_ref[...]).astype(BF16)
            out_ref[tall:, :] = dot(normed_ref[rows, :], w_ref[...]).astype(BF16)


def heads_near_call(places, q, within, entering, down, normed_a, w_out, width):
    rows, cols = q.shape
    tall = rows // 2
    heads = entering.shape[0]
    part = pl.BlockSpec((tall, cols), lambda i, o: (jnp.minimum(i, 1), 0))
    quarter, half = (tall, width), (rows, width)
    return call(
        heads_near_kernel,
        "heads_near",
        4,
        places,
        (q, within, entering, down, normed_a, w_out),
        [
            part,
            part,
            fixed(entering.shape),
            pl.BlockSpec((tall, heads), lambda i, o: (2 + jnp.minimum(i, 1), 0)),
            fixed((rows, cols)),
            pl.BlockSpec((cols, width), lambda i, o: (0, o[jnp.where(i < 2, 3, i - 1)])),
        ],
        (struct((rows, cols), BF16), *[struct(quarter, BF16)] * 2, *[struct(half, BF16)] * 2),
        [fixed((rows, cols)), fixed(quarter), fixed(quarter), fixed(half), fixed(half)],
        2 * rows * cols * (3 * width + 128),
        light=True,
    )


def pair_kernel(_, normed_ref, x_ref, y_ref, w_ref, out_x_ref, out_y_ref):
    tall = x_ref.shape[0]

    @pl.when(pl.program_id(0) == 0)
    def _():
        out_x_ref[...] = (dot(normed_ref[tall:, :], w_ref[...]) + x_ref[...].astype(F32)).astype(BF16)

    @pl.when(pl.program_id(0) == 1)
    def _():
        out_y_ref[...] = (dot(normed_ref[:tall, :], w_ref[...]) + y_ref[...].astype(F32)).astype(BF16)


def pair_call(places, normed, for_x, for_y, w_out, width):
    rows, cols = normed.shape
    quarter = (rows // 2, width)
    return call(
        pair_kernel,
        "sum_pair",
        2,
        places,
        (normed, for_x, for_y, w_out),
        [
            fixed((rows, cols)),
            fixed(quarter),
            fixed(quarter),
            pl.BlockSpec((cols, width), lambda i, o: (0, o[1 + i])),
        ],
        (struct(quarter, BF16),) * 2,
        [fixed(quarter)] * 2,
        2 * rows * cols * width,
        light=True,
    )


def own_kernel(_, normed_ref, w_ref, *refs):
    out_ref = refs[-1]
    tall = out_ref.shape[0]
    each = len(refs) // 2
    for p in range(2):
        rows = slice(p * tall, (p + 1) * tall)

        @pl.when(pl.program_id(0) == p)
        def _(p=p, rows=rows):
            total = dot(normed_ref[rows, :], w_ref[...])
            for ref in refs[p * each : (p + 1) * each]:
                total = total + ref[...].astype(F32)
            out_ref[...] = total.astype(BF16)


def own_call(places, normed, first, second, w_out, width, height):
    rows, cols = normed.shape
    quarter = (rows // 2, width)
    return call(
        own_kernel,
        "own_block",
        2,
        places,
        (normed, w_out, *[a for a, _ in (*first, *second)]),
        [fixed((rows, cols)), pl.BlockSpec((cols, width), lambda i, o: (0, o[0]))]
        + [pl.BlockSpec(quarter, lambda i, o, at=at: (at, 0)) for _, at in (*first, *second)],
        (struct((rows * height, width), BF16),),
        [pl.BlockSpec(quarter, lambda i, o: (i, 0))],
        2 * rows * cols * width,
        light=True,
    )[0]


def last_kernel(_, kept_ref, a_ref, b_ref, above_ref, out_ref):
    del above_ref

    @pl.when(pl.program_id(0) == 0)
    def _():
        out_ref[...] = (kept_ref[...].astype(F32) + a_ref[...].astype(F32)).astype(BF16)

    @pl.when(pl.program_id(0) == 1)
    def _():
        out_ref[...] = (kept_ref[...].astype(F32) + b_ref[...].astype(F32)).astype(BF16)


def last_call(kept, a, b, above):
    tall, width = a.shape
    return call(
        last_kernel,
        "last_add",
        2,
        jnp.zeros((1,), jnp.int32),
        (kept, a, b, above),
        [
            pl.BlockSpec((tall, width), lambda j, o: (j, 0)),
            fixed((tall, width)),
            fixed((tall, width)),
            pl.BlockSpec(memory_space=pl.ANY),
        ],
        (struct(above.shape, BF16),),
        [pl.BlockSpec((tall, width), lambda j, o: (2 + j, 0))],
        tall * width,
        aliases={4: 0},
    )[0]


def local(n_head, n_seq, tokens, w_qkv, w_out, decay_rate, prior_state):
    rows, width = tokens.shape
    heads, size = prior_state.shape[0], prior_state.shape[1]
    square = n_head == 4
    place = lax.axis_index("head").astype(jnp.int32)
    quarter = rows // 4
    group = 2 if heads % 2 == 0 else 1
    cols = group * size

    over_x = functools.partial(lax.ppermute, axis_name="head", perm=[(i, i ^ 1) for i in range(n_head)])
    over_y = functools.partial(lax.ppermute, axis_name="head", perm=[(i, i ^ 2) for i in range(n_head)])

    flips = (0, 1, 2, 3) if square else (0,)
    places = jnp.stack([place ^ f for f in flips])

    along, inside, down, tail = decay_call(decay_rate, quarter)
    tail = tail[:, 0]
    pos = lax.axis_index("seq")
    core, chip = pos % 2, pos // 2
    swap = functools.partial(lax.ppermute, axis_name="seq", perm=[(i, i ^ 1) for i in range(n_seq)])
    tail_other = swap(tail)

    if square:
        q0, q1 = cut_call(tokens, 0)
        x0, y1, x1, y0 = over_x(q0), over_y(q1), over_x(q1), over_y(q0)
        acc = part_call(places, (0,), [(tokens,)], w_qkv, rows, cols)
        q2, q3 = cut_call(after(tokens, acc), 2)
        fy0, fx1 = over_y(x0), over_x(y1)
        x2, y3 = over_x(after(q2, x1, y0)), over_y(after(q3, x1, y0))
        acc_a = part_call(
            places, (1, 2), [(x0, x1), (y0, y1)], w_qkv, 2 * quarter, cols, before=acc, at=0
        )
        x3, y2 = over_x(after(q3, fy0, fx1, acc_a)), over_y(after(q2, fy0, fx1, acc_a))
        query_a, within_a, state = first_call(
            places,
            (3,),
            [(fy0, fx1)],
            (acc_a,),
            w_qkv,
            along,
            inside,
            2 * quarter,
            quarter,
            size,
            group,
        )
        fy2, fx3 = over_y(after(x2, state)), over_x(after(y3, state))
        acc_b = part_call(
            places, (1, 2), [(x2, x3), (y2, y3)], w_qkv, 2 * quarter, cols, before=acc, at=1
        )
        far = (fy2, fx3)
        k, v, mid, state, sent = state_call(
            places, far, w_qkv, acc_b, inside, state, quarter, group
        )
    else:
        gathered = lax.all_gather(tokens, "head", axis=1, tiled=True)
        query, within, state = first_call(
            places, (), [(gathered,)], (), w_qkv, along, inside, rows, quarter, size, group
        )
        sent = state.astype(BF16)

    other = swap(sent).astype(F32)
    first = jnp.where(core == 0, state, other)
    second = jnp.where(core == 0, other, state)
    tail_first = jnp.where(core == 0, tail, tail_other)
    tail_second = jnp.where(core == 0, tail_other, tail)
    share = heads // 2

    def mine(x):
        return lax.dynamic_slice_in_dim(x, core * share, share, 0)

    chip_state = jnp.exp(-mine(tail_second))[:, None, None] * mine(first) + mine(second)
    chip_decay = jnp.exp(-mine(tail + tail_other))[:, None, None]
    chip_entering = mine(prior_state)
    hops = n_seq // 2 - 1
    for hop in range(hops):
        leaving = (chip_decay * chip_entering + chip_state).astype(BF16)
        arriving = lax.ppermute(
            leaving, "seq", perm=[(2 * hop + c, 2 * hop + 2 + c) for c in range(2)]
        )
        if square and hop == hops // 2:
            query_b, within_b = later_call(
                places, far, w_qkv, acc_b, k, v, along, inside, after(mid, leaving), group
            )
            arriving = after(arriving, query_b, within_b)
        chip_entering = jnp.where(chip == hop + 1, arriving.astype(F32), chip_entering)
    there = swap(chip_entering.astype(BF16)).astype(F32)
    entering = jnp.concatenate(
        [jnp.where(core == 0, chip_entering, there), jnp.where(core == 0, there, chip_entering)]
    )
    entering = jnp.where(
        core == 0, entering, jnp.exp(-tail_first)[:, None, None] * entering + first
    ).astype(BF16)

    if not square:
        halves = [
            head_call(
                places,
                0,
                query[r * rows // 2 : (r + 1) * rows // 2],
                within[r * rows // 2 : (r + 1) * rows // 2],
                entering,
                down,
                w_out,
                width,
                r,
            )[0]
            for r in range(2)
        ]
        partial = dot(jnp.concatenate(halves), w_out).astype(BF16)
        return lax.psum_scatter(partial, "head", scatter_dimension=1, tiled=True)

    na, far0, far1 = head_call(places, 3, query_a, within_a, entering, down, w_out, width, 0)
    far0, far1 = over_x(far0), over_y(far1)
    nb, far2, far3, near_x, near_y = heads_near_call(
        places, query_b, within_b, entering, down, na, w_out, width
    )
    near_x, near_y = over_x(after(near_x, far0, far1)), over_y(after(near_y, far0, far1))
    far2, far3 = over_x(far2), over_y(far3)
    sum1, sum0 = pair_call(places, after(na, near_x, near_y), far1, far0, w_out, width)
    far2, far3 = after(far2, sum1), after(far3, sum1)
    sum1, sum0 = over_x(sum1), over_y(sum0)
    sum3, sum2 = pair_call(places, nb, far3, far2, w_out, width)
    sum3, sum2 = over_x(sum3), over_y(sum2)
    below = own_call(places, nb, ((near_x, 1),), ((near_y, 1),), w_out, width, 1)
    above = own_call(
        places, na, ((near_x, 0), (sum0, 0)), ((near_y, 0), (sum1, 0)), w_out, width, 2
    )
    return last_call(below, sum2, sum3, above)


def solution(mesh):
    in_specs = (
        P("seq", "head"),
        P(None, None, "head"),
        P("head", None),
        P("head", "seq"),
        P("head", None, None),
    )
    body = functools.partial(local, mesh.shape["head"], mesh.shape["seq"])
    return jax.shard_map(
        body, mesh=mesh, in_specs=in_specs, out_specs=P("seq", "head"), check_vma=False
    )
```

```python
import functools
import math

import jax
import jax.numpy as jnp
from jax import lax
from jax.experimental import pallas as pl
from jax.experimental.pallas import tpu as pltpu
from jax.sharding import PartitionSpec as P

BF16, F32 = jnp.bfloat16, jnp.float32
MIB = 1024 * 1024


def dot(a, b, contract=((1,), (0,))):
    return lax.dot_general(a, b, (contract, ((), ())), preferred_element_type=F32)


def after(x, *earlier):
    return lax.optimization_barrier((x, *earlier))[0]


def struct(shape, dtype):
    return jax.ShapeDtypeStruct(shape, dtype)


def fixed(shape):
    return pl.BlockSpec(shape, lambda j, o: (0,) * len(shape))


def call(kernel, name, steps, scalars, ins, in_specs, outs, out_specs, flops, scratch=(), aliases=None, light=False):
    moved = sum(a.size * a.dtype.itemsize for a in ins) + sum(
        math.prod(o.shape) * jnp.dtype(o.dtype).itemsize for o in outs
    )
    return pl.pallas_call(
        kernel,
        out_shape=tuple(outs),
        grid_spec=pltpu.PrefetchScalarGridSpec(
            num_scalar_prefetch=1,
            grid=(steps,),
            in_specs=in_specs,
            out_specs=out_specs,
            scratch_shapes=list(scratch),
        ),
        input_output_aliases=aliases or {},
        compiler_params=pltpu.CompilerParams(vmem_limit_bytes=(24 if light else 32) * MIB),
        cost_estimate=pl.CostEstimate(
            flops=1 if light else flops, bytes_accessed=1 if light else moved, transcendentals=0
        ),
        name=name,
    )(scalars, *ins)


def cut_kernel(_, x_ref, a_ref, b_ref):
    tall = a_ref.shape[0]
    a_ref[...] = x_ref[:tall, :]
    b_ref[...] = x_ref[tall:, :]


def cut_call(x):
    rows, width = x.shape
    quarter = (rows // 4, width)
    return call(
        cut_kernel,
        "cut",
        1,
        jnp.zeros((1,), jnp.int32),
        (x,),
        [fixed((rows // 2, width))],
        (struct(quarter, x.dtype),) * 2,
        [fixed(quarter)] * 2,
        1,
    )


def decay_kernel(chunk, _, rate_ref, along_ref, inside_ref, down_ref, tail_ref):
    heads, rows = rate_ref.shape
    lane = lax.broadcasted_iota(jnp.int32, (heads, chunk), 1)
    base = jnp.zeros((heads, 1), F32)
    insides, wholes = [], []
    for c in range(rows // chunk):
        x = rate_ref[:, c * chunk : (c + 1) * chunk]
        step = 1
        while step < chunk:
            x = x + jnp.where(lane >= step, pltpu.roll(x, step, 1), 0.0)
            step *= 2
        insides.append(x)
        wholes.append(x + base)
        base = base + x[:, chunk - 1 :]
    inside = jnp.concatenate(insides, axis=1)
    along_ref[...] = inside
    inside_ref[...] = inside.T
    down_ref[...] = jnp.concatenate(wholes, axis=1).T
    tail_ref[...] = jnp.broadcast_to(base, tail_ref.shape)


def decay_call(rate, chunk):
    heads, rows = rate.shape
    return call(
        functools.partial(decay_kernel, chunk),
        "decay",
        1,
        jnp.zeros((1,), jnp.int32),
        (rate,),
        [fixed((heads, rows))],
        (
            struct((heads, rows), F32),
            struct((rows, heads), F32),
            struct((rows, heads), F32),
            struct((heads, 128), F32),
        ),
        [fixed((heads, rows)), fixed((rows, heads)), fixed((rows, heads)), fixed((heads, 128))],
        heads * rows * 16,
    )


def column(table, head):
    lane = lax.broadcasted_iota(jnp.int32, table.shape, 1)
    return jnp.sum(jnp.where(lane == head, table, 0.0), axis=1, keepdims=True)


def scores(q, k, v, along, down, state):
    rows = q.shape[0]
    causal = lax.broadcasted_iota(jnp.int32, (rows, rows), 0) >= lax.broadcasted_iota(
        jnp.int32, (rows, rows), 1
    )
    decay = jnp.exp(jnp.minimum(along - down, 0.0))
    weights = jnp.where(causal, dot(q, k, ((1,), (1,))) * decay, 0.0).astype(BF16)
    return dot(weights, v) + dot(q, state.astype(BF16)) * jnp.exp(-down)


def advance(k, v, down, state):
    last = down[down.shape[0] - 1 :, :]
    scaled = (k.astype(F32) * jnp.exp(down - last)).astype(BF16)
    return jnp.exp(-last) * state + dot(scaled, v, ((0,), (0,)))


def first_kernel(layout, added, chunk, group, size, _, *refs):
    count = sum(layout)
    x_refs, w_refs, refs = refs[:count], refs[count : count + len(layout)], refs[count + len(layout) :]
    along_ref, inside_ref, q_ref, within_ref, state_ref, held = refs[-6:]
    j = pl.program_id(0)
    rows = held.shape[1]

    @pl.when(j == 0)
    def _():
        at = 0
        for i, parts in enumerate(layout):
            tall = rows // parts
            for p in range(parts):
                held[i, p * tall : (p + 1) * tall, :] = x_refs[at][...]
                at += 1

    def project(c):
        total = dot(held[0], w_refs[0][c])
        for i in range(1, len(layout)):
            total = total + dot(held[i], w_refs[i][c])
        if added:
            total = total + refs[0][c]
        return total.astype(BF16)

    q_all, k_all, v_all = project(0), project(1), project(2)
    q_ref[...] = q_all
    for a in range(group):
        head = j * group + a
        lanes = slice(a * size, (a + 1) * size)
        state = jnp.zeros((size, size), F32)
        for c in range(rows // chunk):
            here = slice(c * chunk, (c + 1) * chunk)
            q, k, v = q_all[here, lanes], k_all[here, lanes], v_all[here, lanes]
            down = column(inside_ref[here, :], head)
            along = along_ref[pl.ds(head, 1), here]
            within_ref[here, lanes] = scores(q, k, v, along, down, state)
            state = advance(k, v, down, state)
        state_ref[a] = state


def first_call(places, blocks, pieces, before, w_qkv, along, inside, rows, chunk, size, group):
    heads = along.shape[0]
    cols = group * size
    flat = [p for piece in pieces for p in piece]
    depth = flat[0].shape[1]

    def block(i):
        return pl.BlockSpec((3, depth, cols), lambda j, o: (0, o[blocks[i]] if blocks else 0, j))

    wide = pl.BlockSpec((rows, cols), lambda j, o: (0, j))
    return call(
        functools.partial(
            first_kernel, tuple(len(p) for p in pieces), bool(before), chunk, group, size
        ),
        "first",
        heads // group,
        places,
        (*flat, *[w_qkv] * len(pieces), *before, along, inside),
        [
            pl.BlockSpec((rows // len(piece), depth), lambda j, o: (0, 0))
            for piece in pieces
            for _ in piece
        ]
        + [block(i) for i in range(len(pieces))]
        + [pl.BlockSpec((3, rows, cols), lambda j, o: (0, 0, j)) for _ in before]
        + [fixed((heads, rows)), fixed((rows, heads))],
        (
            pltpu.HBM((rows, heads * size), BF16),
            pltpu.HBM((rows, heads * size), F32),
            struct((heads, size, size), F32),
        ),
        [wide, wide, pl.BlockSpec((group, size, size), lambda j, o: (j, 0, 0))],
        2 * rows * 3 * heads * size * depth * len(pieces),
        scratch=[pltpu.VMEM((len(pieces), rows, depth), BF16)],
    )


def own_part_kernel(_, x_ref, w_ref, out_ref, c_ref, d_ref):
    rows = x_ref.shape[0]
    tall = c_ref.shape[0]

    @pl.when(pl.program_id(0) == 0)
    def _():
        c_ref[...] = x_ref[rows - 2 * tall : rows - tall, :]
        d_ref[...] = x_ref[rows - tall :, :]

    for c in range(3):
        out_ref[c] = dot(x_ref[...], w_ref[c])


def own_part_call(places, tokens, w_qkv, cols):
    rows, depth = tokens.shape
    width = w_qkv.shape[2]
    quarter = (rows // 4, depth)
    return call(
        own_part_kernel,
        "own_part",
        width // cols,
        places,
        (tokens, w_qkv),
        [fixed((rows, depth)), pl.BlockSpec((3, depth, cols), lambda j, o: (0, o[0], j))],
        (pltpu.HBM((3, rows, width), F32), struct(quarter, BF16), struct(quarter, BF16)),
        [pl.BlockSpec((3, rows, cols), lambda j, o: (0, 0, j)), fixed(quarter), fixed(quarter)],
        2 * rows * depth * width * 3,
    )


def part_kernel(layout, added, _, *refs):
    count = sum(layout)
    x_refs, w_refs = refs[:count], refs[count : count + len(layout)]
    out_ref, held = refs[-2], refs[-1]
    rows = held.shape[1]

    @pl.when(pl.program_id(0) == 0)
    def _():
        at = 0
        for i, parts in enumerate(layout):
            tall = rows // parts
            for p in range(parts):
                held[i, p * tall : (p + 1) * tall, :] = x_refs[at][...]
                at += 1

    for c in range(3):
        total = dot(held[0], w_refs[0][c])
        for i in range(1, len(layout)):
            total = total + dot(held[i], w_refs[i][c])
        if added:
            total = total + refs[-3][c]
        out_ref[c] = total


def part_call(places, blocks, pieces, w_qkv, rows, cols, before=None, at=0):
    flat = [p for piece in pieces for p in piece]
    depth = flat[0].shape[1]
    width = w_qkv.shape[2]

    def block(i):
        return pl.BlockSpec((3, depth, cols), lambda j, o: (0, o[blocks[i]], j))

    ins = [*flat, *[w_qkv] * len(pieces)]
    specs = [
        pl.BlockSpec((rows // len(piece), depth), lambda j, o: (0, 0)) for piece in pieces for _ in piece
    ] + [block(i) for i in range(len(pieces))]
    if before is not None:
        ins.append(before)
        specs.append(pl.BlockSpec((3, rows, cols), lambda j, o: (0, at, j)))
    return call(
        functools.partial(part_kernel, tuple(len(p) for p in pieces), before is not None),
        "part",
        width // cols,
        places,
        ins,
        specs,
        (struct((3, rows, width), F32),),
        [pl.BlockSpec((3, rows, cols), lambda j, o: (0, 0, j))],
        2 * rows * depth * len(pieces) * width * 3,
        scratch=[pltpu.VMEM((len(pieces), rows, depth), BF16)],
    )[0]


def state_kernel(chunk, group, size, _, *refs):
    xa, xb, wk, wv, acc_k, acc_v, inside_ref, state_ref = refs[:8]
    k_ref, v_ref, mid_ref, end_ref, sent_ref, held = refs[8:]
    j = pl.program_id(0)
    rows = held.shape[0]

    @pl.when(j == 0)
    def _():
        held[: rows // 2, :] = xa[...]
        held[rows // 2 :, :] = xb[...]

    k_all = (acc_k[0] + dot(held[...], wk[0])).astype(BF16)
    v_all = (acc_v[0] + dot(held[...], wv[0])).astype(BF16)
    k_ref[...] = k_all
    v_ref[...] = v_all
    for a in range(group):
        head = j * group + a
        lanes = slice(a * size, (a + 1) * size)
        state = state_ref[a]
        for c in range(rows // chunk):
            here = slice(c * chunk, (c + 1) * chunk)
            mid_ref[c, a] = state
            state = advance(
                k_all[here, lanes], v_all[here, lanes], column(inside_ref[here, :], head), state
            )
        end_ref[a] = state
        sent_ref[a] = state.astype(BF16)


def state_call(places, far, w_qkv, acc, inside, state, chunk, group):
    _, rows, width = acc.shape
    heads, size = state.shape[0], state.shape[1]
    depth = far[0].shape[1]
    cols = group * size
    wide = pl.BlockSpec((rows, cols), lambda j, o: (0, j))
    small = pl.BlockSpec((group, size, size), lambda j, o: (j, 0, 0))
    chunks = rows // chunk
    return call(
        functools.partial(state_kernel, chunk, group, size),
        "states",
        heads // group,
        places,
        (*far, w_qkv, w_qkv, acc, acc, inside, state),
        [fixed(far[0].shape), fixed(far[1].shape)]
        + [pl.BlockSpec((1, depth, cols), lambda j, o, c=c: (c, o[3], j)) for c in (1, 2)]
        + [pl.BlockSpec((1, rows, cols), lambda j, o, c=c: (c, 0, j)) for c in (1, 2)]
        + [pl.BlockSpec((rows, heads), lambda j, o: (1, 0)), small],
        (
            pltpu.HBM((rows, width), BF16),
            pltpu.HBM((rows, width), BF16),
            pltpu.HBM((chunks, heads, size, size), F32),
            struct(state.shape, F32),
            struct(state.shape, BF16),
        ),
        [
            wide,
            wide,
            pl.BlockSpec((chunks, group, size, size), lambda j, o: (0, j, 0, 0)),
            small,
            small,
        ],
        4 * rows * depth * width,
        scratch=[pltpu.VMEM((rows, depth), BF16)],
    )


def later_kernel(chunk, group, size, _, *refs):
    xa, xb, wq, acc_q, k_ref, v_ref, along_ref, inside_ref, mid_ref, q_ref, within_ref, held = refs
    j = pl.program_id(0)
    rows = held.shape[0]

    @pl.when(j == 0)
    def _():
        held[: rows // 2, :] = xa[...]
        held[rows // 2 :, :] = xb[...]

    q_all = (acc_q[0] + dot(held[...], wq[0])).astype(BF16)
    q_ref[...] = q_all
    for a in range(group):
        head = j * group + a
        lanes = slice(a * size, (a + 1) * size)
        for c in range(rows // chunk):
            here = slice(c * chunk, (c + 1) * chunk)
            within_ref[here, lanes] = scores(
                q_all[here, lanes],
                k_ref[here, lanes],
                v_ref[here, lanes],
                along_ref[pl.ds(head, 1), here],
                column(inside_ref[here, :], head),
                mid_ref[c, a],
            )


def later_call(places, far, w_qkv, acc, k, v, along, inside, mid, group):
    _, rows, width = acc.shape
    chunks, heads, size = mid.shape[0], mid.shape[1], mid.shape[2]
    chunk = rows // chunks
    depth = far[0].shape[1]
    cols = group * size
    wide = pl.BlockSpec((rows, cols), lambda j, o: (0, j))
    return call(
        functools.partial(later_kernel, chunk, group, size),
        "later",
        heads // group,
        places,
        (*far, w_qkv, acc, k, v, along, inside, mid),
        [
            fixed(far[0].shape),
            fixed(far[1].shape),
            pl.BlockSpec((1, depth, cols), lambda j, o: (0, o[3], j)),
            pl.BlockSpec((1, rows, cols), lambda j, o: (0, 0, j)),
            wide,
            wide,
            pl.BlockSpec((heads, rows), lambda j, o: (0, 1)),
            pl.BlockSpec((rows, heads), lambda j, o: (1, 0)),
            pl.BlockSpec((chunks, group, size, size), lambda j, o: (0, j, 0, 0)),
        ],
        (struct((rows, width), BF16), struct((rows, width), F32)),
        [wide, wide],
        2 * rows * depth * width + 4 * rows * (chunk + size) * width,
        scratch=[pltpu.VMEM((rows, depth), BF16)],
    )


def head_kernel(_, q_ref, within_ref, entering_ref, down_ref, w_ref, normed_ref, *out_refs):
    heads, size = entering_ref.shape[0], entering_ref.shape[1]
    tall = q_ref.shape[0]
    for p, out_ref in enumerate(out_refs):
        rows = slice(p * tall, (p + 1) * tall)

        @pl.when(pl.program_id(0) == p)
        def _(rows=rows, out_ref=out_ref):
            fade = jnp.exp(-down_ref[...])
            for a in range(heads):
                lanes = slice(a * size, (a + 1) * size)
                seen = dot(q_ref[:, lanes], entering_ref[a]) * fade[:, a : a + 1]
                combined = within_ref[:, lanes] + seen
                power = jnp.mean(combined * combined, axis=1, keepdims=True)
                normed_ref[rows, lanes] = (combined * lax.rsqrt(power + 1e-06)).astype(BF16)
            out_ref[...] = dot(normed_ref[rows, :], w_ref[...]).astype(BF16)


def head_call(places, block, q, within, entering, down, w_out, width, at):
    rows, cols = q.shape
    tall = rows // 2
    heads = entering.shape[0]
    part = pl.BlockSpec((tall, cols), lambda i, o: (i, 0))
    return call(
        head_kernel,
        "heads",
        2,
        places,
        (q, within, entering, down, w_out),
        [
            part,
            part,
            fixed(entering.shape),
            pl.BlockSpec((tall, heads), lambda i, o: (2 * at + i, 0)),
            pl.BlockSpec((cols, width), lambda i, o: (0, o[block])),
        ],
        (struct((rows, cols), BF16), *[struct((tall, width), BF16)] * 2),
        [fixed((rows, cols))] + [fixed((tall, width))] * 2,
        2 * rows * cols * (width + 128),
        light=True,
    )


def heads_near_kernel(_, q_ref, within_ref, entering_ref, down_ref, first_ref, w_ref, normed_ref, *out_refs):
    tall = q_ref.shape[0]
    head_kernel(_, q_ref, within_ref, entering_ref, down_ref, w_ref, normed_ref, *out_refs[:2])
    for p, out_ref in enumerate(out_refs[2:]):
        rows = slice(p * tall, (p + 1) * tall)

        @pl.when(pl.program_id(0) == 2 + p)
        def _(rows=rows, out_ref=out_ref):
            out_ref[:tall, :] = dot(first_ref[rows, :], w_ref[...]).astype(BF16)
            out_ref[tall:, :] = dot(normed_ref[rows, :], w_ref[...]).astype(BF16)


def heads_near_call(places, q, within, entering, down, normed_a, w_out, width):
    rows, cols = q.shape
    tall = rows // 2
    heads = entering.shape[0]
    part = pl.BlockSpec((tall, cols), lambda i, o: (jnp.minimum(i, 1), 0))
    quarter, half = (tall, width), (rows, width)
    return call(
        heads_near_kernel,
        "heads_near",
        4,
        places,
        (q, within, entering, down, normed_a, w_out),
        [
            part,
            part,
            fixed(entering.shape),
            pl.BlockSpec((tall, heads), lambda i, o: (2 + jnp.minimum(i, 1), 0)),
            fixed((rows, cols)),
            pl.BlockSpec((cols, width), lambda i, o: (0, o[jnp.where(i < 2, 3, i - 1)])),
        ],
        (struct((rows, cols), BF16), *[struct(quarter, BF16)] * 2, *[struct(half, BF16)] * 2),
        [fixed((rows, cols)), fixed(quarter), fixed(quarter), fixed(half), fixed(half)],
        2 * rows * cols * (3 * width + 128),
        light=True,
    )


def pair_kernel(_, normed_ref, x_ref, y_ref, w_ref, out_x_ref, out_y_ref):
    tall = x_ref.shape[0]

    @pl.when(pl.program_id(0) == 0)
    def _():
        out_x_ref[...] = (dot(normed_ref[tall:, :], w_ref[...]) + x_ref[...].astype(F32)).astype(BF16)

    @pl.when(pl.program_id(0) == 1)
    def _():
        out_y_ref[...] = (dot(normed_ref[:tall, :], w_ref[...]) + y_ref[...].astype(F32)).astype(BF16)


def pair_call(places, normed, for_x, for_y, w_out, width):
    rows, cols = normed.shape
    quarter = (rows // 2, width)
    return call(
        pair_kernel,
        "sum_pair",
        2,
        places,
        (normed, for_x, for_y, w_out),
        [
            fixed((rows, cols)),
            fixed(quarter),
            fixed(quarter),
            pl.BlockSpec((cols, width), lambda i, o: (0, o[1 + i])),
        ],
        (struct(quarter, BF16),) * 2,
        [fixed(quarter)] * 2,
        2 * rows * cols * width,
        light=True,
    )


def own_kernel(_, normed_ref, w_ref, *refs):
    out_ref = refs[-1]
    tall = out_ref.shape[0]
    each = len(refs) // 2
    for p in range(2):
        rows = slice(p * tall, (p + 1) * tall)

        @pl.when(pl.program_id(0) == p)
        def _(p=p, rows=rows):
            total = dot(normed_ref[rows, :], w_ref[...])
            for ref in refs[p * each : (p + 1) * each]:
                total = total + ref[...].astype(F32)
            out_ref[...] = total.astype(BF16)


def own_call(places, normed, first, second, w_out, width, height):
    rows, cols = normed.shape
    quarter = (rows // 2, width)
    return call(
        own_kernel,
        "own_block",
        2,
        places,
        (normed, w_out, *[a for a, _ in (*first, *second)]),
        [fixed((rows, cols)), pl.BlockSpec((cols, width), lambda i, o: (0, o[0]))]
        + [pl.BlockSpec(quarter, lambda i, o, at=at: (at, 0)) for _, at in (*first, *second)],
        (struct((rows * height, width), BF16),),
        [pl.BlockSpec(quarter, lambda i, o: (i, 0))],
        2 * rows * cols * width,
        light=True,
    )[0]


def last_kernel(_, kept_ref, a_ref, b_ref, above_ref, out_ref):
    del above_ref

    @pl.when(pl.program_id(0) == 0)
    def _():
        out_ref[...] = (kept_ref[...].astype(F32) + a_ref[...].astype(F32)).astype(BF16)

    @pl.when(pl.program_id(0) == 1)
    def _():
        out_ref[...] = (kept_ref[...].astype(F32) + b_ref[...].astype(F32)).astype(BF16)


def last_call(kept, a, b, above):
    tall, width = a.shape
    return call(
        last_kernel,
        "last_add",
        2,
        jnp.zeros((1,), jnp.int32),
        (kept, a, b, above),
        [
            pl.BlockSpec((tall, width), lambda j, o: (j, 0)),
            fixed((tall, width)),
            fixed((tall, width)),
            pl.BlockSpec(memory_space=pl.ANY),
        ],
        (struct(above.shape, BF16),),
        [pl.BlockSpec((tall, width), lambda j, o: (2 + j, 0))],
        tall * width,
        aliases={4: 0},
    )[0]


def local(n_head, n_seq, tokens, w_qkv, w_out, decay_rate, prior_state):
    rows, width = tokens.shape
    heads, size = prior_state.shape[0], prior_state.shape[1]
    square = n_head == 4
    place = lax.axis_index("head").astype(jnp.int32)
    quarter = rows // 4
    group = 2 if heads % 2 == 0 else 1
    cols = group * size

    over_x = functools.partial(lax.ppermute, axis_name="head", perm=[(i, i ^ 1) for i in range(n_head)])
    over_y = functools.partial(lax.ppermute, axis_name="head", perm=[(i, i ^ 2) for i in range(n_head)])

    flips = (0, 1, 2, 3) if square else (0,)
    places = jnp.stack([place ^ f for f in flips])

    along, inside, down, tail = decay_call(decay_rate, quarter)
    tail = tail[:, 0]
    pos = lax.axis_index("seq")
    core, chip = pos % 2, pos // 2
    n_chips = n_seq // 2
    swap = functools.partial(lax.ppermute, axis_name="seq", perm=[(i, i ^ 1) for i in range(n_seq)])

    def hop(x, *pairs):
        return lax.ppermute(
            x, "seq", perm=[(2 * a + c, 2 * b + c) for a, b in pairs for c in range(2)]
        )

    tail_other = swap(tail)
    tail_chip = tail + tail_other
    tail_below = hop(tail_chip, (2, 3)) if n_chips == 4 else tail_chip

    if square:
        q0, q1 = cut_call(tokens)
        x0, y1, x1, y0 = over_x(q0), over_y(q1), over_x(q1), over_y(q0)
        acc, q2, q3 = own_part_call(places, tokens, w_qkv, cols)
        fy0, fx1 = over_y(x0), over_x(y1)
        x2 = over_x(after(q2, x1, y0, tail_below, inside))
        y3 = over_y(after(q3, x1, y0, tail_below, inside))
        acc_a = part_call(
            places,
            (1, 2),
            [(x0, x1), (y0, y1)],
            w_qkv,
            2 * quarter,
            cols,
            before=acc,
            at=0,
        )
        x3, y2 = over_x(after(q3, fy0, fx1, acc_a)), over_y(after(q2, fy0, fx1, acc_a))
        query_a, within_a, state = first_call(
            places,
            (3,),
            [(fy0, fx1)],
            (acc_a,),
            w_qkv,
            along,
            inside,
            2 * quarter,
            quarter,
            size,
            group,
        )
        fy2, fx3 = over_y(after(x2, state)), over_x(after(y3, state))
        acc_b = part_call(
            places,
            (1, 2),
            [(x2, x3), (y2, y3)],
            w_qkv,
            2 * quarter,
            cols,
            before=acc,
            at=1,
        )
        far = (fy2, fx3)
        k, v, mid, state, sent = state_call(
            places, far, w_qkv, acc_b, inside, state, quarter, group
        )
    else:
        gathered = lax.all_gather(tokens, "head", axis=1, tiled=True)
        query, within, state = first_call(
            places, (), [(gathered,)], (), w_qkv, along, inside, rows, quarter, size, group
        )
        sent = state.astype(BF16)

    other = swap(sent).astype(F32)
    first = jnp.where(core == 0, state, other)
    second = jnp.where(core == 0, other, state)
    tail_first = jnp.where(core == 0, tail, tail_other)
    tail_second = jnp.where(core == 0, tail_other, tail)
    share = heads // 2

    def mine(x):
        return lax.dynamic_slice_in_dim(x, core * share, share, 0)

    chip_state = jnp.exp(-mine(tail_second))[:, None, None] * mine(first) + mine(second)
    chip_decay = jnp.exp(-mine(tail_chip))[:, None, None]
    chip_entering = mine(prior_state)

    def leaving():
        return (chip_decay * chip_entering + chip_state).astype(BF16)

    if n_chips == 4:
        arriving = hop(jnp.where(chip == 2, chip_state.astype(BF16), leaving()), (0, 1), (2, 3))
        chip_entering = jnp.where(chip == 1, arriving.astype(F32), chip_entering)
        sum_first = leaving()
        to_third, to_second = hop(sum_first, (1, 3)), hop(sum_first, (1, 2))
        if square:
            query_b, within_b = later_call(
                places, far, w_qkv, acc_b, k, v, along, inside, after(mid, sum_first), group
            )
            to_third, to_second, _ = lax.optimization_barrier((to_third, to_second, query_b))
        third = jnp.exp(-mine(tail_below))[:, None, None] * to_third.astype(F32)
        chip_entering = jnp.where(chip == 2, to_second.astype(F32), chip_entering)
        chip_entering = jnp.where(chip == 3, third + arriving.astype(F32), chip_entering)
    else:
        for step in range(n_chips - 1):
            arriving = hop(leaving(), (step, step + 1))
            chip_entering = jnp.where(chip == step + 1, arriving.astype(F32), chip_entering)
        if square:
            query_b, within_b = later_call(
                places, far, w_qkv, acc_b, k, v, along, inside, mid, group
            )
    there = swap(chip_entering.astype(BF16)).astype(F32)
    entering = jnp.concatenate(
        [jnp.where(core == 0, chip_entering, there), jnp.where(core == 0, there, chip_entering)]
    )
    entering = jnp.where(
        core == 0, entering, jnp.exp(-tail_first)[:, None, None] * entering + first
    ).astype(BF16)

    if not square:
        halves = [
            head_call(
                places,
                0,
                query[r * rows // 2 : (r + 1) * rows // 2],
                within[r * rows // 2 : (r + 1) * rows // 2],
                entering,
                down,
                w_out,
                width,
                r,
            )[0]
            for r in range(2)
        ]
        partial = dot(jnp.concatenate(halves), w_out).astype(BF16)
        return lax.psum_scatter(partial, "head", scatter_dimension=1, tiled=True)

    na, far0, far1 = head_call(places, 3, query_a, within_a, entering, down, w_out, width, 0)
    far0, far1 = over_x(far0), over_y(far1)
    nb, far2, far3, near_x, near_y = heads_near_call(
        places, query_b, within_b, entering, down, na, w_out, width
    )
    near_x, near_y = over_x(after(near_x, far0, far1)), over_y(after(near_y, far0, far1))
    far2, far3 = over_x(far2), over_y(far3)
    sum1, sum0 = pair_call(places, after(na, near_x, near_y), far1, far0, w_out, width)
    far2, far3 = after(far2, sum1), after(far3, sum1)
    sum1, sum0 = over_x(sum1), over_y(sum0)
    sum3, sum2 = pair_call(places, nb, far3, far2, w_out, width)
    sum3, sum2 = over_x(sum3), over_y(sum2)
    below = own_call(places, nb, ((near_x, 1),), ((near_y, 1),), w_out, width, 1)
    above = own_call(
        places, na, ((near_x, 0), (sum0, 0)), ((near_y, 0), (sum1, 0)), w_out, width, 2
    )
    return last_call(below, sum2, sum3, above)


def solution(mesh):
    in_specs = (
        P("seq", "head"),
        P(None, None, "head"),
        P("head", None),
        P("head", "seq"),
        P("head", None, None),
    )
    body = functools.partial(local, mesh.shape["head"], mesh.shape["seq"])
    return jax.shard_map(
        body, mesh=mesh, in_specs=in_specs, out_specs=P("seq", "head"), check_vma=False
    )
```

```python
import functools
import math

import jax
import jax.numpy as jnp
from jax import lax
from jax.experimental import pallas as pl
from jax.experimental.pallas import tpu as pltpu
from jax.sharding import PartitionSpec as P

BF16, F32 = jnp.bfloat16, jnp.float32
MIB = 1024 * 1024


def dot(a, b, contract=((1,), (0,))):
    return lax.dot_general(a, b, (contract, ((), ())), preferred_element_type=F32)


def after(x, *earlier):
    return lax.optimization_barrier((x, *earlier))[0]


def struct(shape, dtype):
    return jax.ShapeDtypeStruct(shape, dtype)


def stay(x):
    return pltpu.with_memory_space_constraint(x, pltpu.HBM)


def fixed(shape):
    return pl.BlockSpec(shape, lambda j, o: (0,) * len(shape))


def call(kernel, name, steps, scalars, ins, in_specs, outs, out_specs, flops, scratch=(), aliases=None, light=False):
    moved = sum(a.size * a.dtype.itemsize for a in ins) + sum(
        math.prod(o.shape) * jnp.dtype(o.dtype).itemsize for o in outs
    )
    return pl.pallas_call(
        kernel,
        out_shape=tuple(outs),
        grid_spec=pltpu.PrefetchScalarGridSpec(
            num_scalar_prefetch=1,
            grid=(steps,),
            in_specs=in_specs,
            out_specs=out_specs,
            scratch_shapes=list(scratch),
        ),
        input_output_aliases=aliases or {},
        compiler_params=pltpu.CompilerParams(vmem_limit_bytes=(24 if light else 32) * MIB),
        cost_estimate=pl.CostEstimate(
            flops=1 if light else flops, bytes_accessed=1 if light else moved, transcendentals=0
        ),
        name=name,
    )(scalars, *ins)


def cut_kernel(_, x_ref, a_ref, b_ref):
    tall = a_ref.shape[0]
    a_ref[...] = x_ref[:tall, :]
    b_ref[...] = x_ref[tall:, :]


def cut_call(x):
    rows, width = x.shape
    quarter = (rows // 4, width)
    return call(
        cut_kernel,
        "cut",
        1,
        jnp.zeros((1,), jnp.int32),
        (x,),
        [fixed((rows // 2, width))],
        (struct(quarter, x.dtype),) * 2,
        [fixed(quarter)] * 2,
        1,
    )


def decay_kernel(chunk, _, rate_ref, along_ref, inside_ref, down_ref, tail_ref):
    heads, rows = rate_ref.shape
    lane = lax.broadcasted_iota(jnp.int32, (heads, chunk), 1)
    base = jnp.zeros((heads, 1), F32)
    insides, wholes = [], []
    for c in range(rows // chunk):
        x = rate_ref[:, c * chunk : (c + 1) * chunk]
        step = 1
        while step < chunk:
            x = x + jnp.where(lane >= step, pltpu.roll(x, step, 1), 0.0)
            step *= 2
        insides.append(x)
        wholes.append(x + base)
        base = base + x[:, chunk - 1 :]
    inside = jnp.concatenate(insides, axis=1)
    along_ref[...] = inside
    inside_ref[...] = inside.T
    down_ref[...] = jnp.concatenate(wholes, axis=1).T
    tail_ref[...] = jnp.broadcast_to(base, tail_ref.shape)


def decay_call(rate, chunk):
    heads, rows = rate.shape
    return call(
        functools.partial(decay_kernel, chunk),
        "decay",
        1,
        jnp.zeros((1,), jnp.int32),
        (rate,),
        [fixed((heads, rows))],
        (
            struct((heads, rows), F32),
            struct((rows, heads), F32),
            struct((rows, heads), F32),
            struct((heads, 128), F32),
        ),
        [fixed((heads, rows)), fixed((rows, heads)), fixed((rows, heads)), fixed((heads, 128))],
        heads * rows * 16,
    )


def column(table, head):
    lane = lax.broadcasted_iota(jnp.int32, table.shape, 1)
    return jnp.sum(jnp.where(lane == head, table, 0.0), axis=1, keepdims=True)


def scores(q, k, v, along, down, state):
    rows = q.shape[0]
    causal = lax.broadcasted_iota(jnp.int32, (rows, rows), 0) >= lax.broadcasted_iota(
        jnp.int32, (rows, rows), 1
    )
    decay = jnp.exp(jnp.minimum(along - down, 0.0))
    weights = jnp.where(causal, dot(q, k, ((1,), (1,))) * decay, 0.0).astype(BF16)
    return dot(weights, v) + dot(q, state.astype(BF16)) * jnp.exp(-down)


def advance(k, v, down, state):
    last = down[down.shape[0] - 1 :, :]
    scaled = (k.astype(F32) * jnp.exp(down - last)).astype(BF16)
    return jnp.exp(-last) * state + dot(scaled, v, ((0,), (0,)))


def first_kernel(layout, added, chunk, group, size, _, *refs):
    count = sum(layout)
    x_refs, w_refs, refs = refs[:count], refs[count : count + len(layout)], refs[count + len(layout) :]
    along_ref, inside_ref, q_ref, within_ref, state_ref, held = refs[-6:]
    j = pl.program_id(0)
    rows = held.shape[1]

    @pl.when(j == 0)
    def _():
        at = 0
        for i, parts in enumerate(layout):
            tall = rows // parts
            for p in range(parts):
                held[i, p * tall : (p + 1) * tall, :] = x_refs[at][...]
                at += 1

    def project(c):
        total = dot(held[0], w_refs[0][c])
        for i in range(1, len(layout)):
            total = total + dot(held[i], w_refs[i][c])
        if added:
            total = total + refs[0][c]
        return total.astype(BF16)

    q_all, k_all, v_all = project(0), project(1), project(2)
    q_ref[...] = q_all
    for a in range(group):
        head = j * group + a
        lanes = slice(a * size, (a + 1) * size)
        state = jnp.zeros((size, size), F32)
        for c in range(rows // chunk):
            here = slice(c * chunk, (c + 1) * chunk)
            q, k, v = q_all[here, lanes], k_all[here, lanes], v_all[here, lanes]
            down = column(inside_ref[here, :], head)
            along = along_ref[pl.ds(head, 1), here]
            within_ref[here, lanes] = scores(q, k, v, along, down, state)
            state = advance(k, v, down, state)
        state_ref[a] = state


def first_call(places, blocks, pieces, before, w_qkv, along, inside, rows, chunk, size, group):
    heads = along.shape[0]
    cols = group * size
    flat = [p for piece in pieces for p in piece]
    depth = flat[0].shape[1]

    def block(i):
        return pl.BlockSpec((3, depth, cols), lambda j, o: (0, o[blocks[i]] if blocks else 0, j))

    wide = pl.BlockSpec((rows, cols), lambda j, o: (0, j))
    return call(
        functools.partial(
            first_kernel, tuple(len(p) for p in pieces), bool(before), chunk, group, size
        ),
        "first",
        heads // group,
        places,
        (*flat, *[w_qkv] * len(pieces), *before, along, inside),
        [
            pl.BlockSpec((rows // len(piece), depth), lambda j, o: (0, 0))
            for piece in pieces
            for _ in piece
        ]
        + [block(i) for i in range(len(pieces))]
        + [pl.BlockSpec((3, rows, cols), lambda j, o: (0, 0, j)) for _ in before]
        + [fixed((heads, rows)), fixed((rows, heads))],
        (
            pltpu.HBM((rows, heads * size), BF16),
            pltpu.HBM((rows, heads * size), F32),
            struct((heads, size, size), F32),
        ),
        [wide, wide, pl.BlockSpec((group, size, size), lambda j, o: (j, 0, 0))],
        2 * rows * 3 * heads * size * depth * len(pieces),
        scratch=[pltpu.VMEM((len(pieces), rows, depth), BF16)],
    )


def own_part_kernel(_, x_ref, w_ref, out_ref, c_ref, d_ref):
    rows = x_ref.shape[0]
    tall = c_ref.shape[0]

    @pl.when(pl.program_id(0) == 0)
    def _():
        c_ref[...] = x_ref[rows - 2 * tall : rows - tall, :]
        d_ref[...] = x_ref[rows - tall :, :]

    for c in range(3):
        out_ref[c] = dot(x_ref[...], w_ref[c])


def own_part_call(places, tokens, w_qkv, cols):
    rows, depth = tokens.shape
    width = w_qkv.shape[2]
    quarter = (rows // 4, depth)
    return call(
        own_part_kernel,
        "own_part",
        width // cols,
        places,
        (tokens, w_qkv),
        [fixed((rows, depth)), pl.BlockSpec((3, depth, cols), lambda j, o: (0, o[0], j))],
        (pltpu.HBM((3, rows, width), F32), struct(quarter, BF16), struct(quarter, BF16)),
        [pl.BlockSpec((3, rows, cols), lambda j, o: (0, 0, j)), fixed(quarter), fixed(quarter)],
        2 * rows * depth * width * 3,
    )


def part_kernel(layout, outs, _, *refs):
    count = sum(layout)
    x_refs, w_refs = refs[:count], refs[count : count + len(layout)]
    before_ref, out_refs, held = refs[-2 - outs], refs[-1 - outs : -1], refs[-1]
    targets = [(ref, c) for ref in out_refs for c in range(ref.shape[0])]
    rows = held.shape[1]

    @pl.when(pl.program_id(0) == 0)
    def _():
        at = 0
        for i, parts in enumerate(layout):
            tall = rows // parts
            for p in range(parts):
                held[i, p * tall : (p + 1) * tall, :] = x_refs[at][...]
                at += 1

    for c in range(3):
        total = dot(held[0], w_refs[0][c])
        for i in range(1, len(layout)):
            total = total + dot(held[i], w_refs[i][c])
        ref, at = targets[c]
        ref[at] = total + before_ref[c]


def part_call(places, blocks, pieces, w_qkv, rows, cols, before, at, apart=False):
    flat = [p for piece in pieces for p in piece]
    depth = flat[0].shape[1]
    width = w_qkv.shape[2]

    def block(i):
        return pl.BlockSpec((3, depth, cols), lambda j, o: (0, o[blocks[i]], j))

    ins = [*flat, *[w_qkv] * len(pieces)]
    specs = [
        pl.BlockSpec((rows // len(piece), depth), lambda j, o: (0, 0)) for piece in pieces for _ in piece
    ] + [block(i) for i in range(len(pieces))]
    ins.append(before)
    specs.append(pl.BlockSpec((3, rows, cols), lambda j, o: (0, at, j)))
    outs = [struct((3, rows, width), F32)]
    if apart:
        outs = [pltpu.HBM((1, rows, width), F32), struct((2, rows, width), F32)]
    out = call(
        functools.partial(part_kernel, tuple(len(p) for p in pieces), len(outs)),
        "part",
        width // cols,
        places,
        ins,
        specs,
        outs,
        [pl.BlockSpec((o.shape[0], rows, cols), lambda j, o: (0, 0, j)) for o in outs],
        2 * rows * depth * len(pieces) * width * 3,
        scratch=[pltpu.VMEM((len(pieces), rows, depth), BF16)],
    )
    return out if apart else out[0]


def state_kernel(chunk, group, size, _, *refs):
    xa, xb, wk, wv, acc_k, acc_v, inside_ref, state_ref = refs[:8]
    k_ref, v_ref, mid_ref, end_ref, sent_ref, held = refs[8:]
    j = pl.program_id(0)
    rows = held.shape[0]

    @pl.when(j == 0)
    def _():
        held[: rows // 2, :] = xa[...]
        held[rows // 2 :, :] = xb[...]

    k_all = (acc_k[0] + dot(held[...], wk[0])).astype(BF16)
    v_all = (acc_v[0] + dot(held[...], wv[0])).astype(BF16)
    k_ref[...] = k_all
    v_ref[...] = v_all
    for a in range(group):
        head = j * group + a
        lanes = slice(a * size, (a + 1) * size)
        state = state_ref[a]
        for c in range(rows // chunk):
            here = slice(c * chunk, (c + 1) * chunk)
            mid_ref[c, a] = state
            state = advance(
                k_all[here, lanes], v_all[here, lanes], column(inside_ref[here, :], head), state
            )
        end_ref[a] = state
        sent_ref[a] = state.astype(BF16)


def state_call(places, far, w_qkv, acc, inside, state, chunk, group):
    _, rows, width = acc.shape
    heads, size = state.shape[0], state.shape[1]
    depth = far[0].shape[1]
    cols = group * size
    wide = pl.BlockSpec((rows, cols), lambda j, o: (0, j))
    small = pl.BlockSpec((group, size, size), lambda j, o: (j, 0, 0))
    chunks = rows // chunk
    return call(
        functools.partial(state_kernel, chunk, group, size),
        "states",
        heads // group,
        places,
        (*far, w_qkv, w_qkv, acc, acc, inside, state),
        [fixed(far[0].shape), fixed(far[1].shape)]
        + [pl.BlockSpec((1, depth, cols), lambda j, o, c=c: (c, o[3], j)) for c in (1, 2)]
        + [pl.BlockSpec((1, rows, cols), lambda j, o, c=c: (c, 0, j)) for c in (0, 1)]
        + [pl.BlockSpec((rows, heads), lambda j, o: (1, 0)), small],
        (
            pltpu.HBM((rows, width), BF16),
            pltpu.HBM((rows, width), BF16),
            pltpu.HBM((chunks, heads, size, size), F32),
            struct(state.shape, F32),
            struct(state.shape, BF16),
        ),
        [
            wide,
            wide,
            pl.BlockSpec((chunks, group, size, size), lambda j, o: (0, j, 0, 0)),
            small,
            small,
        ],
        4 * rows * depth * width,
        scratch=[pltpu.VMEM((rows, depth), BF16)],
    )


def later_kernel(chunk, group, size, _, *refs):
    xa, xb, wq, acc_q, k_ref, v_ref, along_ref, inside_ref, mid_ref, q_ref, within_ref, held = refs
    j = pl.program_id(0)
    rows = held.shape[0]

    @pl.when(j == 0)
    def _():
        held[: rows // 2, :] = xa[...]
        held[rows // 2 :, :] = xb[...]

    q_all = (acc_q[0] + dot(held[...], wq[0])).astype(BF16)
    q_ref[...] = q_all
    for a in range(group):
        head = j * group + a
        lanes = slice(a * size, (a + 1) * size)
        for c in range(rows // chunk):
            here = slice(c * chunk, (c + 1) * chunk)
            within_ref[here, lanes] = scores(
                q_all[here, lanes],
                k_ref[here, lanes],
                v_ref[here, lanes],
                along_ref[pl.ds(head, 1), here],
                column(inside_ref[here, :], head),
                mid_ref[c, a],
            )


def later_call(places, far, w_qkv, acc, k, v, along, inside, mid, group):
    _, rows, width = acc.shape
    chunks, heads, size = mid.shape[0], mid.shape[1], mid.shape[2]
    chunk = rows // chunks
    depth = far[0].shape[1]
    cols = group * size
    wide = pl.BlockSpec((rows, cols), lambda j, o: (0, j))
    return call(
        functools.partial(later_kernel, chunk, group, size),
        "later",
        heads // group,
        places,
        (*far, w_qkv, acc, k, v, along, inside, mid),
        [
            fixed(far[0].shape),
            fixed(far[1].shape),
            pl.BlockSpec((1, depth, cols), lambda j, o: (0, o[3], j)),
            pl.BlockSpec((1, rows, cols), lambda j, o: (0, 0, j)),
            wide,
            wide,
            pl.BlockSpec((heads, rows), lambda j, o: (0, 1)),
            pl.BlockSpec((rows, heads), lambda j, o: (1, 0)),
            pl.BlockSpec((chunks, group, size, size), lambda j, o: (0, j, 0, 0)),
        ],
        (struct((rows, width), BF16), struct((rows, width), F32)),
        [wide, wide],
        2 * rows * depth * width + 4 * rows * (chunk + size) * width,
        scratch=[pltpu.VMEM((rows, depth), BF16)],
    )


def head_kernel(_, q_ref, within_ref, entering_ref, down_ref, w_ref, normed_ref, *out_refs):
    heads, size = entering_ref.shape[0], entering_ref.shape[1]
    tall = q_ref.shape[0]
    for p, out_ref in enumerate(out_refs):
        rows = slice(p * tall, (p + 1) * tall)

        @pl.when(pl.program_id(0) == p)
        def _(rows=rows, out_ref=out_ref):
            fade = jnp.exp(-down_ref[...])
            for a in range(heads):
                lanes = slice(a * size, (a + 1) * size)
                seen = dot(q_ref[:, lanes], entering_ref[a]) * fade[:, a : a + 1]
                combined = within_ref[:, lanes] + seen
                power = jnp.mean(combined * combined, axis=1, keepdims=True)
                normed_ref[rows, lanes] = (combined * lax.rsqrt(power + 1e-06)).astype(BF16)
            out_ref[:tall, :] = dot(normed_ref[rows, :], w_ref[...]).astype(BF16)

        @pl.when(pl.program_id(0) == 2 + p)
        def _(rows=rows, out_ref=out_ref):
            out_ref[tall:, :] = dot(normed_ref[rows, :], w_ref[...]).astype(BF16)


def head_call(places, blocks, q, within, entering, down, w_out, width, at):
    rows, cols = q.shape
    tall = rows // 2
    heads = entering.shape[0]
    part = pl.BlockSpec((tall, cols), lambda i, o: (jnp.minimum(i, 1), 0))
    far, x, y = blocks
    return call(
        head_kernel,
        "heads",
        4,
        places,
        (q, within, entering, down, w_out),
        [
            part,
            part,
            fixed(entering.shape),
            pl.BlockSpec((tall, heads), lambda i, o: (2 * at + jnp.minimum(i, 1), 0)),
            pl.BlockSpec(
                (cols, width),
                lambda i, o: (0, o[jnp.where(i < 2, far, jnp.where(i == 2, x, y))]),
            ),
        ],
        (struct((rows, cols), BF16), *[struct((rows, width), BF16)] * 2),
        [fixed((rows, cols))] + [fixed((rows, width))] * 2,
        2 * rows * cols * (2 * width + 128),
        light=True,
    )


def pair_kernel(_, normed_ref, x_ref, y_ref, w_ref, out_x_ref, out_y_ref):
    tall = x_ref.shape[0]

    @pl.when(pl.program_id(0) == 0)
    def _():
        out_x_ref[...] = (dot(normed_ref[tall:, :], w_ref[...]) + x_ref[...].astype(F32)).astype(BF16)

    @pl.when(pl.program_id(0) == 1)
    def _():
        out_y_ref[...] = (dot(normed_ref[:tall, :], w_ref[...]) + y_ref[...].astype(F32)).astype(BF16)


def pair_call(places, normed, for_x, for_y, w_out, width):
    rows, cols = normed.shape
    quarter = (rows // 2, width)
    return call(
        pair_kernel,
        "sum_pair",
        2,
        places,
        (normed, for_x, for_y, w_out),
        [
            fixed((rows, cols)),
            fixed(quarter),
            fixed(quarter),
            pl.BlockSpec((cols, width), lambda i, o: (0, o[1 + i])),
        ],
        (struct(quarter, BF16),) * 2,
        [fixed(quarter)] * 2,
        2 * rows * cols * width,
        light=True,
    )


def own_kernel(_, normed_ref, w_ref, *refs):
    out_ref = refs[-1]
    tall = out_ref.shape[0]
    each = len(refs) // 2
    for p in range(2):
        rows = slice(p * tall, (p + 1) * tall)

        @pl.when(pl.program_id(0) == p)
        def _(p=p, rows=rows):
            total = dot(normed_ref[rows, :], w_ref[...])
            for ref in refs[p * each : (p + 1) * each]:
                total = total + ref[...].astype(F32)
            out_ref[...] = total.astype(BF16)


def own_call(places, normed, first, second, w_out, width, height):
    rows, cols = normed.shape
    quarter = (rows // 2, width)
    return call(
        own_kernel,
        "own_block",
        2,
        places,
        (normed, w_out, *[a for a, _ in (*first, *second)]),
        [fixed((rows, cols)), pl.BlockSpec((cols, width), lambda i, o: (0, o[0]))]
        + [pl.BlockSpec(quarter, lambda i, o, at=at: (at, 0)) for _, at in (*first, *second)],
        (struct((rows * height, width), BF16),),
        [pl.BlockSpec(quarter, lambda i, o: (i, 0))],
        2 * rows * cols * width,
        light=True,
    )[0]


def last_kernel(_, kept_ref, a_ref, b_ref, above_ref, out_ref):
    del above_ref

    @pl.when(pl.program_id(0) == 0)
    def _():
        out_ref[...] = (kept_ref[...].astype(F32) + a_ref[...].astype(F32)).astype(BF16)

    @pl.when(pl.program_id(0) == 1)
    def _():
        out_ref[...] = (kept_ref[...].astype(F32) + b_ref[...].astype(F32)).astype(BF16)


def last_call(kept, a, b, above):
    tall, width = a.shape
    return call(
        last_kernel,
        "last_add",
        2,
        jnp.zeros((1,), jnp.int32),
        (kept, a, b, above),
        [
            pl.BlockSpec((tall, width), lambda j, o: (j, 0)),
            fixed((tall, width)),
            fixed((tall, width)),
            pl.BlockSpec(memory_space=pl.ANY),
        ],
        (struct(above.shape, BF16),),
        [pl.BlockSpec((tall, width), lambda j, o: (2 + j, 0))],
        tall * width,
        aliases={4: 0},
    )[0]


def local(n_head, n_seq, tokens, w_qkv, w_out, decay_rate, prior_state):
    rows, width = tokens.shape
    heads, size = prior_state.shape[0], prior_state.shape[1]
    square = n_head == 4
    place = lax.axis_index("head").astype(jnp.int32)
    quarter = rows // 4
    group = 2 if heads % 2 == 0 else 1
    cols = group * size

    over_x = functools.partial(lax.ppermute, axis_name="head", perm=[(i, i ^ 1) for i in range(n_head)])
    over_y = functools.partial(lax.ppermute, axis_name="head", perm=[(i, i ^ 2) for i in range(n_head)])

    flips = (0, 1, 2, 3) if square else (0,)
    places = jnp.stack([place ^ f for f in flips])

    along, inside, down, tail = decay_call(decay_rate, quarter)
    tail = tail[:, 0]
    pos = lax.axis_index("seq")
    core, chip = pos % 2, pos // 2
    n_chips = n_seq // 2
    swap = functools.partial(lax.ppermute, axis_name="seq", perm=[(i, i ^ 1) for i in range(n_seq)])

    def hop(x, *pairs):
        return lax.ppermute(
            x, "seq", perm=[(2 * a + c, 2 * b + c) for a, b in pairs for c in range(2)]
        )

    def chip_tails(tail):
        other = swap(tail)
        return other, tail + other, hop(tail + other, (2, 3)) if n_chips == 4 else None

    if square:
        tokens = stay(tokens)
        q0, q1 = cut_call(tokens)
        x0, y1, x1, y0 = over_x(q0), over_y(q1), over_x(q1), over_y(q0)
        acc, q2, q3 = own_part_call(places, tokens, w_qkv, cols)
        acc = stay(acc)
        fy0, fx1 = over_y(x0), over_x(y1)
        tail_other, tail_chip, tail_below = chip_tails(after(tail, x0, y1))
        x2 = over_x(after(q2, x1, y0, tail_chip))
        y3 = over_y(after(q3, x1, y0, tail_chip))
        acc_a = part_call(
            places,
            (1, 2),
            [(x0, x1), (y0, y1)],
            w_qkv,
            2 * quarter,
            cols,
            before=stay(after(acc, tail_chip)),
            at=0,
        )
        earlier = (fy0, fx1, acc_a) if tail_below is None else (fy0, fx1, acc_a, tail_below)
        x3, y2 = over_x(after(q3, *earlier)), over_y(after(q2, *earlier))
        query_a, within_a, state = first_call(
            places,
            (3,),
            [(fy0, fx1)],
            (acc_a,),
            w_qkv,
            along,
            inside,
            2 * quarter,
            quarter,
            size,
            group,
        )
        fy2, fx3 = over_y(after(x2, state)), over_x(after(y3, state))
        acc_q, acc_kv = part_call(
            places,
            (1, 2),
            [(x2, x3), (y2, y3)],
            w_qkv,
            2 * quarter,
            cols,
            before=acc,
            at=1,
            apart=True,
        )
        far = (fy2, fx3)
        k, v, mid, state, sent = state_call(
            places, far, w_qkv, acc_kv, inside, state, quarter, group
        )
    else:
        tail_other, tail_chip, tail_below = chip_tails(tail)
        gathered = lax.all_gather(tokens, "head", axis=1, tiled=True)
        query, within, state = first_call(
            places, (), [(gathered,)], (), w_qkv, along, inside, rows, quarter, size, group
        )
        sent = state.astype(BF16)

    other = swap(sent).astype(F32)
    first = jnp.where(core == 0, state, other)
    second = jnp.where(core == 0, other, state)
    tail_first = jnp.where(core == 0, tail, tail_other)
    tail_second = jnp.where(core == 0, tail_other, tail)
    share = heads // 2

    def mine(x):
        return lax.dynamic_slice_in_dim(x, core * share, share, 0)

    chip_state = jnp.exp(-mine(tail_second))[:, None, None] * mine(first) + mine(second)
    chip_decay = jnp.exp(-mine(tail_chip))[:, None, None]
    chip_entering = mine(prior_state)

    def leaving():
        return (chip_decay * chip_entering + chip_state).astype(BF16)

    if n_chips == 4:
        arriving = hop(jnp.where(chip == 2, chip_state.astype(BF16), leaving()), (0, 1), (2, 3))
        chip_entering = jnp.where(chip == 1, arriving.astype(F32), chip_entering)
        sum_first = leaving()
        to_third, to_second = hop(sum_first, (1, 3)), hop(sum_first, (1, 2))
        third = jnp.exp(-mine(tail_below))[:, None, None] * to_third.astype(F32)
        chip_entering = jnp.where(chip == 2, to_second.astype(F32), chip_entering)
        chip_entering = jnp.where(chip == 3, third + arriving.astype(F32), chip_entering)
    else:
        for step in range(n_chips - 1):
            arriving = hop(leaving(), (step, step + 1))
            chip_entering = jnp.where(chip == step + 1, arriving.astype(F32), chip_entering)
    there = swap(chip_entering.astype(BF16)).astype(F32)
    entering = jnp.concatenate(
        [jnp.where(core == 0, chip_entering, there), jnp.where(core == 0, there, chip_entering)]
    )
    entering = jnp.where(
        core == 0, entering, jnp.exp(-tail_first)[:, None, None] * entering + first
    ).astype(BF16)

    if not square:
        halves = [
            head_call(
                places,
                (0, 0, 0),
                query[r * rows // 2 : (r + 1) * rows // 2],
                within[r * rows // 2 : (r + 1) * rows // 2],
                entering,
                down,
                w_out,
                width,
                r,
            )[0]
            for r in range(2)
        ]
        partial = dot(jnp.concatenate(halves), w_out).astype(BF16)
        return lax.psum_scatter(partial, "head", scatter_dimension=1, tiled=True)

    na, by_x, by_y = head_call(
        places, (3, 1, 2), query_a, within_a, entering, down, w_out, width, 0
    )
    by_x, by_y = over_x(by_x), over_y(by_y)
    query_b, within_b = later_call(
        places, far, w_qkv, stay(acc_q), stay(k), stay(v), along, inside, stay(after(mid, na)), group
    )
    nb, by_x2, by_y2 = head_call(
        places, (3, 1, 2), query_b, within_b, entering, down, w_out, width, 1
    )
    by_x2, by_y2 = over_x(by_x2), over_y(by_y2)
    sum1, sum0 = pair_call(places, after(na, nb), by_y, by_x, w_out, width)
    by_x2, by_y2 = after(by_x2, sum1), after(by_y2, sum1)
    sum1, sum0 = over_x(sum1), over_y(sum0)
    sum3, sum2 = pair_call(places, nb, by_y2, by_x2, w_out, width)
    sum3, sum2 = over_x(sum3), over_y(sum2)
    below = own_call(places, after(nb, sum1, sum0), ((by_x2, 1),), ((by_y2, 1),), w_out, width, 1)
    above = own_call(
        places, na, ((by_x, 1), (sum0, 0)), ((by_y, 1), (sum1, 0)), w_out, width, 2
    )
    return last_call(below, sum2, sum3, above)


def solution(mesh):
    in_specs = (
        P("seq", "head"),
        P(None, None, "head"),
        P("head", None),
        P("head", "seq"),
        P("head", None, None),
    )
    body = functools.partial(local, mesh.shape["head"], mesh.shape["seq"])
    return jax.shard_map(
        body, mesh=mesh, in_specs=in_specs, out_specs=P("seq", "head"), check_vma=False
    )
```

```python
import functools
import math

import jax
import jax.numpy as jnp
from jax import lax
from jax.experimental import pallas as pl
from jax.experimental.pallas import tpu as pltpu
from jax.sharding import PartitionSpec as P

BF16, F32 = jnp.bfloat16, jnp.float32
MIB = 1024 * 1024


def dot(a, b, contract=((1,), (0,))):
    return lax.dot_general(a, b, (contract, ((), ())), preferred_element_type=F32)


def after(x, *earlier):
    return lax.optimization_barrier((x, *earlier))[0]


def struct(shape, dtype):
    return jax.ShapeDtypeStruct(shape, dtype)


def stay(x):
    return pltpu.with_memory_space_constraint(x, pltpu.HBM)


def near(x):
    return pltpu.with_memory_space_constraint(x, pltpu.VMEM)


def fixed(shape):
    return pl.BlockSpec(shape, lambda j, o: (0,) * len(shape))


def call(kernel, name, steps, scalars, ins, in_specs, outs, out_specs, flops, scratch=(), aliases=None, light=False):
    moved = sum(a.size * a.dtype.itemsize for a in ins) + sum(
        math.prod(o.shape) * jnp.dtype(o.dtype).itemsize for o in outs
    )
    return pl.pallas_call(
        kernel,
        out_shape=tuple(outs),
        grid_spec=pltpu.PrefetchScalarGridSpec(
            num_scalar_prefetch=1,
            grid=(steps,),
            in_specs=in_specs,
            out_specs=out_specs,
            scratch_shapes=list(scratch),
        ),
        input_output_aliases=aliases or {},
        compiler_params=pltpu.CompilerParams(vmem_limit_bytes=(24 if light else 32) * MIB),
        cost_estimate=pl.CostEstimate(
            flops=1 if light else flops, bytes_accessed=1 if light else moved, transcendentals=0
        ),
        name=name,
    )(scalars, *ins)


def cut_kernel(_, x_ref, a_ref, b_ref):
    tall = a_ref.shape[0]
    a_ref[...] = x_ref[:tall, :]
    b_ref[...] = x_ref[tall:, :]


def cut_call(x):
    rows, width = x.shape
    quarter = (rows // 4, width)
    return call(
        cut_kernel,
        "cut",
        1,
        jnp.zeros((1,), jnp.int32),
        (x,),
        [fixed((rows // 2, width))],
        (struct(quarter, x.dtype),) * 2,
        [fixed(quarter)] * 2,
        1,
    )


def decay_kernel(chunk, _, rate_ref, along_ref, inside_ref, down_ref, tail_ref):
    heads, rows = rate_ref.shape
    lane = lax.broadcasted_iota(jnp.int32, (heads, chunk), 1)
    base = jnp.zeros((heads, 1), F32)
    insides, wholes = [], []
    for c in range(rows // chunk):
        x = rate_ref[:, c * chunk : (c + 1) * chunk]
        step = 1
        while step < chunk:
            x = x + jnp.where(lane >= step, pltpu.roll(x, step, 1), 0.0)
            step *= 2
        insides.append(x)
        wholes.append(x + base)
        base = base + x[:, chunk - 1 :]
    inside = jnp.concatenate(insides, axis=1)
    along_ref[...] = inside
    inside_ref[...] = inside.T
    down_ref[...] = jnp.concatenate(wholes, axis=1).T
    tail_ref[...] = jnp.broadcast_to(base, tail_ref.shape)


def decay_call(rate, chunk):
    heads, rows = rate.shape
    return call(
        functools.partial(decay_kernel, chunk),
        "decay",
        1,
        jnp.zeros((1,), jnp.int32),
        (rate,),
        [fixed((heads, rows))],
        (
            struct((heads, rows), F32),
            struct((rows, heads), F32),
            struct((rows, heads), F32),
            struct((heads, 128), F32),
        ),
        [fixed((heads, rows)), fixed((rows, heads)), fixed((rows, heads)), fixed((heads, 128))],
        heads * rows * 16,
    )


def column(table, head):
    lane = lax.broadcasted_iota(jnp.int32, table.shape, 1)
    return jnp.sum(jnp.where(lane == head, table, 0.0), axis=1, keepdims=True)


def scores(q, k, v, along, down, state):
    rows = q.shape[0]
    causal = lax.broadcasted_iota(jnp.int32, (rows, rows), 0) >= lax.broadcasted_iota(
        jnp.int32, (rows, rows), 1
    )
    decay = jnp.exp(jnp.minimum(along - down, 0.0))
    weights = jnp.where(causal, dot(q, k, ((1,), (1,))) * decay, 0.0).astype(BF16)
    return dot(weights, v) + dot(q, state.astype(BF16)) * jnp.exp(-down)


def advance(k, v, down, state):
    last = down[down.shape[0] - 1 :, :]
    scaled = (k.astype(F32) * jnp.exp(down - last)).astype(BF16)
    return jnp.exp(-last) * state + dot(scaled, v, ((0,), (0,)))


def first_kernel(layout, added, chunk, group, size, _, *refs):
    count = sum(layout)
    x_refs, w_refs, refs = refs[:count], refs[count : count + len(layout)], refs[count + len(layout) :]
    along_ref, inside_ref, q_ref, within_ref, state_ref, held = refs[-6:]
    j = pl.program_id(0)
    rows = held.shape[1]

    @pl.when(j == 0)
    def _():
        at = 0
        for i, parts in enumerate(layout):
            tall = rows // parts
            for p in range(parts):
                held[i, p * tall : (p + 1) * tall, :] = x_refs[at][...]
                at += 1

    def project(c):
        total = dot(held[0], w_refs[0][c])
        for i in range(1, len(layout)):
            total = total + dot(held[i], w_refs[i][c])
        if added:
            total = total + refs[0][c]
        return total.astype(BF16)

    q_all, k_all, v_all = project(0), project(1), project(2)
    q_ref[...] = q_all
    for a in range(group):
        head = j * group + a
        lanes = slice(a * size, (a + 1) * size)
        state = jnp.zeros((size, size), F32)
        for c in range(rows // chunk):
            here = slice(c * chunk, (c + 1) * chunk)
            q, k, v = q_all[here, lanes], k_all[here, lanes], v_all[here, lanes]
            down = column(inside_ref[here, :], head)
            along = along_ref[pl.ds(head, 1), here]
            within_ref[here, lanes] = scores(q, k, v, along, down, state)
            state = advance(k, v, down, state)
        state_ref[a] = state


def first_call(places, blocks, pieces, before, w_qkv, along, inside, rows, chunk, size, group):
    heads = along.shape[0]
    cols = group * size
    flat = [p for piece in pieces for p in piece]
    depth = flat[0].shape[1]

    def block(i):
        return pl.BlockSpec((3, depth, cols), lambda j, o: (0, o[blocks[i]] if blocks else 0, j))

    wide = pl.BlockSpec((rows, cols), lambda j, o: (0, j))
    return call(
        functools.partial(
            first_kernel, tuple(len(p) for p in pieces), bool(before), chunk, group, size
        ),
        "first",
        heads // group,
        places,
        (*flat, *[w_qkv] * len(pieces), *before, along, inside),
        [
            pl.BlockSpec((rows // len(piece), depth), lambda j, o: (0, 0))
            for piece in pieces
            for _ in piece
        ]
        + [block(i) for i in range(len(pieces))]
        + [pl.BlockSpec((3, rows, cols), lambda j, o: (0, 0, j)) for _ in before]
        + [fixed((heads, rows)), fixed((rows, heads))],
        (
            pltpu.HBM((rows, heads * size), BF16),
            pltpu.HBM((rows, heads * size), F32),
            struct((heads, size, size), F32),
        ),
        [wide, wide, pl.BlockSpec((group, size, size), lambda j, o: (j, 0, 0))],
        2 * rows * 3 * heads * size * depth * len(pieces),
        scratch=[pltpu.VMEM((len(pieces), rows, depth), BF16)],
    )


def own_part_kernel(_, x_ref, w_ref, out_ref, c_ref, d_ref):
    rows = x_ref.shape[0]
    tall = c_ref.shape[0]

    @pl.when(pl.program_id(0) == 0)
    def _():
        c_ref[...] = x_ref[rows - 2 * tall : rows - tall, :]
        d_ref[...] = x_ref[rows - tall :, :]

    for c in range(3):
        out_ref[c] = dot(x_ref[...], w_ref[c])


def own_part_call(places, tokens, w_qkv, cols):
    rows, depth = tokens.shape
    width = w_qkv.shape[2]
    quarter = (rows // 4, depth)
    return call(
        own_part_kernel,
        "own_part",
        width // cols,
        places,
        (tokens, w_qkv),
        [fixed((rows, depth)), pl.BlockSpec((3, depth, cols), lambda j, o: (0, o[0], j))],
        (pltpu.HBM((3, rows, width), F32), pltpu.HBM(quarter, BF16), pltpu.HBM(quarter, BF16)),
        [pl.BlockSpec((3, rows, cols), lambda j, o: (0, 0, j)), fixed(quarter), fixed(quarter)],
        2 * rows * depth * width * 3,
    )


def part_kernel(layout, outs, _, *refs):
    count = sum(layout)
    x_refs, w_refs = refs[:count], refs[count : count + len(layout)]
    before_ref, out_refs, held = refs[-2 - outs], refs[-1 - outs : -1], refs[-1]
    targets = [(ref, c) for ref in out_refs for c in range(ref.shape[0])]
    rows = held.shape[1]

    @pl.when(pl.program_id(0) == 0)
    def _():
        at = 0
        for i, parts in enumerate(layout):
            tall = rows // parts
            for p in range(parts):
                held[i, p * tall : (p + 1) * tall, :] = x_refs[at][...]
                at += 1

    for c in range(3):
        total = dot(held[0], w_refs[0][c])
        for i in range(1, len(layout)):
            total = total + dot(held[i], w_refs[i][c])
        ref, at = targets[c]
        ref[at] = total + before_ref[c]


def part_call(places, blocks, pieces, w_qkv, rows, cols, before, at, apart=False):
    flat = [p for piece in pieces for p in piece]
    depth = flat[0].shape[1]
    width = w_qkv.shape[2]

    def block(i):
        return pl.BlockSpec((3, depth, cols), lambda j, o: (0, o[blocks[i]], j))

    ins = [*flat, *[w_qkv] * len(pieces)]
    specs = [
        pl.BlockSpec((rows // len(piece), depth), lambda j, o: (0, 0)) for piece in pieces for _ in piece
    ] + [block(i) for i in range(len(pieces))]
    ins.append(before)
    specs.append(pl.BlockSpec((3, rows, cols), lambda j, o: (0, at, j)))
    outs = [struct((3, rows, width), F32)]
    if apart:
        outs = [pltpu.HBM((1, rows, width), F32), struct((2, rows, width), F32)]
    out = call(
        functools.partial(part_kernel, tuple(len(p) for p in pieces), len(outs)),
        "part",
        width // cols,
        places,
        ins,
        specs,
        outs,
        [pl.BlockSpec((o.shape[0], rows, cols), lambda j, o: (0, 0, j)) for o in outs],
        2 * rows * depth * len(pieces) * width * 3,
        scratch=[pltpu.VMEM((len(pieces), rows, depth), BF16)],
    )
    return out if apart else out[0]


def state_kernel(chunk, group, size, places, *refs):
    xa, xb, wk, wv, acc_k, acc_v, inside_ref, state_ref = refs[:8]
    k_ref, v_ref, mid_ref, end_ref, sent_ref, held = refs[8:]
    j = pl.program_id(0)
    rows = held.shape[0]

    @pl.when(j == 0)
    def _():
        held[: rows // 2, :] = xa[...]
        held[rows // 2 :, :] = xb[...]

    k_all = (acc_k[0] + dot(held[...], wk[0])).astype(BF16)
    v_all = (acc_v[0] + dot(held[...], wv[0])).astype(BF16)
    k_ref[...] = k_all
    v_ref[...] = v_all
    ends = []
    for a in range(group):
        head = j * group + a
        lanes = slice(a * size, (a + 1) * size)
        state = state_ref[a]
        for c in range(rows // chunk):
            here = slice(c * chunk, (c + 1) * chunk)
            mid_ref[c, a] = state
            state = advance(
                k_all[here, lanes], v_all[here, lanes], column(inside_ref[here, :], head), state
            )
        end_ref[a] = state
        ends.append(state.astype(BF16))
    core = places[4]
    half = pl.num_programs(0) // 2

    @pl.when(jnp.where(core == 0, j >= half, j < half))
    def _():
        for a in range(group):
            sent_ref[a] = ends[a]


def state_call(places, far, w_qkv, acc, inside, state, chunk, group):
    _, rows, width = acc.shape
    heads, size = state.shape[0], state.shape[1]
    depth = far[0].shape[1]
    cols = group * size
    wide = pl.BlockSpec((rows, cols), lambda j, o: (0, j))
    small = pl.BlockSpec((group, size, size), lambda j, o: (j, 0, 0))
    chunks = rows // chunk
    half = heads // group // 2

    def sent_block(j, o):
        return jnp.where(o[4] == 0, jnp.maximum(j - half, 0), jnp.minimum(j, half - 1)), 0, 0

    return call(
        functools.partial(state_kernel, chunk, group, size),
        "states",
        heads // group,
        places,
        (*far, w_qkv, w_qkv, acc, acc, inside, state),
        [fixed(far[0].shape), fixed(far[1].shape)]
        + [pl.BlockSpec((1, depth, cols), lambda j, o, c=c: (c, o[3], j)) for c in (1, 2)]
        + [pl.BlockSpec((1, rows, cols), lambda j, o, c=c: (c, 0, j)) for c in (0, 1)]
        + [pl.BlockSpec((rows, heads), lambda j, o: (1, 0)), small],
        (
            pltpu.HBM((rows, width), BF16),
            pltpu.HBM((rows, width), BF16),
            pltpu.HBM((chunks, heads, size, size), F32),
            struct(state.shape, F32),
            struct((heads // 2, size, size), BF16),
        ),
        [
            wide,
            wide,
            pl.BlockSpec((chunks, group, size, size), lambda j, o: (0, j, 0, 0)),
            small,
            pl.BlockSpec((group, size, size), sent_block),
        ],
        4 * rows * depth * width,
        scratch=[pltpu.VMEM((rows, depth), BF16)],
    )


def later_kernel(chunk, group, size, _, *refs):
    xa, xb, wq, acc_q, k_ref, v_ref, along_ref, inside_ref, mid_ref, q_ref, within_ref, held = refs
    j = pl.program_id(0)
    rows = held.shape[0]

    @pl.when(j == 0)
    def _():
        held[: rows // 2, :] = xa[...]
        held[rows // 2 :, :] = xb[...]

    q_all = (acc_q[0] + dot(held[...], wq[0])).astype(BF16)
    q_ref[...] = q_all
    for a in range(group):
        head = j * group + a
        lanes = slice(a * size, (a + 1) * size)
        for c in range(rows // chunk):
            here = slice(c * chunk, (c + 1) * chunk)
            within_ref[here, lanes] = scores(
                q_all[here, lanes],
                k_ref[here, lanes],
                v_ref[here, lanes],
                along_ref[pl.ds(head, 1), here],
                column(inside_ref[here, :], head),
                mid_ref[c, a],
            )


def later_call(places, far, w_qkv, acc, k, v, along, inside, mid, group):
    _, rows, width = acc.shape
    chunks, heads, size = mid.shape[0], mid.shape[1], mid.shape[2]
    chunk = rows // chunks
    depth = far[0].shape[1]
    cols = group * size
    wide = pl.BlockSpec((rows, cols), lambda j, o: (0, j))
    return call(
        functools.partial(later_kernel, chunk, group, size),
        "later",
        heads // group,
        places,
        (*far, w_qkv, acc, k, v, along, inside, mid),
        [
            fixed(far[0].shape),
            fixed(far[1].shape),
            pl.BlockSpec((1, depth, cols), lambda j, o: (0, o[3], j)),
            pl.BlockSpec((1, rows, cols), lambda j, o: (0, 0, j)),
            wide,
            wide,
            pl.BlockSpec((heads, rows), lambda j, o: (0, 1)),
            pl.BlockSpec((rows, heads), lambda j, o: (1, 0)),
            pl.BlockSpec((chunks, group, size, size), lambda j, o: (0, j, 0, 0)),
        ],
        (struct((rows, width), BF16), struct((rows, width), F32)),
        [wide, wide],
        2 * rows * depth * width + 4 * rows * (chunk + size) * width,
        scratch=[pltpu.VMEM((rows, depth), BF16)],
    )


def fades(tail_ref, other_ref, place, head):
    own, other = tail_ref[pl.ds(head, 1), :], other_ref[pl.ds(head, 1), :]
    first = jnp.where(place == 0, own, other)
    return jnp.exp(-first), jnp.exp(first - (own + other)), jnp.exp(-(own + other))


def chip_kernel(places, state_ref, come_ref, tail_ref, other_ref, prior_ref, *out_refs):
    leaving_ref, chip_ref, first_ref = out_refs
    core, chip = places[4], places[5]
    share = come_ref.shape[0]
    for i in range(share):
        head = core * share + i
        _, second_fade, fade = fades(tail_ref, other_ref, core, head)
        ours, come = state_ref[head], come_ref[i].astype(F32)
        first, second = jnp.where(core == 0, ours, come), jnp.where(core == 0, come, ours)
        total = second_fade * first + second
        first_ref[i] = first
        chip_ref[i] = total
        leaving_ref[i] = jnp.where(chip == 2, total, fade * prior_ref[head] + total).astype(BF16)


def pass_kernel(places, come_ref, chip_ref, tail_ref, other_ref, leaving_ref):
    share = come_ref.shape[0]
    for i in range(share):
        fade = fades(tail_ref, other_ref, places[4], places[4] * share + i)[2]
        leaving_ref[i] = (fade * come_ref[i].astype(F32) + chip_ref[i]).astype(BF16)


def enter_kernel(
    places, come_ref, second_ref, third_ref, first_ref, tail_ref, other_ref, below_ref, prior_ref, *out_refs
):
    here_ref, passed_ref = out_refs
    core, chip = places[4], places[5]
    share = come_ref.shape[0]
    for i in range(share):
        head = core * share + i
        come = come_ref[i].astype(F32)
        below = jnp.exp(-below_ref[pl.ds(head, 1), :])
        state = jnp.where(chip == 0, prior_ref[head], come)
        state = jnp.where(chip == 2, second_ref[i].astype(F32), state)
        state = jnp.where(chip == 3, below * third_ref[i].astype(F32) + come, state)
        later = fades(tail_ref, other_ref, core, head)[0] * state + first_ref[i]
        here_ref[i] = jnp.where(core == 0, state, later).astype(BF16)
        passed_ref[i] = jnp.where(core == 0, later, state).astype(BF16)


def small_call(kernel, name, places, ins, outs):
    whole = pl.BlockSpec(memory_space=pltpu.VMEM)
    return pl.pallas_call(
        kernel,
        out_shape=tuple(outs),
        in_specs=[pl.BlockSpec(memory_space=pltpu.SMEM)] + [whole] * len(ins),
        out_specs=[whole] * len(outs),
        compiler_params=pltpu.CompilerParams(vmem_limit_bytes=4 * MIB),
        cost_estimate=pl.CostEstimate(flops=1, bytes_accessed=1, transcendentals=0),
        name=name,
    )(places, *ins)


def chip_call(places, state, come, tails, prior):
    outs = (struct(come.shape, BF16), struct(come.shape, F32), struct(come.shape, F32))
    return small_call(chip_kernel, "chip_state", places, (state, come, *tails, prior), outs)


def pass_call(places, come, chip_state, tails):
    outs = (struct(come.shape, BF16),)
    return small_call(pass_kernel, "pass_on", places, (come, chip_state, *tails), outs)[0]


def enter_call(places, come, second, third, first, tails, below, prior):
    outs = (struct(come.shape, BF16),) * 2
    ins = (come, second, third, first, *tails, below, prior)
    return small_call(enter_kernel, "enter", places, ins, outs)


def head_kernel(places, q_ref, within_ref, here_ref, there_ref, down_ref, w_ref, normed_ref, *out_refs):
    share, size = here_ref.shape[0], here_ref.shape[1]
    tall = q_ref.shape[0]
    for p, out_ref in enumerate(out_refs):
        rows = slice(p * tall, (p + 1) * tall)

        @pl.when(pl.program_id(0) == p)
        def _(rows=rows, out_ref=out_ref):
            fade = jnp.exp(-down_ref[...])
            for a in range(2 * share):
                lanes = slice(a * size, (a + 1) * size)
                ours = places[4] == a // share
                entering = jnp.where(ours, here_ref[a % share], there_ref[a % share])
                seen = dot(q_ref[:, lanes], entering) * fade[:, a : a + 1]
                combined = within_ref[:, lanes] + seen
                power = jnp.mean(combined * combined, axis=1, keepdims=True)
                normed_ref[rows, lanes] = (combined * lax.rsqrt(power + 1e-06)).astype(BF16)
            out_ref[:tall, :] = dot(normed_ref[rows, :], w_ref[...]).astype(BF16)

        @pl.when(pl.program_id(0) == 2 + p)
        def _(rows=rows, out_ref=out_ref):
            out_ref[tall:, :] = dot(normed_ref[rows, :], w_ref[...]).astype(BF16)


def head_call(places, blocks, q, within, entering, down, w_out, width, at):
    rows, cols = q.shape
    tall = rows // 2
    heads = down.shape[1]
    part = pl.BlockSpec((tall, cols), lambda i, o: (jnp.minimum(i, 1), 0))
    far, x, y = blocks
    return call(
        head_kernel,
        "heads",
        4,
        places,
        (q, within, *entering, down, w_out),
        [
            part,
            part,
            fixed(entering[0].shape),
            fixed(entering[1].shape),
            pl.BlockSpec((tall, heads), lambda i, o: (2 * at + jnp.minimum(i, 1), 0)),
            pl.BlockSpec(
                (cols, width),
                lambda i, o: (0, o[jnp.where(i < 2, far, jnp.where(i == 2, x, y))]),
            ),
        ],
        (struct((rows, cols), BF16), *[struct((rows, width), BF16)] * 2),
        [fixed((rows, cols))] + [fixed((rows, width))] * 2,
        2 * rows * cols * (2 * width + 128),
        light=True,
    )


def pair_kernel(_, normed_ref, x_ref, y_ref, w_ref, out_x_ref, out_y_ref):
    tall = x_ref.shape[0]

    @pl.when(pl.program_id(0) == 0)
    def _():
        out_x_ref[...] = (dot(normed_ref[tall:, :], w_ref[...]) + x_ref[...].astype(F32)).astype(BF16)

    @pl.when(pl.program_id(0) == 1)
    def _():
        out_y_ref[...] = (dot(normed_ref[:tall, :], w_ref[...]) + y_ref[...].astype(F32)).astype(BF16)


def pair_call(places, normed, for_x, for_y, w_out, width):
    rows, cols = normed.shape
    quarter = (rows // 2, width)
    return call(
        pair_kernel,
        "sum_pair",
        2,
        places,
        (normed, for_x, for_y, w_out),
        [
            fixed((rows, cols)),
            fixed(quarter),
            fixed(quarter),
            pl.BlockSpec((cols, width), lambda i, o: (0, o[1 + i])),
        ],
        (struct(quarter, BF16),) * 2,
        [fixed(quarter)] * 2,
        2 * rows * cols * width,
        light=True,
    )


def own_kernel(_, normed_ref, w_ref, *refs):
    out_ref = refs[-1]
    tall = out_ref.shape[0]
    each = len(refs) // 2
    for p in range(2):
        rows = slice(p * tall, (p + 1) * tall)

        @pl.when(pl.program_id(0) == p)
        def _(p=p, rows=rows):
            total = dot(normed_ref[rows, :], w_ref[...])
            for ref in refs[p * each : (p + 1) * each]:
                total = total + ref[...].astype(F32)
            out_ref[...] = total.astype(BF16)


def own_call(places, normed, first, second, w_out, width, height):
    rows, cols = normed.shape
    quarter = (rows // 2, width)
    return call(
        own_kernel,
        "own_block",
        2,
        places,
        (normed, w_out, *[a for a, _ in (*first, *second)]),
        [fixed((rows, cols)), pl.BlockSpec((cols, width), lambda i, o: (0, o[0]))]
        + [pl.BlockSpec(quarter, lambda i, o, at=at: (at, 0)) for _, at in (*first, *second)],
        (struct((rows * height, width), BF16),),
        [pl.BlockSpec(quarter, lambda i, o: (i, 0))],
        2 * rows * cols * width,
        light=True,
    )[0]


def last_kernel(_, kept_ref, a_ref, b_ref, above_ref, out_ref):
    del above_ref

    @pl.when(pl.program_id(0) == 0)
    def _():
        out_ref[...] = (kept_ref[...].astype(F32) + a_ref[...].astype(F32)).astype(BF16)

    @pl.when(pl.program_id(0) == 1)
    def _():
        out_ref[...] = (kept_ref[...].astype(F32) + b_ref[...].astype(F32)).astype(BF16)


def last_call(kept, a, b, above):
    tall, width = a.shape
    return call(
        last_kernel,
        "last_add",
        2,
        jnp.zeros((1,), jnp.int32),
        (kept, a, b, above),
        [
            pl.BlockSpec((tall, width), lambda j, o: (j, 0)),
            fixed((tall, width)),
            fixed((tall, width)),
            pl.BlockSpec(memory_space=pl.ANY),
        ],
        (struct(above.shape, BF16),),
        [pl.BlockSpec((tall, width), lambda j, o: (2 + j, 0))],
        tall * width,
        aliases={4: 0},
    )[0]


def local(n_head, n_seq, tokens, w_qkv, w_out, decay_rate, prior_state):
    rows, width = tokens.shape
    heads, size = prior_state.shape[0], prior_state.shape[1]
    square = n_head == 4
    place = lax.axis_index("head").astype(jnp.int32)
    quarter = rows // 4
    group = 2 if heads % 2 == 0 else 1
    cols = group * size

    over_x = functools.partial(lax.ppermute, axis_name="head", perm=[(i, i ^ 1) for i in range(n_head)])
    over_y = functools.partial(lax.ppermute, axis_name="head", perm=[(i, i ^ 2) for i in range(n_head)])

    pos = lax.axis_index("seq").astype(jnp.int32)
    core, chip = pos % 2, pos // 2
    flips = (0, 1, 2, 3) if square else (0, 0, 0, 0)
    places = jnp.stack([*[place ^ f for f in flips], core, chip])

    along, inside, down, tail = decay_call(decay_rate, quarter)
    n_chips = n_seq // 2
    swap = functools.partial(lax.ppermute, axis_name="seq", perm=[(i, i ^ 1) for i in range(n_seq)])

    def hop(x, *pairs):
        perm = [(2 * a + c, 2 * b + c) for a, b in pairs for c in range(2)]
        return lax.ppermute(x, "seq", perm=perm)

    def chip_tails(tail):
        other = swap(tail)
        return other, tail + other, hop(tail + other, (2, 3)) if n_chips == 4 else None

    if square:
        tokens = stay(tokens)
        q0, q1 = cut_call(tokens)
        x0, y1 = over_x(q0), over_y(q1)
        x1, y0 = over_x(after(q1, inside)), over_y(after(q0, inside))
        acc, q2, q3 = own_part_call(places, after(tokens, inside), w_qkv, cols)
        acc = stay(acc)
        fy0, fx1 = over_y(x0), over_x(y1)
        tail_other, tail_chip, tail_below = chip_tails(after(tail, x0, y1, acc))
        x2 = over_x(after(q2, x1, y0, tail_chip))
        y3 = over_y(after(q3, x1, y0, tail_chip))
        acc_a = part_call(
            places,
            (1, 2),
            [(x0, x1), (y0, y1)],
            w_qkv,
            2 * quarter,
            cols,
            before=stay(after(acc, tail_chip)),
            at=0,
        )
        earlier = (fy0, fx1, acc_a) if tail_below is None else (fy0, fx1, acc_a, tail_below)
        x3, y2 = over_x(after(q3, *earlier)), over_y(after(q2, *earlier))
        query_a, within_a, state = first_call(
            places,
            (3,),
            [(fy0, fx1)],
            (acc_a,),
            w_qkv,
            along,
            inside,
            2 * quarter,
            quarter,
            size,
            group,
        )
        fy2, fx3 = over_y(after(x2, state)), over_x(after(y3, state))
        acc_q, acc_kv = part_call(
            places,
            (1, 2),
            [(x2, x3), (y2, y3)],
            w_qkv,
            2 * quarter,
            cols,
            before=acc,
            at=1,
            apart=True,
        )
        far = (fy2, fx3)
        k, v, mid, state, sent = state_call(
            places, far, w_qkv, acc_kv, inside, state, quarter, group
        )
    else:
        tail_other, tail_chip, tail_below = chip_tails(tail)
        gathered = lax.all_gather(tokens, "head", axis=1, tiled=True)
        query, within, state = first_call(
            places, (), [(gathered,)], (), w_qkv, along, inside, rows, quarter, size, group
        )

    tails = (tail, tail_other)
    if square and n_chips == 4:
        leaving, chip_state, first = chip_call(places, state, near(swap(sent)), tails, prior_state)
        arriving = near(hop(leaving, (0, 1), (2, 3)))
        leaving = pass_call(places, arriving, chip_state, tails)
        to_third, to_second = near(hop(leaving, (1, 3))), near(hop(leaving, (1, 2)))
        here, passed = enter_call(
            places, arriving, to_second, to_third, first, tails, tail_below, prior_state
        )
    else:
        share = heads // 2

        def mine(x, core=core):
            return lax.dynamic_slice_in_dim(x, core * share, share, 0)

        def decay(tail):
            return jnp.exp(-mine(tail)[:, :1, None])

        ours = mine(state)
        other = swap(mine(state, 1 - core).astype(BF16)).astype(F32)
        first = jnp.where(core == 0, ours, other)
        second = jnp.where(core == 0, other, ours)
        chip_state = decay(jnp.where(core == 0, tail_other, tail)) * first + second
        chip_entering = mine(prior_state)
        for step in range(n_chips - 1):
            leaving = (decay(tail_chip) * chip_entering + chip_state).astype(BF16)
            arriving = hop(leaving, (step, step + 1))
            chip_entering = jnp.where(chip == step + 1, arriving.astype(F32), chip_entering)
        other = decay(jnp.where(core == 0, tail, tail_other)) * chip_entering + first
        here = jnp.where(core == 0, chip_entering, other).astype(BF16)
        passed = jnp.where(core == 0, other, chip_entering).astype(BF16)
    entering = (here, swap(passed))

    if not square:
        halves = [
            head_call(
                places,
                (0, 0, 0),
                query[r * rows // 2 : (r + 1) * rows // 2],
                within[r * rows // 2 : (r + 1) * rows // 2],
                entering,
                down,
                w_out,
                width,
                r,
            )[0]
            for r in range(2)
        ]
        partial = dot(jnp.concatenate(halves), w_out).astype(BF16)
        return lax.psum_scatter(partial, "head", scatter_dimension=1, tiled=True)

    na, by_x, by_y = head_call(
        places, (3, 1, 2), stay(query_a), stay(within_a), entering, down, w_out, width, 0
    )
    by_x, by_y = over_x(by_x), over_y(by_y)
    query_b, within_b = later_call(
        places, far, w_qkv, stay(acc_q), stay(k), stay(v), along, inside, stay(after(mid, na)), group
    )
    nb, by_x2, by_y2 = head_call(
        places, (3, 1, 2), query_b, within_b, entering, down, w_out, width, 1
    )
    by_x2, by_y2 = over_x(by_x2), over_y(by_y2)
    sum1, sum0 = pair_call(places, after(na, nb), by_y, by_x, w_out, width)
    by_x2, by_y2 = after(by_x2, sum1), after(by_y2, sum1)
    sum1, sum0 = over_x(sum1), over_y(sum0)
    sum3, sum2 = pair_call(places, nb, by_y2, by_x2, w_out, width)
    sum3, sum2 = over_x(sum3), over_y(sum2)
    below = own_call(places, after(nb, sum1, sum0), ((by_x2, 1),), ((by_y2, 1),), w_out, width, 1)
    above = own_call(
        places, na, ((by_x, 1), (sum0, 0)), ((by_y, 1), (sum1, 0)), w_out, width, 2
    )
    return last_call(below, sum2, sum3, above)


def solution(mesh):
    in_specs = (
        P("seq", "head"),
        P(None, None, "head"),
        P("head", None),
        P("head", "seq"),
        P("head", None, None),
    )
    body = functools.partial(local, mesh.shape["head"], mesh.shape["seq"])
    return jax.shard_map(
        body, mesh=mesh, in_specs=in_specs, out_specs=P("seq", "head"), check_vma=False
    )
```

```python
import functools
import math

import jax
import jax.numpy as jnp
from jax import lax
from jax.experimental import pallas as pl
from jax.experimental.pallas import tpu as pltpu
from jax.sharding import PartitionSpec as P

BF16, F32 = jnp.bfloat16, jnp.float32
MIB = 1024 * 1024


def dot(a, b, contract=((1,), (0,))):
    return lax.dot_general(a, b, (contract, ((), ())), preferred_element_type=F32)


def after(x, *earlier):
    return lax.optimization_barrier((x, *earlier))[0]


def struct(shape, dtype):
    return jax.ShapeDtypeStruct(shape, dtype)


def stay(x):
    return pltpu.with_memory_space_constraint(x, pltpu.HBM)


def near(x):
    return pltpu.with_memory_space_constraint(x, pltpu.VMEM)


def fixed(shape):
    return pl.BlockSpec(shape, lambda j, o: (0,) * len(shape))


def call(kernel, name, steps, scalars, ins, in_specs, outs, out_specs, flops, scratch=(), aliases=None, light=False):
    moved = sum(a.size * a.dtype.itemsize for a in ins) + sum(
        math.prod(o.shape) * jnp.dtype(o.dtype).itemsize for o in outs
    )
    return pl.pallas_call(
        kernel,
        out_shape=tuple(outs),
        grid_spec=pltpu.PrefetchScalarGridSpec(
            num_scalar_prefetch=1,
            grid=(steps,),
            in_specs=in_specs,
            out_specs=out_specs,
            scratch_shapes=list(scratch),
        ),
        input_output_aliases=aliases or {},
        compiler_params=pltpu.CompilerParams(vmem_limit_bytes=(24 if light else 32) * MIB),
        cost_estimate=pl.CostEstimate(
            flops=1 if light else flops, bytes_accessed=1 if light else moved, transcendentals=0
        ),
        name=name,
    )(scalars, *ins)


def cut_kernel(_, x_ref, a_ref, b_ref):
    tall = a_ref.shape[0]
    a_ref[...] = x_ref[:tall, :]
    b_ref[...] = x_ref[tall:, :]


def cut_call(x):
    rows, width = x.shape
    quarter = (rows // 4, width)
    return call(
        cut_kernel,
        "cut",
        1,
        jnp.zeros((1,), jnp.int32),
        (x,),
        [fixed((rows // 2, width))],
        (struct(quarter, x.dtype),) * 2,
        [fixed(quarter)] * 2,
        1,
    )


def decay_kernel(chunk, _, rate_ref, along_ref, inside_ref, down_ref, tail_ref, end_ref, half_ref):
    heads, rows = rate_ref.shape
    lane = lax.broadcasted_iota(jnp.int32, (heads, chunk), 1)
    base = jnp.zeros((heads, 1), F32)
    insides, wholes = [], []
    for c in range(rows // chunk):
        x = rate_ref[:, c * chunk : (c + 1) * chunk]
        step = 1
        while step < chunk:
            x = x + jnp.where(lane >= step, pltpu.roll(x, step, 1), 0.0)
            step *= 2
        insides.append(x)
        wholes.append(x + base)
        base = base + x[:, chunk - 1 :]
    inside, whole = jnp.concatenate(insides, axis=1), jnp.concatenate(wholes, axis=1)
    along_ref[...] = inside
    inside_ref[...] = inside.T
    down_ref[...] = whole.T
    tail_ref[...] = jnp.broadcast_to(base, tail_ref.shape)
    end_ref[...] = jnp.exp(whole - base)
    half_ref[...] = jnp.broadcast_to(jnp.exp(whole[:, rows // 2 - 1 : rows // 2] - base), half_ref.shape)


def decay_call(rate, chunk):
    heads, rows = rate.shape
    return call(
        functools.partial(decay_kernel, chunk),
        "decay",
        1,
        jnp.zeros((1,), jnp.int32),
        (rate,),
        [fixed((heads, rows))],
        (
            struct((heads, rows), F32),
            struct((rows, heads), F32),
            struct((rows, heads), F32),
            struct((heads, 128), F32),
            struct((heads, rows), F32),
            struct((heads, 128), F32),
        ),
        [
            fixed((heads, rows)),
            fixed((rows, heads)),
            fixed((rows, heads)),
            fixed((heads, 128)),
            fixed((heads, rows)),
            fixed((heads, 128)),
        ],
        heads * rows * 16,
    )


def column(table, head):
    lane = lax.broadcasted_iota(jnp.int32, table.shape, 1)
    return jnp.sum(jnp.where(lane == head, table, 0.0), axis=1, keepdims=True)


def scores(q, k, v, along, down, state):
    rows = q.shape[0]
    causal = lax.broadcasted_iota(jnp.int32, (rows, rows), 0) >= lax.broadcasted_iota(
        jnp.int32, (rows, rows), 1
    )
    decay = jnp.exp(jnp.minimum(along - down, 0.0))
    weights = jnp.where(causal, dot(q, k, ((1,), (1,))) * decay, 0.0).astype(BF16)
    return dot(weights, v) + dot(q, state.astype(BF16)) * jnp.exp(-down)


def advance(k, v, down, state):
    last = down[down.shape[0] - 1 :, :]
    scaled = (k.astype(F32) * jnp.exp(down - last)).astype(BF16)
    return jnp.exp(-last) * state + dot(scaled, v, ((0,), (0,)))


def first_kernel(layout, added, chunk, group, size, _, *refs):
    count = sum(layout)
    x_refs, w_refs, refs = refs[:count], refs[count : count + len(layout)], refs[count + len(layout) :]
    along_ref, inside_ref, q_ref, within_ref, state_ref, held = refs[-6:]
    j = pl.program_id(0)
    rows = held.shape[1]

    @pl.when(j == 0)
    def _():
        at = 0
        for i, parts in enumerate(layout):
            tall = rows // parts
            for p in range(parts):
                held[i, p * tall : (p + 1) * tall, :] = x_refs[at][...]
                at += 1

    def project(c):
        total = dot(held[0], w_refs[0][c])
        for i in range(1, len(layout)):
            total = total + dot(held[i], w_refs[i][c])
        if added:
            total = total + refs[0][c]
        return total.astype(BF16)

    q_all, k_all, v_all = project(0), project(1), project(2)
    q_ref[...] = q_all
    for a in range(group):
        head = j * group + a
        lanes = slice(a * size, (a + 1) * size)
        state = jnp.zeros((size, size), F32)
        for c in range(rows // chunk):
            here = slice(c * chunk, (c + 1) * chunk)
            q, k, v = q_all[here, lanes], k_all[here, lanes], v_all[here, lanes]
            down = column(inside_ref[here, :], head)
            along = along_ref[pl.ds(head, 1), here]
            within_ref[here, lanes] = scores(q, k, v, along, down, state)
            state = advance(k, v, down, state)
        state_ref[a] = state


def first_call(places, blocks, pieces, before, w_qkv, along, inside, rows, chunk, size, group):
    heads = along.shape[0]
    cols = group * size
    flat = [p for piece in pieces for p in piece]
    depth = flat[0].shape[1]

    def block(i):
        return pl.BlockSpec((3, depth, cols), lambda j, o: (0, o[blocks[i]] if blocks else 0, j))

    wide = pl.BlockSpec((rows, cols), lambda j, o: (0, j))
    return call(
        functools.partial(
            first_kernel, tuple(len(p) for p in pieces), bool(before), chunk, group, size
        ),
        "first",
        heads // group,
        places,
        (*flat, *[w_qkv] * len(pieces), *before, along, inside),
        [
            pl.BlockSpec((rows // len(piece), depth), lambda j, o: (0, 0))
            for piece in pieces
            for _ in piece
        ]
        + [block(i) for i in range(len(pieces))]
        + [pl.BlockSpec((3, rows, cols), lambda j, o: (0, 0, j)) for _ in before]
        + [fixed((heads, rows)), fixed((rows, heads))],
        (
            pltpu.HBM((rows, heads * size), BF16),
            pltpu.HBM((rows, heads * size), F32),
            struct((heads, size, size), F32),
        ),
        [wide, wide, pl.BlockSpec((group, size, size), lambda j, o: (j, 0, 0))],
        2 * rows * 3 * heads * size * depth * len(pieces),
        scratch=[pltpu.VMEM((len(pieces), rows, depth), BF16)],
    )


def own_part_kernel(_, x_ref, w_ref, out_ref, *cut_refs):
    @pl.when(pl.program_id(0) == 0)
    def _():
        for i, ref in enumerate(cut_refs):
            tall = ref.shape[0]
            ref[...] = x_ref[i * tall : (i + 1) * tall, :]

    for c in range(3):
        out_ref[c] = dot(x_ref[...], w_ref[c])


def own_part_call(places, tokens, w_qkv, cols, half, cuts):
    rows, depth = tokens.shape[0] // 2, tokens.shape[1]
    width = w_qkv.shape[2]
    quarter = (rows // 2, depth)
    return call(
        own_part_kernel,
        "own_part",
        width // cols,
        places,
        (tokens, w_qkv),
        [
            pl.BlockSpec((rows, depth), lambda j, o: (half, 0)),
            pl.BlockSpec((3, depth, cols), lambda j, o: (0, o[0], j)),
        ],
        (pltpu.HBM((3, rows, width), F32), *[pltpu.HBM(quarter, BF16)] * cuts),
        [pl.BlockSpec((3, rows, cols), lambda j, o: (0, 0, j))] + [fixed(quarter)] * cuts,
        2 * rows * depth * width * 3,
    )


def part_kernel(layout, outs, _, *refs):
    count = sum(layout)
    x_refs, w_refs = refs[:count], refs[count : count + len(layout)]
    before_ref, out_refs, held = refs[-2 - outs], refs[-1 - outs : -1], refs[-1]
    targets = [(ref, c) for ref in out_refs for c in range(ref.shape[0])]
    rows = held.shape[1]

    @pl.when(pl.program_id(0) == 0)
    def _():
        at = 0
        for i, parts in enumerate(layout):
            tall = rows // parts
            for p in range(parts):
                held[i, p * tall : (p + 1) * tall, :] = x_refs[at][...]
                at += 1

    for c in range(3):
        total = dot(held[0], w_refs[0][c])
        for i in range(1, len(layout)):
            total = total + dot(held[i], w_refs[i][c])
        ref, at = targets[c]
        ref[at] = total + before_ref[c]


def part_call(places, blocks, pieces, w_qkv, rows, cols, before, apart=False):
    flat = [p for piece in pieces for p in piece]
    depth = flat[0].shape[1]
    width = w_qkv.shape[2]

    def block(i):
        return pl.BlockSpec((3, depth, cols), lambda j, o: (0, o[blocks[i]], j))

    ins = [*flat, *[w_qkv] * len(pieces)]
    specs = [
        pl.BlockSpec((rows // len(piece), depth), lambda j, o: (0, 0)) for piece in pieces for _ in piece
    ] + [block(i) for i in range(len(pieces))]
    ins.append(before)
    specs.append(pl.BlockSpec((3, rows, cols), lambda j, o: (0, 0, j)))
    outs = [struct((3, rows, width), F32)]
    if apart:
        outs = [pltpu.HBM((1, rows, width), F32), struct((2, rows, width), F32)]
    out = call(
        functools.partial(part_kernel, tuple(len(p) for p in pieces), len(outs)),
        "part",
        width // cols,
        places,
        ins,
        specs,
        outs,
        [pl.BlockSpec((o.shape[0], rows, cols), lambda j, o: (0, 0, j)) for o in outs],
        2 * rows * depth * len(pieces) * width * 3,
        scratch=[pltpu.VMEM((len(pieces), rows, depth), BF16)],
    )
    return out if apart else out[0]


def state_kernel(group, size, places, *refs):
    xa, xb, wk, wv, acc_k, acc_v, end_ref, half_ref, state_ref = refs[:9]
    k_ref, v_ref, out_ref, sent_ref, held = refs[9:]
    j = pl.program_id(0)
    rows = held.shape[0]

    @pl.when(j == 0)
    def _():
        held[: rows // 2, :] = xa[...]
        held[rows // 2 :, :] = xb[...]

    k_all = (acc_k[0] + dot(held[...], wk[0])).astype(BF16)
    v_all = (acc_v[0] + dot(held[...], wv[0])).astype(BF16)
    k_ref[...] = k_all
    v_ref[...] = v_all
    ends = []
    for a in range(group):
        head = pl.ds(j * group + a, 1)
        lanes = slice(a * size, (a + 1) * size)
        scaled = (k_all[:, lanes].astype(F32).T * end_ref[head, :]).astype(BF16)
        end = half_ref[head, :] * state_ref[a] + dot(scaled, v_all[:, lanes])
        out_ref[a] = end
        ends.append(end.astype(BF16))
    half = pl.num_programs(0) // 2

    @pl.when(jnp.where(places[4] == 0, j >= half, j < half))
    def _():
        for a in range(group):
            sent_ref[a] = ends[a]


def state_call(places, far, w_qkv, acc, to_end, half_fade, state, group):
    _, rows, width = acc.shape
    heads, size = state.shape[0], state.shape[1]
    depth = far[0].shape[1]
    cols = group * size
    wide = pl.BlockSpec((rows, cols), lambda j, o: (0, j))
    small = pl.BlockSpec((group, size, size), lambda j, o: (j, 0, 0))
    half = heads // group // 2

    def sent_block(j, o):
        return jnp.where(o[4] == 0, jnp.maximum(j - half, 0), jnp.minimum(j, half - 1)), 0, 0

    return call(
        functools.partial(state_kernel, group, size),
        "states",
        heads // group,
        places,
        (*far, w_qkv, w_qkv, acc, acc, to_end, half_fade, state),
        [fixed(far[0].shape), fixed(far[1].shape)]
        + [pl.BlockSpec((1, depth, cols), lambda j, o, c=c: (c, o[3], j)) for c in (1, 2)]
        + [pl.BlockSpec((1, rows, cols), lambda j, o, c=c: (c, 0, j)) for c in (0, 1)]
        + [pl.BlockSpec((heads, rows), lambda j, o: (0, 1)), fixed(half_fade.shape), small],
        (
            pltpu.HBM((rows, width), BF16),
            pltpu.HBM((rows, width), BF16),
            struct(state.shape, F32),
            struct((heads // 2, size, size), BF16),
        ),
        [wide, wide, small, pl.BlockSpec((group, size, size), sent_block)],
        4 * rows * depth * width,
        scratch=[pltpu.VMEM((rows, depth), BF16)],
    )


def later_kernel(chunk, group, size, _, *refs):
    xa, xb, wq, acc_q, k_ref, v_ref, along_ref, inside_ref, state_ref, q_ref, within_ref, held = refs
    j = pl.program_id(0)
    rows = held.shape[0]

    @pl.when(j == 0)
    def _():
        held[: rows // 2, :] = xa[...]
        held[rows // 2 :, :] = xb[...]

    q_all = (acc_q[0] + dot(held[...], wq[0])).astype(BF16)
    q_ref[...] = q_all
    for a in range(group):
        head = j * group + a
        lanes = slice(a * size, (a + 1) * size)
        state = state_ref[a]
        for c in range(rows // chunk):
            here = slice(c * chunk, (c + 1) * chunk)
            q, k, v = q_all[here, lanes], k_ref[here, lanes], v_ref[here, lanes]
            along, down = along_ref[pl.ds(head, 1), here], column(inside_ref[here, :], head)
            within_ref[here, lanes] = scores(q, k, v, along, down, state)
            if c + 1 < rows // chunk:
                state = advance(k, v, down, state)


def later_call(places, far, w_qkv, acc, k, v, along, inside, state, chunk, group):
    _, rows, width = acc.shape
    heads, size = state.shape[0], state.shape[1]
    depth = far[0].shape[1]
    cols = group * size
    wide = pl.BlockSpec((rows, cols), lambda j, o: (0, j))
    return call(
        functools.partial(later_kernel, chunk, group, size),
        "later",
        heads // group,
        places,
        (*far, w_qkv, acc, k, v, along, inside, state),
        [
            fixed(far[0].shape),
            fixed(far[1].shape),
            pl.BlockSpec((1, depth, cols), lambda j, o: (0, o[3], j)),
            pl.BlockSpec((1, rows, cols), lambda j, o: (0, 0, j)),
            wide,
            wide,
            pl.BlockSpec((heads, rows), lambda j, o: (0, 1)),
            pl.BlockSpec((rows, heads), lambda j, o: (1, 0)),
            pl.BlockSpec((group, size, size), lambda j, o: (j, 0, 0)),
        ],
        (struct((rows, width), BF16), struct((rows, width), F32)),
        [wide, wide],
        2 * rows * depth * width + 4 * rows * (chunk + size) * width,
        scratch=[pltpu.VMEM((rows, depth), BF16)],
    )


def fades(tail_ref, other_ref, place, head):
    own, other = tail_ref[pl.ds(head, 1), :], other_ref[pl.ds(head, 1), :]
    first = jnp.where(place == 0, own, other)
    return jnp.exp(-first), jnp.exp(first - (own + other)), jnp.exp(-(own + other))


def chip_kernel(places, state_ref, come_ref, tail_ref, other_ref, prior_ref, *out_refs):
    leaving_ref, chip_ref, first_ref = out_refs
    core, chip = places[4], places[5]
    share = come_ref.shape[0]
    for i in range(share):
        head = core * share + i
        _, second_fade, fade = fades(tail_ref, other_ref, core, head)
        ours, come = state_ref[head], come_ref[i].astype(F32)
        first, second = jnp.where(core == 0, ours, come), jnp.where(core == 0, come, ours)
        total = second_fade * first + second
        first_ref[i] = first
        chip_ref[i] = total
        leaving_ref[i] = jnp.where(chip == 2, total, fade * prior_ref[head] + total).astype(BF16)


def pass_kernel(places, come_ref, chip_ref, tail_ref, other_ref, leaving_ref):
    share = come_ref.shape[0]
    for i in range(share):
        fade = fades(tail_ref, other_ref, places[4], places[4] * share + i)[2]
        leaving_ref[i] = (fade * come_ref[i].astype(F32) + chip_ref[i]).astype(BF16)


def enter_kernel(
    places, come_ref, second_ref, third_ref, first_ref, tail_ref, other_ref, below_ref, prior_ref, *out_refs
):
    here_ref, passed_ref = out_refs
    core, chip = places[4], places[5]
    share = come_ref.shape[0]
    for i in range(share):
        head = core * share + i
        come = come_ref[i].astype(F32)
        below = jnp.exp(-below_ref[pl.ds(head, 1), :])
        state = jnp.where(chip == 0, prior_ref[head], come)
        state = jnp.where(chip == 2, second_ref[i].astype(F32), state)
        state = jnp.where(chip == 3, below * third_ref[i].astype(F32) + come, state)
        later = fades(tail_ref, other_ref, core, head)[0] * state + first_ref[i]
        here_ref[i] = jnp.where(core == 0, state, later).astype(BF16)
        passed_ref[i] = jnp.where(core == 0, later, state).astype(BF16)


def small_call(kernel, name, places, ins, outs):
    whole = pl.BlockSpec(memory_space=pltpu.VMEM)
    return pl.pallas_call(
        kernel,
        out_shape=tuple(outs),
        in_specs=[pl.BlockSpec(memory_space=pltpu.SMEM)] + [whole] * len(ins),
        out_specs=[whole] * len(outs),
        compiler_params=pltpu.CompilerParams(vmem_limit_bytes=4 * MIB),
        cost_estimate=pl.CostEstimate(flops=1, bytes_accessed=1, transcendentals=0),
        name=name,
    )(places, *ins)


def chip_call(places, state, come, tails, prior):
    outs = (struct(come.shape, BF16), struct(come.shape, F32), struct(come.shape, F32))
    return small_call(chip_kernel, "chip_state", places, (state, come, *tails, prior), outs)


def pass_call(places, come, chip_state, tails):
    outs = (struct(come.shape, BF16),)
    return small_call(pass_kernel, "pass_on", places, (come, chip_state, *tails), outs)[0]


def enter_call(places, come, second, third, first, tails, below, prior):
    outs = (struct(come.shape, BF16),) * 2
    ins = (come, second, third, first, *tails, below, prior)
    return small_call(enter_kernel, "enter", places, ins, outs)


def head_kernel(places, q_ref, within_ref, here_ref, there_ref, down_ref, w_ref, normed_ref, *out_refs):
    share, size = here_ref.shape[0], here_ref.shape[1]
    tall = q_ref.shape[0]
    for p, out_ref in enumerate(out_refs):
        rows = slice(p * tall, (p + 1) * tall)

        @pl.when(pl.program_id(0) == p)
        def _(rows=rows, out_ref=out_ref):
            fade = jnp.exp(-down_ref[...])
            for a in range(2 * share):
                lanes = slice(a * size, (a + 1) * size)
                ours = places[4] == a // share
                entering = jnp.where(ours, here_ref[a % share], there_ref[a % share])
                seen = dot(q_ref[:, lanes], entering) * fade[:, a : a + 1]
                combined = within_ref[:, lanes] + seen
                power = jnp.mean(combined * combined, axis=1, keepdims=True)
                normed_ref[rows, lanes] = (combined * lax.rsqrt(power + 1e-06)).astype(BF16)
            out_ref[:tall, :] = dot(normed_ref[rows, :], w_ref[...]).astype(BF16)

        if out_ref.shape[0] > tall:

            @pl.when(pl.program_id(0) == 2 + p)
            def _(rows=rows, out_ref=out_ref):
                out_ref[tall:, :] = dot(normed_ref[rows, :], w_ref[...]).astype(BF16)


def head_call(places, blocks, q, within, entering, down, w_out, width, at):
    rows, cols = q.shape
    tall = rows // 2
    heads = down.shape[1]
    part = pl.BlockSpec((tall, cols), lambda i, o: (jnp.minimum(i, 1), 0))
    near = len(blocks) > 1
    out = (tall * (2 if near else 1), width)

    def columns(i, o):
        if not near:
            return 0, o[blocks[0]]
        return 0, o[jnp.where(i < 2, blocks[0], jnp.where(i == 2, blocks[1], blocks[2]))]

    return call(
        head_kernel,
        "heads",
        4 if near else 2,
        places,
        (q, within, *entering, down, w_out),
        [
            part,
            part,
            fixed(entering[0].shape),
            fixed(entering[1].shape),
            pl.BlockSpec((tall, heads), lambda i, o: (2 * at + jnp.minimum(i, 1), 0)),
            pl.BlockSpec((cols, width), columns),
        ],
        (struct((rows, cols), BF16), *[struct(out, BF16)] * 2),
        [fixed((rows, cols))] + [fixed(out)] * 2,
        2 * rows * cols * (2 * width + 128),
        light=True,
    )


def pair_kernel(_, normed_ref, x_ref, y_ref, w_ref, out_x_ref, out_y_ref):
    tall = x_ref.shape[0]

    @pl.when(pl.program_id(0) == 0)
    def _():
        out_x_ref[...] = (dot(normed_ref[tall:, :], w_ref[...]) + x_ref[...].astype(F32)).astype(BF16)

    @pl.when(pl.program_id(0) == 1)
    def _():
        out_y_ref[...] = (dot(normed_ref[:tall, :], w_ref[...]) + y_ref[...].astype(F32)).astype(BF16)


def pair_call(places, normed, for_x, for_y, w_out, width):
    rows, cols = normed.shape
    quarter = (rows // 2, width)
    return call(
        pair_kernel,
        "sum_pair",
        2,
        places,
        (normed, for_x, for_y, w_out),
        [
            fixed((rows, cols)),
            fixed(quarter),
            fixed(quarter),
            pl.BlockSpec((cols, width), lambda i, o: (0, o[1 + i])),
        ],
        (struct(quarter, BF16),) * 2,
        [fixed(quarter)] * 2,
        2 * rows * cols * width,
        light=True,
    )


def own_kernel(_, normed_ref, w_ref, *refs):
    out_ref = refs[-1]
    tall = out_ref.shape[0]
    each = len(refs) // 2
    for p in range(2):
        rows = slice(p * tall, (p + 1) * tall)

        @pl.when(pl.program_id(0) == p)
        def _(p=p, rows=rows):
            total = dot(normed_ref[rows, :], w_ref[...])
            for ref in refs[p * each : (p + 1) * each]:
                total = total + ref[...].astype(F32)
            out_ref[...] = total.astype(BF16)


def own_call(places, normed, first, second, w_out, width, height):
    rows, cols = normed.shape
    quarter = (rows // 2, width)
    return call(
        own_kernel,
        "own_block",
        2,
        places,
        (normed, w_out, *[a for a, _ in (*first, *second)]),
        [fixed((rows, cols)), pl.BlockSpec((cols, width), lambda i, o: (0, o[0]))]
        + [pl.BlockSpec(quarter, lambda i, o, at=at: (at, 0)) for _, at in (*first, *second)],
        (struct((rows * height, width), BF16),),
        [pl.BlockSpec(quarter, lambda i, o: (i, 0))],
        2 * rows * cols * width,
        light=True,
    )[0]


def last_kernel(_, kept_ref, a_ref, b_ref, above_ref, out_ref):
    del above_ref

    @pl.when(pl.program_id(0) == 0)
    def _():
        out_ref[...] = (kept_ref[...].astype(F32) + a_ref[...].astype(F32)).astype(BF16)

    @pl.when(pl.program_id(0) == 1)
    def _():
        out_ref[...] = (kept_ref[...].astype(F32) + b_ref[...].astype(F32)).astype(BF16)


def last_call(kept, a, b, above):
    tall, width = a.shape
    return call(
        last_kernel,
        "last_add",
        2,
        jnp.zeros((1,), jnp.int32),
        (kept, a, b, above),
        [
            pl.BlockSpec((tall, width), lambda j, o: (j, 0)),
            fixed((tall, width)),
            fixed((tall, width)),
            pl.BlockSpec(memory_space=pl.ANY),
        ],
        (struct(above.shape, BF16),),
        [pl.BlockSpec((tall, width), lambda j, o: (2 + j, 0))],
        tall * width,
        aliases={4: 0},
    )[0]


def local(n_head, n_seq, tokens, w_qkv, w_out, decay_rate, prior_state):
    rows, width = tokens.shape
    heads, size = prior_state.shape[0], prior_state.shape[1]
    square = n_head == 4
    place = lax.axis_index("head").astype(jnp.int32)
    quarter = rows // 4
    group = 2 if heads % 2 == 0 else 1
    cols = group * size

    over_x = functools.partial(lax.ppermute, axis_name="head", perm=[(i, i ^ 1) for i in range(n_head)])
    over_y = functools.partial(lax.ppermute, axis_name="head", perm=[(i, i ^ 2) for i in range(n_head)])

    pos = lax.axis_index("seq").astype(jnp.int32)
    core, chip = pos % 2, pos // 2
    flips = (0, 1, 2, 3) if square else (0, 0, 0, 0)
    places = jnp.stack([*[place ^ f for f in flips], core, chip])

    along, inside, down, tail, to_end, half_fade = decay_call(decay_rate, quarter)
    n_chips = n_seq // 2
    swap = functools.partial(lax.ppermute, axis_name="seq", perm=[(i, i ^ 1) for i in range(n_seq)])

    def hop(x, *pairs):
        perm = [(2 * a + c, 2 * b + c) for a, b in pairs for c in range(2)]
        return lax.ppermute(x, "seq", perm=perm)

    def chip_tails(tail):
        other = swap(tail)
        return other, tail + other, hop(tail + other, (2, 3)) if n_chips == 4 else None

    if square:
        tokens = stay(tokens)
        q0, q1 = cut_call(tokens)
        x0, y1, x1, y0 = over_x(q0), over_y(q1), over_x(q1), over_y(q0)
        (acc_a,) = own_part_call(places, tokens, w_qkv, cols, 0, 0)
        acc_b, q2, q3 = own_part_call(places, stay(after(tokens, acc_a, x0, y1)), w_qkv, cols, 1, 2)
        fy0, fx1 = over_y(x0), over_x(y1)
        tail_other, tail_chip, tail_below = chip_tails(after(tail, acc_a, x0, y1))
        x2 = over_x(after(q2, x1, y0, tail_chip))
        y3 = over_y(after(q3, x1, y0, tail_chip))
        acc_a = part_call(
            places,
            (1, 2),
            [(x0, x1), (y0, y1)],
            w_qkv,
            2 * quarter,
            cols,
            before=stay(after(acc_a, tail_chip, acc_b)),
        )
        earlier = (fy0, fx1, acc_a) if tail_below is None else (fy0, fx1, acc_a, tail_below)
        x3, y2 = over_x(after(q3, *earlier)), over_y(after(q2, *earlier))
        query_a, within_a, state = first_call(
            places,
            (3,),
            [(fy0, fx1)],
            (acc_a,),
            w_qkv,
            along,
            inside,
            2 * quarter,
            quarter,
            size,
            group,
        )
        fy2, fx3 = over_y(after(x2, state)), over_x(after(y3, state))
        acc_q, acc_kv = part_call(
            places,
            (1, 2),
            [(x2, x3), (y2, y3)],
            w_qkv,
            2 * quarter,
            cols,
            before=stay(acc_b),
            apart=True,
        )
        far = (fy2, fx3)
        middle = state
        k, v, state, sent = state_call(
            places, far, w_qkv, acc_kv, to_end, half_fade, middle, group
        )
    else:
        tail_other, tail_chip, tail_below = chip_tails(tail)
        gathered = lax.all_gather(tokens, "head", axis=1, tiled=True)
        query, within, state = first_call(
            places, (), [(gathered,)], (), w_qkv, along, inside, rows, quarter, size, group
        )

    tails = (tail, tail_other)
    if square and n_chips == 4:
        leaving, chip_state, first = chip_call(places, state, near(swap(sent)), tails, prior_state)
        arriving = near(hop(leaving, (0, 1), (2, 3)))
        leaving = pass_call(places, arriving, chip_state, tails)
        to_third, to_second = near(hop(leaving, (1, 3))), near(hop(leaving, (1, 2)))
        here, passed = enter_call(
            places, arriving, to_second, to_third, first, tails, tail_below, prior_state
        )
    else:
        share = heads // 2

        def mine(x, core=core):
            return lax.dynamic_slice_in_dim(x, core * share, share, 0)

        def decay(tail):
            return jnp.exp(-mine(tail)[:, :1, None])

        ours = mine(state)
        other = swap(mine(state, 1 - core).astype(BF16)).astype(F32)
        first = jnp.where(core == 0, ours, other)
        second = jnp.where(core == 0, other, ours)
        chip_state = decay(jnp.where(core == 0, tail_other, tail)) * first + second
        chip_entering = mine(prior_state)
        for step in range(n_chips - 1):
            leaving = (decay(tail_chip) * chip_entering + chip_state).astype(BF16)
            arriving = hop(leaving, (step, step + 1))
            chip_entering = jnp.where(chip == step + 1, arriving.astype(F32), chip_entering)
        other = decay(jnp.where(core == 0, tail, tail_other)) * chip_entering + first
        here = jnp.where(core == 0, chip_entering, other).astype(BF16)
        passed = jnp.where(core == 0, other, chip_entering).astype(BF16)
    entering = (here, swap(passed))

    if not square:
        halves = [
            head_call(
                places,
                (0,),
                query[r * rows // 2 : (r + 1) * rows // 2],
                within[r * rows // 2 : (r + 1) * rows // 2],
                entering,
                down,
                w_out,
                width,
                r,
            )[0]
            for r in range(2)
        ]
        partial = dot(jnp.concatenate(halves), w_out).astype(BF16)
        return lax.psum_scatter(partial, "head", scatter_dimension=1, tiled=True)

    na, by_x, by_y = head_call(
        places, (3, 1, 2), stay(query_a), stay(within_a), entering, down, w_out, width, 0
    )
    middle = stay(after(middle, na))
    by_x, by_y = over_x(by_x), over_y(by_y)
    query_b, within_b = later_call(
        places, far, w_qkv, stay(acc_q), stay(k), stay(v), along, inside, middle, quarter, group
    )
    nb, by_x2, by_y2 = head_call(
        places, (3, 1, 2), query_b, within_b, entering, down, w_out, width, 1
    )
    by_x2, by_y2 = over_x(by_x2), over_y(by_y2)
    sum1, sum0 = pair_call(places, after(na, nb), by_y, by_x, w_out, width)
    by_x2, by_y2 = after(by_x2, sum1), after(by_y2, sum1)
    sum1, sum0 = over_x(sum1), over_y(sum0)
    sum3, sum2 = pair_call(places, nb, by_y2, by_x2, w_out, width)
    sum3, sum2 = over_x(sum3), over_y(sum2)
    below = own_call(places, after(nb, sum1, sum0), ((by_x2, 1),), ((by_y2, 1),), w_out, width, 1)
    above = own_call(
        places, na, ((by_x, 1), (sum0, 0)), ((by_y, 1), (sum1, 0)), w_out, width, 2
    )
    return last_call(below, sum2, sum3, above)


def solution(mesh):
    in_specs = (
        P("seq", "head"),
        P(None, None, "head"),
        P("head", None),
        P("head", "seq"),
        P("head", None, None),
    )
    body = functools.partial(local, mesh.shape["head"], mesh.shape["seq"])
    return jax.shard_map(
        body, mesh=mesh, in_specs=in_specs, out_specs=P("seq", "head"), check_vma=False
    )
```

```python
import functools
import math

import jax
import jax.numpy as jnp
from jax import lax
from jax.experimental import pallas as pl
from jax.experimental.pallas import tpu as pltpu
from jax.sharding import PartitionSpec as P

BF16, F32 = jnp.bfloat16, jnp.float32
MIB = 1024 * 1024


def dot(a, b, contract=((1,), (0,))):
    return lax.dot_general(a, b, (contract, ((), ())), preferred_element_type=F32)


def after(x, *earlier):
    return lax.optimization_barrier((x, *earlier))[0]


def struct(shape, dtype):
    return jax.ShapeDtypeStruct(shape, dtype)


def stay(x):
    return pltpu.with_memory_space_constraint(x, pltpu.HBM)


def near(x):
    return pltpu.with_memory_space_constraint(x, pltpu.VMEM)


def fixed(shape):
    return pl.BlockSpec(shape, lambda j, o: (0,) * len(shape))


def call(kernel, name, steps, scalars, ins, in_specs, outs, out_specs, flops, scratch=(), aliases=None, light=False):
    moved = sum(a.size * a.dtype.itemsize for a in ins) + sum(
        math.prod(o.shape) * jnp.dtype(o.dtype).itemsize for o in outs
    )
    return pl.pallas_call(
        kernel,
        out_shape=tuple(outs),
        grid_spec=pltpu.PrefetchScalarGridSpec(
            num_scalar_prefetch=1,
            grid=(steps,),
            in_specs=in_specs,
            out_specs=out_specs,
            scratch_shapes=list(scratch),
        ),
        input_output_aliases=aliases or {},
        compiler_params=pltpu.CompilerParams(vmem_limit_bytes=(24 if light else 32) * MIB),
        cost_estimate=pl.CostEstimate(
            flops=1 if light else flops, bytes_accessed=1 if light else moved, transcendentals=0
        ),
        name=name,
    )(scalars, *ins)


def cut_kernel(x_ref, a_ref, b_ref, sems):
    tall = a_ref.shape[0]
    copies = [
        pltpu.make_async_copy(x_ref.at[pl.ds(i * tall, tall)], out_ref, sems.at[i])
        for i, out_ref in enumerate((a_ref, b_ref))
    ]
    for copy in copies:
        copy.start()
    for copy in copies:
        copy.wait()


def cut_call(x):
    rows, width = x.shape
    quarter = struct((rows // 4, width), x.dtype)
    return pl.pallas_call(
        cut_kernel,
        out_shape=(quarter, quarter),
        in_specs=[pl.BlockSpec(memory_space=pl.ANY)],
        out_specs=[pl.BlockSpec(memory_space=pltpu.VMEM)] * 2,
        scratch_shapes=[pltpu.SemaphoreType.DMA((2,))],
        compiler_params=pltpu.CompilerParams(vmem_limit_bytes=4 * MIB),
        cost_estimate=pl.CostEstimate(flops=1, bytes_accessed=x.size * 2, transcendentals=0),
        name="cut",
    )(x)


def decay_kernel(chunk, _, rate_ref, along_ref, inside_ref, down_ref, tail_ref, end_ref, half_ref):
    heads, rows = rate_ref.shape
    lane = lax.broadcasted_iota(jnp.int32, (heads, chunk), 1)
    base = jnp.zeros((heads, 1), F32)
    insides, wholes = [], []
    for c in range(rows // chunk):
        x = rate_ref[:, c * chunk : (c + 1) * chunk]
        step = 1
        while step < chunk:
            x = x + jnp.where(lane >= step, pltpu.roll(x, step, 1), 0.0)
            step *= 2
        insides.append(x)
        wholes.append(x + base)
        base = base + x[:, chunk - 1 :]
    inside, whole = jnp.concatenate(insides, axis=1), jnp.concatenate(wholes, axis=1)
    along_ref[...] = inside
    inside_ref[...] = inside.T
    down_ref[...] = whole.T
    tail_ref[...] = jnp.broadcast_to(base, tail_ref.shape)
    end_ref[...] = jnp.exp(whole - base)
    half_ref[...] = jnp.broadcast_to(jnp.exp(whole[:, rows // 2 - 1 : rows // 2] - base), half_ref.shape)


def decay_call(rate, chunk):
    heads, rows = rate.shape
    return call(
        functools.partial(decay_kernel, chunk),
        "decay",
        1,
        jnp.zeros((1,), jnp.int32),
        (rate,),
        [fixed((heads, rows))],
        (
            struct((heads, rows), F32),
            struct((rows, heads), F32),
            struct((rows, heads), F32),
            struct((heads, 128), F32),
            struct((heads, rows), F32),
            struct((heads, 128), F32),
        ),
        [
            fixed((heads, rows)),
            fixed((rows, heads)),
            fixed((rows, heads)),
            fixed((heads, 128)),
            fixed((heads, rows)),
            fixed((heads, 128)),
        ],
        heads * rows * 16,
    )


def column(table, head):
    lane = lax.broadcasted_iota(jnp.int32, table.shape, 1)
    return jnp.sum(jnp.where(lane == head, table, 0.0), axis=1, keepdims=True)


def scores(q, k, v, along, down, state):
    rows = q.shape[0]
    causal = lax.broadcasted_iota(jnp.int32, (rows, rows), 0) >= lax.broadcasted_iota(
        jnp.int32, (rows, rows), 1
    )
    decay = jnp.exp(jnp.minimum(along - down, 0.0))
    weights = jnp.where(causal, dot(q, k, ((1,), (1,))) * decay, 0.0).astype(BF16)
    return dot(weights, v) + dot(q, state.astype(BF16)) * jnp.exp(-down)


def advance(k, v, down, state):
    last = down[down.shape[0] - 1 :, :]
    scaled = (k.astype(F32) * jnp.exp(down - last)).astype(BF16)
    return jnp.exp(-last) * state + dot(scaled, v, ((0,), (0,)))


def first_kernel(layout, added, chunk, group, size, _, *refs):
    count = sum(layout)
    x_refs, w_refs, refs = refs[:count], refs[count : count + len(layout)], refs[count + len(layout) :]
    along_ref, inside_ref, q_ref, within_ref, state_ref, held = refs[-6:]
    j = pl.program_id(0)
    rows = held.shape[1]

    @pl.when(j == 0)
    def _():
        at = 0
        for i, parts in enumerate(layout):
            tall = rows // parts
            for p in range(parts):
                held[i, p * tall : (p + 1) * tall, :] = x_refs[at][...]
                at += 1

    def project(c):
        total = dot(held[0], w_refs[0][c])
        for i in range(1, len(layout)):
            total = total + dot(held[i], w_refs[i][c])
        if added:
            total = total + refs[0][c]
        return total.astype(BF16)

    q_all, k_all, v_all = project(0), project(1), project(2)
    q_ref[...] = q_all
    for a in range(group):
        head = j * group + a
        lanes = slice(a * size, (a + 1) * size)
        state = jnp.zeros((size, size), F32)
        for c in range(rows // chunk):
            here = slice(c * chunk, (c + 1) * chunk)
            q, k, v = q_all[here, lanes], k_all[here, lanes], v_all[here, lanes]
            down = column(inside_ref[here, :], head)
            along = along_ref[pl.ds(head, 1), here]
            within_ref[here, lanes] = scores(q, k, v, along, down, state)
            state = advance(k, v, down, state)
        state_ref[a] = state


def first_call(places, blocks, pieces, before, w_qkv, along, inside, rows, chunk, size, group):
    heads = along.shape[0]
    cols = group * size
    flat = [p for piece in pieces for p in piece]
    depth = flat[0].shape[1]

    def block(i):
        return pl.BlockSpec((3, depth, cols), lambda j, o: (0, o[blocks[i]] if blocks else 0, j))

    wide = pl.BlockSpec((rows, cols), lambda j, o: (0, j))
    return call(
        functools.partial(
            first_kernel, tuple(len(p) for p in pieces), bool(before), chunk, group, size
        ),
        "first",
        heads // group,
        places,
        (*flat, *[w_qkv] * len(pieces), *before, along, inside),
        [
            pl.BlockSpec((rows // len(piece), depth), lambda j, o: (0, 0))
            for piece in pieces
            for _ in piece
        ]
        + [block(i) for i in range(len(pieces))]
        + [pl.BlockSpec((3, rows, cols), lambda j, o: (0, 0, j)) for _ in before]
        + [fixed((heads, rows)), fixed((rows, heads))],
        (
            pltpu.HBM((rows, heads * size), BF16),
            pltpu.HBM((rows, heads * size), F32),
            struct((heads, size, size), F32),
        ),
        [wide, wide, pl.BlockSpec((group, size, size), lambda j, o: (j, 0, 0))],
        2 * rows * 3 * heads * size * depth * len(pieces),
        scratch=[pltpu.VMEM((len(pieces), rows, depth), BF16)],
    )


def own_part_kernel(_, x_ref, w_ref, out_ref, *cut_refs):
    @pl.when(pl.program_id(0) == 0)
    def _():
        for i, ref in enumerate(cut_refs):
            tall = ref.shape[0]
            ref[...] = x_ref[i * tall : (i + 1) * tall, :]

    out_ref[0] = dot(x_ref[...], w_ref[0])


def own_part_call(places, tokens, w_qkv, half, cuts):
    rows, depth = tokens.shape[0] // 2, tokens.shape[1]
    width = w_qkv.shape[2]
    quarter = (rows // 2, depth)
    return call(
        own_part_kernel,
        "own_part",
        3,
        places,
        (tokens, w_qkv),
        [
            pl.BlockSpec((rows, depth), lambda c, o: (half, 0)),
            pl.BlockSpec((1, depth, width), lambda c, o: (c, o[0], 0)),
        ],
        (pltpu.HBM((3, rows, width), F32), *[pltpu.HBM(quarter, BF16)] * cuts),
        [pl.BlockSpec((1, rows, width), lambda c, o: (c, 0, 0))] + [fixed(quarter)] * cuts,
        2 * rows * depth * width * 3,
    )


def part_kernel(apart, _, xa, xb, ya, yb, w_ref, before_ref, *refs):
    out_refs, held = refs[:-1], refs[-1]
    j = pl.program_id(0)
    tall = xa.shape[0]

    @pl.when(j == 0)
    def _():
        held[0, :tall, :] = xa[...]
        held[0, tall:, :] = xb[...]
        held[1, :tall, :] = ya[...]
        held[1, tall:, :] = yb[...]

    def add(ref):
        @pl.when(j % 2 == 0)
        def _():
            ref[0] = before_ref[0] + dot(held[0], w_ref[0])

        @pl.when(j % 2 == 1)
        def _():
            ref[0] = ref[0] + dot(held[1], w_ref[0])

    if not apart:
        add(out_refs[0])
        return

    @pl.when(j < 2)
    def _():
        add(out_refs[0])

    @pl.when(j >= 2)
    def _():
        add(out_refs[1])


def part_call(places, pieces, w_qkv, before, apart=False):
    tall, depth = pieces[0].shape
    rows, width = 2 * tall, w_qkv.shape[2]
    outs = [struct((3, rows, width), F32)]
    places_out = [lambda j, o: (j // 2, 0, 0)]
    if apart:
        outs = [pltpu.HBM((1, rows, width), F32), struct((2, rows, width), F32)]
        places_out = [lambda j, o: (0, 0, 0), lambda j, o: (jnp.maximum(j // 2 - 1, 0), 0, 0)]
    out = call(
        functools.partial(part_kernel, apart),
        "part",
        6,
        places,
        (*pieces, w_qkv, before),
        [fixed((tall, depth))] * 4
        + [
            pl.BlockSpec((1, depth, width), lambda j, o: (j // 2, o[1 + j % 2], 0)),
            pl.BlockSpec((1, rows, width), lambda j, o: (j // 2, 0, 0)),
        ],
        outs,
        [pl.BlockSpec((1, rows, width), place) for place in places_out],
        2 * rows * depth * 2 * width * 3,
        scratch=[pltpu.VMEM((2, rows, depth), BF16)],
    )
    return out if apart else out[0]


def state_kernel(size, places, *refs):
    xa, xb, w_ref, acc_ref, end_ref, half_ref, state_ref, k_ref, v_ref, out_ref, sent_ref, held = refs
    j = pl.program_id(0)
    tall = xa.shape[0]
    share = sent_ref.shape[0]

    @pl.when(j == 0)
    def _():
        held[:tall, :] = xa[...]
        held[tall:, :] = xb[...]

    total = (acc_ref[0] + dot(held[...], w_ref[0])).astype(BF16)

    @pl.when(j % 2 == 0)
    def _():
        k_ref[...] = total

    @pl.when(j % 2 == 1)
    def _():
        v_ref[...] = total
        for a in range(share):
            head = pl.ds((j // 2) * share + a, 1)
            lanes = slice(a * size, (a + 1) * size)
            scaled = (k_ref[:, lanes].astype(F32).T * end_ref[head, :]).astype(BF16)
            end = half_ref[head, :] * state_ref[a] + dot(scaled, total[:, lanes])
            out_ref[a] = end

            @pl.when(j // 2 != places[4])
            def _(a=a, end=end):
                sent_ref[a] = end.astype(BF16)


def state_call(places, far, w_qkv, acc, to_end, half_fade, state):
    _, rows, width = acc.shape
    heads, size = state.shape[0], state.shape[1]
    depth = far[0].shape[1]
    share, cols = heads // 2, width // 2
    wide = pl.BlockSpec((rows, cols), lambda j, o: (0, j // 2))
    small = pl.BlockSpec((share, size, size), lambda j, o: (j // 2, 0, 0))
    return call(
        functools.partial(state_kernel, size),
        "states",
        4,
        places,
        (*far, w_qkv, acc, to_end, half_fade, state),
        [
            fixed(far[0].shape),
            fixed(far[1].shape),
            pl.BlockSpec((1, depth, cols), lambda j, o: (1 + j % 2, o[3], j // 2)),
            pl.BlockSpec((1, rows, cols), lambda j, o: (j % 2, 0, j // 2)),
            pl.BlockSpec((heads, rows), lambda j, o: (0, 1)),
            fixed(half_fade.shape),
            small,
        ],
        (
            pltpu.HBM((rows, width), BF16),
            pltpu.HBM((rows, width), BF16),
            struct(state.shape, F32),
            struct((share, size, size), BF16),
        ),
        [wide, wide, small, fixed((share, size, size))],
        4 * rows * depth * width,
        scratch=[pltpu.VMEM((rows, depth), BF16)],
    )


def later_kernel(chunk, group, size, _, *refs):
    xa, xb, wq, acc_q, k_ref, v_ref, along_ref, inside_ref, state_ref, q_ref, within_ref, held = refs
    j = pl.program_id(0)
    rows = held.shape[0]

    @pl.when(j == 0)
    def _():
        held[: rows // 2, :] = xa[...]
        held[rows // 2 :, :] = xb[...]

    q_all = (acc_q[0] + dot(held[...], wq[0])).astype(BF16)
    q_ref[...] = q_all
    for a in range(group):
        head = j * group + a
        lanes = slice(a * size, (a + 1) * size)
        state = state_ref[a]
        for c in range(rows // chunk):
            here = slice(c * chunk, (c + 1) * chunk)
            q, k, v = q_all[here, lanes], k_ref[here, lanes], v_ref[here, lanes]
            along, down = along_ref[pl.ds(head, 1), here], column(inside_ref[here, :], head)
            within_ref[here, lanes] = scores(q, k, v, along, down, state)
            if c + 1 < rows // chunk:
                state = advance(k, v, down, state)


def later_call(places, far, w_qkv, acc, k, v, along, inside, state, chunk, group):
    _, rows, width = acc.shape
    heads, size = state.shape[0], state.shape[1]
    depth = far[0].shape[1]
    cols = group * size
    wide = pl.BlockSpec((rows, cols), lambda j, o: (0, j))
    return call(
        functools.partial(later_kernel, chunk, group, size),
        "later",
        heads // group,
        places,
        (*far, w_qkv, acc, k, v, along, inside, state),
        [
            fixed(far[0].shape),
            fixed(far[1].shape),
            pl.BlockSpec((1, depth, cols), lambda j, o: (0, o[3], j)),
            pl.BlockSpec((1, rows, cols), lambda j, o: (0, 0, j)),
            wide,
            wide,
            pl.BlockSpec((heads, rows), lambda j, o: (0, 1)),
            pl.BlockSpec((rows, heads), lambda j, o: (1, 0)),
            pl.BlockSpec((group, size, size), lambda j, o: (j, 0, 0)),
        ],
        (struct((rows, width), BF16), struct((rows, width), F32)),
        [wide, wide],
        2 * rows * depth * width + 4 * rows * (chunk + size) * width,
        scratch=[pltpu.VMEM((rows, depth), BF16)],
    )


def fades(tail_ref, other_ref, place, head):
    own, other = tail_ref[pl.ds(head, 1), :], other_ref[pl.ds(head, 1), :]
    first = jnp.where(place == 0, own, other)
    return jnp.exp(-first), jnp.exp(first - (own + other)), jnp.exp(-(own + other))


def chip_kernel(places, state_ref, come_ref, tail_ref, other_ref, prior_ref, *out_refs):
    leaving_ref, chip_ref, first_ref = out_refs
    core, chip = places[4], places[5]
    share = come_ref.shape[0]
    for i in range(share):
        head = core * share + i
        _, second_fade, fade = fades(tail_ref, other_ref, core, head)
        ours, come = state_ref[head], come_ref[i].astype(F32)
        first, second = jnp.where(core == 0, ours, come), jnp.where(core == 0, come, ours)
        total = second_fade * first + second
        first_ref[i] = first
        chip_ref[i] = total
        leaving_ref[i] = jnp.where(chip == 2, total, fade * prior_ref[head] + total).astype(BF16)


def pass_kernel(places, come_ref, chip_ref, tail_ref, other_ref, leaving_ref):
    share = come_ref.shape[0]
    for i in range(share):
        fade = fades(tail_ref, other_ref, places[4], places[4] * share + i)[2]
        leaving_ref[i] = (fade * come_ref[i].astype(F32) + chip_ref[i]).astype(BF16)


def enter_kernel(
    places, come_ref, second_ref, third_ref, first_ref, tail_ref, other_ref, below_ref, prior_ref, *out_refs
):
    here_ref, passed_ref = out_refs
    core, chip = places[4], places[5]
    share = come_ref.shape[0]
    for i in range(share):
        head = core * share + i
        come = come_ref[i].astype(F32)
        below = jnp.exp(-below_ref[pl.ds(head, 1), :])
        state = jnp.where(chip == 0, prior_ref[head], come)
        state = jnp.where(chip == 2, second_ref[i].astype(F32), state)
        state = jnp.where(chip == 3, below * third_ref[i].astype(F32) + come, state)
        later = fades(tail_ref, other_ref, core, head)[0] * state + first_ref[i]
        here_ref[i] = jnp.where(core == 0, state, later).astype(BF16)
        passed_ref[i] = jnp.where(core == 0, later, state).astype(BF16)


def small_call(kernel, name, places, ins, outs):
    whole = pl.BlockSpec(memory_space=pltpu.VMEM)
    return pl.pallas_call(
        kernel,
        out_shape=tuple(outs),
        in_specs=[pl.BlockSpec(memory_space=pltpu.SMEM)] + [whole] * len(ins),
        out_specs=[whole] * len(outs),
        compiler_params=pltpu.CompilerParams(vmem_limit_bytes=4 * MIB),
        cost_estimate=pl.CostEstimate(flops=1, bytes_accessed=1, transcendentals=0),
        name=name,
    )(places, *ins)


def chip_call(places, state, come, tails, prior):
    outs = (struct(come.shape, BF16), struct(come.shape, F32), struct(come.shape, F32))
    return small_call(chip_kernel, "chip_state", places, (state, come, *tails, prior), outs)


def pass_call(places, come, chip_state, tails):
    outs = (struct(come.shape, BF16),)
    return small_call(pass_kernel, "pass_on", places, (come, chip_state, *tails), outs)[0]


def enter_call(places, come, second, third, first, tails, below, prior):
    outs = (struct(come.shape, BF16),) * 2
    ins = (come, second, third, first, *tails, below, prior)
    return small_call(enter_kernel, "enter", places, ins, outs)


def head_kernel(places, q_ref, within_ref, here_ref, there_ref, down_ref, w_ref, normed_ref, *out_refs):
    share, size = here_ref.shape[0], here_ref.shape[1]
    tall = q_ref.shape[0]
    for p, out_ref in enumerate(out_refs):
        rows = slice(p * tall, (p + 1) * tall)

        @pl.when(pl.program_id(0) == p)
        def _(rows=rows, out_ref=out_ref):
            fade = jnp.exp(-down_ref[...])
            for a in range(2 * share):
                lanes = slice(a * size, (a + 1) * size)
                ours = places[4] == a // share
                entering = jnp.where(ours, here_ref[a % share], there_ref[a % share])
                seen = dot(q_ref[:, lanes], entering) * fade[:, a : a + 1]
                combined = within_ref[:, lanes] + seen
                power = jnp.mean(combined * combined, axis=1, keepdims=True)
                normed_ref[rows, lanes] = (combined * lax.rsqrt(power + 1e-06)).astype(BF16)
            out_ref[:tall, :] = dot(normed_ref[rows, :], w_ref[...]).astype(BF16)

        if out_ref.shape[0] > tall:

            @pl.when(pl.program_id(0) == 2 + p)
            def _(rows=rows, out_ref=out_ref):
                out_ref[tall:, :] = dot(normed_ref[rows, :], w_ref[...]).astype(BF16)


def head_call(places, blocks, q, within, entering, down, w_out, width, at):
    rows, cols = q.shape
    tall = rows // 2
    heads = down.shape[1]
    part = pl.BlockSpec((tall, cols), lambda i, o: (jnp.minimum(i, 1), 0))
    near = len(blocks) > 1
    out = (tall * (2 if near else 1), width)

    def columns(i, o):
        if not near:
            return 0, o[blocks[0]]
        return 0, o[jnp.where(i < 2, blocks[0], jnp.where(i == 2, blocks[1], blocks[2]))]

    return call(
        head_kernel,
        "heads",
        4 if near else 2,
        places,
        (q, within, *entering, down, w_out),
        [
            part,
            part,
            fixed(entering[0].shape),
            fixed(entering[1].shape),
            pl.BlockSpec((tall, heads), lambda i, o: (2 * at + jnp.minimum(i, 1), 0)),
            pl.BlockSpec((cols, width), columns),
        ],
        (struct((rows, cols), BF16), *[struct(out, BF16)] * 2),
        [fixed((rows, cols))] + [fixed(out)] * 2,
        2 * rows * cols * (2 * width + 128),
        light=True,
    )


def pair_kernel(_, normed_ref, x_ref, y_ref, w_ref, out_x_ref, out_y_ref):
    tall = x_ref.shape[0]

    @pl.when(pl.program_id(0) == 0)
    def _():
        out_x_ref[...] = (dot(normed_ref[tall:, :], w_ref[...]) + x_ref[...].astype(F32)).astype(BF16)

    @pl.when(pl.program_id(0) == 1)
    def _():
        out_y_ref[...] = (dot(normed_ref[:tall, :], w_ref[...]) + y_ref[...].astype(F32)).astype(BF16)


def pair_call(places, normed, for_x, for_y, w_out, width):
    rows, cols = normed.shape
    quarter = (rows // 2, width)
    return call(
        pair_kernel,
        "sum_pair",
        2,
        places,
        (normed, for_x, for_y, w_out),
        [
            fixed((rows, cols)),
            fixed(quarter),
            fixed(quarter),
            pl.BlockSpec((cols, width), lambda i, o: (0, o[1 + i])),
        ],
        (struct(quarter, BF16),) * 2,
        [fixed(quarter)] * 2,
        2 * rows * cols * width,
        light=True,
    )


def own_kernel(_, normed_ref, w_ref, *refs):
    out_ref = refs[-1]
    tall = out_ref.shape[0]
    each = len(refs) // 2
    for p in range(2):
        rows = slice(p * tall, (p + 1) * tall)

        @pl.when(pl.program_id(0) == p)
        def _(p=p, rows=rows):
            total = dot(normed_ref[rows, :], w_ref[...])
            for ref in refs[p * each : (p + 1) * each]:
                total = total + ref[...].astype(F32)
            out_ref[...] = total.astype(BF16)


def own_call(places, normed, first, second, w_out, width, height):
    rows, cols = normed.shape
    quarter = (rows // 2, width)
    return call(
        own_kernel,
        "own_block",
        2,
        places,
        (normed, w_out, *[a for a, _ in (*first, *second)]),
        [fixed((rows, cols)), pl.BlockSpec((cols, width), lambda i, o: (0, o[0]))]
        + [pl.BlockSpec(quarter, lambda i, o, at=at: (at, 0)) for _, at in (*first, *second)],
        (struct((rows * height, width), BF16),),
        [pl.BlockSpec(quarter, lambda i, o: (i, 0))],
        2 * rows * cols * width,
        light=True,
    )[0]


def last_kernel(_, kept_ref, a_ref, b_ref, above_ref, out_ref):
    del above_ref

    @pl.when(pl.program_id(0) == 0)
    def _():
        out_ref[...] = (kept_ref[...].astype(F32) + a_ref[...].astype(F32)).astype(BF16)

    @pl.when(pl.program_id(0) == 1)
    def _():
        out_ref[...] = (kept_ref[...].astype(F32) + b_ref[...].astype(F32)).astype(BF16)


def last_call(kept, a, b, above):
    tall, width = a.shape
    return call(
        last_kernel,
        "last_add",
        2,
        jnp.zeros((1,), jnp.int32),
        (kept, a, b, above),
        [
            pl.BlockSpec((tall, width), lambda j, o: (j, 0)),
            fixed((tall, width)),
            fixed((tall, width)),
            pl.BlockSpec(memory_space=pl.ANY),
        ],
        (struct(above.shape, BF16),),
        [pl.BlockSpec((tall, width), lambda j, o: (2 + j, 0))],
        tall * width,
        aliases={4: 0},
    )[0]


def local(n_head, n_seq, tokens, w_qkv, w_out, decay_rate, prior_state):
    rows, width = tokens.shape
    heads, size = prior_state.shape[0], prior_state.shape[1]
    square = n_head == 4
    place = lax.axis_index("head").astype(jnp.int32)
    quarter = rows // 4
    group = 2 if heads % 2 == 0 else 1

    over_x = functools.partial(lax.ppermute, axis_name="head", perm=[(i, i ^ 1) for i in range(n_head)])
    over_y = functools.partial(lax.ppermute, axis_name="head", perm=[(i, i ^ 2) for i in range(n_head)])

    pos = lax.axis_index("seq").astype(jnp.int32)
    core, chip = pos % 2, pos // 2
    flips = (0, 1, 2, 3) if square else (0, 0, 0, 0)
    places = jnp.stack([*[place ^ f for f in flips], core, chip])

    along, inside, down, tail, to_end, half_fade = decay_call(decay_rate, quarter)
    n_chips = n_seq // 2
    swap = functools.partial(lax.ppermute, axis_name="seq", perm=[(i, i ^ 1) for i in range(n_seq)])

    def hop(x, *pairs):
        perm = [(2 * a + c, 2 * b + c) for a, b in pairs for c in range(2)]
        return lax.ppermute(x, "seq", perm=perm)

    def chip_tails(tail):
        other = swap(tail)
        return other, tail + other, hop(tail + other, (2, 3)) if n_chips == 4 else None

    if square:
        tokens = stay(tokens)
        q0, q1 = cut_call(tokens)
        x0, y1, x1, y0 = over_x(q0), over_y(q1), over_x(q1), over_y(q0)
        (acc_a,) = own_part_call(places, tokens, w_qkv, 0, 0)
        acc_b, q2, q3 = own_part_call(places, stay(after(tokens, acc_a, x0, y1)), w_qkv, 1, 2)
        fy0, fx1 = over_y(x0), over_x(y1)
        tail_other, tail_chip, tail_below = chip_tails(after(tail, acc_a, x0, y1))
        x2 = over_x(after(q2, x1, y0, tail_chip))
        y3 = over_y(after(q3, x1, y0, tail_chip))
        acc_a = part_call(
            places, (x0, x1, y0, y1), w_qkv, stay(after(acc_a, tail_chip, acc_b))
        )
        earlier = (fy0, fx1, acc_a) if tail_below is None else (fy0, fx1, acc_a, tail_below)
        x3, y2 = over_x(after(q3, *earlier)), over_y(after(q2, *earlier))
        query_a, within_a, state = first_call(
            places,
            (3,),
            [(fy0, fx1)],
            (acc_a,),
            w_qkv,
            along,
            inside,
            2 * quarter,
            quarter,
            size,
            group,
        )
        fy2, fx3 = over_y(after(x2, state)), over_x(after(y3, state))
        acc_q, acc_kv = part_call(places, (x2, x3, y2, y3), w_qkv, stay(acc_b), apart=True)
        far = (fy2, fx3)
        middle = state
        k, v, state, sent = state_call(places, far, w_qkv, acc_kv, to_end, half_fade, middle)
    else:
        tail_other, tail_chip, tail_below = chip_tails(tail)
        gathered = lax.all_gather(tokens, "head", axis=1, tiled=True)
        query, within, state = first_call(
            places, (), [(gathered,)], (), w_qkv, along, inside, rows, quarter, size, group
        )

    tails = (tail, tail_other)
    if square and n_chips == 4:
        leaving, chip_state, first = chip_call(places, state, near(swap(sent)), tails, prior_state)
        arriving = near(hop(leaving, (0, 1), (2, 3)))
        leaving = pass_call(places, arriving, chip_state, tails)
        to_third, to_second = near(hop(leaving, (1, 3))), near(hop(leaving, (1, 2)))
        here, passed = enter_call(
            places, arriving, to_second, to_third, first, tails, tail_below, prior_state
        )
    else:
        share = heads // 2

        def mine(x, core=core):
            return lax.dynamic_slice_in_dim(x, core * share, share, 0)

        def decay(tail):
            return jnp.exp(-mine(tail)[:, :1, None])

        ours = mine(state)
        other = swap(mine(state, 1 - core).astype(BF16)).astype(F32)
        first = jnp.where(core == 0, ours, other)
        second = jnp.where(core == 0, other, ours)
        chip_state = decay(jnp.where(core == 0, tail_other, tail)) * first + second
        chip_entering = mine(prior_state)
        for step in range(n_chips - 1):
            leaving = (decay(tail_chip) * chip_entering + chip_state).astype(BF16)
            arriving = hop(leaving, (step, step + 1))
            chip_entering = jnp.where(chip == step + 1, arriving.astype(F32), chip_entering)
        other = decay(jnp.where(core == 0, tail, tail_other)) * chip_entering + first
        here = jnp.where(core == 0, chip_entering, other).astype(BF16)
        passed = jnp.where(core == 0, other, chip_entering).astype(BF16)
    entering = (here, swap(passed))

    if not square:
        halves = [
            head_call(
                places,
                (0,),
                query[r * rows // 2 : (r + 1) * rows // 2],
                within[r * rows // 2 : (r + 1) * rows // 2],
                entering,
                down,
                w_out,
                width,
                r,
            )[0]
            for r in range(2)
        ]
        partial = dot(jnp.concatenate(halves), w_out).astype(BF16)
        return lax.psum_scatter(partial, "head", scatter_dimension=1, tiled=True)

    na, by_x, by_y = head_call(
        places, (3, 1, 2), stay(query_a), stay(within_a), entering, down, w_out, width, 0
    )
    middle = stay(after(middle, na))
    by_x, by_y = over_x(by_x), over_y(by_y)
    query_b, within_b = later_call(
        places, far, w_qkv, stay(acc_q), stay(k), stay(v), along, inside, middle, quarter, group
    )
    nb, by_x2, by_y2 = head_call(
        places, (3, 1, 2), query_b, within_b, entering, down, w_out, width, 1
    )
    by_x2, by_y2 = over_x(by_x2), over_y(by_y2)
    sum1, sum0 = pair_call(places, after(na, nb), by_y, by_x, w_out, width)
    by_x2, by_y2 = after(by_x2, sum1), after(by_y2, sum1)
    sum1, sum0 = over_x(sum1), over_y(sum0)
    sum3, sum2 = pair_call(places, nb, by_y2, by_x2, w_out, width)
    sum3, sum2 = over_x(sum3), over_y(sum2)
    below = own_call(places, after(nb, sum1, sum0), ((by_x2, 1),), ((by_y2, 1),), w_out, width, 1)
    above = own_call(
        places, na, ((by_x, 1), (sum0, 0)), ((by_y, 1), (sum1, 0)), w_out, width, 2
    )
    return last_call(below, sum2, sum3, above)


def solution(mesh):
    in_specs = (
        P("seq", "head"),
        P(None, None, "head"),
        P("head", None),
        P("head", "seq"),
        P("head", None, None),
    )
    body = functools.partial(local, mesh.shape["head"], mesh.shape["seq"])
    return jax.shard_map(
        body, mesh=mesh, in_specs=in_specs, out_specs=P("seq", "head"), check_vma=False
    )
```

```python
import functools
import math

import jax
import jax.numpy as jnp
from jax import lax
from jax.experimental import pallas as pl
from jax.experimental.pallas import tpu as pltpu
from jax.sharding import PartitionSpec as P

BF16, F32 = jnp.bfloat16, jnp.float32
MIB = 1024 * 1024


def dot(a, b, contract=((1,), (0,))):
    return lax.dot_general(a, b, (contract, ((), ())), preferred_element_type=F32)


def after(x, *earlier):
    return lax.optimization_barrier((x, *earlier))[0]


def struct(shape, dtype):
    return jax.ShapeDtypeStruct(shape, dtype)


def stay(x):
    return pltpu.with_memory_space_constraint(x, pltpu.HBM)


def near(x):
    return pltpu.with_memory_space_constraint(x, pltpu.VMEM)


def fixed(shape):
    return pl.BlockSpec(shape, lambda j, o: (0,) * len(shape))


def call(kernel, name, steps, scalars, ins, in_specs, outs, out_specs, flops, scratch=(), aliases=None, light=False):
    moved = sum(a.size * a.dtype.itemsize for a in ins) + sum(
        math.prod(o.shape) * jnp.dtype(o.dtype).itemsize for o in outs
    )
    return pl.pallas_call(
        kernel,
        out_shape=tuple(outs),
        grid_spec=pltpu.PrefetchScalarGridSpec(
            num_scalar_prefetch=1,
            grid=(steps,),
            in_specs=in_specs,
            out_specs=out_specs,
            scratch_shapes=list(scratch),
        ),
        input_output_aliases=aliases or {},
        compiler_params=pltpu.CompilerParams(vmem_limit_bytes=(24 if light else 32) * MIB),
        cost_estimate=pl.CostEstimate(
            flops=1 if light else flops, bytes_accessed=1 if light else moved, transcendentals=0
        ),
        name=name,
    )(scalars, *ins)


def cut_kernel(_, x_ref, a_ref, b_ref):
    tall = a_ref.shape[0]
    a_ref[...] = x_ref[:tall, :]
    b_ref[...] = x_ref[tall:, :]


def cut_call(x, half, cost):
    rows, width = x.shape
    quarter = (rows // 4, width)
    return call(
        cut_kernel,
        "cut",
        1,
        jnp.zeros((1,), jnp.int32),
        (x,),
        [pl.BlockSpec((rows // 2, width), lambda j, o: (half, 0))],
        (struct(quarter, x.dtype),) * 2,
        [fixed(quarter)] * 2,
        cost,
    )


def decay_kernel(chunk, _, rate_ref, along_ref, inside_ref, down_ref, tail_ref, end_ref, half_ref):
    heads, rows = rate_ref.shape
    lane = lax.broadcasted_iota(jnp.int32, (heads, chunk), 1)
    base = jnp.zeros((heads, 1), F32)
    insides, wholes = [], []
    for c in range(rows // chunk):
        x = rate_ref[:, c * chunk : (c + 1) * chunk]
        step = 1
        while step < chunk:
            x = x + jnp.where(lane >= step, pltpu.roll(x, step, 1), 0.0)
            step *= 2
        insides.append(x)
        wholes.append(x + base)
        base = base + x[:, chunk - 1 :]
    inside, whole = jnp.concatenate(insides, axis=1), jnp.concatenate(wholes, axis=1)
    along_ref[...] = inside
    inside_ref[...] = inside.T
    down_ref[...] = whole.T
    tail_ref[...] = jnp.broadcast_to(base, tail_ref.shape)
    end_ref[...] = jnp.exp(whole - base)
    half_ref[...] = jnp.broadcast_to(jnp.exp(whole[:, rows // 2 - 1 : rows // 2] - base), half_ref.shape)


def decay_call(rate, chunk):
    heads, rows = rate.shape
    return call(
        functools.partial(decay_kernel, chunk),
        "decay",
        1,
        jnp.zeros((1,), jnp.int32),
        (rate,),
        [fixed((heads, rows))],
        (
            struct((heads, rows), F32),
            struct((rows, heads), F32),
            struct((rows, heads), F32),
            struct((heads, 128), F32),
            struct((heads, rows), F32),
            struct((heads, 128), F32),
        ),
        [
            fixed((heads, rows)),
            fixed((rows, heads)),
            fixed((rows, heads)),
            fixed((heads, 128)),
            fixed((heads, rows)),
            fixed((heads, 128)),
        ],
        heads * rows * 16,
    )


def column(table, head):
    lane = lax.broadcasted_iota(jnp.int32, table.shape, 1)
    return jnp.sum(jnp.where(lane == head, table, 0.0), axis=1, keepdims=True)


def scores(q, k, v, along, down, state):
    rows = q.shape[0]
    causal = lax.broadcasted_iota(jnp.int32, (rows, rows), 0) >= lax.broadcasted_iota(
        jnp.int32, (rows, rows), 1
    )
    decay = jnp.exp(jnp.minimum(along - down, 0.0))
    weights = jnp.where(causal, dot(q, k, ((1,), (1,))) * decay, 0.0).astype(BF16)
    return dot(weights, v) + dot(q, state.astype(BF16)) * jnp.exp(-down)


def advance(k, v, down, state):
    last = down[down.shape[0] - 1 :, :]
    scaled = (k.astype(F32) * jnp.exp(down - last)).astype(BF16)
    return jnp.exp(-last) * state + dot(scaled, v, ((0,), (0,)))


def first_kernel(layout, added, chunk, group, size, _, *refs):
    count = sum(layout)
    x_refs, w_refs, refs = refs[:count], refs[count : count + len(layout)], refs[count + len(layout) :]
    along_ref, inside_ref, q_ref, within_ref, state_ref, held = refs[-6:]
    j = pl.program_id(0)
    rows = held.shape[1]

    @pl.when(j == 0)
    def _():
        at = 0
        for i, parts in enumerate(layout):
            tall = rows // parts
            for p in range(parts):
                held[i, p * tall : (p + 1) * tall, :] = x_refs[at][...]
                at += 1

    def project(c):
        total = dot(held[0], w_refs[0][c])
        for i in range(1, len(layout)):
            total = total + dot(held[i], w_refs[i][c])
        if added:
            total = total + refs[0][c]
        return total.astype(BF16)

    q_all, k_all, v_all = project(0), project(1), project(2)
    q_ref[...] = q_all
    for a in range(group):
        head = j * group + a
        lanes = slice(a * size, (a + 1) * size)
        state = jnp.zeros((size, size), F32)
        for c in range(rows // chunk):
            here = slice(c * chunk, (c + 1) * chunk)
            q, k, v = q_all[here, lanes], k_all[here, lanes], v_all[here, lanes]
            down = column(inside_ref[here, :], head)
            along = along_ref[pl.ds(head, 1), here]
            within_ref[here, lanes] = scores(q, k, v, along, down, state)
            state = advance(k, v, down, state)
        state_ref[a] = state


def first_call(places, blocks, pieces, before, w_qkv, along, inside, rows, chunk, size, group):
    heads = along.shape[0]
    cols = group * size
    flat = [p for piece in pieces for p in piece]
    depth = flat[0].shape[1]

    def block(i):
        return pl.BlockSpec((3, depth, cols), lambda j, o: (0, o[blocks[i]] if blocks else 0, j))

    wide = pl.BlockSpec((rows, cols), lambda j, o: (0, j))
    return call(
        functools.partial(
            first_kernel, tuple(len(p) for p in pieces), bool(before), chunk, group, size
        ),
        "first",
        heads // group,
        places,
        (*flat, *[w_qkv] * len(pieces), *before, along, inside),
        [
            pl.BlockSpec((rows // len(piece), depth), lambda j, o: (0, 0))
            for piece in pieces
            for _ in piece
        ]
        + [block(i) for i in range(len(pieces))]
        + [pl.BlockSpec((3, rows, cols), lambda j, o: (0, 0, j)) for _ in before]
        + [fixed((heads, rows)), fixed((rows, heads))],
        (
            pltpu.HBM((rows, heads * size), BF16),
            pltpu.HBM((rows, heads * size), F32),
            struct((heads, size, size), F32),
        ),
        [wide, wide, pl.BlockSpec((group, size, size), lambda j, o: (j, 0, 0))],
        2 * rows * 3 * heads * size * depth * len(pieces),
        scratch=[pltpu.VMEM((len(pieces), rows, depth), BF16)],
    )


def own_part_kernel(_, x_ref, w_ref, out_ref):
    for c in range(3):
        out_ref[c] = dot(x_ref[...], w_ref[c])


def own_part_call(places, tokens, w_qkv, cols):
    rows, depth = tokens.shape
    width = w_qkv.shape[2]
    return call(
        own_part_kernel,
        "own_part",
        width // cols,
        places,
        (tokens, w_qkv),
        [fixed((rows, depth)), pl.BlockSpec((3, depth, cols), lambda j, o: (0, o[0], j))],
        (pltpu.HBM((3, rows, width), F32),),
        [pl.BlockSpec((3, rows, cols), lambda j, o: (0, 0, j))],
        2 * rows * depth * width * 3,
    )[0]


def part_kernel(layout, outs, _, *refs):
    count = sum(layout)
    x_refs, w_refs = refs[:count], refs[count : count + len(layout)]
    before_ref, out_refs, held = refs[-2 - outs], refs[-1 - outs : -1], refs[-1]
    targets = [(ref, c) for ref in out_refs for c in range(ref.shape[0])]
    rows = held.shape[1]

    @pl.when(pl.program_id(0) == 0)
    def _():
        at = 0
        for i, parts in enumerate(layout):
            tall = rows // parts
            for p in range(parts):
                held[i, p * tall : (p + 1) * tall, :] = x_refs[at][...]
                at += 1

    for c in range(3):
        total = dot(held[0], w_refs[0][c])
        for i in range(1, len(layout)):
            total = total + dot(held[i], w_refs[i][c])
        ref, at = targets[c]
        ref[at] = total + before_ref[c]


def part_call(places, blocks, pieces, w_qkv, rows, cols, before, at, apart=False):
    flat = [p for piece in pieces for p in piece]
    depth = flat[0].shape[1]
    width = w_qkv.shape[2]

    def block(i):
        return pl.BlockSpec((3, depth, cols), lambda j, o: (0, o[blocks[i]], j))

    ins = [*flat, *[w_qkv] * len(pieces)]
    specs = [
        pl.BlockSpec((rows // len(piece), depth), lambda j, o: (0, 0)) for piece in pieces for _ in piece
    ] + [block(i) for i in range(len(pieces))]
    ins.append(before)
    specs.append(pl.BlockSpec((3, rows, cols), lambda j, o: (0, at, j)))
    outs = [struct((3, rows, width), F32)]
    if apart:
        outs = [pltpu.HBM((1, rows, width), F32), struct((2, rows, width), F32)]
    out = call(
        functools.partial(part_kernel, tuple(len(p) for p in pieces), len(outs)),
        "part",
        width // cols,
        places,
        ins,
        specs,
        outs,
        [pl.BlockSpec((o.shape[0], rows, cols), lambda j, o: (0, 0, j)) for o in outs],
        2 * rows * depth * len(pieces) * width * 3,
        scratch=[pltpu.VMEM((len(pieces), rows, depth), BF16)],
    )
    return out if apart else out[0]


def state_kernel(group, size, places, *refs):
    xa, xb, wk, wv, acc_k, acc_v, end_ref, half_ref, state_ref = refs[:9]
    k_ref, v_ref, out_ref, sent_ref, held = refs[9:]
    j = pl.program_id(0)
    rows = held.shape[0]

    @pl.when(j == 0)
    def _():
        held[: rows // 2, :] = xa[...]
        held[rows // 2 :, :] = xb[...]

    k_all = (acc_k[0] + dot(held[...], wk[0])).astype(BF16)
    v_all = (acc_v[0] + dot(held[...], wv[0])).astype(BF16)
    k_ref[...] = k_all
    v_ref[...] = v_all
    ends = []
    for a in range(group):
        head = pl.ds(j * group + a, 1)
        lanes = slice(a * size, (a + 1) * size)
        scaled = (k_all[:, lanes].T.astype(F32) * end_ref[head, :]).astype(BF16)
        end = half_ref[head, :] * state_ref[a] + dot(scaled, v_all[:, lanes])
        out_ref[a] = end
        ends.append(end.astype(BF16))
    half = pl.num_programs(0) // 2

    @pl.when(jnp.where(places[4] == 0, j >= half, j < half))
    def _():
        for a in range(group):
            sent_ref[a] = ends[a]


def state_call(places, far, w_qkv, acc, to_end, half_fade, state, group):
    _, rows, width = acc.shape
    heads, size = state.shape[0], state.shape[1]
    depth = far[0].shape[1]
    cols = group * size
    wide = pl.BlockSpec((rows, cols), lambda j, o: (0, j))
    small = pl.BlockSpec((group, size, size), lambda j, o: (j, 0, 0))
    half = heads // group // 2

    def sent_block(j, o):
        return jnp.where(o[4] == 0, jnp.maximum(j - half, 0), jnp.minimum(j, half - 1)), 0, 0

    return call(
        functools.partial(state_kernel, group, size),
        "states",
        heads // group,
        places,
        (*far, w_qkv, w_qkv, acc, acc, to_end, half_fade, state),
        [fixed(far[0].shape), fixed(far[1].shape)]
        + [pl.BlockSpec((1, depth, cols), lambda j, o, c=c: (c, o[3], j)) for c in (1, 2)]
        + [pl.BlockSpec((1, rows, cols), lambda j, o, c=c: (c, 0, j)) for c in (0, 1)]
        + [pl.BlockSpec((heads, rows), lambda j, o: (0, 1)), fixed(half_fade.shape), small],
        (
            pltpu.HBM((rows, width), BF16),
            pltpu.HBM((rows, width), BF16),
            struct(state.shape, F32),
            struct((heads // 2, size, size), BF16),
        ),
        [wide, wide, small, pl.BlockSpec((group, size, size), sent_block)],
        4 * rows * depth * width,
        scratch=[pltpu.VMEM((rows, depth), BF16)],
    )


def later_kernel(chunk, group, size, _, *refs):
    xa, xb, wq, acc_q, k_ref, v_ref, along_ref, inside_ref, state_ref, q_ref, within_ref, held = refs
    j = pl.program_id(0)
    rows = held.shape[0]

    @pl.when(j == 0)
    def _():
        held[: rows // 2, :] = xa[...]
        held[rows // 2 :, :] = xb[...]

    q_all = (acc_q[0] + dot(held[...], wq[0])).astype(BF16)
    q_ref[...] = q_all
    for a in range(group):
        head = j * group + a
        lanes = slice(a * size, (a + 1) * size)
        state = state_ref[a]
        for c in range(rows // chunk):
            here = slice(c * chunk, (c + 1) * chunk)
            q, k, v = q_all[here, lanes], k_ref[here, lanes], v_ref[here, lanes]
            along, down = along_ref[pl.ds(head, 1), here], column(inside_ref[here, :], head)
            within_ref[here, lanes] = scores(q, k, v, along, down, state)
            if c + 1 < rows // chunk:
                state = advance(k, v, down, state)


def later_call(places, far, w_qkv, acc, k, v, along, inside, state, chunk, group):
    _, rows, width = acc.shape
    heads, size = state.shape[0], state.shape[1]
    depth = far[0].shape[1]
    cols = group * size
    wide = pl.BlockSpec((rows, cols), lambda j, o: (0, j))
    return call(
        functools.partial(later_kernel, chunk, group, size),
        "later",
        heads // group,
        places,
        (*far, w_qkv, acc, k, v, along, inside, state),
        [
            fixed(far[0].shape),
            fixed(far[1].shape),
            pl.BlockSpec((1, depth, cols), lambda j, o: (0, o[3], j)),
            pl.BlockSpec((1, rows, cols), lambda j, o: (0, 0, j)),
            wide,
            wide,
            pl.BlockSpec((heads, rows), lambda j, o: (0, 1)),
            pl.BlockSpec((rows, heads), lambda j, o: (1, 0)),
            pl.BlockSpec((group, size, size), lambda j, o: (j, 0, 0)),
        ],
        (struct((rows, width), BF16), struct((rows, width), F32)),
        [wide, wide],
        2 * rows * depth * width + 4 * rows * (chunk + size) * width,
        scratch=[pltpu.VMEM((rows, depth), BF16)],
    )


def fades(tail_ref, other_ref, place, head):
    own, other = tail_ref[pl.ds(head, 1), :], other_ref[pl.ds(head, 1), :]
    first = jnp.where(place == 0, own, other)
    return jnp.exp(-first), jnp.exp(first - (own + other)), jnp.exp(-(own + other))


def chip_kernel(places, state_ref, come_ref, tail_ref, other_ref, prior_ref, *out_refs):
    leaving_ref, chip_ref, first_ref = out_refs
    core, chip = places[4], places[5]
    share = come_ref.shape[0]
    for i in range(share):
        head = core * share + i
        _, second_fade, fade = fades(tail_ref, other_ref, core, head)
        ours, come = state_ref[head], come_ref[i].astype(F32)
        first, second = jnp.where(core == 0, ours, come), jnp.where(core == 0, come, ours)
        total = second_fade * first + second
        first_ref[i] = first
        chip_ref[i] = total
        leaving_ref[i] = jnp.where(chip == 2, total, fade * prior_ref[head] + total).astype(BF16)


def pass_kernel(places, come_ref, chip_ref, tail_ref, other_ref, leaving_ref):
    share = come_ref.shape[0]
    for i in range(share):
        fade = fades(tail_ref, other_ref, places[4], places[4] * share + i)[2]
        leaving_ref[i] = (fade * come_ref[i].astype(F32) + chip_ref[i]).astype(BF16)


def enter_kernel(
    places, come_ref, second_ref, third_ref, first_ref, tail_ref, other_ref, below_ref, prior_ref, *out_refs
):
    here_ref, passed_ref = out_refs
    core, chip = places[4], places[5]
    share = come_ref.shape[0]
    for i in range(share):
        head = core * share + i
        come = come_ref[i].astype(F32)
        below = jnp.exp(-below_ref[pl.ds(head, 1), :])
        state = jnp.where(chip == 0, prior_ref[head], come)
        state = jnp.where(chip == 2, second_ref[i].astype(F32), state)
        state = jnp.where(chip == 3, below * third_ref[i].astype(F32) + come, state)
        later = fades(tail_ref, other_ref, core, head)[0] * state + first_ref[i]
        here_ref[i] = jnp.where(core == 0, state, later).astype(BF16)
        passed_ref[i] = jnp.where(core == 0, later, state).astype(BF16)


def small_call(kernel, name, places, ins, outs):
    whole = pl.BlockSpec(memory_space=pltpu.VMEM)
    return pl.pallas_call(
        kernel,
        out_shape=tuple(outs),
        in_specs=[pl.BlockSpec(memory_space=pltpu.SMEM)] + [whole] * len(ins),
        out_specs=[whole] * len(outs),
        compiler_params=pltpu.CompilerParams(vmem_limit_bytes=4 * MIB),
        cost_estimate=pl.CostEstimate(flops=1, bytes_accessed=1, transcendentals=0),
        name=name,
    )(places, *ins)


def chip_call(places, state, come, tails, prior):
    outs = (struct(come.shape, BF16), struct(come.shape, F32), struct(come.shape, F32))
    return small_call(chip_kernel, "chip_state", places, (state, come, *tails, prior), outs)


def pass_call(places, come, chip_state, tails):
    outs = (struct(come.shape, BF16),)
    return small_call(pass_kernel, "pass_on", places, (come, chip_state, *tails), outs)[0]


def enter_call(places, come, second, third, first, tails, below, prior):
    outs = (struct(come.shape, BF16),) * 2
    ins = (come, second, third, first, *tails, below, prior)
    return small_call(enter_kernel, "enter", places, ins, outs)


def columns(w_ref, block, width):
    return w_ref[:, pl.ds(pl.multiple_of(block * width, width), width)]


WHOLE = pl.BlockSpec(memory_space=pltpu.VMEM)


def head_kernel(blocks, places, q_ref, within_ref, here_ref, there_ref, down_ref, w_ref, *refs):
    normed_ref, out_refs, held = refs[0], refs[1:3], refs[3]
    share, size = here_ref.shape[0], here_ref.shape[1]
    tall, width = out_refs[0].shape
    step = pl.program_id(0)
    for p, out_ref in enumerate(out_refs):

        @pl.when(step == p)
        def _(p=p, out_ref=out_ref):
            fade = jnp.exp(-down_ref[...])
            for a in range(2 * share):
                lanes = slice(a * size, (a + 1) * size)
                ours = places[4] == a // share
                entering = jnp.where(ours, here_ref[a % share], there_ref[a % share])
                seen = dot(q_ref[:, lanes], entering) * fade[:, a : a + 1]
                combined = within_ref[:, lanes] + seen
                power = jnp.mean(combined * combined, axis=1, keepdims=True)
                held[p, :, lanes] = (combined * lax.rsqrt(power + 1e-06)).astype(BF16)
            normed_ref[...] = held[p]
            out_ref[...] = dot(held[p], columns(w_ref, places[blocks[0]], width)).astype(BF16)

        @pl.when(step == 2 + p)
        def _(p=p, out_ref=out_ref):
            out_ref[...] = dot(held[p], columns(w_ref, places[blocks[1 + p]], width)).astype(BF16)


def head_call(places, blocks, q, within, entering, down, w_out, width, at):
    rows, cols = q.shape
    tall = rows // 2
    heads = down.shape[1]
    part = pl.BlockSpec((tall, cols), lambda i, o: (jnp.minimum(i, 1), 0))
    return call(
        functools.partial(head_kernel, blocks),
        "heads",
        4,
        places,
        (q, within, *entering, down, w_out),
        [
            part,
            part,
            fixed(entering[0].shape),
            fixed(entering[1].shape),
            pl.BlockSpec((tall, heads), lambda i, o: (2 * at + jnp.minimum(i, 1), 0)),
            WHOLE,
        ],
        (struct((rows, cols), BF16), *[struct((rows, width), BF16)] * 2),
        [
            part,
            pl.BlockSpec((tall, width), lambda i, o: (i // 2, 0)),
            pl.BlockSpec((tall, width), lambda i, o: (jnp.maximum(i - 2, 0), 0)),
        ],
        2 * rows * cols * (2 * width + 128),
        scratch=[pltpu.VMEM((2, tall, cols), BF16)],
        light=True,
    )


def pair_kernel(places, normed_ref, x_ref, y_ref, w_ref, out_x_ref, out_y_ref):
    tall, width = out_x_ref.shape

    @pl.when(pl.program_id(0) == 0)
    def _():
        total = dot(normed_ref[tall:, :], columns(w_ref, places[1], width)) + x_ref[...].astype(F32)
        out_x_ref[...] = total.astype(BF16)

    @pl.when(pl.program_id(0) == 1)
    def _():
        total = dot(normed_ref[:tall, :], columns(w_ref, places[2], width)) + y_ref[...].astype(F32)
        out_y_ref[...] = total.astype(BF16)


def pair_call(places, normed, for_x, for_y, w_out, width):
    rows, cols = normed.shape
    quarter = (rows // 2, width)
    return call(
        pair_kernel,
        "sum_pair",
        2,
        places,
        (normed, for_x, for_y, w_out),
        [fixed((rows, cols)), fixed(quarter), fixed(quarter), WHOLE],
        (struct(quarter, BF16),) * 2,
        [fixed(quarter)] * 2,
        2 * rows * cols * width,
        light=True,
    )


def own_kernel(places, normed_ref, w_ref, *refs):
    out_ref = refs[-1]
    tall, width = out_ref.shape
    each = len(refs) // 2
    for p in range(2):
        rows = slice(p * tall, (p + 1) * tall)

        @pl.when(pl.program_id(0) == p)
        def _(p=p, rows=rows):
            total = dot(normed_ref[rows, :], columns(w_ref, places[0], width))
            for ref in refs[p * each : (p + 1) * each]:
                total = total + ref[...].astype(F32)
            out_ref[...] = total.astype(BF16)


def own_call(places, normed, first, second, w_out, width, height):
    rows, cols = normed.shape
    quarter = (rows // 2, width)
    return call(
        own_kernel,
        "own_block",
        2,
        places,
        (normed, w_out, *[a for a, _ in (*first, *second)]),
        [fixed((rows, cols)), WHOLE]
        + [pl.BlockSpec(quarter, lambda i, o, at=at: (at, 0)) for _, at in (*first, *second)],
        (struct((rows * height, width), BF16),),
        [pl.BlockSpec(quarter, lambda i, o: (i, 0))],
        2 * rows * cols * width,
        light=True,
    )[0]


def last_kernel(_, kept_ref, a_ref, b_ref, above_ref, out_ref):
    del above_ref

    @pl.when(pl.program_id(0) == 0)
    def _():
        out_ref[...] = (kept_ref[...].astype(F32) + a_ref[...].astype(F32)).astype(BF16)

    @pl.when(pl.program_id(0) == 1)
    def _():
        out_ref[...] = (kept_ref[...].astype(F32) + b_ref[...].astype(F32)).astype(BF16)


def last_call(kept, a, b, above):
    tall, width = a.shape
    return call(
        last_kernel,
        "last_add",
        2,
        jnp.zeros((1,), jnp.int32),
        (kept, a, b, above),
        [
            pl.BlockSpec((tall, width), lambda j, o: (j, 0)),
            fixed((tall, width)),
            fixed((tall, width)),
            pl.BlockSpec(memory_space=pl.ANY),
        ],
        (struct(above.shape, BF16),),
        [pl.BlockSpec((tall, width), lambda j, o: (2 + j, 0))],
        tall * width,
        aliases={4: 0},
    )[0]


def local(n_head, n_seq, tokens, w_qkv, w_out, decay_rate, prior_state):
    rows, width = tokens.shape
    heads, size = prior_state.shape[0], prior_state.shape[1]
    square = n_head == 4
    place = lax.axis_index("head").astype(jnp.int32)
    quarter = rows // 4
    group = 2 if heads % 2 == 0 else 1
    cols = group * size

    over_x = functools.partial(lax.ppermute, axis_name="head", perm=[(i, i ^ 1) for i in range(n_head)])
    over_y = functools.partial(lax.ppermute, axis_name="head", perm=[(i, i ^ 2) for i in range(n_head)])

    pos = lax.axis_index("seq").astype(jnp.int32)
    core, chip = pos % 2, pos // 2
    flips = (0, 1, 2, 3) if square else (0, 0, 0, 0)
    places = jnp.stack([*[place ^ f for f in flips], core, chip])

    along, inside, down, tail, to_end, half_fade = decay_call(decay_rate, quarter)
    n_chips = n_seq // 2
    swap = functools.partial(lax.ppermute, axis_name="seq", perm=[(i, i ^ 1) for i in range(n_seq)])

    def hop(x, *pairs):
        perm = [(2 * a + c, 2 * b + c) for a, b in pairs for c in range(2)]
        return lax.ppermute(x, "seq", perm=perm)

    def chip_tails(tail):
        other = swap(tail)
        return other, tail + other, hop(tail + other, (2, 3)) if n_chips == 4 else None

    if square:
        tokens = stay(tokens)
        q0, q1 = cut_call(tokens, 0, 1)
        x0, y1 = over_x(q0), over_y(q1)
        x1, y0 = over_x(after(q1, tail)), over_y(after(q0, tail))
        acc = own_part_call(places, tokens, w_qkv, cols)
        q2, q3 = cut_call(stay(after(tokens, acc, x0, y1)), 1, 10**10)
        fy0, fx1 = over_y(x0), over_x(y1)
        tail_other, tail_chip, tail_below = chip_tails(after(tail, acc, x0, y1))
        x2 = over_x(after(q2, x1, y0, tail_chip))
        y3 = over_y(after(q3, x1, y0, tail_chip))
        acc_a = part_call(
            places,
            (1, 2),
            [(x0, x1), (y0, y1)],
            w_qkv,
            2 * quarter,
            cols,
            before=stay(after(acc, tail_chip)),
            at=0,
        )
        earlier = (fy0, fx1, acc_a) if tail_below is None else (fy0, fx1, acc_a, tail_below)
        x3, y2 = over_x(after(q3, *earlier)), over_y(after(q2, *earlier))
        query_a, within_a, state = first_call(
            places,
            (3,),
            [(fy0, fx1)],
            (acc_a,),
            w_qkv,
            along,
            inside,
            2 * quarter,
            quarter,
            size,
            group,
        )
        fy2, fx3 = over_y(after(x2, state)), over_x(after(y3, state))
        acc_q, acc_kv = part_call(
            places,
            (1, 2),
            [(x2, x3), (y2, y3)],
            w_qkv,
            2 * quarter,
            cols,
            before=stay(acc),
            at=1,
            apart=True,
        )
        far = (fy2, fx3)
        middle = state
        k, v, state, sent = state_call(
            places, far, w_qkv, acc_kv, to_end, half_fade, middle, group
        )
    else:
        tail_other, tail_chip, tail_below = chip_tails(tail)
        gathered = lax.all_gather(tokens, "head", axis=1, tiled=True)
        query, within, state = first_call(
            places, (), [(gathered,)], (), w_qkv, along, inside, rows, quarter, size, group
        )

    tails = (tail, tail_other)
    if square and n_chips == 4:
        leaving, chip_state, first = chip_call(places, state, near(swap(sent)), tails, prior_state)
        arriving = near(hop(leaving, (0, 1), (2, 3)))
        leaving = pass_call(places, arriving, chip_state, tails)
        to_third, to_second = near(hop(leaving, (1, 3))), near(hop(leaving, (1, 2)))
        here, passed = enter_call(
            places, arriving, to_second, to_third, first, tails, tail_below, prior_state
        )
    else:
        share = heads // 2

        def mine(x, core=core):
            return lax.dynamic_slice_in_dim(x, core * share, share, 0)

        def decay(tail):
            return jnp.exp(-mine(tail)[:, :1, None])

        ours = mine(state)
        other = swap(mine(state, 1 - core).astype(BF16)).astype(F32)
        first = jnp.where(core == 0, ours, other)
        second = jnp.where(core == 0, other, ours)
        chip_state = decay(jnp.where(core == 0, tail_other, tail)) * first + second
        chip_entering = mine(prior_state)
        for step in range(n_chips - 1):
            leaving = (decay(tail_chip) * chip_entering + chip_state).astype(BF16)
            arriving = hop(leaving, (step, step + 1))
            chip_entering = jnp.where(chip == step + 1, arriving.astype(F32), chip_entering)
        other = decay(jnp.where(core == 0, tail, tail_other)) * chip_entering + first
        here = jnp.where(core == 0, chip_entering, other).astype(BF16)
        passed = jnp.where(core == 0, other, chip_entering).astype(BF16)
    entering = (here, swap(passed))

    w_whole, w_out = w_out, near(w_out)
    if not square:
        halves = [
            head_call(
                places,
                (0, 0, 0),
                query[r * rows // 2 : (r + 1) * rows // 2],
                within[r * rows // 2 : (r + 1) * rows // 2],
                entering,
                down,
                w_out,
                width,
                r,
            )[0]
            for r in range(2)
        ]
        partial = dot(jnp.concatenate(halves), w_whole).astype(BF16)
        return lax.psum_scatter(partial, "head", scatter_dimension=1, tiled=True)

    na, by_x, by_y = head_call(
        places, (3, 1, 2), stay(query_a), stay(within_a), entering, down, w_out, width, 0
    )
    middle = stay(after(middle, na))
    by_x, by_y = over_x(by_x), over_y(by_y)
    query_b, within_b = later_call(
        places, far, w_qkv, stay(acc_q), stay(k), stay(v), along, inside, middle, quarter, group
    )
    nb, by_x2, by_y2 = head_call(
        places, (3, 1, 2), query_b, within_b, entering, down, w_out, width, 1
    )
    by_x2, by_y2 = over_x(by_x2), over_y(by_y2)
    sum1, sum0 = pair_call(places, after(na, nb), by_y, by_x, w_out, width)
    by_x2, by_y2 = after(by_x2, sum1), after(by_y2, sum1)
    sum1, sum0 = over_x(sum1), over_y(sum0)
    sum3, sum2 = pair_call(places, nb, by_y2, by_x2, w_out, width)
    sum3, sum2 = over_x(sum3), over_y(sum2)
    below = own_call(places, after(nb, sum1, sum0), ((by_x2, 1),), ((by_y2, 1),), w_out, width, 1)
    above = own_call(
        places, na, ((by_x, 1), (sum0, 0)), ((by_y, 1), (sum1, 0)), w_out, width, 2
    )
    return last_call(below, sum2, sum3, above)


def solution(mesh):
    in_specs = (
        P("seq", "head"),
        P(None, None, "head"),
        P("head", None),
        P("head", "seq"),
        P("head", None, None),
    )
    body = functools.partial(local, mesh.shape["head"], mesh.shape["seq"])
    return jax.shard_map(
        body, mesh=mesh, in_specs=in_specs, out_specs=P("seq", "head"), check_vma=False
    )
```

```python
import functools
import math

import jax
import jax.numpy as jnp
from jax import lax
from jax.experimental import pallas as pl
from jax.experimental.pallas import tpu as pltpu
from jax.sharding import PartitionSpec as P

BF16, F32 = jnp.bfloat16, jnp.float32
MIB = 1024 * 1024


def dot(a, b, contract=((1,), (0,))):
    return lax.dot_general(a, b, (contract, ((), ())), preferred_element_type=F32)


def after(x, *earlier):
    return lax.optimization_barrier((x, *earlier))[0]


def struct(shape, dtype):
    return jax.ShapeDtypeStruct(shape, dtype)


def stay(x):
    return pltpu.with_memory_space_constraint(x, pltpu.HBM)


def near(x):
    return pltpu.with_memory_space_constraint(x, pltpu.VMEM)


def fixed(shape):
    return pl.BlockSpec(shape, lambda j, o: (0,) * len(shape))


def call(kernel, name, steps, scalars, ins, in_specs, outs, out_specs, flops, scratch=(), aliases=None, light=False):
    moved = sum(a.size * a.dtype.itemsize for a in ins) + sum(
        math.prod(o.shape) * jnp.dtype(o.dtype).itemsize for o in outs
    )
    return pl.pallas_call(
        kernel,
        out_shape=tuple(outs),
        grid_spec=pltpu.PrefetchScalarGridSpec(
            num_scalar_prefetch=1,
            grid=(steps,),
            in_specs=in_specs,
            out_specs=out_specs,
            scratch_shapes=list(scratch),
        ),
        input_output_aliases=aliases or {},
        compiler_params=pltpu.CompilerParams(vmem_limit_bytes=(24 if light else 32) * MIB),
        cost_estimate=pl.CostEstimate(
            flops=1 if light else flops, bytes_accessed=1 if light else moved, transcendentals=0
        ),
        name=name,
    )(scalars, *ins)


def cut_kernel(_, x_ref, a_ref, b_ref):
    tall = a_ref.shape[0]
    a_ref[...] = x_ref[:tall, :]
    b_ref[...] = x_ref[tall:, :]


def cut_call(x, half, cost):
    rows, width = x.shape
    quarter = (rows // 4, width)
    return call(
        cut_kernel,
        "cut",
        1,
        jnp.zeros((1,), jnp.int32),
        (x,),
        [pl.BlockSpec((rows // 2, width), lambda j, o: (half, 0))],
        (struct(quarter, x.dtype),) * 2,
        [fixed(quarter)] * 2,
        cost,
    )


def decay_kernel(chunk, _, rate_ref, along_ref, inside_ref, down_ref, tail_ref, end_ref, half_ref):
    heads, rows = rate_ref.shape
    lane = lax.broadcasted_iota(jnp.int32, (heads, chunk), 1)
    base = jnp.zeros((heads, 1), F32)
    insides, wholes = [], []
    for c in range(rows // chunk):
        x = rate_ref[:, c * chunk : (c + 1) * chunk]
        step = 1
        while step < chunk:
            x = x + jnp.where(lane >= step, pltpu.roll(x, step, 1), 0.0)
            step *= 2
        insides.append(x)
        wholes.append(x + base)
        base = base + x[:, chunk - 1 :]
    inside, whole = jnp.concatenate(insides, axis=1), jnp.concatenate(wholes, axis=1)
    along_ref[...] = inside
    inside_ref[...] = inside.T
    down_ref[...] = whole.T
    tail_ref[...] = jnp.broadcast_to(base, tail_ref.shape)
    end_ref[...] = jnp.exp(whole - base)
    half_ref[...] = jnp.broadcast_to(jnp.exp(whole[:, rows // 2 - 1 : rows // 2] - base), half_ref.shape)


def decay_call(rate, chunk):
    heads, rows = rate.shape
    return call(
        functools.partial(decay_kernel, chunk),
        "decay",
        1,
        jnp.zeros((1,), jnp.int32),
        (rate,),
        [fixed((heads, rows))],
        (
            struct((heads, rows), F32),
            struct((rows, heads), F32),
            struct((rows, heads), F32),
            struct((heads, 128), F32),
            struct((heads, rows), F32),
            struct((heads, 128), F32),
        ),
        [
            fixed((heads, rows)),
            fixed((rows, heads)),
            fixed((rows, heads)),
            fixed((heads, 128)),
            fixed((heads, rows)),
            fixed((heads, 128)),
        ],
        heads * rows * 16,
    )


def column(table, head):
    lane = lax.broadcasted_iota(jnp.int32, table.shape, 1)
    return jnp.sum(jnp.where(lane == head, table, 0.0), axis=1, keepdims=True)


def scores(q, k, v, along, down, state):
    rows = q.shape[0]
    causal = lax.broadcasted_iota(jnp.int32, (rows, rows), 0) >= lax.broadcasted_iota(
        jnp.int32, (rows, rows), 1
    )
    decay = jnp.exp(jnp.minimum(along - down, 0.0))
    weights = jnp.where(causal, dot(q, k, ((1,), (1,))) * decay, 0.0).astype(BF16)
    return dot(weights, v) + dot(q, state.astype(BF16)) * jnp.exp(-down)


def faded(q, down):
    return (q.astype(F32) * jnp.exp(-down)).astype(BF16)


def advance(k, v, down, state):
    last = down[down.shape[0] - 1 :, :]
    scaled = (k.astype(F32) * jnp.exp(down - last)).astype(BF16)
    return jnp.exp(-last) * state + dot(scaled, v, ((0,), (0,)))


def first_kernel(layout, added, chunk, group, size, _, *refs):
    count = sum(layout)
    x_refs, w_refs, refs = refs[:count], refs[count : count + len(layout)], refs[count + len(layout) :]
    along_ref, inside_ref, q_ref, within_ref, state_ref, held = refs[-6:]
    j = pl.program_id(0)
    rows = held.shape[1]

    @pl.when(j == 0)
    def _():
        at = 0
        for i, parts in enumerate(layout):
            tall = rows // parts
            for p in range(parts):
                held[i, p * tall : (p + 1) * tall, :] = x_refs[at][...]
                at += 1

    def project(c):
        total = dot(held[0], w_refs[0][c])
        for i in range(1, len(layout)):
            total = total + dot(held[i], w_refs[i][c])
        if added:
            total = total + refs[0][c]
        return total.astype(BF16)

    q_all, k_all, v_all = project(0), project(1), project(2)
    for a in range(group):
        head = j * group + a
        lanes = slice(a * size, (a + 1) * size)
        state, base = jnp.zeros((size, size), F32), jnp.zeros((1, 1), F32)
        for c in range(rows // chunk):
            here = slice(c * chunk, (c + 1) * chunk)
            q, k, v = q_all[here, lanes], k_all[here, lanes], v_all[here, lanes]
            down = column(inside_ref[here, :], head)
            along = along_ref[pl.ds(head, 1), here]
            q_ref[here, lanes] = faded(q, base + down)
            within_ref[here, lanes] = scores(q, k, v, along, down, state).astype(BF16)
            state, base = advance(k, v, down, state), base + down[chunk - 1 :, :]
        state_ref[a] = state


def first_call(places, blocks, pieces, before, w_qkv, along, inside, rows, chunk, size, group):
    heads = along.shape[0]
    cols = group * size
    flat = [p for piece in pieces for p in piece]
    depth = flat[0].shape[1]

    def block(i):
        return pl.BlockSpec((3, depth, cols), lambda j, o: (0, o[blocks[i]] if blocks else 0, j))

    wide = pl.BlockSpec((rows, cols), lambda j, o: (0, j))
    return call(
        functools.partial(
            first_kernel, tuple(len(p) for p in pieces), bool(before), chunk, group, size
        ),
        "first",
        heads // group,
        places,
        (*flat, *[w_qkv] * len(pieces), *before, along, inside),
        [
            pl.BlockSpec((rows // len(piece), depth), lambda j, o: (0, 0))
            for piece in pieces
            for _ in piece
        ]
        + [block(i) for i in range(len(pieces))]
        + [pl.BlockSpec((3, rows, cols), lambda j, o: (0, 0, j)) for _ in before]
        + [fixed((heads, rows)), fixed((rows, heads))],
        (
            pltpu.HBM((rows, heads * size), BF16),
            pltpu.HBM((rows, heads * size), BF16),
            struct((heads, size, size), F32),
        ),
        [wide, wide, pl.BlockSpec((group, size, size), lambda j, o: (j, 0, 0))],
        2 * rows * 3 * heads * size * depth * len(pieces),
        scratch=[pltpu.VMEM((len(pieces), rows, depth), BF16)],
    )


def own_part_kernel(_, x_ref, w_ref, out_ref):
    for c in range(3):
        out_ref[c] = dot(x_ref[...], w_ref[c])


def own_part_call(places, tokens, w_qkv, cols):
    rows, depth = tokens.shape
    width = w_qkv.shape[2]
    return call(
        own_part_kernel,
        "own_part",
        width // cols,
        places,
        (tokens, w_qkv),
        [fixed((rows, depth)), pl.BlockSpec((3, depth, cols), lambda j, o: (0, o[0], j))],
        (pltpu.HBM((3, rows, width), F32),),
        [pl.BlockSpec((3, rows, cols), lambda j, o: (0, 0, j))],
        2 * rows * depth * width * 3,
    )[0]


def part_kernel(layout, outs, _, *refs):
    count = sum(layout)
    x_refs, w_refs = refs[:count], refs[count : count + len(layout)]
    before_ref, out_refs, held = refs[-2 - outs], refs[-1 - outs : -1], refs[-1]
    targets = [(ref, c) for ref in out_refs for c in range(ref.shape[0])]
    rows = held.shape[1]

    @pl.when(pl.program_id(0) == 0)
    def _():
        at = 0
        for i, parts in enumerate(layout):
            tall = rows // parts
            for p in range(parts):
                held[i, p * tall : (p + 1) * tall, :] = x_refs[at][...]
                at += 1

    for c in range(3):
        total = dot(held[0], w_refs[0][c])
        for i in range(1, len(layout)):
            total = total + dot(held[i], w_refs[i][c])
        ref, at = targets[c]
        ref[at] = total + before_ref[c]


def part_call(places, blocks, pieces, w_qkv, rows, cols, before, at, apart=False):
    flat = [p for piece in pieces for p in piece]
    depth = flat[0].shape[1]
    width = w_qkv.shape[2]

    def block(i):
        return pl.BlockSpec((3, depth, cols), lambda j, o: (0, o[blocks[i]], j))

    ins = [*flat, *[w_qkv] * len(pieces)]
    specs = [
        pl.BlockSpec((rows // len(piece), depth), lambda j, o: (0, 0)) for piece in pieces for _ in piece
    ] + [block(i) for i in range(len(pieces))]
    ins.append(before)
    specs.append(pl.BlockSpec((3, rows, cols), lambda j, o: (0, at, j)))
    outs = [struct((3, rows, width), F32)]
    if apart:
        outs = [pltpu.HBM((1, rows, width), F32), struct((2, rows, width), F32)]
    out = call(
        functools.partial(part_kernel, tuple(len(p) for p in pieces), len(outs)),
        "part",
        width // cols,
        places,
        ins,
        specs,
        outs,
        [pl.BlockSpec((o.shape[0], rows, cols), lambda j, o: (0, 0, j)) for o in outs],
        2 * rows * depth * len(pieces) * width * 3,
        scratch=[pltpu.VMEM((len(pieces), rows, depth), BF16)],
    )
    return out if apart else out[0]


def state_kernel(group, size, places, *refs):
    xa, xb, wk, wv, acc_k, acc_v, end_ref, half_ref, state_ref = refs[:9]
    k_ref, v_ref, out_ref, sent_ref, held = refs[9:]
    j = pl.program_id(0)
    rows = held.shape[0]

    @pl.when(j == 0)
    def _():
        held[: rows // 2, :] = xa[...]
        held[rows // 2 :, :] = xb[...]

    k_all = (acc_k[0] + dot(held[...], wk[0])).astype(BF16)
    v_all = (acc_v[0] + dot(held[...], wv[0])).astype(BF16)
    k_ref[...] = k_all
    v_ref[...] = v_all
    ends = []
    for a in range(group):
        head = pl.ds(j * group + a, 1)
        lanes = slice(a * size, (a + 1) * size)
        scaled = (k_all[:, lanes].T.astype(F32) * end_ref[head, :]).astype(BF16)
        end = half_ref[head, :] * state_ref[a] + dot(scaled, v_all[:, lanes])
        out_ref[a] = end
        ends.append(end.astype(BF16))
    half = pl.num_programs(0) // 2

    @pl.when(jnp.where(places[4] == 0, j >= half, j < half))
    def _():
        for a in range(group):
            sent_ref[a] = ends[a]


def state_call(places, far, w_qkv, acc, to_end, half_fade, state, group):
    _, rows, width = acc.shape
    heads, size = state.shape[0], state.shape[1]
    depth = far[0].shape[1]
    cols = group * size
    wide = pl.BlockSpec((rows, cols), lambda j, o: (0, j))
    small = pl.BlockSpec((group, size, size), lambda j, o: (j, 0, 0))
    half = heads // group // 2

    def sent_block(j, o):
        return jnp.where(o[4] == 0, jnp.maximum(j - half, 0), jnp.minimum(j, half - 1)), 0, 0

    return call(
        functools.partial(state_kernel, group, size),
        "states",
        heads // group,
        places,
        (*far, w_qkv, w_qkv, acc, acc, to_end, half_fade, state),
        [fixed(far[0].shape), fixed(far[1].shape)]
        + [pl.BlockSpec((1, depth, cols), lambda j, o, c=c: (c, o[3], j)) for c in (1, 2)]
        + [pl.BlockSpec((1, rows, cols), lambda j, o, c=c: (c, 0, j)) for c in (0, 1)]
        + [pl.BlockSpec((heads, rows), lambda j, o: (0, 1)), fixed(half_fade.shape), small],
        (
            pltpu.HBM((rows, width), BF16),
            pltpu.HBM((rows, width), BF16),
            struct(state.shape, F32),
            struct((heads // 2, size, size), BF16),
        ),
        [wide, wide, small, pl.BlockSpec((group, size, size), sent_block)],
        4 * rows * depth * width,
        scratch=[pltpu.VMEM((rows, depth), BF16)],
    )


def later_kernel(chunk, group, size, _, *refs):
    xa, xb, wq, acc_q, k_ref, v_ref, along_ref, inside_ref, down_ref, state_ref = refs[:10]
    q_ref, within_ref, held = refs[10:]
    j = pl.program_id(0)
    rows = held.shape[0]

    @pl.when(j == 0)
    def _():
        held[: rows // 2, :] = xa[...]
        held[rows // 2 :, :] = xb[...]

    q_all = (acc_q[0] + dot(held[...], wq[0])).astype(BF16)
    for a in range(group):
        head = j * group + a
        lanes = slice(a * size, (a + 1) * size)
        state = state_ref[a]
        for c in range(rows // chunk):
            here = slice(c * chunk, (c + 1) * chunk)
            q, k, v = q_all[here, lanes], k_ref[here, lanes], v_ref[here, lanes]
            along, down = along_ref[pl.ds(head, 1), here], column(inside_ref[here, :], head)
            q_ref[here, lanes] = faded(q, column(down_ref[here, :], head))
            within_ref[here, lanes] = scores(q, k, v, along, down, state).astype(BF16)
            if c + 1 < rows // chunk:
                state = advance(k, v, down, state)


def later_call(places, far, w_qkv, acc, k, v, along, inside, down, state, chunk, group):
    _, rows, width = acc.shape
    heads, size = state.shape[0], state.shape[1]
    depth = far[0].shape[1]
    cols = group * size
    wide = pl.BlockSpec((rows, cols), lambda j, o: (0, j))
    return call(
        functools.partial(later_kernel, chunk, group, size),
        "later",
        heads // group,
        places,
        (*far, w_qkv, acc, k, v, along, inside, down, state),
        [
            fixed(far[0].shape),
            fixed(far[1].shape),
            pl.BlockSpec((1, depth, cols), lambda j, o: (0, o[3], j)),
            pl.BlockSpec((1, rows, cols), lambda j, o: (0, 0, j)),
            wide,
            wide,
            pl.BlockSpec((heads, rows), lambda j, o: (0, 1)),
            pl.BlockSpec((rows, heads), lambda j, o: (1, 0)),
            pl.BlockSpec((rows, heads), lambda j, o: (1, 0)),
            pl.BlockSpec((group, size, size), lambda j, o: (j, 0, 0)),
        ],
        (struct((rows, width), BF16), struct((rows, width), BF16)),
        [wide, wide],
        2 * rows * depth * width + 4 * rows * (chunk + size) * width,
        scratch=[pltpu.VMEM((rows, depth), BF16)],
    )


def fades(tail_ref, other_ref, place, head):
    own, other = tail_ref[pl.ds(head, 1), :], other_ref[pl.ds(head, 1), :]
    first = jnp.where(place == 0, own, other)
    return jnp.exp(-first), jnp.exp(first - (own + other)), jnp.exp(-(own + other))


def chip_kernel(places, state_ref, come_ref, tail_ref, other_ref, prior_ref, *out_refs):
    leaving_ref, chip_ref, first_ref = out_refs
    core, chip = places[4], places[5]
    share = come_ref.shape[0]
    for i in range(share):
        head = core * share + i
        _, second_fade, fade = fades(tail_ref, other_ref, core, head)
        ours, come = state_ref[head], come_ref[i].astype(F32)
        first, second = jnp.where(core == 0, ours, come), jnp.where(core == 0, come, ours)
        total = second_fade * first + second
        first_ref[i] = first
        chip_ref[i] = total
        leaving_ref[i] = jnp.where(chip == 2, total, fade * prior_ref[head] + total).astype(BF16)


def pass_kernel(places, come_ref, chip_ref, tail_ref, other_ref, leaving_ref):
    share = come_ref.shape[0]
    for i in range(share):
        fade = fades(tail_ref, other_ref, places[4], places[4] * share + i)[2]
        leaving_ref[i] = (fade * come_ref[i].astype(F32) + chip_ref[i]).astype(BF16)


def enter_kernel(
    places, come_ref, second_ref, third_ref, first_ref, tail_ref, other_ref, below_ref, prior_ref, *out_refs
):
    here_ref, passed_ref = out_refs
    core, chip = places[4], places[5]
    share = come_ref.shape[0]
    for i in range(share):
        head = core * share + i
        come = come_ref[i].astype(F32)
        below = jnp.exp(-below_ref[pl.ds(head, 1), :])
        state = jnp.where(chip == 0, prior_ref[head], come)
        state = jnp.where(chip == 2, second_ref[i].astype(F32), state)
        state = jnp.where(chip == 3, below * third_ref[i].astype(F32) + come, state)
        later = fades(tail_ref, other_ref, core, head)[0] * state + first_ref[i]
        here_ref[i] = jnp.where(core == 0, state, later).astype(BF16)
        passed_ref[i] = jnp.where(core == 0, later, state).astype(BF16)


def small_call(kernel, name, places, ins, outs):
    whole = pl.BlockSpec(memory_space=pltpu.VMEM)
    return pl.pallas_call(
        kernel,
        out_shape=tuple(outs),
        in_specs=[pl.BlockSpec(memory_space=pltpu.SMEM)] + [whole] * len(ins),
        out_specs=[whole] * len(outs),
        compiler_params=pltpu.CompilerParams(vmem_limit_bytes=4 * MIB),
        cost_estimate=pl.CostEstimate(flops=1, bytes_accessed=1, transcendentals=0),
        name=name,
    )(places, *ins)


def chip_call(places, state, come, tails, prior):
    outs = (struct(come.shape, BF16), struct(come.shape, F32), struct(come.shape, F32))
    return small_call(chip_kernel, "chip_state", places, (state, come, *tails, prior), outs)


def pass_call(places, come, chip_state, tails):
    outs = (struct(come.shape, BF16),)
    return small_call(pass_kernel, "pass_on", places, (come, chip_state, *tails), outs)[0]


def enter_call(places, come, second, third, first, tails, below, prior):
    outs = (struct(come.shape, BF16),) * 2
    ins = (come, second, third, first, *tails, below, prior)
    return small_call(enter_kernel, "enter", places, ins, outs)


def columns(w_ref, block, width):
    return w_ref[:, pl.ds(pl.multiple_of(block * width, width), width)]


WHOLE = pl.BlockSpec(memory_space=pltpu.VMEM)


def head_kernel(blocks, places, q_ref, within_ref, here_ref, there_ref, w_ref, *refs):
    normed_ref, out_refs, held = refs[0], refs[1:3], refs[3]
    share, size = here_ref.shape[0], here_ref.shape[1]
    tall, width = out_refs[0].shape
    step = pl.program_id(0)
    for p, out_ref in enumerate(out_refs):

        @pl.when(step == p)
        def _(p=p, out_ref=out_ref):
            ones = jnp.ones((size, size), BF16)
            for a in range(2 * share):
                lanes = slice(a * size, (a + 1) * size)
                ours = places[4] == a // share
                entering = jnp.where(ours, here_ref[a % share], there_ref[a % share])
                combined = within_ref[:, lanes].astype(F32) + dot(q_ref[:, lanes], entering)
                square = combined * combined
                high = square.astype(BF16)
                low = (square - high.astype(F32)).astype(BF16)
                power = (dot(high, ones) + dot(low, ones)) * (1.0 / size)
                held[p, :, lanes] = (combined * lax.rsqrt(power + 1e-06)).astype(BF16)
            normed_ref[...] = held[p]
            out_ref[...] = dot(held[p], columns(w_ref, places[blocks[0]], width)).astype(BF16)

        @pl.when(step == 2 + p)
        def _(p=p, out_ref=out_ref):
            out_ref[...] = dot(held[p], columns(w_ref, places[blocks[1 + p]], width)).astype(BF16)


def head_call(places, blocks, q, within, entering, w_out, width):
    rows, cols = q.shape
    tall = rows // 2
    part = pl.BlockSpec((tall, cols), lambda i, o: (jnp.minimum(i, 1), 0))
    return call(
        functools.partial(head_kernel, blocks),
        "heads",
        4,
        places,
        (q, within, *entering, w_out),
        [
            part,
            part,
            fixed(entering[0].shape),
            fixed(entering[1].shape),
            WHOLE,
        ],
        (struct((rows, cols), BF16), *[struct((rows, width), BF16)] * 2),
        [
            part,
            pl.BlockSpec((tall, width), lambda i, o: (i // 2, 0)),
            pl.BlockSpec((tall, width), lambda i, o: (jnp.maximum(i - 2, 0), 0)),
        ],
        2 * rows * cols * (2 * width + 128),
        scratch=[pltpu.VMEM((2, tall, cols), BF16)],
        light=True,
    )


def pair_kernel(places, normed_ref, x_ref, y_ref, w_ref, out_x_ref, out_y_ref):
    tall, width = out_x_ref.shape

    @pl.when(pl.program_id(0) == 0)
    def _():
        total = dot(normed_ref[tall:, :], columns(w_ref, places[1], width)) + x_ref[...].astype(F32)
        out_x_ref[...] = total.astype(BF16)

    @pl.when(pl.program_id(0) == 1)
    def _():
        total = dot(normed_ref[:tall, :], columns(w_ref, places[2], width)) + y_ref[...].astype(F32)
        out_y_ref[...] = total.astype(BF16)


def pair_call(places, normed, for_x, for_y, w_out, width):
    rows, cols = normed.shape
    quarter = (rows // 2, width)
    return call(
        pair_kernel,
        "sum_pair",
        2,
        places,
        (normed, for_x, for_y, w_out),
        [fixed((rows, cols)), fixed(quarter), fixed(quarter), WHOLE],
        (struct(quarter, BF16),) * 2,
        [fixed(quarter)] * 2,
        2 * rows * cols * width,
        light=True,
    )


def own_kernel(places, normed_ref, w_ref, *refs):
    out_ref = refs[-1]
    tall, width = out_ref.shape
    each = len(refs) // 2
    for p in range(2):
        rows = slice(p * tall, (p + 1) * tall)

        @pl.when(pl.program_id(0) == p)
        def _(p=p, rows=rows):
            total = dot(normed_ref[rows, :], columns(w_ref, places[0], width))
            for ref in refs[p * each : (p + 1) * each]:
                total = total + ref[...].astype(F32)
            out_ref[...] = total.astype(BF16)


def own_call(places, normed, first, second, w_out, width, height):
    rows, cols = normed.shape
    quarter = (rows // 2, width)
    return call(
        own_kernel,
        "own_block",
        2,
        places,
        (normed, w_out, *[a for a, _ in (*first, *second)]),
        [fixed((rows, cols)), WHOLE]
        + [pl.BlockSpec(quarter, lambda i, o, at=at: (at, 0)) for _, at in (*first, *second)],
        (struct((rows * height, width), BF16),),
        [pl.BlockSpec(quarter, lambda i, o: (i, 0))],
        2 * rows * cols * width,
        light=True,
    )[0]


def last_kernel(_, kept_ref, a_ref, b_ref, above_ref, out_ref):
    del above_ref

    @pl.when(pl.program_id(0) == 0)
    def _():
        out_ref[...] = (kept_ref[...].astype(F32) + a_ref[...].astype(F32)).astype(BF16)

    @pl.when(pl.program_id(0) == 1)
    def _():
        out_ref[...] = (kept_ref[...].astype(F32) + b_ref[...].astype(F32)).astype(BF16)


def last_call(kept, a, b, above):
    tall, width = a.shape
    return call(
        last_kernel,
        "last_add",
        2,
        jnp.zeros((1,), jnp.int32),
        (kept, a, b, above),
        [
            pl.BlockSpec((tall, width), lambda j, o: (j, 0)),
            fixed((tall, width)),
            fixed((tall, width)),
            pl.BlockSpec(memory_space=pl.ANY),
        ],
        (struct(above.shape, BF16),),
        [pl.BlockSpec((tall, width), lambda j, o: (2 + j, 0))],
        tall * width,
        aliases={4: 0},
    )[0]


def local(n_head, n_seq, tokens, w_qkv, w_out, decay_rate, prior_state):
    rows, width = tokens.shape
    heads, size = prior_state.shape[0], prior_state.shape[1]
    square = n_head == 4
    place = lax.axis_index("head").astype(jnp.int32)
    quarter = rows // 4
    group = 2 if heads % 2 == 0 else 1
    cols = group * size

    over_x = functools.partial(lax.ppermute, axis_name="head", perm=[(i, i ^ 1) for i in range(n_head)])
    over_y = functools.partial(lax.ppermute, axis_name="head", perm=[(i, i ^ 2) for i in range(n_head)])

    pos = lax.axis_index("seq").astype(jnp.int32)
    core, chip = pos % 2, pos // 2
    flips = (0, 1, 2, 3) if square else (0, 0, 0, 0)
    places = jnp.stack([*[place ^ f for f in flips], core, chip])

    along, inside, down, tail, to_end, half_fade = decay_call(decay_rate, quarter)
    n_chips = n_seq // 2
    swap = functools.partial(lax.ppermute, axis_name="seq", perm=[(i, i ^ 1) for i in range(n_seq)])

    def hop(x, *pairs):
        perm = [(2 * a + c, 2 * b + c) for a, b in pairs for c in range(2)]
        return lax.ppermute(x, "seq", perm=perm)

    def chip_tails(tail):
        other = swap(tail)
        return other, tail + other, hop(tail + other, (2, 3)) if n_chips == 4 else None

    if square:
        tokens = stay(tokens)
        q0, q1 = cut_call(tokens, 0, 1)
        x0, y1 = over_x(q0), over_y(q1)
        x1, y0 = over_x(after(q1, tail)), over_y(after(q0, tail))
        acc = own_part_call(places, tokens, w_qkv, cols)
        q2, q3 = cut_call(stay(after(tokens, acc, x0, y1)), 1, 10**10)
        fy0, fx1 = over_y(x0), over_x(y1)
        tail_other, tail_chip, tail_below = chip_tails(after(tail, acc, x0, y1))
        x2 = over_x(after(q2, x1, y0, tail_chip))
        y3 = over_y(after(q3, x1, y0, tail_chip))
        acc_a = part_call(
            places,
            (1, 2),
            [(x0, x1), (y0, y1)],
            w_qkv,
            2 * quarter,
            cols,
            before=stay(after(acc, tail_chip)),
            at=0,
        )
        earlier = (fy0, fx1, acc_a) if tail_below is None else (fy0, fx1, acc_a, tail_below)
        x3, y2 = over_x(after(q3, *earlier)), over_y(after(q2, *earlier))
        query_a, within_a, state = first_call(
            places,
            (3,),
            [(fy0, fx1)],
            (acc_a,),
            w_qkv,
            along,
            inside,
            2 * quarter,
            quarter,
            size,
            group,
        )
        fy2, fx3 = over_y(after(x2, state)), over_x(after(y3, state))
        acc_q, acc_kv = part_call(
            places,
            (1, 2),
            [(x2, x3), (y2, y3)],
            w_qkv,
            2 * quarter,
            cols,
            before=stay(acc),
            at=1,
            apart=True,
        )
        far = (fy2, fx3)
        middle = state
        k, v, state, sent = state_call(
            places, far, w_qkv, acc_kv, to_end, half_fade, middle, group
        )
    else:
        tail_other, tail_chip, tail_below = chip_tails(tail)
        gathered = lax.all_gather(tokens, "head", axis=1, tiled=True)
        query, within, state = first_call(
            places, (), [(gathered,)], (), w_qkv, along, inside, rows, quarter, size, group
        )

    tails = (tail, tail_other)
    if square and n_chips == 4:
        leaving, chip_state, first = chip_call(places, state, near(swap(sent)), tails, prior_state)
        arriving = near(hop(leaving, (0, 1), (2, 3)))
        leaving = pass_call(places, arriving, chip_state, tails)
        to_third, to_second = near(hop(leaving, (1, 3))), near(hop(leaving, (1, 2)))
        here, passed = enter_call(
            places, arriving, to_second, to_third, first, tails, tail_below, prior_state
        )
    else:
        share = heads // 2

        def mine(x, core=core):
            return lax.dynamic_slice_in_dim(x, core * share, share, 0)

        def decay(tail):
            return jnp.exp(-mine(tail)[:, :1, None])

        ours = mine(state)
        other = swap(mine(state, 1 - core).astype(BF16)).astype(F32)
        first = jnp.where(core == 0, ours, other)
        second = jnp.where(core == 0, other, ours)
        chip_state = decay(jnp.where(core == 0, tail_other, tail)) * first + second
        chip_entering = mine(prior_state)
        for step in range(n_chips - 1):
            leaving = (decay(tail_chip) * chip_entering + chip_state).astype(BF16)
            arriving = hop(leaving, (step, step + 1))
            chip_entering = jnp.where(chip == step + 1, arriving.astype(F32), chip_entering)
        other = decay(jnp.where(core == 0, tail, tail_other)) * chip_entering + first
        here = jnp.where(core == 0, chip_entering, other).astype(BF16)
        passed = jnp.where(core == 0, other, chip_entering).astype(BF16)
    entering = (here, swap(passed))

    w_whole, w_out = w_out, near(w_out)
    if not square:
        halves = [
            head_call(
                places,
                (0, 0, 0),
                query[r * rows // 2 : (r + 1) * rows // 2],
                within[r * rows // 2 : (r + 1) * rows // 2],
                entering,
                w_out,
                width,
            )[0]
            for r in range(2)
        ]
        partial = dot(jnp.concatenate(halves), w_whole).astype(BF16)
        return lax.psum_scatter(partial, "head", scatter_dimension=1, tiled=True)

    na, by_x, by_y = head_call(
        places, (3, 1, 2), stay(query_a), stay(within_a), entering, w_out, width
    )
    middle = stay(after(middle, na))
    by_x, by_y = over_x(by_x), over_y(by_y)
    query_b, within_b = later_call(
        places, far, w_qkv, stay(acc_q), stay(k), stay(v), along, inside, down, middle, quarter, group
    )
    nb, by_x2, by_y2 = head_call(
        places, (3, 1, 2), query_b, within_b, entering, w_out, width
    )
    by_x2, by_y2 = over_x(by_x2), over_y(by_y2)
    sum1, sum0 = pair_call(places, after(na, nb), by_y, by_x, w_out, width)
    by_x2, by_y2 = after(by_x2, sum1), after(by_y2, sum1)
    sum1, sum0 = over_x(sum1), over_y(sum0)
    sum3, sum2 = pair_call(places, nb, by_y2, by_x2, w_out, width)
    sum3, sum2 = over_x(sum3), over_y(sum2)
    below = own_call(places, after(nb, sum1, sum0), ((by_x2, 1),), ((by_y2, 1),), w_out, width, 1)
    above = own_call(
        places, na, ((by_x, 1), (sum0, 0)), ((by_y, 1), (sum1, 0)), w_out, width, 2
    )
    return last_call(below, sum2, sum3, above)


def solution(mesh):
    in_specs = (
        P("seq", "head"),
        P(None, None, "head"),
        P("head", None),
        P("head", "seq"),
        P("head", None, None),
    )
    body = functools.partial(local, mesh.shape["head"], mesh.shape["seq"])
    return jax.shard_map(
        body, mesh=mesh, in_specs=in_specs, out_specs=P("seq", "head"), check_vma=False
    )
```

```python
import functools
import math

import jax
import jax.numpy as jnp
from jax import lax
from jax.experimental import pallas as pl
from jax.experimental.pallas import tpu as pltpu
from jax.sharding import PartitionSpec as P

BF16, F32 = jnp.bfloat16, jnp.float32
MIB = 1024 * 1024


def dot(a, b, contract=((1,), (0,))):
    return lax.dot_general(a, b, (contract, ((), ())), preferred_element_type=F32)


def after(x, *earlier):
    return lax.optimization_barrier((x, *earlier))[0]


def struct(shape, dtype):
    return jax.ShapeDtypeStruct(shape, dtype)


def stay(x):
    return pltpu.with_memory_space_constraint(x, pltpu.HBM)


def near(x):
    return pltpu.with_memory_space_constraint(x, pltpu.VMEM)


def fixed(shape):
    return pl.BlockSpec(shape, lambda j, o: (0,) * len(shape))


def call(kernel, name, steps, scalars, ins, in_specs, outs, out_specs, flops, scratch=(), aliases=None, light=False):
    moved = sum(a.size * a.dtype.itemsize for a in ins) + sum(
        math.prod(o.shape) * jnp.dtype(o.dtype).itemsize for o in outs
    )
    return pl.pallas_call(
        kernel,
        out_shape=tuple(outs),
        grid_spec=pltpu.PrefetchScalarGridSpec(
            num_scalar_prefetch=1,
            grid=(steps,),
            in_specs=in_specs,
            out_specs=out_specs,
            scratch_shapes=list(scratch),
        ),
        input_output_aliases=aliases or {},
        compiler_params=pltpu.CompilerParams(vmem_limit_bytes=(24 if light else 32) * MIB),
        cost_estimate=pl.CostEstimate(
            flops=1 if light else flops, bytes_accessed=1 if light else moved, transcendentals=0
        ),
        name=name,
    )(scalars, *ins)


def cut_kernel(_, x_ref, a_ref, b_ref):
    tall = a_ref.shape[0]
    a_ref[...] = x_ref[:tall, :]
    b_ref[...] = x_ref[tall:, :]


def cut_call(x, half, cost):
    rows, width = x.shape
    quarter = (rows // 4, width)
    return call(
        cut_kernel,
        "cut",
        1,
        jnp.zeros((1,), jnp.int32),
        (x,),
        [pl.BlockSpec((rows // 2, width), lambda j, o: (half, 0))],
        (struct(quarter, x.dtype),) * 2,
        [fixed(quarter)] * 2,
        cost,
    )


def decay_kernel(chunk, _, rate_ref, along_ref, inside_ref, down_ref, tail_ref, end_ref, half_ref):
    heads, rows = rate_ref.shape
    lane = lax.broadcasted_iota(jnp.int32, (heads, chunk), 1)
    base = jnp.zeros((heads, 1), F32)
    insides, wholes = [], []
    for c in range(rows // chunk):
        x = rate_ref[:, c * chunk : (c + 1) * chunk]
        step = 1
        while step < chunk:
            x = x + jnp.where(lane >= step, pltpu.roll(x, step, 1), 0.0)
            step *= 2
        insides.append(x)
        wholes.append(x + base)
        base = base + x[:, chunk - 1 :]
    inside, whole = jnp.concatenate(insides, axis=1), jnp.concatenate(wholes, axis=1)
    along_ref[...] = inside
    inside_ref[...] = inside.T
    down_ref[...] = whole.T
    tail_ref[...] = jnp.broadcast_to(base, tail_ref.shape)
    end_ref[...] = jnp.exp(whole - base)
    half_ref[...] = jnp.broadcast_to(jnp.exp(whole[:, rows // 2 - 1 : rows // 2] - base), half_ref.shape)


def decay_call(rate, chunk):
    heads, rows = rate.shape
    return call(
        functools.partial(decay_kernel, chunk),
        "decay",
        1,
        jnp.zeros((1,), jnp.int32),
        (rate,),
        [fixed((heads, rows))],
        (
            struct((heads, rows), F32),
            struct((rows, heads), F32),
            struct((rows, heads), F32),
            struct((heads, 128), F32),
            struct((heads, rows), F32),
            struct((heads, 128), F32),
        ),
        [
            fixed((heads, rows)),
            fixed((rows, heads)),
            fixed((rows, heads)),
            fixed((heads, 128)),
            fixed((heads, rows)),
            fixed((heads, 128)),
        ],
        heads * rows * 16,
    )


def column(table, head):
    lane = lax.broadcasted_iota(jnp.int32, table.shape, 1)
    return jnp.sum(jnp.where(lane == head, table, 0.0), axis=1, keepdims=True)


def scores(q, k, v, along, down, state):
    rows = q.shape[0]
    causal = lax.broadcasted_iota(jnp.int32, (rows, rows), 0) >= lax.broadcasted_iota(
        jnp.int32, (rows, rows), 1
    )
    decay = jnp.exp(jnp.minimum(along - down, 0.0))
    weights = jnp.where(causal, dot(q, k, ((1,), (1,))) * decay, 0.0).astype(BF16)
    return dot(weights, v) + dot(q, state.astype(BF16)) * jnp.exp(-down)


def faded(q, down):
    return (q.astype(F32) * jnp.exp(-down)).astype(BF16)


def advance(k, v, down, state):
    last = down[down.shape[0] - 1 :, :]
    scaled = (k.astype(F32) * jnp.exp(down - last)).astype(BF16)
    return jnp.exp(-last) * state + dot(scaled, v, ((0,), (0,)))


def first_kernel(layout, added, chunk, group, size, _, *refs):
    count = sum(layout)
    x_refs, w_refs, refs = refs[:count], refs[count : count + len(layout)], refs[count + len(layout) :]
    along_ref, inside_ref, q_ref, within_ref, state_ref, held = refs[-6:]
    j = pl.program_id(0)
    rows = held.shape[1]

    @pl.when(j == 0)
    def _():
        at = 0
        for i, parts in enumerate(layout):
            tall = rows // parts
            for p in range(parts):
                held[i, p * tall : (p + 1) * tall, :] = x_refs[at][...]
                at += 1

    def project(c):
        total = dot(held[0], w_refs[0][c])
        for i in range(1, len(layout)):
            total = total + dot(held[i], w_refs[i][c])
        if added:
            total = total + refs[0][c]
        return total.astype(BF16)

    q_all, k_all, v_all = project(0), project(1), project(2)
    for a in range(group):
        head = j * group + a
        lanes = slice(a * size, (a + 1) * size)
        state, base = jnp.zeros((size, size), F32), jnp.zeros((1, 1), F32)
        for c in range(rows // chunk):
            here = slice(c * chunk, (c + 1) * chunk)
            q, k, v = q_all[here, lanes], k_all[here, lanes], v_all[here, lanes]
            down = column(inside_ref[here, :], head)
            along = along_ref[pl.ds(head, 1), here]
            q_ref[here, lanes] = faded(q, base + down)
            within_ref[here, lanes] = scores(q, k, v, along, down, state).astype(BF16)
            state, base = advance(k, v, down, state), base + down[chunk - 1 :, :]
        state_ref[a] = state


def first_call(places, blocks, pieces, before, w_qkv, along, inside, rows, chunk, size, group):
    heads = along.shape[0]
    cols = group * size
    flat = [p for piece in pieces for p in piece]
    depth = flat[0].shape[1]

    def block(i):
        return pl.BlockSpec((3, depth, cols), lambda j, o: (0, o[blocks[i]] if blocks else 0, j))

    wide = pl.BlockSpec((rows, cols), lambda j, o: (0, j))
    return call(
        functools.partial(
            first_kernel, tuple(len(p) for p in pieces), bool(before), chunk, group, size
        ),
        "first",
        heads // group,
        places,
        (*flat, *[w_qkv] * len(pieces), *before, along, inside),
        [
            pl.BlockSpec((rows // len(piece), depth), lambda j, o: (0, 0))
            for piece in pieces
            for _ in piece
        ]
        + [block(i) for i in range(len(pieces))]
        + [pl.BlockSpec((3, rows, cols), lambda j, o: (0, 0, j)) for _ in before]
        + [fixed((heads, rows)), fixed((rows, heads))],
        (
            pltpu.HBM((rows, heads * size), BF16),
            pltpu.HBM((rows, heads * size), BF16),
            struct((heads, size, size), F32),
        ),
        [wide, wide, pl.BlockSpec((group, size, size), lambda j, o: (j, 0, 0))],
        2 * rows * 3 * heads * size * depth * len(pieces),
        scratch=[pltpu.VMEM((len(pieces), rows, depth), BF16)],
    )


def own_part_kernel(_, x_ref, w_ref, out_ref):
    for c in range(3):
        out_ref[c] = dot(x_ref[...], w_ref[c])


def own_part_call(places, tokens, w_qkv, cols):
    rows, depth = tokens.shape
    width = w_qkv.shape[2]
    return call(
        own_part_kernel,
        "own_part",
        width // cols,
        places,
        (tokens, w_qkv),
        [fixed((rows, depth)), pl.BlockSpec((3, depth, cols), lambda j, o: (0, o[0], j))],
        (pltpu.HBM((3, rows, width), F32),),
        [pl.BlockSpec((3, rows, cols), lambda j, o: (0, 0, j))],
        2 * rows * depth * width * 3,
    )[0]


def part_kernel(layout, outs, _, *refs):
    count = sum(layout)
    x_refs, w_refs = refs[:count], refs[count : count + len(layout)]
    before_ref, out_refs, held = refs[-2 - outs], refs[-1 - outs : -1], refs[-1]
    targets = [(ref, c) for ref in out_refs for c in range(ref.shape[0])]
    rows = held.shape[1]

    @pl.when(pl.program_id(0) == 0)
    def _():
        at = 0
        for i, parts in enumerate(layout):
            tall = rows // parts
            for p in range(parts):
                held[i, p * tall : (p + 1) * tall, :] = x_refs[at][...]
                at += 1

    for c in range(3):
        total = dot(held[0], w_refs[0][c])
        for i in range(1, len(layout)):
            total = total + dot(held[i], w_refs[i][c])
        ref, at = targets[c]
        ref[at] = total + before_ref[c]


def part_call(places, blocks, pieces, w_qkv, rows, cols, before, at, apart=False):
    flat = [p for piece in pieces for p in piece]
    depth = flat[0].shape[1]
    width = w_qkv.shape[2]

    def block(i):
        return pl.BlockSpec((3, depth, cols), lambda j, o: (0, o[blocks[i]], j))

    ins = [*flat, *[w_qkv] * len(pieces)]
    specs = [
        pl.BlockSpec((rows // len(piece), depth), lambda j, o: (0, 0)) for piece in pieces for _ in piece
    ] + [block(i) for i in range(len(pieces))]
    ins.append(before)
    specs.append(pl.BlockSpec((3, rows, cols), lambda j, o: (0, at, j)))
    outs = [struct((3, rows, width), F32)]
    if apart:
        outs = [pltpu.HBM((1, rows, width), F32), struct((2, rows, width), F32)]
    out = call(
        functools.partial(part_kernel, tuple(len(p) for p in pieces), len(outs)),
        "part",
        width // cols,
        places,
        ins,
        specs,
        outs,
        [pl.BlockSpec((o.shape[0], rows, cols), lambda j, o: (0, 0, j)) for o in outs],
        2 * rows * depth * len(pieces) * width * 3,
        scratch=[pltpu.VMEM((len(pieces), rows, depth), BF16)],
    )
    return out if apart else out[0]


def state_kernel(group, size, places, *refs):
    xa, xb, wk, wv, acc_k, acc_v, end_ref, half_ref, state_ref = refs[:9]
    k_ref, v_ref, out_ref, sent_ref, held = refs[9:]
    j = pl.program_id(0)
    rows = held.shape[0]

    @pl.when(j == 0)
    def _():
        held[: rows // 2, :] = xa[...]
        held[rows // 2 :, :] = xb[...]

    k_all = (acc_k[0] + dot(held[...], wk[0])).astype(BF16)
    v_all = (acc_v[0] + dot(held[...], wv[0])).astype(BF16)
    k_ref[...] = k_all
    v_ref[...] = v_all
    ends = []
    for a in range(group):
        head = pl.ds(j * group + a, 1)
        lanes = slice(a * size, (a + 1) * size)
        scaled = (k_all[:, lanes].T.astype(F32) * end_ref[head, :]).astype(BF16)
        end = half_ref[head, :] * state_ref[a] + dot(scaled, v_all[:, lanes])
        out_ref[a] = end
        ends.append(end.astype(BF16))
    half = pl.num_programs(0) // 2

    @pl.when(jnp.where(places[4] == 0, j >= half, j < half))
    def _():
        for a in range(group):
            sent_ref[a] = ends[a]


def state_call(places, far, w_qkv, acc, to_end, half_fade, state, group):
    _, rows, width = acc.shape
    heads, size = state.shape[0], state.shape[1]
    depth = far[0].shape[1]
    cols = group * size
    wide = pl.BlockSpec((rows, cols), lambda j, o: (0, j))
    small = pl.BlockSpec((group, size, size), lambda j, o: (j, 0, 0))
    half = heads // group // 2

    def sent_block(j, o):
        return jnp.where(o[4] == 0, jnp.maximum(j - half, 0), jnp.minimum(j, half - 1)), 0, 0

    return call(
        functools.partial(state_kernel, group, size),
        "states",
        heads // group,
        places,
        (*far, w_qkv, w_qkv, acc, acc, to_end, half_fade, state),
        [fixed(far[0].shape), fixed(far[1].shape)]
        + [pl.BlockSpec((1, depth, cols), lambda j, o, c=c: (c, o[3], j)) for c in (1, 2)]
        + [pl.BlockSpec((1, rows, cols), lambda j, o, c=c: (c, 0, j)) for c in (0, 1)]
        + [pl.BlockSpec((heads, rows), lambda j, o: (0, 1)), fixed(half_fade.shape), small],
        (
            pltpu.HBM((rows, width), BF16),
            pltpu.HBM((rows, width), BF16),
            struct(state.shape, F32),
            struct((heads // 2, size, size), BF16),
        ),
        [wide, wide, small, pl.BlockSpec((group, size, size), sent_block)],
        4 * rows * depth * width,
        scratch=[pltpu.VMEM((rows, depth), BF16)],
    )


def later_kernel(first, chunk, group, size, _, *refs):
    xa, xb, wq, acc_q, k_ref, v_ref, along_ref, inside_ref, down_ref, state_ref = refs[:10]
    q_ref, within_ref, held = refs[10:]
    j = pl.program_id(0)
    rows = held.shape[0]

    @pl.when(j == 0)
    def _():
        held[: rows // 2, :] = xa[...]
        held[rows // 2 :, :] = xb[...]

    q_all = (acc_q[0] + dot(held[...], wq[0])).astype(BF16)
    for a in range(group):
        head = (first + j) * group + a
        lanes = slice(a * size, (a + 1) * size)
        state = state_ref[a]
        for c in range(rows // chunk):
            here = slice(c * chunk, (c + 1) * chunk)
            q, k, v = q_all[here, lanes], k_ref[here, lanes], v_ref[here, lanes]
            along, down = along_ref[pl.ds(head, 1), here], column(inside_ref[here, :], head)
            q_ref[here, lanes] = faded(q, column(down_ref[here, :], head))
            within_ref[here, lanes] = scores(q, k, v, along, down, state).astype(BF16)
            if c + 1 < rows // chunk:
                state = advance(k, v, down, state)


def later_call(places, far, w_qkv, acc, k, v, along, inside, down, state, chunk, group, half):
    _, rows, width = acc.shape
    heads, size = state.shape[0], state.shape[1]
    depth = far[0].shape[1]
    cols = group * size
    steps = heads // group // 2
    first = half * steps
    wide = pl.BlockSpec((rows, cols), lambda j, o: (0, first + j))
    out = pl.BlockSpec((rows, cols), lambda j, o: (0, j))
    return call(
        functools.partial(later_kernel, first, chunk, group, size),
        "later",
        steps,
        places,
        (*far, w_qkv, acc, k, v, along, inside, down, state),
        [
            fixed(far[0].shape),
            fixed(far[1].shape),
            pl.BlockSpec((1, depth, cols), lambda j, o: (0, o[3], first + j)),
            pl.BlockSpec((1, rows, cols), lambda j, o: (0, 0, first + j)),
            wide,
            wide,
            pl.BlockSpec((heads, rows), lambda j, o: (0, 1)),
            pl.BlockSpec((rows, heads), lambda j, o: (1, 0)),
            pl.BlockSpec((rows, heads), lambda j, o: (1, 0)),
            pl.BlockSpec((group, size, size), lambda j, o: (first + j, 0, 0)),
        ],
        (struct((rows, width // 2), BF16), struct((rows, width // 2), BF16)),
        [out, out],
        rows * depth * width + 2 * rows * (chunk + size) * width,
        scratch=[pltpu.VMEM((rows, depth), BF16)],
    )


def fades(tail_ref, other_ref, place, head):
    own, other = tail_ref[pl.ds(head, 1), :], other_ref[pl.ds(head, 1), :]
    first = jnp.where(place == 0, own, other)
    return jnp.exp(-first), jnp.exp(first - (own + other)), jnp.exp(-(own + other))


def chip_kernel(places, state_ref, come_ref, tail_ref, other_ref, prior_ref, *out_refs):
    leaving_ref, chip_ref, first_ref = out_refs
    core, chip = places[4], places[5]
    share = come_ref.shape[0]
    for i in range(share):
        head = core * share + i
        _, second_fade, fade = fades(tail_ref, other_ref, core, head)
        ours, come = state_ref[head], come_ref[i].astype(F32)
        first, second = jnp.where(core == 0, ours, come), jnp.where(core == 0, come, ours)
        total = second_fade * first + second
        first_ref[i] = first
        chip_ref[i] = total
        leaving_ref[i] = jnp.where(chip == 2, total, fade * prior_ref[head] + total).astype(BF16)


def pass_kernel(places, come_ref, chip_ref, tail_ref, other_ref, leaving_ref):
    share = come_ref.shape[0]
    for i in range(share):
        fade = fades(tail_ref, other_ref, places[4], places[4] * share + i)[2]
        leaving_ref[i] = (fade * come_ref[i].astype(F32) + chip_ref[i]).astype(BF16)


def enter_kernel(
    places, come_ref, second_ref, third_ref, first_ref, tail_ref, other_ref, below_ref, prior_ref, *out_refs
):
    here_ref, passed_ref = out_refs
    core, chip = places[4], places[5]
    share = come_ref.shape[0]
    for i in range(share):
        head = core * share + i
        come = come_ref[i].astype(F32)
        below = jnp.exp(-below_ref[pl.ds(head, 1), :])
        state = jnp.where(chip == 0, prior_ref[head], come)
        state = jnp.where(chip == 2, second_ref[i].astype(F32), state)
        state = jnp.where(chip == 3, below * third_ref[i].astype(F32) + come, state)
        later = fades(tail_ref, other_ref, core, head)[0] * state + first_ref[i]
        here_ref[i] = jnp.where(core == 0, state, later).astype(BF16)
        passed_ref[i] = jnp.where(core == 0, later, state).astype(BF16)


def small_call(kernel, name, places, ins, outs):
    whole = pl.BlockSpec(memory_space=pltpu.VMEM)
    return pl.pallas_call(
        kernel,
        out_shape=tuple(outs),
        in_specs=[pl.BlockSpec(memory_space=pltpu.SMEM)] + [whole] * len(ins),
        out_specs=[whole] * len(outs),
        compiler_params=pltpu.CompilerParams(vmem_limit_bytes=4 * MIB),
        cost_estimate=pl.CostEstimate(flops=1, bytes_accessed=1, transcendentals=0),
        name=name,
    )(places, *ins)


def chip_call(places, state, come, tails, prior):
    outs = (struct(come.shape, BF16), struct(come.shape, F32), struct(come.shape, F32))
    return small_call(chip_kernel, "chip_state", places, (state, come, *tails, prior), outs)


def pass_call(places, come, chip_state, tails):
    outs = (struct(come.shape, BF16),)
    return small_call(pass_kernel, "pass_on", places, (come, chip_state, *tails), outs)[0]


def enter_call(places, come, second, third, first, tails, below, prior):
    outs = (struct(come.shape, BF16),) * 2
    ins = (come, second, third, first, *tails, below, prior)
    return small_call(enter_kernel, "enter", places, ins, outs)


def columns(w_ref, block, width):
    return w_ref[:, pl.ds(pl.multiple_of(block * width, width), width)]


WHOLE = pl.BlockSpec(memory_space=pltpu.VMEM)


def head_kernel(count, blocks, places, *refs):
    q_refs, within_refs, refs = refs[:count], refs[count : 2 * count], refs[2 * count :]
    here_ref, there_ref, w_ref, normed_ref = refs[:4]
    out_refs, held = refs[4:6], refs[6]
    share, size = here_ref.shape[0], here_ref.shape[1]
    tall, width = out_refs[0].shape
    step = pl.program_id(0)
    for p, out_ref in enumerate(out_refs):

        @pl.when(step == p)
        def _(p=p, out_ref=out_ref):
            ones = jnp.ones((size, size), BF16)
            for a in range(2 * share):
                part, at = divmod(a, 2 * share // count)
                here = slice(at * size, (at + 1) * size)
                ours = places[4] == a // share
                entering = jnp.where(ours, here_ref[a % share], there_ref[a % share])
                seen = dot(q_refs[part][:, here], entering)
                combined = within_refs[part][:, here].astype(F32) + seen
                square = combined * combined
                high = square.astype(BF16)
                low = (square - high.astype(F32)).astype(BF16)
                power = (dot(high, ones) + dot(low, ones)) * (1.0 / size)
                lanes = slice(a * size, (a + 1) * size)
                held[p, :, lanes] = (combined * lax.rsqrt(power + 1e-06)).astype(BF16)
            normed_ref[...] = held[p]
            out_ref[...] = dot(held[p], columns(w_ref, places[blocks[0]], width)).astype(BF16)

        if len(blocks) > 1:

            @pl.when(step == 2 + p)
            def _(p=p, out_ref=out_ref):
                out_ref[...] = dot(held[p], columns(w_ref, places[blocks[1 + p]], width)).astype(BF16)


def head_call(places, blocks, q, within, entering, w_out, width):
    rows, cols = q[0].shape[0], w_out.shape[0]
    tall = rows // 2
    near = len(blocks) > 1
    part = pl.BlockSpec((tall, cols), lambda i, o: (jnp.minimum(i, 1), 0))
    some = pl.BlockSpec((tall, cols // len(q)), lambda i, o: (jnp.minimum(i, 1), 0))
    out = struct((rows if near else tall, width), BF16)
    return call(
        functools.partial(head_kernel, len(q), blocks),
        "heads",
        4 if near else 2,
        places,
        (*q, *within, *entering, w_out),
        [some] * (2 * len(q)) + [fixed(entering[0].shape), fixed(entering[1].shape), WHOLE],
        (struct((rows, cols), BF16), out, out),
        [
            part,
            pl.BlockSpec((tall, width), lambda i, o: (i // 2, 0)),
            pl.BlockSpec((tall, width), lambda i, o: (jnp.maximum(i - 2, 0), 0)),
        ],
        2 * rows * cols * (2 * width + 128),
        scratch=[pltpu.VMEM((2, tall, cols), BF16)],
        light=True,
    )


def mixed_kernel(places, normed_ref, x_ref, y_ref, w_ref, out_x_ref, out_y_ref):
    tall, width = x_ref.shape
    for p, (out_ref, come_ref) in enumerate(((out_x_ref, x_ref), (out_y_ref, y_ref))):

        @pl.when(pl.program_id(0) == p)
        def _(p=p, out_ref=out_ref, come_ref=come_ref):
            total = dot(normed_ref[...], columns(w_ref, places[1 + p], width))
            summed = total[(1 - p) * tall : (2 - p) * tall] + come_ref[...].astype(F32)
            out_ref[:tall, :] = summed.astype(BF16)
            out_ref[tall:, :] = total[p * tall : (p + 1) * tall].astype(BF16)


def mixed_call(places, normed, for_x, for_y, w_out, width):
    rows, cols = normed.shape
    quarter, half = (rows // 2, width), (rows, width)
    return call(
        mixed_kernel,
        "sum_and_near",
        2,
        places,
        (normed, for_x, for_y, w_out),
        [fixed((rows, cols)), fixed(quarter), fixed(quarter), WHOLE],
        (struct(half, BF16),) * 2,
        [fixed(half)] * 2,
        4 * rows * cols * width,
        light=True,
    )


def pair_kernel(places, normed_ref, x_ref, y_ref, w_ref, out_x_ref, out_y_ref):
    tall, width = out_x_ref.shape

    @pl.when(pl.program_id(0) == 0)
    def _():
        total = dot(normed_ref[tall:, :], columns(w_ref, places[1], width)) + x_ref[...].astype(F32)
        out_x_ref[...] = total.astype(BF16)

    @pl.when(pl.program_id(0) == 1)
    def _():
        total = dot(normed_ref[:tall, :], columns(w_ref, places[2], width)) + y_ref[...].astype(F32)
        out_y_ref[...] = total.astype(BF16)


def pair_call(places, normed, for_x, for_y, w_out, width):
    rows, cols = normed.shape
    quarter = (rows // 2, width)
    return call(
        pair_kernel,
        "sum_pair",
        2,
        places,
        (normed, for_x, for_y, w_out),
        [fixed((rows, cols)), fixed(quarter), fixed(quarter), WHOLE],
        (struct(quarter, BF16),) * 2,
        [fixed(quarter)] * 2,
        2 * rows * cols * width,
        light=True,
    )


def own_kernel(places, normed_ref, w_ref, *refs):
    out_ref = refs[-1]
    tall, width = out_ref.shape
    each = len(refs) // 2
    for p in range(2):
        rows = slice(p * tall, (p + 1) * tall)

        @pl.when(pl.program_id(0) == p)
        def _(p=p, rows=rows):
            total = dot(normed_ref[rows, :], columns(w_ref, places[0], width))
            for ref in refs[p * each : (p + 1) * each]:
                total = total + ref[...].astype(F32)
            out_ref[...] = total.astype(BF16)


def own_call(places, normed, first, second, w_out, width, height):
    rows, cols = normed.shape
    quarter = (rows // 2, width)
    return call(
        own_kernel,
        "own_block",
        2,
        places,
        (normed, w_out, *[a for a, _ in (*first, *second)]),
        [fixed((rows, cols)), WHOLE]
        + [pl.BlockSpec(quarter, lambda i, o, at=at: (at, 0)) for _, at in (*first, *second)],
        (struct((rows * height, width), BF16),),
        [pl.BlockSpec(quarter, lambda i, o: (i, 0))],
        2 * rows * cols * width,
        light=True,
    )[0]


def last_kernel(_, kept_ref, a_ref, b_ref, above_ref, out_ref):
    del above_ref

    @pl.when(pl.program_id(0) == 0)
    def _():
        out_ref[...] = (kept_ref[...].astype(F32) + a_ref[...].astype(F32)).astype(BF16)

    @pl.when(pl.program_id(0) == 1)
    def _():
        out_ref[...] = (kept_ref[...].astype(F32) + b_ref[...].astype(F32)).astype(BF16)


def last_call(kept, a, b, above):
    tall, width = a.shape
    return call(
        last_kernel,
        "last_add",
        2,
        jnp.zeros((1,), jnp.int32),
        (kept, a, b, above),
        [
            pl.BlockSpec((tall, width), lambda j, o: (j, 0)),
            fixed((tall, width)),
            fixed((tall, width)),
            pl.BlockSpec(memory_space=pl.ANY),
        ],
        (struct(above.shape, BF16),),
        [pl.BlockSpec((tall, width), lambda j, o: (2 + j, 0))],
        tall * width,
        aliases={4: 0},
    )[0]


def local(n_head, n_seq, tokens, w_qkv, w_out, decay_rate, prior_state):
    rows, width = tokens.shape
    heads, size = prior_state.shape[0], prior_state.shape[1]
    square = n_head == 4
    place = lax.axis_index("head").astype(jnp.int32)
    quarter = rows // 4
    group = 2 if heads % 2 == 0 else 1
    cols = group * size

    over_x = functools.partial(lax.ppermute, axis_name="head", perm=[(i, i ^ 1) for i in range(n_head)])
    over_y = functools.partial(lax.ppermute, axis_name="head", perm=[(i, i ^ 2) for i in range(n_head)])

    pos = lax.axis_index("seq").astype(jnp.int32)
    core, chip = pos % 2, pos // 2
    flips = (0, 1, 2, 3) if square else (0, 0, 0, 0)
    places = jnp.stack([*[place ^ f for f in flips], core, chip])

    along, inside, down, tail, to_end, half_fade = decay_call(decay_rate, quarter)
    n_chips = n_seq // 2
    swap = functools.partial(lax.ppermute, axis_name="seq", perm=[(i, i ^ 1) for i in range(n_seq)])

    def hop(x, *pairs):
        perm = [(2 * a + c, 2 * b + c) for a, b in pairs for c in range(2)]
        return lax.ppermute(x, "seq", perm=perm)

    def chip_tails(tail):
        other = swap(tail)
        return other, tail + other, hop(tail + other, (2, 3)) if n_chips == 4 else None

    if square:
        tokens = stay(tokens)
        q0, q1 = cut_call(tokens, 0, 1)
        x0, y1 = over_x(q0), over_y(q1)
        x1, y0 = over_x(after(q1, tail)), over_y(after(q0, tail))
        acc = own_part_call(places, tokens, w_qkv, cols)
        q2, q3 = cut_call(stay(after(tokens, acc, x0, y1)), 1, 10**10)
        fy0, fx1 = over_y(x0), over_x(y1)
        tail_other, tail_chip, tail_below = chip_tails(after(tail, acc, x0, y1))
        x2 = over_x(after(q2, x1, y0, tail_chip))
        y3 = over_y(after(q3, x1, y0, tail_chip))
        acc_a = part_call(
            places,
            (1, 2),
            [(x0, x1), (y0, y1)],
            w_qkv,
            2 * quarter,
            cols,
            before=stay(after(acc, tail_chip)),
            at=0,
        )
        earlier = (fy0, fx1, acc_a) if tail_below is None else (fy0, fx1, acc_a, tail_below)
        x3, y2 = over_x(after(q3, *earlier)), over_y(after(q2, *earlier))
        query_a, within_a, state = first_call(
            places,
            (3,),
            [(fy0, fx1)],
            (acc_a,),
            w_qkv,
            along,
            inside,
            2 * quarter,
            quarter,
            size,
            group,
        )
        fy2, fx3 = over_y(after(x2, state)), over_x(after(y3, state))
        acc_q, acc_kv = part_call(
            places,
            (1, 2),
            [(x2, x3), (y2, y3)],
            w_qkv,
            2 * quarter,
            cols,
            before=stay(acc),
            at=1,
            apart=True,
        )
        far = (fy2, fx3)
        middle = state
        k, v, state, sent = state_call(
            places, far, w_qkv, acc_kv, to_end, half_fade, middle, group
        )
    else:
        tail_other, tail_chip, tail_below = chip_tails(tail)
        gathered = lax.all_gather(tokens, "head", axis=1, tiled=True)
        query, within, state = first_call(
            places, (), [(gathered,)], (), w_qkv, along, inside, rows, quarter, size, group
        )

    tails = (tail, tail_other)

    def scores_of_later(half, *earlier):
        start = stay(after(middle, *earlier))
        ins = (far, w_qkv, stay(acc_q), stay(k), stay(v), along, inside, down, start)
        return later_call(places, *ins, quarter, group, half)

    if square and n_chips == 4:
        leaving, chip_state, first = chip_call(places, state, near(swap(sent)), tails, prior_state)
        arriving = hop(leaving, (0, 1), (2, 3))
        query_b, within_b = scores_of_later(0, leaving)
        arriving = near(after(arriving, query_b))
        leaving = pass_call(places, arriving, chip_state, tails)
        to_third, to_second = hop(leaving, (1, 3)), hop(leaving, (1, 2))
        query_c, within_c = scores_of_later(1, leaving)
        to_third, to_second, _ = lax.optimization_barrier((to_third, to_second, query_c))
        to_third, to_second = near(to_third), near(to_second)
        here, passed = enter_call(
            places, arriving, to_second, to_third, first, tails, tail_below, prior_state
        )
    else:
        share = heads // 2

        def mine(x, core=core):
            return lax.dynamic_slice_in_dim(x, core * share, share, 0)

        def decay(tail):
            return jnp.exp(-mine(tail)[:, :1, None])

        ours = mine(state)
        other = swap(mine(state, 1 - core).astype(BF16)).astype(F32)
        first = jnp.where(core == 0, ours, other)
        second = jnp.where(core == 0, other, ours)
        chip_state = decay(jnp.where(core == 0, tail_other, tail)) * first + second
        chip_entering = mine(prior_state)
        for step in range(n_chips - 1):
            leaving = (decay(tail_chip) * chip_entering + chip_state).astype(BF16)
            arriving = hop(leaving, (step, step + 1))
            chip_entering = jnp.where(chip == step + 1, arriving.astype(F32), chip_entering)
        other = decay(jnp.where(core == 0, tail, tail_other)) * chip_entering + first
        here = jnp.where(core == 0, chip_entering, other).astype(BF16)
        passed = jnp.where(core == 0, other, chip_entering).astype(BF16)
    entering = (here, swap(passed))

    w_whole, w_out = w_out, near(w_out)
    if not square:
        halves = [
            head_call(
                places,
                (0,),
                (query[r * rows // 2 : (r + 1) * rows // 2],),
                (within[r * rows // 2 : (r + 1) * rows // 2],),
                entering,
                w_out,
                width,
            )[0]
            for r in range(2)
        ]
        partial = dot(jnp.concatenate(halves), w_whole).astype(BF16)
        return lax.psum_scatter(partial, "head", scatter_dimension=1, tiled=True)

    if n_chips != 4:
        (query_b, within_b), (query_c, within_c) = scores_of_later(0), scores_of_later(1)
    na, far0, far1 = head_call(
        places, (3,), (stay(query_a),), (stay(within_a),), entering, w_out, width
    )
    query_b = after(query_b, na)
    far0, far1 = over_x(far0), over_y(far1)
    nb, by_x2, by_y2 = head_call(
        places, (3, 1, 2), (query_b, query_c), (within_b, within_c), entering, w_out, width
    )
    by_x2, by_y2 = over_x(by_x2), over_y(by_y2)
    by_x, by_y = mixed_call(places, after(na, nb), far1, far0, w_out, width)
    by_x2, by_y2 = after(by_x2, by_x), after(by_y2, by_x)
    by_x, by_y = over_x(by_x), over_y(by_y)
    sum3, sum2 = pair_call(places, nb, by_y2, by_x2, w_out, width)
    sum3, sum2 = over_x(sum3), over_y(sum2)
    below = own_call(places, after(nb, by_x, by_y), ((by_x2, 1),), ((by_y2, 1),), w_out, width, 1)
    above = own_call(places, na, ((by_x, 1), (by_y, 0)), ((by_y, 1), (by_x, 0)), w_out, width, 2)
    return last_call(below, sum2, sum3, above)


def solution(mesh):
    in_specs = (
        P("seq", "head"),
        P(None, None, "head"),
        P("head", None),
        P("head", "seq"),
        P("head", None, None),
    )
    body = functools.partial(local, mesh.shape["head"], mesh.shape["seq"])
    return jax.shard_map(
        body, mesh=mesh, in_specs=in_specs, out_specs=P("seq", "head"), check_vma=False
    )
```

```python
import functools
import math

import jax
import jax.numpy as jnp
from jax import lax
from jax.experimental import pallas as pl
from jax.experimental.pallas import tpu as pltpu
from jax.sharding import PartitionSpec as P

BF16, F32 = jnp.bfloat16, jnp.float32
MIB = 1024 * 1024


def dot(a, b, contract=((1,), (0,))):
    return lax.dot_general(a, b, (contract, ((), ())), preferred_element_type=F32)


def after(x, *earlier):
    return lax.optimization_barrier((x, *earlier))[0]


def struct(shape, dtype):
    return jax.ShapeDtypeStruct(shape, dtype)


def stay(x):
    return pltpu.with_memory_space_constraint(x, pltpu.HBM)


def near(x):
    return pltpu.with_memory_space_constraint(x, pltpu.VMEM)


def fixed(shape):
    return pl.BlockSpec(shape, lambda j, o: (0,) * len(shape))


def call(kernel, name, steps, scalars, ins, in_specs, outs, out_specs, flops, scratch=(), aliases=None, light=False):
    moved = sum(a.size * a.dtype.itemsize for a in ins) + sum(
        math.prod(o.shape) * jnp.dtype(o.dtype).itemsize for o in outs
    )
    return pl.pallas_call(
        kernel,
        out_shape=tuple(outs),
        grid_spec=pltpu.PrefetchScalarGridSpec(
            num_scalar_prefetch=1,
            grid=(steps,),
            in_specs=in_specs,
            out_specs=out_specs,
            scratch_shapes=list(scratch),
        ),
        input_output_aliases=aliases or {},
        compiler_params=pltpu.CompilerParams(vmem_limit_bytes=(24 if light else 32) * MIB),
        cost_estimate=pl.CostEstimate(
            flops=1 if light else flops, bytes_accessed=1 if light else moved, transcendentals=0
        ),
        name=name,
    )(scalars, *ins)


def cut_kernel(_, x_ref, a_ref, b_ref):
    tall = a_ref.shape[0]
    a_ref[...] = x_ref[:tall, :]
    b_ref[...] = x_ref[tall:, :]


def cut_call(x, half, cost):
    rows, width = x.shape
    quarter = (rows // 4, width)
    return call(
        cut_kernel,
        "cut",
        1,
        jnp.zeros((1,), jnp.int32),
        (x,),
        [pl.BlockSpec((rows // 2, width), lambda j, o: (half, 0))],
        (struct(quarter, x.dtype),) * 2,
        [fixed(quarter)] * 2,
        cost,
    )


def decay_kernel(chunk, _, rate_ref, along_ref, inside_ref, down_ref, tail_ref, end_ref, half_ref):
    heads, rows = rate_ref.shape
    lane = lax.broadcasted_iota(jnp.int32, (heads, chunk), 1)
    base = jnp.zeros((heads, 1), F32)
    insides, wholes = [], []
    for c in range(rows // chunk):
        x = rate_ref[:, c * chunk : (c + 1) * chunk]
        step = 1
        while step < chunk:
            x = x + jnp.where(lane >= step, pltpu.roll(x, step, 1), 0.0)
            step *= 2
        insides.append(x)
        wholes.append(x + base)
        base = base + x[:, chunk - 1 :]
    inside, whole = jnp.concatenate(insides, axis=1), jnp.concatenate(wholes, axis=1)
    along_ref[...] = inside
    inside_ref[...] = inside.T
    down_ref[...] = whole.T
    tail_ref[...] = jnp.broadcast_to(base, tail_ref.shape)
    end_ref[...] = jnp.exp(whole - base)
    half_ref[...] = jnp.broadcast_to(jnp.exp(whole[:, rows // 2 - 1 : rows // 2] - base), half_ref.shape)


def decay_call(rate, chunk):
    heads, rows = rate.shape
    return call(
        functools.partial(decay_kernel, chunk),
        "decay",
        1,
        jnp.zeros((1,), jnp.int32),
        (rate,),
        [fixed((heads, rows))],
        (
            struct((heads, rows), F32),
            struct((rows, heads), F32),
            struct((rows, heads), F32),
            struct((heads, 128), F32),
            struct((heads, rows), F32),
            struct((heads, 128), F32),
        ),
        [
            fixed((heads, rows)),
            fixed((rows, heads)),
            fixed((rows, heads)),
            fixed((heads, 128)),
            fixed((heads, rows)),
            fixed((heads, 128)),
        ],
        heads * rows * 16,
    )


def column(table, head):
    lane = lax.broadcasted_iota(jnp.int32, table.shape, 1)
    return jnp.sum(jnp.where(lane == head, table, 0.0), axis=1, keepdims=True)


def scores(q, k, v, along, down, state):
    rows = q.shape[0]
    causal = lax.broadcasted_iota(jnp.int32, (rows, rows), 0) >= lax.broadcasted_iota(
        jnp.int32, (rows, rows), 1
    )
    decay = jnp.exp(jnp.minimum(along - down, 0.0))
    weights = jnp.where(causal, dot(q, k, ((1,), (1,))) * decay, 0.0).astype(BF16)
    return dot(weights, v) + dot(q, state.astype(BF16)) * jnp.exp(-down)


def faded(q, down):
    return (q.astype(F32) * jnp.exp(-down)).astype(BF16)


def advance(k, v, down, state):
    last = down[down.shape[0] - 1 :, :]
    scaled = (k.astype(F32) * jnp.exp(down - last)).astype(BF16)
    return jnp.exp(-last) * state + dot(scaled, v, ((0,), (0,)))


def first_kernel(layout, added, chunk, group, size, _, *refs):
    count = sum(layout)
    x_refs, w_refs, refs = refs[:count], refs[count : count + len(layout)], refs[count + len(layout) :]
    along_ref, inside_ref, q_ref, within_ref, state_ref, held = refs[-6:]
    j = pl.program_id(0)
    rows = held.shape[1]

    @pl.when(j == 0)
    def _():
        at = 0
        for i, parts in enumerate(layout):
            tall = rows // parts
            for p in range(parts):
                held[i, p * tall : (p + 1) * tall, :] = x_refs[at][...]
                at += 1

    def project(c):
        total = dot(held[0], w_refs[0][c])
        for i in range(1, len(layout)):
            total = total + dot(held[i], w_refs[i][c])
        if added:
            total = total + refs[0][c]
        return total.astype(BF16)

    q_all, k_all, v_all = project(0), project(1), project(2)
    for a in range(group):
        head = j * group + a
        lanes = slice(a * size, (a + 1) * size)
        state, base = jnp.zeros((size, size), F32), jnp.zeros((1, 1), F32)
        for c in range(rows // chunk):
            here = slice(c * chunk, (c + 1) * chunk)
            q, k, v = q_all[here, lanes], k_all[here, lanes], v_all[here, lanes]
            down = column(inside_ref[here, :], head)
            along = along_ref[pl.ds(head, 1), here]
            q_ref[here, lanes] = faded(q, base + down)
            within_ref[here, lanes] = scores(q, k, v, along, down, state).astype(BF16)
            state, base = advance(k, v, down, state), base + down[chunk - 1 :, :]
        state_ref[a] = state


def first_call(places, blocks, pieces, before, w_qkv, along, inside, rows, chunk, size, group):
    heads = along.shape[0]
    cols = group * size
    flat = [p for piece in pieces for p in piece]
    depth = flat[0].shape[1]

    def block(i):
        return pl.BlockSpec((3, depth, cols), lambda j, o: (0, o[blocks[i]] if blocks else 0, j))

    wide = pl.BlockSpec((rows, cols), lambda j, o: (0, j))
    return call(
        functools.partial(
            first_kernel, tuple(len(p) for p in pieces), bool(before), chunk, group, size
        ),
        "first",
        heads // group,
        places,
        (*flat, *[w_qkv] * len(pieces), *before, along, inside),
        [
            pl.BlockSpec((rows // len(piece), depth), lambda j, o: (0, 0))
            for piece in pieces
            for _ in piece
        ]
        + [block(i) for i in range(len(pieces))]
        + [pl.BlockSpec((3, rows, cols), lambda j, o: (0, 0, j)) for _ in before]
        + [fixed((heads, rows)), fixed((rows, heads))],
        (
            pltpu.HBM((rows, heads * size), BF16),
            pltpu.HBM((rows, heads * size), BF16),
            struct((heads, size, size), F32),
        ),
        [wide, wide, pl.BlockSpec((group, size, size), lambda j, o: (j, 0, 0))],
        2 * rows * 3 * heads * size * depth * len(pieces),
        scratch=[pltpu.VMEM((len(pieces), rows, depth), BF16)],
    )


def own_part_kernel(_, x_ref, w_ref, out_ref):
    for c in range(3):
        out_ref[c] = dot(x_ref[...], w_ref[c])


def own_part_call(places, tokens, w_qkv, cols):
    rows, depth = tokens.shape
    width = w_qkv.shape[2]
    return call(
        own_part_kernel,
        "own_part",
        width // cols,
        places,
        (tokens, w_qkv),
        [fixed((rows, depth)), pl.BlockSpec((3, depth, cols), lambda j, o: (0, o[0], j))],
        (pltpu.HBM((3, rows, width), F32),),
        [pl.BlockSpec((3, rows, cols), lambda j, o: (0, 0, j))],
        2 * rows * depth * width * 3,
    )[0]


def part_kernel(layout, outs, _, *refs):
    count = sum(layout)
    x_refs, w_refs = refs[:count], refs[count : count + len(layout)]
    before_ref, out_refs, held = refs[-2 - outs], refs[-1 - outs : -1], refs[-1]
    targets = [(ref, c) for ref in out_refs for c in range(ref.shape[0])]
    rows = held.shape[1]

    @pl.when(pl.program_id(0) == 0)
    def _():
        at = 0
        for i, parts in enumerate(layout):
            tall = rows // parts
            for p in range(parts):
                held[i, p * tall : (p + 1) * tall, :] = x_refs[at][...]
                at += 1

    for c in range(3):
        total = dot(held[0], w_refs[0][c])
        for i in range(1, len(layout)):
            total = total + dot(held[i], w_refs[i][c])
        ref, at = targets[c]
        ref[at] = total + before_ref[c]


def part_call(places, blocks, pieces, w_qkv, rows, cols, before, at, apart=False):
    flat = [p for piece in pieces for p in piece]
    depth = flat[0].shape[1]
    width = w_qkv.shape[2]

    def block(i):
        return pl.BlockSpec((3, depth, cols), lambda j, o: (0, o[blocks[i]], j))

    ins = [*flat, *[w_qkv] * len(pieces)]
    specs = [
        pl.BlockSpec((rows // len(piece), depth), lambda j, o: (0, 0)) for piece in pieces for _ in piece
    ] + [block(i) for i in range(len(pieces))]
    ins.append(before)
    specs.append(pl.BlockSpec((3, rows, cols), lambda j, o: (0, at, j)))
    outs = [struct((3, rows, width), F32)]
    if apart:
        outs = [pltpu.HBM((1, rows, width), F32), struct((2, rows, width), F32)]
    out = call(
        functools.partial(part_kernel, tuple(len(p) for p in pieces), len(outs)),
        "part",
        width // cols,
        places,
        ins,
        specs,
        outs,
        [pl.BlockSpec((o.shape[0], rows, cols), lambda j, o: (0, 0, j)) for o in outs],
        2 * rows * depth * len(pieces) * width * 3,
        scratch=[pltpu.VMEM((len(pieces), rows, depth), BF16)],
    )
    return out if apart else out[0]


def state_kernel(group, size, places, *refs):
    xa, xb, wk, wv, acc_k, acc_v, end_ref, half_ref, state_ref = refs[:9]
    k_ref, v_ref, out_ref, sent_ref, held = refs[9:]
    j = pl.program_id(0)
    rows = held.shape[0]

    @pl.when(j == 0)
    def _():
        held[: rows // 2, :] = xa[...]
        held[rows // 2 :, :] = xb[...]

    k_all = (acc_k[0] + dot(held[...], wk[0])).astype(BF16)
    v_all = (acc_v[0] + dot(held[...], wv[0])).astype(BF16)
    k_ref[...] = k_all
    v_ref[...] = v_all
    ends = []
    for a in range(group):
        head = pl.ds(j * group + a, 1)
        lanes = slice(a * size, (a + 1) * size)
        scaled = (k_all[:, lanes].T.astype(F32) * end_ref[head, :]).astype(BF16)
        end = half_ref[head, :] * state_ref[a] + dot(scaled, v_all[:, lanes])
        out_ref[a] = end
        ends.append(end.astype(BF16))
    half = pl.num_programs(0) // 2

    @pl.when(jnp.where(places[4] == 0, j >= half, j < half))
    def _():
        for a in range(group):
            sent_ref[a] = ends[a]


def state_call(places, far, w_qkv, acc, to_end, half_fade, state, group):
    _, rows, width = acc.shape
    heads, size = state.shape[0], state.shape[1]
    depth = far[0].shape[1]
    cols = group * size
    wide = pl.BlockSpec((rows, cols), lambda j, o: (0, j))
    small = pl.BlockSpec((group, size, size), lambda j, o: (j, 0, 0))
    half = heads // group // 2

    def sent_block(j, o):
        return jnp.where(o[4] == 0, jnp.maximum(j - half, 0), jnp.minimum(j, half - 1)), 0, 0

    return call(
        functools.partial(state_kernel, group, size),
        "states",
        heads // group,
        places,
        (*far, w_qkv, w_qkv, acc, acc, to_end, half_fade, state),
        [fixed(far[0].shape), fixed(far[1].shape)]
        + [pl.BlockSpec((1, depth, cols), lambda j, o, c=c: (c, o[3], j)) for c in (1, 2)]
        + [pl.BlockSpec((1, rows, cols), lambda j, o, c=c: (c, 0, j)) for c in (0, 1)]
        + [pl.BlockSpec((heads, rows), lambda j, o: (0, 1)), fixed(half_fade.shape), small],
        (
            pltpu.HBM((rows, width), BF16),
            pltpu.HBM((rows, width), BF16),
            struct(state.shape, F32),
            struct((heads // 2, size, size), BF16),
        ),
        [wide, wide, small, pl.BlockSpec((group, size, size), sent_block)],
        4 * rows * depth * width,
        scratch=[pltpu.VMEM((rows, depth), BF16)],
    )


def later_kernel(first, chunk, group, size, _, *refs):
    xa, xb, wq, acc_q, k_ref, v_ref, along_ref, inside_ref, down_ref, state_ref = refs[:10]
    q_ref, within_ref, held = refs[10:]
    j = pl.program_id(0)
    rows = held.shape[0]

    @pl.when(j == 0)
    def _():
        held[: rows // 2, :] = xa[...]
        held[rows // 2 :, :] = xb[...]

    q_all = (acc_q[0] + dot(held[...], wq[0])).astype(BF16)
    for a in range(group):
        head = (first + j) * group + a
        lanes = slice(a * size, (a + 1) * size)
        state = state_ref[a]
        for c in range(rows // chunk):
            here = slice(c * chunk, (c + 1) * chunk)
            q, k, v = q_all[here, lanes], k_ref[here, lanes], v_ref[here, lanes]
            along, down = along_ref[pl.ds(head, 1), here], column(inside_ref[here, :], head)
            q_ref[here, lanes] = faded(q, column(down_ref[here, :], head))
            within_ref[here, lanes] = scores(q, k, v, along, down, state).astype(BF16)
            if c + 1 < rows // chunk:
                state = advance(k, v, down, state)


def later_call(places, far, w_qkv, acc, k, v, along, inside, down, state, chunk, group, half):
    _, rows, width = acc.shape
    heads, size = state.shape[0], state.shape[1]
    depth = far[0].shape[1]
    cols = group * size
    steps = heads // group // 2
    first = half * steps
    wide = pl.BlockSpec((rows, cols), lambda j, o: (0, first + j))
    out = pl.BlockSpec((rows, cols), lambda j, o: (0, j))
    return call(
        functools.partial(later_kernel, first, chunk, group, size),
        "later",
        steps,
        places,
        (*far, w_qkv, acc, k, v, along, inside, down, state),
        [
            fixed(far[0].shape),
            fixed(far[1].shape),
            pl.BlockSpec((1, depth, cols), lambda j, o: (0, o[3], first + j)),
            pl.BlockSpec((1, rows, cols), lambda j, o: (0, 0, first + j)),
            wide,
            wide,
            pl.BlockSpec((heads, rows), lambda j, o: (0, 1)),
            pl.BlockSpec((rows, heads), lambda j, o: (1, 0)),
            pl.BlockSpec((rows, heads), lambda j, o: (1, 0)),
            pl.BlockSpec((group, size, size), lambda j, o: (first + j, 0, 0)),
        ],
        (struct((rows, width // 2), BF16), struct((rows, width // 2), BF16)),
        [out, out],
        rows * depth * width + 2 * rows * (chunk + size) * width,
        scratch=[pltpu.VMEM((rows, depth), BF16)],
    )


def fades(tail_ref, other_ref, place, head):
    own, other = tail_ref[pl.ds(head, 1), :], other_ref[pl.ds(head, 1), :]
    first = jnp.where(place == 0, own, other)
    return jnp.exp(-first), jnp.exp(first - (own + other)), jnp.exp(-(own + other))


def chip_kernel(places, state_ref, come_ref, tail_ref, other_ref, prior_ref, *out_refs):
    leaving_ref, alone_ref, chip_ref, first_ref = out_refs
    core = places[4]
    share = come_ref.shape[0]
    for i in range(share):
        head = core * share + i
        _, second_fade, fade = fades(tail_ref, other_ref, core, head)
        ours, come = state_ref[head], come_ref[i].astype(F32)
        first, second = jnp.where(core == 0, ours, come), jnp.where(core == 0, come, ours)
        total = second_fade * first + second
        first_ref[i] = first
        chip_ref[i] = total
        alone_ref[i] = total.astype(BF16)
        leaving_ref[i] = (fade * prior_ref[head] + total).astype(BF16)


def pass_kernel(places, come_ref, chip_ref, tail_ref, other_ref, leaving_ref):
    share = come_ref.shape[0]
    for i in range(share):
        fade = fades(tail_ref, other_ref, places[4], places[4] * share + i)[2]
        leaving_ref[i] = (fade * come_ref[i].astype(F32) + chip_ref[i]).astype(BF16)


def enter_kernel(
    places, come_ref, alone_ref, second_ref, third_ref, first_ref, tail_ref, other_ref, below_ref, prior_ref, *out_refs
):
    here_ref, passed_ref = out_refs
    core, chip = places[4], places[5]
    share = come_ref.shape[0]
    for i in range(share):
        head = core * share + i
        below = jnp.exp(-below_ref[pl.ds(head, 1), :])
        through = below * third_ref[i].astype(F32) + alone_ref[i].astype(F32)
        state = jnp.where(chip == 0, prior_ref[head], come_ref[i].astype(F32))
        state = jnp.where(chip == 2, second_ref[i].astype(F32), state)
        state = jnp.where(chip == 3, through, state)
        later = fades(tail_ref, other_ref, core, head)[0] * state + first_ref[i]
        here_ref[i] = jnp.where(core == 0, state, later).astype(BF16)
        passed_ref[i] = jnp.where(core == 0, later, state).astype(BF16)


def small_call(kernel, name, places, ins, outs):
    whole = pl.BlockSpec(memory_space=pltpu.VMEM)
    return pl.pallas_call(
        kernel,
        out_shape=tuple(outs),
        in_specs=[pl.BlockSpec(memory_space=pltpu.SMEM)] + [whole] * len(ins),
        out_specs=[whole] * len(outs),
        compiler_params=pltpu.CompilerParams(vmem_limit_bytes=4 * MIB),
        cost_estimate=pl.CostEstimate(flops=1, bytes_accessed=1, transcendentals=0),
        name=name,
    )(places, *ins)


def chip_call(places, state, come, tails, prior):
    outs = [struct(come.shape, kind) for kind in (BF16, BF16, F32, F32)]
    return small_call(chip_kernel, "chip_state", places, (state, come, *tails, prior), outs)


def pass_call(places, come, chip_state, tails):
    outs = (struct(come.shape, BF16),)
    return small_call(pass_kernel, "pass_on", places, (come, chip_state, *tails), outs)[0]


def enter_call(places, come, alone, second, third, first, tails, below, prior):
    outs = (struct(come.shape, BF16),) * 2
    ins = (come, alone, second, third, first, *tails, below, prior)
    return small_call(enter_kernel, "enter", places, ins, outs)


def columns(w_ref, block, width):
    return w_ref[:, pl.ds(pl.multiple_of(block * width, width), width)]


WHOLE = pl.BlockSpec(memory_space=pltpu.VMEM)


def head_kernel(count, blocks, places, *refs):
    q_refs, within_refs, refs = refs[:count], refs[count : 2 * count], refs[2 * count :]
    here_ref, there_ref, w_ref, normed_ref = refs[:4]
    out_refs, held = refs[4:6], refs[6]
    share, size = here_ref.shape[0], here_ref.shape[1]
    tall, width = out_refs[0].shape
    step = pl.program_id(0)
    for p, out_ref in enumerate(out_refs):

        @pl.when(step == p)
        def _(p=p, out_ref=out_ref):
            ones = jnp.ones((size, size), BF16)
            for a in range(2 * share):
                part, at = divmod(a, 2 * share // count)
                here = slice(at * size, (at + 1) * size)
                ours = places[4] == a // share
                entering = jnp.where(ours, here_ref[a % share], there_ref[a % share])
                seen = dot(q_refs[part][:, here], entering)
                combined = within_refs[part][:, here].astype(F32) + seen
                square = combined * combined
                high = square.astype(BF16)
                low = (square - high.astype(F32)).astype(BF16)
                power = (dot(high, ones) + dot(low, ones)) * (1.0 / size)
                lanes = slice(a * size, (a + 1) * size)
                held[p, :, lanes] = (combined * lax.rsqrt(power + 1e-06)).astype(BF16)
            normed_ref[...] = held[p]
            out_ref[...] = dot(held[p], columns(w_ref, places[blocks[0]], width)).astype(BF16)

        if len(blocks) > 1:

            @pl.when(step == 2 + p)
            def _(p=p, out_ref=out_ref):
                out_ref[...] = dot(held[p], columns(w_ref, places[blocks[1 + p]], width)).astype(BF16)


def head_call(places, blocks, q, within, entering, w_out, width):
    rows, cols = q[0].shape[0], w_out.shape[0]
    tall = rows // 2
    near = len(blocks) > 1
    part = pl.BlockSpec((tall, cols), lambda i, o: (jnp.minimum(i, 1), 0))
    some = pl.BlockSpec((tall, cols // len(q)), lambda i, o: (jnp.minimum(i, 1), 0))
    out = struct((rows if near else tall, width), BF16)
    return call(
        functools.partial(head_kernel, len(q), blocks),
        "heads",
        4 if near else 2,
        places,
        (*q, *within, *entering, w_out),
        [some] * (2 * len(q)) + [fixed(entering[0].shape), fixed(entering[1].shape), WHOLE],
        (struct((rows, cols), BF16), out, out),
        [
            part,
            pl.BlockSpec((tall, width), lambda i, o: (i // 2, 0)),
            pl.BlockSpec((tall, width), lambda i, o: (jnp.maximum(i - 2, 0), 0)),
        ],
        2 * rows * cols * (2 * width + 128),
        scratch=[pltpu.VMEM((2, tall, cols), BF16)],
        light=True,
    )


def mixed_kernel(places, normed_ref, x_ref, y_ref, w_ref, out_x_ref, out_y_ref):
    tall, width = x_ref.shape
    for p, (out_ref, come_ref) in enumerate(((out_x_ref, x_ref), (out_y_ref, y_ref))):

        @pl.when(pl.program_id(0) == p)
        def _(p=p, out_ref=out_ref, come_ref=come_ref):
            total = dot(normed_ref[...], columns(w_ref, places[1 + p], width))
            summed = total[(1 - p) * tall : (2 - p) * tall] + come_ref[...].astype(F32)
            out_ref[:tall, :] = summed.astype(BF16)
            out_ref[tall:, :] = total[p * tall : (p + 1) * tall].astype(BF16)


def mixed_call(places, normed, for_x, for_y, w_out, width):
    rows, cols = normed.shape
    quarter, half = (rows // 2, width), (rows, width)
    return call(
        mixed_kernel,
        "sum_and_near",
        2,
        places,
        (normed, for_x, for_y, w_out),
        [fixed((rows, cols)), fixed(quarter), fixed(quarter), WHOLE],
        (struct(half, BF16),) * 2,
        [fixed(half)] * 2,
        4 * rows * cols * width,
        light=True,
    )


def pair_kernel(places, normed_ref, x_ref, y_ref, w_ref, out_x_ref, out_y_ref):
    tall, width = out_x_ref.shape

    @pl.when(pl.program_id(0) == 0)
    def _():
        total = dot(normed_ref[tall:, :], columns(w_ref, places[1], width)) + x_ref[...].astype(F32)
        out_x_ref[...] = total.astype(BF16)

    @pl.when(pl.program_id(0) == 1)
    def _():
        total = dot(normed_ref[:tall, :], columns(w_ref, places[2], width)) + y_ref[...].astype(F32)
        out_y_ref[...] = total.astype(BF16)


def pair_call(places, normed, for_x, for_y, w_out, width):
    rows, cols = normed.shape
    quarter = (rows // 2, width)
    return call(
        pair_kernel,
        "sum_pair",
        2,
        places,
        (normed, for_x, for_y, w_out),
        [fixed((rows, cols)), fixed(quarter), fixed(quarter), WHOLE],
        (struct(quarter, BF16),) * 2,
        [fixed(quarter)] * 2,
        2 * rows * cols * width,
        light=True,
    )


def own_kernel(places, normed_ref, w_ref, *refs):
    out_ref = refs[-1]
    tall, width = out_ref.shape
    each = len(refs) // 2
    for p in range(2):
        rows = slice(p * tall, (p + 1) * tall)

        @pl.when(pl.program_id(0) == p)
        def _(p=p, rows=rows):
            total = dot(normed_ref[rows, :], columns(w_ref, places[0], width))
            for ref in refs[p * each : (p + 1) * each]:
                total = total + ref[...].astype(F32)
            out_ref[...] = total.astype(BF16)


def own_call(places, normed, first, second, w_out, width, height):
    rows, cols = normed.shape
    quarter = (rows // 2, width)
    return call(
        own_kernel,
        "own_block",
        2,
        places,
        (normed, w_out, *[a for a, _ in (*first, *second)]),
        [fixed((rows, cols)), WHOLE]
        + [pl.BlockSpec(quarter, lambda i, o, at=at: (at, 0)) for _, at in (*first, *second)],
        (struct((rows * height, width), BF16),),
        [pl.BlockSpec(quarter, lambda i, o: (i, 0))],
        2 * rows * cols * width,
        light=True,
    )[0]


def last_kernel(_, kept_ref, a_ref, b_ref, above_ref, out_ref):
    del above_ref

    @pl.when(pl.program_id(0) == 0)
    def _():
        out_ref[...] = (kept_ref[...].astype(F32) + a_ref[...].astype(F32)).astype(BF16)

    @pl.when(pl.program_id(0) == 1)
    def _():
        out_ref[...] = (kept_ref[...].astype(F32) + b_ref[...].astype(F32)).astype(BF16)


def last_call(kept, a, b, above):
    tall, width = a.shape
    return call(
        last_kernel,
        "last_add",
        2,
        jnp.zeros((1,), jnp.int32),
        (kept, a, b, above),
        [
            pl.BlockSpec((tall, width), lambda j, o: (j, 0)),
            fixed((tall, width)),
            fixed((tall, width)),
            pl.BlockSpec(memory_space=pl.ANY),
        ],
        (struct(above.shape, BF16),),
        [pl.BlockSpec((tall, width), lambda j, o: (2 + j, 0))],
        tall * width,
        aliases={4: 0},
    )[0]


def local(n_head, n_seq, tokens, w_qkv, w_out, decay_rate, prior_state):
    rows, width = tokens.shape
    heads, size = prior_state.shape[0], prior_state.shape[1]
    square = n_head == 4
    place = lax.axis_index("head").astype(jnp.int32)
    quarter = rows // 4
    group = 2 if heads % 2 == 0 else 1
    cols = group * size

    over_x = functools.partial(lax.ppermute, axis_name="head", perm=[(i, i ^ 1) for i in range(n_head)])
    over_y = functools.partial(lax.ppermute, axis_name="head", perm=[(i, i ^ 2) for i in range(n_head)])

    pos = lax.axis_index("seq").astype(jnp.int32)
    core, chip = pos % 2, pos // 2
    flips = (0, 1, 2, 3) if square else (0, 0, 0, 0)
    places = jnp.stack([*[place ^ f for f in flips], core, chip])

    along, inside, down, tail, to_end, half_fade = decay_call(decay_rate, quarter)
    n_chips = n_seq // 2
    swap = functools.partial(lax.ppermute, axis_name="seq", perm=[(i, i ^ 1) for i in range(n_seq)])

    def hop(x, *pairs):
        perm = [(2 * a + c, 2 * b + c) for a, b in pairs for c in range(2)]
        return lax.ppermute(x, "seq", perm=perm)

    def chip_tails(tail):
        other = swap(tail)
        return other, tail + other, hop(tail + other, (2, 3)) if n_chips == 4 else None

    if square:
        tokens = stay(tokens)
        q0, q1 = cut_call(tokens, 0, 1)
        x0, y1 = over_x(q0), over_y(q1)
        x1, y0 = over_x(after(q1, tail)), over_y(after(q0, tail))
        acc = own_part_call(places, tokens, w_qkv, cols)
        q2, q3 = cut_call(stay(after(tokens, acc, x0, y1)), 1, 10**10)
        fy0, fx1 = over_y(x0), over_x(y1)
        tail_other, tail_chip, tail_below = chip_tails(after(tail, acc, x0, y1))
        x2 = over_x(after(q2, x1, y0, tail_chip))
        y3 = over_y(after(q3, x1, y0, tail_chip))
        acc_a = part_call(
            places,
            (1, 2),
            [(x0, x1), (y0, y1)],
            w_qkv,
            2 * quarter,
            cols,
            before=stay(after(acc, tail_chip)),
            at=0,
        )
        earlier = (fy0, fx1, acc_a) if tail_below is None else (fy0, fx1, acc_a, tail_below)
        x3, y2 = over_x(after(q3, *earlier)), over_y(after(q2, *earlier))
        query_a, within_a, state = first_call(
            places,
            (3,),
            [(fy0, fx1)],
            (acc_a,),
            w_qkv,
            along,
            inside,
            2 * quarter,
            quarter,
            size,
            group,
        )
        fy2, fx3 = over_y(after(x2, state)), over_x(after(y3, state))
        acc_q, acc_kv = part_call(
            places,
            (1, 2),
            [(x2, x3), (y2, y3)],
            w_qkv,
            2 * quarter,
            cols,
            before=stay(acc),
            at=1,
            apart=True,
        )
        far = (fy2, fx3)
        middle = state
        k, v, state, sent = state_call(
            places, far, w_qkv, acc_kv, to_end, half_fade, middle, group
        )
    else:
        tail_other, tail_chip, tail_below = chip_tails(tail)
        gathered = lax.all_gather(tokens, "head", axis=1, tiled=True)
        query, within, state = first_call(
            places, (), [(gathered,)], (), w_qkv, along, inside, rows, quarter, size, group
        )

    tails = (tail, tail_other)

    def scores_of_later(half, *earlier):
        start = stay(after(middle, *earlier))
        ins = (far, w_qkv, stay(acc_q), stay(k), stay(v), along, inside, down, start)
        return later_call(places, *ins, quarter, group, half)

    if square and n_chips == 4:
        leaving, alone, chip_state, first = chip_call(
            places, state, near(swap(sent)), tails, prior_state
        )
        alone = hop(alone, (2, 3))
        arriving = near(hop(leaving, (0, 1)))
        leaving = pass_call(places, arriving, chip_state, tails)
        to_third, to_second = hop(leaving, (1, 3)), hop(leaving, (1, 2))
        query_b, within_b = scores_of_later(0, leaving)
        alone, to_third, to_second, _ = lax.optimization_barrier((alone, to_third, to_second, query_b))
        here, passed = enter_call(
            places,
            arriving,
            near(alone),
            near(to_second),
            near(to_third),
            first,
            tails,
            tail_below,
            prior_state,
        )
    else:
        share = heads // 2

        def mine(x, core=core):
            return lax.dynamic_slice_in_dim(x, core * share, share, 0)

        def decay(tail):
            return jnp.exp(-mine(tail)[:, :1, None])

        ours = mine(state)
        other = swap(mine(state, 1 - core).astype(BF16)).astype(F32)
        first = jnp.where(core == 0, ours, other)
        second = jnp.where(core == 0, other, ours)
        chip_state = decay(jnp.where(core == 0, tail_other, tail)) * first + second
        chip_entering = mine(prior_state)
        for step in range(n_chips - 1):
            leaving = (decay(tail_chip) * chip_entering + chip_state).astype(BF16)
            arriving = hop(leaving, (step, step + 1))
            chip_entering = jnp.where(chip == step + 1, arriving.astype(F32), chip_entering)
        other = decay(jnp.where(core == 0, tail, tail_other)) * chip_entering + first
        here = jnp.where(core == 0, chip_entering, other).astype(BF16)
        passed = jnp.where(core == 0, other, chip_entering).astype(BF16)
    entering = (here, swap(passed))

    w_whole, w_out = w_out, near(w_out)
    if not square:
        halves = [
            head_call(
                places,
                (0,),
                (query[r * rows // 2 : (r + 1) * rows // 2],),
                (within[r * rows // 2 : (r + 1) * rows // 2],),
                entering,
                w_out,
                width,
            )[0]
            for r in range(2)
        ]
        partial = dot(jnp.concatenate(halves), w_whole).astype(BF16)
        return lax.psum_scatter(partial, "head", scatter_dimension=1, tiled=True)

    if n_chips != 4:
        query_b, within_b = scores_of_later(0)
    na, far0, far1 = head_call(
        places, (3,), (stay(query_a),), (stay(within_a),), entering, w_out, width
    )
    query_c, within_c = scores_of_later(1, na)
    far0, far1 = over_x(far0), over_y(far1)
    nb, by_x2, by_y2 = head_call(
        places, (3, 1, 2), (query_b, query_c), (within_b, within_c), entering, w_out, width
    )
    by_x2, by_y2 = over_x(by_x2), over_y(by_y2)
    by_x, by_y = mixed_call(places, after(na, nb), far1, far0, w_out, width)
    by_x2, by_y2 = after(by_x2, by_x), after(by_y2, by_x)
    by_x, by_y = over_x(by_x), over_y(by_y)
    sum3, sum2 = pair_call(places, nb, by_y2, by_x2, w_out, width)
    sum3, sum2 = over_x(sum3), over_y(sum2)
    below = own_call(places, after(nb, by_x, by_y), ((by_x2, 1),), ((by_y2, 1),), w_out, width, 1)
    above = own_call(places, na, ((by_x, 1), (by_y, 0)), ((by_y, 1), (by_x, 0)), w_out, width, 2)
    return last_call(below, sum2, sum3, above)


def solution(mesh):
    in_specs = (
        P("seq", "head"),
        P(None, None, "head"),
        P("head", None),
        P("head", "seq"),
        P("head", None, None),
    )
    body = functools.partial(local, mesh.shape["head"], mesh.shape["seq"])
    return jax.shard_map(
        body, mesh=mesh, in_specs=in_specs, out_specs=P("seq", "head"), check_vma=False
    )
```

```python
import functools
import math

import jax
import jax.numpy as jnp
from jax import lax
from jax.experimental import pallas as pl
from jax.experimental.pallas import tpu as pltpu
from jax.sharding import PartitionSpec as P

BF16, F32 = jnp.bfloat16, jnp.float32
MIB = 1024 * 1024


def dot(a, b, contract=((1,), (0,))):
    return lax.dot_general(a, b, (contract, ((), ())), preferred_element_type=F32)


def after(x, *earlier):
    return lax.optimization_barrier((x, *earlier))[0]


def struct(shape, dtype):
    return jax.ShapeDtypeStruct(shape, dtype)


def stay(x):
    return pltpu.with_memory_space_constraint(x, pltpu.HBM)


def near(x):
    return pltpu.with_memory_space_constraint(x, pltpu.VMEM)


def fixed(shape):
    return pl.BlockSpec(shape, lambda j, o: (0,) * len(shape))


def call(kernel, name, steps, scalars, ins, in_specs, outs, out_specs, flops, scratch=(), aliases=None, light=False):
    moved = sum(a.size * a.dtype.itemsize for a in ins) + sum(
        math.prod(o.shape) * jnp.dtype(o.dtype).itemsize for o in outs
    )
    return pl.pallas_call(
        kernel,
        out_shape=tuple(outs),
        grid_spec=pltpu.PrefetchScalarGridSpec(
            num_scalar_prefetch=1,
            grid=(steps,),
            in_specs=in_specs,
            out_specs=out_specs,
            scratch_shapes=list(scratch),
        ),
        input_output_aliases=aliases or {},
        compiler_params=pltpu.CompilerParams(vmem_limit_bytes=(16 if light else 24) * MIB),
        cost_estimate=pl.CostEstimate(
            flops=1 if light else flops, bytes_accessed=1 if light else moved, transcendentals=0
        ),
        name=name,
    )(scalars, *ins)


def cut_kernel(_, x_ref, a_ref, b_ref):
    tall = a_ref.shape[0]
    a_ref[...] = x_ref[:tall, :]
    b_ref[...] = x_ref[tall:, :]


def cut_call(x, half, cost):
    rows, width = x.shape
    quarter = (rows // 4, width)
    return call(
        cut_kernel,
        "cut",
        1,
        jnp.zeros((1,), jnp.int32),
        (x,),
        [pl.BlockSpec((rows // 2, width), lambda j, o: (half, 0))],
        (struct(quarter, x.dtype),) * 2,
        [fixed(quarter)] * 2,
        cost,
    )


def decay_kernel(chunk, _, rate_ref, along_ref, inside_ref, down_ref, tail_ref, end_ref, half_ref):
    heads, rows = rate_ref.shape
    lane = lax.broadcasted_iota(jnp.int32, (heads, chunk), 1)
    base = jnp.zeros((heads, 1), F32)
    insides, wholes = [], []
    for c in range(rows // chunk):
        x = rate_ref[:, c * chunk : (c + 1) * chunk]
        step = 1
        while step < chunk:
            x = x + jnp.where(lane >= step, pltpu.roll(x, step, 1), 0.0)
            step *= 2
        insides.append(x)
        wholes.append(x + base)
        base = base + x[:, chunk - 1 :]
    inside, whole = jnp.concatenate(insides, axis=1), jnp.concatenate(wholes, axis=1)
    along_ref[...] = inside
    inside_ref[...] = inside.T
    down_ref[...] = whole.T
    tail_ref[...] = jnp.broadcast_to(base, tail_ref.shape)
    end_ref[...] = jnp.exp(whole - base)
    half_ref[...] = jnp.broadcast_to(jnp.exp(whole[:, rows // 2 - 1 : rows // 2] - base), half_ref.shape)


def decay_call(rate, chunk):
    heads, rows = rate.shape
    return call(
        functools.partial(decay_kernel, chunk),
        "decay",
        1,
        jnp.zeros((1,), jnp.int32),
        (rate,),
        [fixed((heads, rows))],
        (
            struct((heads, rows), F32),
            struct((rows, heads), F32),
            struct((rows, heads), F32),
            struct((heads, 128), F32),
            struct((heads, rows), F32),
            struct((heads, 128), F32),
        ),
        [
            fixed((heads, rows)),
            fixed((rows, heads)),
            fixed((rows, heads)),
            fixed((heads, 128)),
            fixed((heads, rows)),
            fixed((heads, 128)),
        ],
        heads * rows * 16,
    )


def column(table, head):
    lane = lax.broadcasted_iota(jnp.int32, table.shape, 1)
    return jnp.sum(jnp.where(lane == head, table, 0.0), axis=1, keepdims=True)


def scores(q, k, v, along, down, state):
    rows = q.shape[0]
    causal = lax.broadcasted_iota(jnp.int32, (rows, rows), 0) >= lax.broadcasted_iota(
        jnp.int32, (rows, rows), 1
    )
    decay = jnp.exp(jnp.minimum(along - down, 0.0))
    weights = jnp.where(causal, dot(q, k, ((1,), (1,))) * decay, 0.0).astype(BF16)
    return dot(weights, v) + dot(q, state.astype(BF16)) * jnp.exp(-down)


def faded(q, down):
    return (q.astype(F32) * jnp.exp(-down)).astype(BF16)


def advance(k, v, down, state):
    last = down[down.shape[0] - 1 :, :]
    scaled = (k.astype(F32) * jnp.exp(down - last)).astype(BF16)
    return jnp.exp(-last) * state + dot(scaled, v, ((0,), (0,)))


def first_kernel(layout, added, chunk, group, size, _, *refs):
    count = sum(layout)
    x_refs, w_refs, refs = refs[:count], refs[count : count + len(layout)], refs[count + len(layout) :]
    passed_refs, held = refs[added + 5 : -1], refs[-1]
    along_ref, inside_ref, q_ref, within_ref, state_ref = refs[added : added + 5]
    for ref in passed_refs:
        ref[...] = w_refs[0][1:]
    j = pl.program_id(0)
    rows = held.shape[1]

    @pl.when(j == 0)
    def _():
        at = 0
        for i, parts in enumerate(layout):
            tall = rows // parts
            for p in range(parts):
                held[i, p * tall : (p + 1) * tall, :] = x_refs[at][...]
                at += 1

    def project(c):
        total = dot(held[0], w_refs[0][c])
        for i in range(1, len(layout)):
            total = total + dot(held[i], w_refs[i][c])
        if added:
            total = total + refs[0][c]
        return total.astype(BF16)

    q_all, k_all, v_all = project(0), project(1), project(2)
    for a in range(group):
        head = j * group + a
        lanes = slice(a * size, (a + 1) * size)
        state, base = jnp.zeros((size, size), F32), jnp.zeros((1, 1), F32)
        for c in range(rows // chunk):
            here = slice(c * chunk, (c + 1) * chunk)
            q, k, v = q_all[here, lanes], k_all[here, lanes], v_all[here, lanes]
            down = column(inside_ref[here, :], head)
            along = along_ref[pl.ds(head, 1), here]
            q_ref[here, lanes] = faded(q, base + down)
            within_ref[here, lanes] = scores(q, k, v, along, down, state).astype(BF16)
            state, base = advance(k, v, down, state), base + down[chunk - 1 :, :]
        state_ref[a] = state


def first_call(places, blocks, pieces, before, w_qkv, along, inside, rows, chunk, size, group):
    heads = along.shape[0]
    cols = group * size
    flat = [p for piece in pieces for p in piece]
    depth = flat[0].shape[1]

    def block(i):
        return pl.BlockSpec((3, depth, cols), lambda j, o: (0, o[blocks[i]] if blocks else 0, j))

    wide = pl.BlockSpec((rows, cols), lambda j, o: (0, j))
    return call(
        functools.partial(
            first_kernel, tuple(len(p) for p in pieces), bool(before), chunk, group, size
        ),
        "first",
        heads // group,
        places,
        (*flat, *[w_qkv] * len(pieces), *before, along, inside),
        [
            pl.BlockSpec((rows // len(piece), depth), lambda j, o: (0, 0))
            for piece in pieces
            for _ in piece
        ]
        + [block(i) for i in range(len(pieces))]
        + [pl.BlockSpec((3, rows, cols), lambda j, o: (0, 0, j)) for _ in before]
        + [fixed((heads, rows)), fixed((rows, heads))],
        (
            struct((rows, heads * size), BF16),
            struct((rows, heads * size), BF16),
            struct((heads, size, size), F32),
            *[struct((2, depth, heads * size), BF16) for _ in before],
        ),
        [wide, wide, pl.BlockSpec((group, size, size), lambda j, o: (j, 0, 0))]
        + [pl.BlockSpec((2, depth, cols), lambda j, o: (0, 0, j)) for _ in before],
        2 * rows * 3 * heads * size * depth * len(pieces),
        scratch=[pltpu.VMEM((len(pieces), rows, depth), BF16)],
    )


def own_part_kernel(_, x_ref, w_ref, out_ref):
    for c in range(3):
        out_ref[c] = dot(x_ref[...], w_ref[c])


def own_part_call(places, tokens, w_qkv, cols):
    rows, depth = tokens.shape
    width = w_qkv.shape[2]
    return call(
        own_part_kernel,
        "own_part",
        width // cols,
        places,
        (tokens, w_qkv),
        [fixed((rows, depth)), pl.BlockSpec((3, depth, cols), lambda j, o: (0, o[0], j))],
        (pltpu.HBM((3, rows, width), F32),),
        [pl.BlockSpec((3, rows, cols), lambda j, o: (0, 0, j))],
        2 * rows * depth * width * 3,
    )[0]


def part_kernel(layout, outs, _, *refs):
    count = sum(layout)
    x_refs, w_refs = refs[:count], refs[count : count + len(layout)]
    before_ref, out_refs, held = refs[-2 - outs], refs[-1 - outs : -1], refs[-1]
    targets = [(ref, c) for ref in out_refs for c in range(ref.shape[0])]
    rows = held.shape[1]

    @pl.when(pl.program_id(0) == 0)
    def _():
        at = 0
        for i, parts in enumerate(layout):
            tall = rows // parts
            for p in range(parts):
                held[i, p * tall : (p + 1) * tall, :] = x_refs[at][...]
                at += 1

    for c in range(3):
        total = dot(held[0], w_refs[0][c])
        for i in range(1, len(layout)):
            total = total + dot(held[i], w_refs[i][c])
        ref, at = targets[c]
        ref[at] = total + before_ref[c]


def part_call(places, blocks, pieces, w_qkv, rows, cols, before, at, apart=False):
    flat = [p for piece in pieces for p in piece]
    depth = flat[0].shape[1]
    width = w_qkv.shape[2]

    def block(i):
        return pl.BlockSpec((3, depth, cols), lambda j, o: (0, o[blocks[i]], j))

    ins = [*flat, *[w_qkv] * len(pieces)]
    specs = [
        pl.BlockSpec((rows // len(piece), depth), lambda j, o: (0, 0)) for piece in pieces for _ in piece
    ] + [block(i) for i in range(len(pieces))]
    ins.append(before)
    specs.append(pl.BlockSpec((3, rows, cols), lambda j, o: (0, at, j)))
    outs = [struct((3, rows, width), F32)]
    if apart:
        outs = [pltpu.HBM((1, rows, width), F32), struct((2, rows, width), F32)]
    out = call(
        functools.partial(part_kernel, tuple(len(p) for p in pieces), len(outs)),
        "part",
        width // cols,
        places,
        ins,
        specs,
        outs,
        [pl.BlockSpec((o.shape[0], rows, cols), lambda j, o: (0, 0, j)) for o in outs],
        2 * rows * depth * len(pieces) * width * 3,
        scratch=[pltpu.VMEM((len(pieces), rows, depth), BF16)],
    )
    return out if apart else out[0]


def state_kernel(places, xa, xb, w_ref, acc_ref, end_ref, half_ref, state_ref, *refs):
    k_ref, v_ref, out_ref, sent_ref, held = refs
    tall = xa.shape[0]
    heads, size = state_ref.shape[0], state_ref.shape[1]
    held[:tall, :] = xa[...]
    held[tall:, :] = xb[...]
    for pair in range(heads // 2):
        cols = slice(2 * pair * size, 2 * (pair + 1) * size)
        keys = (acc_ref[0, :, cols] + dot(held[...], w_ref[0, :, cols])).astype(BF16)
        values = (acc_ref[1, :, cols] + dot(held[...], w_ref[1, :, cols])).astype(BF16)
        k_ref[:, cols] = keys
        v_ref[:, cols] = values
        for a in range(2):
            head = 2 * pair + a
            lanes = slice(a * size, (a + 1) * size)
            scaled = (keys[:, lanes].T.astype(F32) * end_ref[head : head + 1, tall * 2 :]).astype(BF16)
            end = half_ref[head : head + 1, :] * state_ref[head] + dot(scaled, values[:, lanes])
            out_ref[head] = end

            @pl.when(places[4] != 2 * head // heads)
            def _(head=head, end=end):
                sent_ref[head % (heads // 2)] = end.astype(BF16)


def state_call(places, far, w_far, acc, to_end, half_fade, state):
    _, rows, width = acc.shape
    heads, size = state.shape[0], state.shape[1]
    depth = far[0].shape[1]
    ins = [near(x) for x in (*far, w_far, acc)] + [to_end, half_fade, near(state)]
    outs = (
        struct((rows, width), BF16),
        struct((rows, width), BF16),
        struct(state.shape, F32),
        struct((heads // 2, size, size), BF16),
    )
    scratch = [pltpu.VMEM((rows, depth), BF16)]
    return small_call(state_kernel, "states", places, ins, outs, 16, scratch)


def later_kernel(first, chunk, group, size, _, *refs):
    xa, xb, wq, acc_q, k_ref, v_ref, along_ref, inside_ref, down_ref, state_ref = refs[:10]
    q_ref, within_ref, held = refs[10:]
    j = pl.program_id(0)
    rows = held.shape[0]

    @pl.when(j == 0)
    def _():
        held[: rows // 2, :] = xa[...]
        held[rows // 2 :, :] = xb[...]

    q_all = (acc_q[0] + dot(held[...], wq[0])).astype(BF16)
    for a in range(group):
        head = (first + j) * group + a
        lanes = slice(a * size, (a + 1) * size)
        state = state_ref[a]
        for c in range(rows // chunk):
            here = slice(c * chunk, (c + 1) * chunk)
            q, k, v = q_all[here, lanes], k_ref[here, lanes], v_ref[here, lanes]
            along, down = along_ref[pl.ds(head, 1), here], column(inside_ref[here, :], head)
            q_ref[here, lanes] = faded(q, column(down_ref[here, :], head))
            within_ref[here, lanes] = scores(q, k, v, along, down, state).astype(BF16)
            if c + 1 < rows // chunk:
                state = advance(k, v, down, state)


def later_call(places, far, w_qkv, acc, k, v, along, inside, down, state, chunk, group, half):
    _, rows, width = acc.shape
    heads, size = state.shape[0], state.shape[1]
    depth = far[0].shape[1]
    cols = group * size
    steps = heads // group // 2
    first = half * steps
    wide = pl.BlockSpec((rows, cols), lambda j, o: (0, first + j))
    out = pl.BlockSpec((rows, cols), lambda j, o: (0, j))
    return call(
        functools.partial(later_kernel, first, chunk, group, size),
        "later",
        steps,
        places,
        (*far, w_qkv, acc, k, v, along, inside, down, state),
        [
            fixed(far[0].shape),
            fixed(far[1].shape),
            pl.BlockSpec((1, depth, cols), lambda j, o: (0, o[3], first + j)),
            pl.BlockSpec((1, rows, cols), lambda j, o: (0, 0, first + j)),
            wide,
            wide,
            pl.BlockSpec((heads, rows), lambda j, o: (0, 1)),
            pl.BlockSpec((rows, heads), lambda j, o: (1, 0)),
            pl.BlockSpec((rows, heads), lambda j, o: (1, 0)),
            pl.BlockSpec((group, size, size), lambda j, o: (first + j, 0, 0)),
        ],
        (struct((rows, width // 2), BF16), struct((rows, width // 2), BF16)),
        [out, out],
        rows * depth * width + 2 * rows * (chunk + size) * width,
        scratch=[pltpu.VMEM((rows, depth), BF16)],
    )


def fades(tail_ref, other_ref, place, head):
    own, other = tail_ref[pl.ds(head, 1), :], other_ref[pl.ds(head, 1), :]
    first = jnp.where(place == 0, own, other)
    return jnp.exp(-first), jnp.exp(first - (own + other)), jnp.exp(-(own + other))


def chip_kernel(places, state_ref, come_ref, tail_ref, other_ref, prior_ref, *out_refs):
    leaving_ref, alone_ref, chip_ref, first_ref = out_refs
    core = places[4]
    share = come_ref.shape[0]
    for i in range(share):
        head = core * share + i
        _, second_fade, fade = fades(tail_ref, other_ref, core, head)
        ours, come = state_ref[head], come_ref[i].astype(F32)
        first, second = jnp.where(core == 0, ours, come), jnp.where(core == 0, come, ours)
        total = second_fade * first + second
        first_ref[i] = first
        chip_ref[i] = total
        alone_ref[i] = total.astype(BF16)
        leaving_ref[i] = (fade * prior_ref[head] + total).astype(BF16)


def pass_kernel(places, come_ref, chip_ref, tail_ref, other_ref, leaving_ref):
    share = come_ref.shape[0]
    for i in range(share):
        fade = fades(tail_ref, other_ref, places[4], places[4] * share + i)[2]
        leaving_ref[i] = (fade * come_ref[i].astype(F32) + chip_ref[i]).astype(BF16)


def enter_kernel(
    places, come_ref, alone_ref, second_ref, third_ref, first_ref, tail_ref, other_ref, below_ref, prior_ref, *out_refs
):
    here_ref, passed_ref = out_refs
    core, chip = places[4], places[5]
    share = come_ref.shape[0]
    for i in range(share):
        head = core * share + i
        below = jnp.exp(-below_ref[pl.ds(head, 1), :])
        through = below * third_ref[i].astype(F32) + alone_ref[i].astype(F32)
        state = jnp.where(chip == 0, prior_ref[head], come_ref[i].astype(F32))
        state = jnp.where(chip == 2, second_ref[i].astype(F32), state)
        state = jnp.where(chip == 3, through, state)
        later = fades(tail_ref, other_ref, core, head)[0] * state + first_ref[i]
        here_ref[i] = jnp.where(core == 0, state, later).astype(BF16)
        passed_ref[i] = jnp.where(core == 0, later, state).astype(BF16)


def small_call(kernel, name, places, ins, outs, limit=4, scratch=()):
    whole = pl.BlockSpec(memory_space=pltpu.VMEM)
    return pl.pallas_call(
        kernel,
        out_shape=tuple(outs),
        in_specs=[pl.BlockSpec(memory_space=pltpu.SMEM)] + [whole] * len(ins),
        out_specs=[whole] * len(outs),
        scratch_shapes=list(scratch),
        compiler_params=pltpu.CompilerParams(vmem_limit_bytes=limit * MIB),
        cost_estimate=pl.CostEstimate(flops=1, bytes_accessed=1, transcendentals=0),
        name=name,
    )(places, *ins)


def chip_call(places, state, come, tails, prior):
    outs = [struct(come.shape, kind) for kind in (BF16, BF16, F32, F32)]
    return small_call(chip_kernel, "chip_state", places, (state, come, *tails, prior), outs)


def pass_call(places, come, chip_state, tails):
    outs = (struct(come.shape, BF16),)
    return small_call(pass_kernel, "pass_on", places, (come, chip_state, *tails), outs)[0]


def enter_call(places, come, alone, second, third, first, tails, below, prior):
    outs = (struct(come.shape, BF16),) * 2
    ins = (come, alone, second, third, first, *tails, below, prior)
    return small_call(enter_kernel, "enter", places, ins, outs)


def columns(w_ref, block, width):
    return w_ref[:, pl.ds(pl.multiple_of(block * width, width), width)]


WHOLE = pl.BlockSpec(memory_space=pltpu.VMEM)


def normalise(core, q_refs, within_refs, here_ref, there_ref, rows, out_ref):
    share, size = here_ref.shape[0], here_ref.shape[1]
    ones = jnp.ones((size, size), BF16)
    for a in range(2 * share):
        part, at = divmod(a, 2 * share // len(q_refs))
        here = slice(at * size, (at + 1) * size)
        entering = jnp.where(core == a // share, here_ref[a % share], there_ref[a % share])
        seen = dot(q_refs[part][rows, here], entering)
        combined = within_refs[part][rows, here].astype(F32) + seen
        square = combined * combined
        high = square.astype(BF16)
        low = (square - high.astype(F32)).astype(BF16)
        power = (dot(high, ones) + dot(low, ones)) * (1.0 / size)
        out_ref[:, a * size : (a + 1) * size] = (combined * lax.rsqrt(power + 1e-06)).astype(BF16)


def far_kernel(places, q_ref, within_ref, here_ref, there_ref, w_ref, normed_ref, *out_refs):
    tall, width = out_refs[0].shape
    for p, out_ref in enumerate(out_refs):
        rows = slice(p * tall, (p + 1) * tall)
        normed = normed_ref.at[rows]
        normalise(places[4], (q_ref,), (within_ref,), here_ref, there_ref, rows, normed)
        out_ref[...] = dot(normed[...], columns(w_ref, places[3], width)).astype(BF16)


def far_call(places, q, within, entering, w_out, width):
    out = struct((q.shape[0] // 2, width), BF16)
    ins = (near(q), near(within), *[near(e) for e in entering], w_out)
    return small_call(far_kernel, "heads_far", places, ins, (struct(q.shape, BF16), out, out), 8)


def head_kernel(count, blocks, places, *refs):
    q_refs, within_refs, refs = refs[:count], refs[count : 2 * count], refs[2 * count :]
    here_ref, there_ref, w_ref, normed_ref = refs[:4]
    out_refs, held = refs[4:6], refs[6]
    width = out_refs[0].shape[1]
    step = pl.program_id(0)
    for p, out_ref in enumerate(out_refs):

        @pl.when(step == p)
        def _(p=p, out_ref=out_ref):
            normalise(places[4], q_refs, within_refs, here_ref, there_ref, slice(None), held.at[p])
            normed_ref[...] = held[p]
            out_ref[...] = dot(held[p], columns(w_ref, places[blocks[0]], width)).astype(BF16)

        if len(blocks) > 1:

            @pl.when(step == 2 + p)
            def _(p=p, out_ref=out_ref):
                out_ref[...] = dot(held[p], columns(w_ref, places[blocks[1 + p]], width)).astype(BF16)


def head_call(places, blocks, q, within, entering, w_out, width):
    rows, cols = q[0].shape[0], w_out.shape[0]
    tall = rows // 2
    near = len(blocks) > 1
    part = pl.BlockSpec((tall, cols), lambda i, o: (jnp.minimum(i, 1), 0))
    some = pl.BlockSpec((tall, cols // len(q)), lambda i, o: (jnp.minimum(i, 1), 0))
    out = struct((rows if near else tall, width), BF16)
    return call(
        functools.partial(head_kernel, len(q), blocks),
        "heads",
        4 if near else 2,
        places,
        (*q, *within, *entering, w_out),
        [some] * (2 * len(q)) + [fixed(entering[0].shape), fixed(entering[1].shape), WHOLE],
        (struct((rows, cols), BF16), out, out),
        [
            part,
            pl.BlockSpec((tall, width), lambda i, o: (i // 2, 0)),
            pl.BlockSpec((tall, width), lambda i, o: (jnp.maximum(i - 2, 0), 0)),
        ],
        2 * rows * cols * (2 * width + 128),
        scratch=[pltpu.VMEM((2, tall, cols), BF16)],
        light=True,
    )


def mixed_kernel(places, normed_ref, x_ref, y_ref, w_ref, out_x_ref, out_y_ref):
    tall, width = x_ref.shape
    for p, (out_ref, come_ref) in enumerate(((out_x_ref, x_ref), (out_y_ref, y_ref))):

        @pl.when(pl.program_id(0) == p)
        def _(p=p, out_ref=out_ref, come_ref=come_ref):
            total = dot(normed_ref[...], columns(w_ref, places[1 + p], width))
            summed = total[(1 - p) * tall : (2 - p) * tall] + come_ref[...].astype(F32)
            out_ref[:tall, :] = summed.astype(BF16)
            out_ref[tall:, :] = total[p * tall : (p + 1) * tall].astype(BF16)


def mixed_call(places, normed, for_x, for_y, w_out, width):
    rows, cols = normed.shape
    quarter, half = (rows // 2, width), (rows, width)
    return call(
        mixed_kernel,
        "sum_and_near",
        2,
        places,
        (normed, for_x, for_y, w_out),
        [fixed((rows, cols)), fixed(quarter), fixed(quarter), WHOLE],
        (struct(half, BF16),) * 2,
        [fixed(half)] * 2,
        4 * rows * cols * width,
        light=True,
    )


def pair_kernel(places, normed_ref, x_ref, y_ref, w_ref, out_x_ref, out_y_ref):
    tall, width = out_x_ref.shape

    @pl.when(pl.program_id(0) == 0)
    def _():
        total = dot(normed_ref[tall:, :], columns(w_ref, places[1], width)) + x_ref[...].astype(F32)
        out_x_ref[...] = total.astype(BF16)

    @pl.when(pl.program_id(0) == 1)
    def _():
        total = dot(normed_ref[:tall, :], columns(w_ref, places[2], width)) + y_ref[...].astype(F32)
        out_y_ref[...] = total.astype(BF16)


def pair_call(places, normed, for_x, for_y, w_out, width):
    rows, cols = normed.shape
    quarter = (rows // 2, width)
    return call(
        pair_kernel,
        "sum_pair",
        2,
        places,
        (normed, for_x, for_y, w_out),
        [fixed((rows, cols)), fixed(quarter), fixed(quarter), WHOLE],
        (struct(quarter, BF16),) * 2,
        [fixed(quarter)] * 2,
        2 * rows * cols * width,
        light=True,
    )


def own_kernel(places, normed_ref, w_ref, *refs):
    out_ref = refs[-1]
    tall, width = out_ref.shape
    each = len(refs) // 2
    for p in range(2):
        rows = slice(p * tall, (p + 1) * tall)

        @pl.when(pl.program_id(0) == p)
        def _(p=p, rows=rows):
            total = dot(normed_ref[rows, :], columns(w_ref, places[0], width))
            for ref in refs[p * each : (p + 1) * each]:
                total = total + ref[...].astype(F32)
            out_ref[...] = total.astype(BF16)


def own_call(places, normed, first, second, w_out, width, height):
    rows, cols = normed.shape
    quarter = (rows // 2, width)
    return call(
        own_kernel,
        "own_block",
        2,
        places,
        (normed, w_out, *[a for a, _ in (*first, *second)]),
        [fixed((rows, cols)), WHOLE]
        + [pl.BlockSpec(quarter, lambda i, o, at=at: (at, 0)) for _, at in (*first, *second)],
        (struct((rows * height, width), BF16),),
        [pl.BlockSpec(quarter, lambda i, o: (i, 0))],
        2 * rows * cols * width,
        light=True,
    )[0]


def last_kernel(_, kept_ref, a_ref, b_ref, above_ref, out_ref):
    del above_ref

    @pl.when(pl.program_id(0) == 0)
    def _():
        out_ref[...] = (kept_ref[...].astype(F32) + a_ref[...].astype(F32)).astype(BF16)

    @pl.when(pl.program_id(0) == 1)
    def _():
        out_ref[...] = (kept_ref[...].astype(F32) + b_ref[...].astype(F32)).astype(BF16)


def last_call(kept, a, b, above):
    tall, width = a.shape
    return call(
        last_kernel,
        "last_add",
        2,
        jnp.zeros((1,), jnp.int32),
        (kept, a, b, above),
        [
            pl.BlockSpec((tall, width), lambda j, o: (j, 0)),
            fixed((tall, width)),
            fixed((tall, width)),
            pl.BlockSpec(memory_space=pl.ANY),
        ],
        (struct(above.shape, BF16),),
        [pl.BlockSpec((tall, width), lambda j, o: (2 + j, 0))],
        tall * width,
        aliases={4: 0},
    )[0]


def local(n_head, n_seq, tokens, w_qkv, w_out, decay_rate, prior_state):
    rows, width = tokens.shape
    heads, size = prior_state.shape[0], prior_state.shape[1]
    square = n_head == 4
    place = lax.axis_index("head").astype(jnp.int32)
    quarter = rows // 4
    group = 2 if heads % 2 == 0 else 1
    cols = group * size

    over_x = functools.partial(lax.ppermute, axis_name="head", perm=[(i, i ^ 1) for i in range(n_head)])
    over_y = functools.partial(lax.ppermute, axis_name="head", perm=[(i, i ^ 2) for i in range(n_head)])

    pos = lax.axis_index("seq").astype(jnp.int32)
    core, chip = pos % 2, pos // 2
    flips = (0, 1, 2, 3) if square else (0, 0, 0, 0)
    places = jnp.stack([*[place ^ f for f in flips], core, chip])

    along, inside, down, tail, to_end, half_fade = decay_call(decay_rate, quarter)
    n_chips = n_seq // 2
    swap = functools.partial(lax.ppermute, axis_name="seq", perm=[(i, i ^ 1) for i in range(n_seq)])

    def hop(x, *pairs):
        perm = [(2 * a + c, 2 * b + c) for a, b in pairs for c in range(2)]
        return lax.ppermute(x, "seq", perm=perm)

    def chip_tails(tail):
        other = swap(tail)
        return other, tail + other, hop(tail + other, (2, 3)) if n_chips == 4 else None

    if square:
        tokens, w_qkv = stay(tokens), stay(w_qkv)
        q0, q1 = cut_call(tokens, 0, 1)
        x0, y1 = over_x(q0), over_y(q1)
        x1, y0 = over_x(after(q1, tail)), over_y(after(q0, tail))
        acc = own_part_call(places, tokens, w_qkv, cols)
        q2, q3 = cut_call(stay(after(tokens, acc, x0, y1)), 1, 10**10)
        fy0, fx1 = over_y(x0), over_x(y1)
        tail_other, tail_chip, tail_below = chip_tails(after(tail, acc, x0, y1))
        x2 = over_x(after(q2, x1, y0, tail_chip))
        y3 = over_y(after(q3, x1, y0, tail_chip))
        acc_a = part_call(
            places,
            (1, 2),
            [(x0, x1), (y0, y1)],
            w_qkv,
            2 * quarter,
            cols,
            before=stay(after(acc, tail_chip)),
            at=0,
        )
        earlier = (fy0, fx1, acc_a) if tail_below is None else (fy0, fx1, acc_a, tail_below)
        x3, y2 = over_x(after(q3, *earlier)), over_y(after(q2, *earlier))
        query_a, within_a, state, w_far = first_call(
            places,
            (3,),
            [(fy0, fx1)],
            (acc_a,),
            w_qkv,
            along,
            inside,
            2 * quarter,
            quarter,
            size,
            group,
        )
        fy2, fx3 = over_y(after(x2, state)), over_x(after(y3, state))
        acc_q, acc_kv = part_call(
            places,
            (1, 2),
            [(x2, x3), (y2, y3)],
            w_qkv,
            2 * quarter,
            cols,
            before=stay(acc),
            at=1,
            apart=True,
        )
        far = (fy2, fx3)
        middle = state
        k, v, state, sent = state_call(places, far, w_far, acc_kv, to_end, half_fade, middle)
    else:
        tail_other, tail_chip, tail_below = chip_tails(tail)
        gathered = lax.all_gather(tokens, "head", axis=1, tiled=True)
        query, within, state = first_call(
            places, (), [(gathered,)], (), w_qkv, along, inside, rows, quarter, size, group
        )

    tails = (tail, tail_other)

    def scores_of_later(half, *earlier):
        start = after(middle, *earlier)
        ins = (far, w_qkv, stay(acc_q), k, v, along, inside, down, start)
        return later_call(places, *ins, quarter, group, half)

    if square and n_chips == 4:
        leaving, alone, chip_state, first = chip_call(
            places, state, near(swap(sent)), tails, prior_state
        )
        alone = hop(alone, (2, 3))
        arriving = near(hop(leaving, (0, 1)))
        leaving = pass_call(places, arriving, chip_state, tails)
        to_third, to_second = hop(leaving, (1, 3)), hop(leaving, (1, 2))
        query_b, within_b = scores_of_later(0, leaving)
        alone, to_third, to_second, _ = lax.optimization_barrier((alone, to_third, to_second, query_b))
        here, passed = enter_call(
            places,
            arriving,
            near(alone),
            near(to_second),
            near(to_third),
            first,
            tails,
            tail_below,
            prior_state,
        )
    else:
        share = heads // 2

        def mine(x, core=core):
            return lax.dynamic_slice_in_dim(x, core * share, share, 0)

        def decay(tail):
            return jnp.exp(-mine(tail)[:, :1, None])

        ours = mine(state)
        other = swap(mine(state, 1 - core).astype(BF16)).astype(F32)
        first = jnp.where(core == 0, ours, other)
        second = jnp.where(core == 0, other, ours)
        chip_state = decay(jnp.where(core == 0, tail_other, tail)) * first + second
        chip_entering = mine(prior_state)
        for step in range(n_chips - 1):
            leaving = (decay(tail_chip) * chip_entering + chip_state).astype(BF16)
            arriving = hop(leaving, (step, step + 1))
            chip_entering = jnp.where(chip == step + 1, arriving.astype(F32), chip_entering)
        other = decay(jnp.where(core == 0, tail, tail_other)) * chip_entering + first
        here = jnp.where(core == 0, chip_entering, other).astype(BF16)
        passed = jnp.where(core == 0, other, chip_entering).astype(BF16)
    entering = (here, swap(passed))

    w_whole, w_out = w_out, near(w_out)
    if not square:
        halves = [
            head_call(
                places,
                (0,),
                (query[r * rows // 2 : (r + 1) * rows // 2],),
                (within[r * rows // 2 : (r + 1) * rows // 2],),
                entering,
                w_out,
                width,
            )[0]
            for r in range(2)
        ]
        partial = dot(jnp.concatenate(halves), w_whole).astype(BF16)
        return lax.psum_scatter(partial, "head", scatter_dimension=1, tiled=True)

    if n_chips != 4:
        query_b, within_b = scores_of_later(0)
    na, far0, far1 = far_call(places, query_a, within_a, entering, w_out, width)
    query_c, within_c = scores_of_later(1, na)
    far0, far1 = over_x(far0), over_y(far1)
    nb, by_x2, by_y2 = head_call(
        places, (3, 1, 2), (query_b, query_c), (within_b, within_c), entering, w_out, width
    )
    by_x2, by_y2 = over_x(by_x2), over_y(by_y2)
    by_x, by_y = mixed_call(places, after(na, nb), far1, far0, w_out, width)
    by_x2, by_y2 = after(by_x2, by_x), after(by_y2, by_x)
    by_x, by_y = over_x(by_x), over_y(by_y)
    sum3, sum2 = pair_call(places, nb, by_y2, by_x2, w_out, width)
    sum3, sum2 = over_x(sum3), over_y(sum2)
    below = own_call(places, after(nb, by_x, by_y), ((by_x2, 1),), ((by_y2, 1),), w_out, width, 1)
    above = own_call(places, na, ((by_x, 1), (by_y, 0)), ((by_y, 1), (by_x, 0)), w_out, width, 2)
    return last_call(below, sum2, sum3, above)


def solution(mesh):
    in_specs = (
        P("seq", "head"),
        P(None, None, "head"),
        P("head", None),
        P("head", "seq"),
        P("head", None, None),
    )
    body = functools.partial(local, mesh.shape["head"], mesh.shape["seq"])
    return jax.shard_map(
        body, mesh=mesh, in_specs=in_specs, out_specs=P("seq", "head"), check_vma=False
    )
```

```python
import functools
import math

import jax
import jax.numpy as jnp
from jax import lax
from jax.experimental import pallas as pl
from jax.experimental.pallas import tpu as pltpu
from jax.sharding import PartitionSpec as P

BF16, F32 = jnp.bfloat16, jnp.float32
MIB = 1024 * 1024


def dot(a, b, contract=((1,), (0,))):
    return lax.dot_general(a, b, (contract, ((), ())), preferred_element_type=F32)


def after(x, *earlier):
    return lax.optimization_barrier((x, *earlier))[0]


def struct(shape, dtype):
    return jax.ShapeDtypeStruct(shape, dtype)


def stay(x):
    return pltpu.with_memory_space_constraint(x, pltpu.HBM)


def near(x):
    return pltpu.with_memory_space_constraint(x, pltpu.VMEM)


def fixed(shape):
    return pl.BlockSpec(shape, lambda j, o: (0,) * len(shape))


def call(kernel, name, steps, scalars, ins, in_specs, outs, out_specs, flops, scratch=(), aliases=None, light=False):
    moved = sum(a.size * a.dtype.itemsize for a in ins) + sum(
        math.prod(o.shape) * jnp.dtype(o.dtype).itemsize for o in outs
    )
    return pl.pallas_call(
        kernel,
        out_shape=tuple(outs),
        grid_spec=pltpu.PrefetchScalarGridSpec(
            num_scalar_prefetch=1,
            grid=(steps,),
            in_specs=in_specs,
            out_specs=out_specs,
            scratch_shapes=list(scratch),
        ),
        input_output_aliases=aliases or {},
        compiler_params=pltpu.CompilerParams(vmem_limit_bytes=(16 if light else 24) * MIB),
        cost_estimate=pl.CostEstimate(
            flops=1 if light else flops, bytes_accessed=1 if light else moved, transcendentals=0
        ),
        name=name,
    )(scalars, *ins)


def cut_kernel(_, x_ref, a_ref, b_ref):
    tall = a_ref.shape[0]
    a_ref[...] = x_ref[:tall, :]
    b_ref[...] = x_ref[tall:, :]


def cut_call(x, half, cost):
    rows, width = x.shape
    quarter = (rows // 4, width)
    return call(
        cut_kernel,
        "cut",
        1,
        jnp.zeros((1,), jnp.int32),
        (x,),
        [pl.BlockSpec((rows // 2, width), lambda j, o: (half, 0))],
        (struct(quarter, x.dtype),) * 2,
        [fixed(quarter)] * 2,
        cost,
    )


def decay_kernel(chunk, _, rate_ref, along_ref, inside_ref, down_ref, tail_ref, end_ref, half_ref):
    heads, rows = rate_ref.shape
    lane = lax.broadcasted_iota(jnp.int32, (heads, chunk), 1)
    base = jnp.zeros((heads, 1), F32)
    insides, wholes = [], []
    for c in range(rows // chunk):
        x = rate_ref[:, c * chunk : (c + 1) * chunk]
        step = 1
        while step < chunk:
            x = x + jnp.where(lane >= step, pltpu.roll(x, step, 1), 0.0)
            step *= 2
        insides.append(x)
        wholes.append(x + base)
        base = base + x[:, chunk - 1 :]
    inside, whole = jnp.concatenate(insides, axis=1), jnp.concatenate(wholes, axis=1)
    along_ref[...] = inside
    inside_ref[...] = inside.T
    down_ref[...] = whole.T
    tail_ref[...] = jnp.broadcast_to(base, tail_ref.shape)
    end_ref[...] = jnp.exp(whole - base)
    half_ref[...] = jnp.broadcast_to(jnp.exp(whole[:, rows // 2 - 1 : rows // 2] - base), half_ref.shape)


def decay_call(rate, chunk):
    heads, rows = rate.shape
    return call(
        functools.partial(decay_kernel, chunk),
        "decay",
        1,
        jnp.zeros((1,), jnp.int32),
        (rate,),
        [fixed((heads, rows))],
        (
            struct((heads, rows), F32),
            struct((rows, heads), F32),
            struct((rows, heads), F32),
            struct((heads, 128), F32),
            struct((heads, rows), F32),
            struct((heads, 128), F32),
        ),
        [
            fixed((heads, rows)),
            fixed((rows, heads)),
            fixed((rows, heads)),
            fixed((heads, 128)),
            fixed((heads, rows)),
            fixed((heads, 128)),
        ],
        heads * rows * 16,
    )


def column(table, head):
    lane = lax.broadcasted_iota(jnp.int32, table.shape, 1)
    return jnp.sum(jnp.where(lane == head, table, 0.0), axis=1, keepdims=True)


def scores(q, k, v, along, down, state):
    rows = q.shape[0]
    causal = lax.broadcasted_iota(jnp.int32, (rows, rows), 0) >= lax.broadcasted_iota(
        jnp.int32, (rows, rows), 1
    )
    decay = jnp.exp(jnp.minimum(along - down, 0.0))
    weights = jnp.where(causal, dot(q, k, ((1,), (1,))) * decay, 0.0).astype(BF16)
    return dot(weights, v) + dot(q, state.astype(BF16)) * jnp.exp(-down)


def faded(q, down):
    return (q.astype(F32) * jnp.exp(-down)).astype(BF16)


def advance(k, v, down, state):
    last = down[down.shape[0] - 1 :, :]
    scaled = (k.astype(F32) * jnp.exp(down - last)).astype(BF16)
    return jnp.exp(-last) * state + dot(scaled, v, ((0,), (0,)))


def first_kernel(layout, added, chunk, group, size, _, *refs):
    count = sum(layout)
    x_refs, w_refs, refs = refs[:count], refs[count : count + len(layout)], refs[count + len(layout) :]
    passed_refs, held = refs[added + 5 : -1], refs[-1]
    along_ref, inside_ref, q_ref, within_ref, state_ref = refs[added : added + 5]
    for ref in passed_refs:
        ref[...] = w_refs[0][...]
    j = pl.program_id(0)
    rows = held.shape[1]

    @pl.when(j == 0)
    def _():
        at = 0
        for i, parts in enumerate(layout):
            tall = rows // parts
            for p in range(parts):
                held[i, p * tall : (p + 1) * tall, :] = x_refs[at][...]
                at += 1

    def project(c):
        total = dot(held[0], w_refs[0][c])
        for i in range(1, len(layout)):
            total = total + dot(held[i], w_refs[i][c])
        if added:
            total = total + refs[0][c]
        return total.astype(BF16)

    q_all, k_all, v_all = project(0), project(1), project(2)
    for a in range(group):
        head = j * group + a
        lanes = slice(a * size, (a + 1) * size)
        state, base = jnp.zeros((size, size), F32), jnp.zeros((1, 1), F32)
        for c in range(rows // chunk):
            here = slice(c * chunk, (c + 1) * chunk)
            q, k, v = q_all[here, lanes], k_all[here, lanes], v_all[here, lanes]
            down = column(inside_ref[here, :], head)
            along = along_ref[pl.ds(head, 1), here]
            q_ref[here, lanes] = faded(q, base + down)
            within_ref[here, lanes] = scores(q, k, v, along, down, state).astype(BF16)
            state, base = advance(k, v, down, state), base + down[chunk - 1 :, :]
        state_ref[a] = state


def first_call(places, blocks, pieces, before, w_qkv, along, inside, rows, chunk, size, group):
    heads = along.shape[0]
    cols = group * size
    flat = [p for piece in pieces for p in piece]
    depth = flat[0].shape[1]

    def block(i):
        return pl.BlockSpec((3, depth, cols), lambda j, o: (0, o[blocks[i]] if blocks else 0, j))

    wide = pl.BlockSpec((rows, cols), lambda j, o: (0, j))
    return call(
        functools.partial(
            first_kernel, tuple(len(p) for p in pieces), bool(before), chunk, group, size
        ),
        "first",
        heads // group,
        places,
        (*flat, *[w_qkv] * len(pieces), *before, along, inside),
        [
            pl.BlockSpec((rows // len(piece), depth), lambda j, o: (0, 0))
            for piece in pieces
            for _ in piece
        ]
        + [block(i) for i in range(len(pieces))]
        + [pl.BlockSpec((3, rows, cols), lambda j, o: (0, 0, j)) for _ in before]
        + [fixed((heads, rows)), fixed((rows, heads))],
        (
            struct((rows, heads * size), BF16),
            struct((rows, heads * size), BF16),
            struct((heads, size, size), F32),
            *[struct((3, depth, heads * size), BF16) for _ in before],
        ),
        [wide, wide, pl.BlockSpec((group, size, size), lambda j, o: (j, 0, 0))]
        + [pl.BlockSpec((3, depth, cols), lambda j, o: (0, 0, j)) for _ in before],
        2 * rows * 3 * heads * size * depth * len(pieces),
        scratch=[pltpu.VMEM((len(pieces), rows, depth), BF16)],
    )


def own_part_kernel(_, x_ref, w_ref, out_ref):
    for c in range(3):
        out_ref[c] = dot(x_ref[...], w_ref[c])


def own_part_call(places, tokens, w_qkv, cols):
    rows, depth = tokens.shape
    width = w_qkv.shape[2]
    return call(
        own_part_kernel,
        "own_part",
        width // cols,
        places,
        (tokens, w_qkv),
        [fixed((rows, depth)), pl.BlockSpec((3, depth, cols), lambda j, o: (0, o[0], j))],
        (pltpu.HBM((3, rows, width), F32),),
        [pl.BlockSpec((3, rows, cols), lambda j, o: (0, 0, j))],
        2 * rows * depth * width * 3,
    )[0]


def part_kernel(layout, _, *refs):
    count = sum(layout)
    x_refs, w_refs = refs[:count], refs[count : count + len(layout)]
    before_ref, out_ref, held = refs[-3:]
    rows = held.shape[1]

    @pl.when(pl.program_id(0) == 0)
    def _():
        at = 0
        for i, parts in enumerate(layout):
            tall = rows // parts
            for p in range(parts):
                held[i, p * tall : (p + 1) * tall, :] = x_refs[at][...]
                at += 1

    for c in range(3):
        total = dot(held[0], w_refs[0][c])
        for i in range(1, len(layout)):
            total = total + dot(held[i], w_refs[i][c])
        out_ref[c] = total + before_ref[c]


def part_call(places, blocks, pieces, w_qkv, rows, cols, before, at):
    flat = [p for piece in pieces for p in piece]
    depth = flat[0].shape[1]
    width = w_qkv.shape[2]

    def block(i):
        return pl.BlockSpec((3, depth, cols), lambda j, o: (0, o[blocks[i]], j))

    ins = [*flat, *[w_qkv] * len(pieces)]
    specs = [
        pl.BlockSpec((rows // len(piece), depth), lambda j, o: (0, 0)) for piece in pieces for _ in piece
    ] + [block(i) for i in range(len(pieces))]
    ins.append(before)
    specs.append(pl.BlockSpec((3, rows, cols), lambda j, o: (0, at, j)))
    return call(
        functools.partial(part_kernel, tuple(len(p) for p in pieces)),
        "part",
        width // cols,
        places,
        ins,
        specs,
        (struct((3, rows, width), F32),),
        [pl.BlockSpec((3, rows, cols), lambda j, o: (0, 0, j))],
        2 * rows * depth * len(pieces) * width * 3,
        scratch=[pltpu.VMEM((len(pieces), rows, depth), BF16)],
    )[0]


def state_kernel(places, xa, xb, w_ref, acc_ref, end_ref, half_ref, state_ref, *refs):
    k_ref, v_ref, out_ref, sent_ref, held = refs
    tall = xa.shape[0]
    heads, size = state_ref.shape[0], state_ref.shape[1]
    held[:tall, :] = xa[...]
    held[tall:, :] = xb[...]
    for pair in range(heads // 2):
        cols = slice(2 * pair * size, 2 * (pair + 1) * size)
        keys = (acc_ref[1, :, cols] + dot(held[...], w_ref[1, :, cols])).astype(BF16)
        values = (acc_ref[2, :, cols] + dot(held[...], w_ref[2, :, cols])).astype(BF16)
        k_ref[:, cols] = keys
        v_ref[:, cols] = values
        for a in range(2):
            head = 2 * pair + a
            lanes = slice(a * size, (a + 1) * size)
            scaled = (keys[:, lanes].T.astype(F32) * end_ref[head : head + 1, tall * 2 :]).astype(BF16)
            end = half_ref[head : head + 1, :] * state_ref[head] + dot(scaled, values[:, lanes])
            out_ref[head] = end

            @pl.when(places[4] != 2 * head // heads)
            def _(head=head, end=end):
                sent_ref[head % (heads // 2)] = end.astype(BF16)


def state_call(places, far, w_far, acc, to_end, half_fade, state):
    _, rows, width = acc.shape
    heads, size = state.shape[0], state.shape[1]
    depth = far[0].shape[1]
    ins = [near(x) for x in (*far, w_far, acc)] + [to_end, half_fade, near(state)]
    outs = (
        struct((rows, width), BF16),
        struct((rows, width), BF16),
        struct(state.shape, F32),
        struct((heads // 2, size, size), BF16),
    )
    scratch = [pltpu.VMEM((rows, depth), BF16)]
    return small_call(state_kernel, "states", places, ins, outs, 16, scratch)


def later_kernel(half, chunk, _, xa, xb, w_ref, acc_ref, k_ref, v_ref, *refs):
    along_ref, inside_ref, down_ref, state_ref, q_ref, within_ref, held = refs
    tall, rows = xa.shape[0], held.shape[0]
    heads, size = state_ref.shape[0], state_ref.shape[1]
    held[:tall, :] = xa[...]
    held[tall:, :] = xb[...]
    for a in range(heads // 2):
        head = half * heads // 2 + a
        lanes, out = slice(head * size, (head + 1) * size), slice(a * size, (a + 1) * size)
        if a % 2 == 0:
            pair = slice(head * size, (head + 2) * size)
            queries = (acc_ref[0, :, pair] + dot(held[...], w_ref[0, :, pair])).astype(BF16)
        state = state_ref[head]
        for c in range(rows // chunk):
            here, there = slice(c * chunk, (c + 1) * chunk), slice(rows + c * chunk, rows + (c + 1) * chunk)
            q = queries[here, (a % 2) * size : (a % 2 + 1) * size]
            k, v = k_ref[here, lanes], v_ref[here, lanes]
            along, down = along_ref[head : head + 1, there], inside_ref[there, head : head + 1]
            q_ref[here, out] = faded(q, down_ref[there, head : head + 1])
            within_ref[here, out] = scores(q, k, v, along, down, state).astype(BF16)
            if c + 1 < rows // chunk:
                state = advance(k, v, down, state)


def later_call(places, far, w_far, acc, k, v, along, inside, down, state, chunk, half):
    _, rows, width = acc.shape
    ins = [near(x) for x in (*far, w_far, acc, k, v)] + [along, inside, down, near(state)]
    outs = (struct((rows, width // 2), BF16),) * 2
    scratch = [pltpu.VMEM((rows, far[0].shape[1]), BF16)]
    kernel = functools.partial(later_kernel, half, chunk)
    return small_call(kernel, "later", places, ins, outs, 16, scratch)


def fades(tail_ref, other_ref, place, head):
    own, other = tail_ref[pl.ds(head, 1), :], other_ref[pl.ds(head, 1), :]
    first = jnp.where(place == 0, own, other)
    return jnp.exp(-first), jnp.exp(first - (own + other)), jnp.exp(-(own + other))


def chip_kernel(places, state_ref, come_ref, tail_ref, other_ref, prior_ref, *out_refs):
    leaving_ref, alone_ref, chip_ref, first_ref = out_refs
    core = places[4]
    share = come_ref.shape[0]
    for i in range(share):
        head = core * share + i
        _, second_fade, fade = fades(tail_ref, other_ref, core, head)
        ours, come = state_ref[head], come_ref[i].astype(F32)
        first, second = jnp.where(core == 0, ours, come), jnp.where(core == 0, come, ours)
        total = second_fade * first + second
        first_ref[i] = first
        chip_ref[i] = total
        alone_ref[i] = total.astype(BF16)
        leaving_ref[i] = (fade * prior_ref[head] + total).astype(BF16)


def pass_kernel(places, come_ref, chip_ref, tail_ref, other_ref, leaving_ref):
    share = come_ref.shape[0]
    for i in range(share):
        fade = fades(tail_ref, other_ref, places[4], places[4] * share + i)[2]
        leaving_ref[i] = (fade * come_ref[i].astype(F32) + chip_ref[i]).astype(BF16)


def enter_kernel(
    places, come_ref, alone_ref, second_ref, third_ref, first_ref, tail_ref, other_ref, below_ref, prior_ref, *out_refs
):
    here_ref, passed_ref = out_refs
    core, chip = places[4], places[5]
    share = come_ref.shape[0]
    for i in range(share):
        head = core * share + i
        below = jnp.exp(-below_ref[pl.ds(head, 1), :])
        through = below * third_ref[i].astype(F32) + alone_ref[i].astype(F32)
        state = jnp.where(chip == 0, prior_ref[head], come_ref[i].astype(F32))
        state = jnp.where(chip == 2, second_ref[i].astype(F32), state)
        state = jnp.where(chip == 3, through, state)
        later = fades(tail_ref, other_ref, core, head)[0] * state + first_ref[i]
        here_ref[i] = jnp.where(core == 0, state, later).astype(BF16)
        passed_ref[i] = jnp.where(core == 0, later, state).astype(BF16)


def small_call(kernel, name, places, ins, outs, limit=4, scratch=()):
    whole = pl.BlockSpec(memory_space=pltpu.VMEM)
    return pl.pallas_call(
        kernel,
        out_shape=tuple(outs),
        in_specs=[pl.BlockSpec(memory_space=pltpu.SMEM)] + [whole] * len(ins),
        out_specs=[whole] * len(outs),
        scratch_shapes=list(scratch),
        compiler_params=pltpu.CompilerParams(vmem_limit_bytes=limit * MIB),
        cost_estimate=pl.CostEstimate(flops=1, bytes_accessed=1, transcendentals=0),
        name=name,
    )(places, *ins)


def chip_call(places, state, come, tails, prior):
    outs = [struct(come.shape, kind) for kind in (BF16, BF16, F32, F32)]
    return small_call(chip_kernel, "chip_state", places, (state, come, *tails, prior), outs)


def pass_call(places, come, chip_state, tails):
    outs = (struct(come.shape, BF16),)
    return small_call(pass_kernel, "pass_on", places, (come, chip_state, *tails), outs)[0]


def enter_call(places, come, alone, second, third, first, tails, below, prior):
    outs = (struct(come.shape, BF16),) * 2
    ins = (come, alone, second, third, first, *tails, below, prior)
    return small_call(enter_kernel, "enter", places, ins, outs)


def columns(w_ref, block, width):
    return w_ref[:, pl.ds(pl.multiple_of(block * width, width), width)]


WHOLE = pl.BlockSpec(memory_space=pltpu.VMEM)


def normalise(core, q_refs, within_refs, here_ref, there_ref, rows, out_ref):
    share, size = here_ref.shape[0], here_ref.shape[1]
    ones = jnp.ones((size, size), BF16)
    for a in range(2 * share):
        part, at = divmod(a, 2 * share // len(q_refs))
        here = slice(at * size, (at + 1) * size)
        entering = jnp.where(core == a // share, here_ref[a % share], there_ref[a % share])
        seen = dot(q_refs[part][rows, here], entering)
        combined = within_refs[part][rows, here].astype(F32) + seen
        square = combined * combined
        high = square.astype(BF16)
        low = (square - high.astype(F32)).astype(BF16)
        power = (dot(high, ones) + dot(low, ones)) * (1.0 / size)
        out_ref[:, a * size : (a + 1) * size] = (combined * lax.rsqrt(power + 1e-06)).astype(BF16)


def head_kernel(count, places, *refs):
    q_refs, within_refs, refs = refs[:count], refs[count : 2 * count], refs[2 * count :]
    here_ref, there_ref, w_ref, normed_ref = refs[:4]
    out_refs = refs[4:]
    tall, width = normed_ref.shape[0] // 2, out_refs[0].shape[1]
    for p, out_ref in enumerate(out_refs):
        rows = slice(p * tall, (p + 1) * tall)
        normed = normed_ref.at[rows]
        normalise(places[4], q_refs, within_refs, here_ref, there_ref, rows, normed)
        out_ref[:tall, :] = dot(normed[...], columns(w_ref, places[3], width)).astype(BF16)
        if out_ref.shape[0] > tall:
            out_ref[tall:, :] = dot(normed[...], columns(w_ref, places[1 + p], width)).astype(BF16)


def head_call(places, q, within, entering, w_out, width, near_too):
    rows, cols = q[0].shape[0], w_out.shape[0]
    out = struct((rows if near_too else rows // 2, width), BF16)
    ins = [near(x) for x in (*q, *within, *entering)] + [w_out]
    outs = (struct((rows, cols), BF16), out, out)
    return small_call(functools.partial(head_kernel, len(q)), "heads", places, ins, outs, 12)


def mixed_kernel(places, normed_ref, x_ref, y_ref, w_ref, out_x_ref, out_y_ref):
    tall, width = x_ref.shape
    for p, (out_ref, come_ref) in enumerate(((out_x_ref, x_ref), (out_y_ref, y_ref))):

        @pl.when(pl.program_id(0) == p)
        def _(p=p, out_ref=out_ref, come_ref=come_ref):
            total = dot(normed_ref[...], columns(w_ref, places[1 + p], width))
            summed = total[(1 - p) * tall : (2 - p) * tall] + come_ref[...].astype(F32)
            out_ref[:tall, :] = summed.astype(BF16)
            out_ref[tall:, :] = total[p * tall : (p + 1) * tall].astype(BF16)


def mixed_call(places, normed, for_x, for_y, w_out, width):
    rows, cols = normed.shape
    quarter, half = (rows // 2, width), (rows, width)
    return call(
        mixed_kernel,
        "sum_and_near",
        2,
        places,
        (normed, for_x, for_y, w_out),
        [fixed((rows, cols)), fixed(quarter), fixed(quarter), WHOLE],
        (struct(half, BF16),) * 2,
        [fixed(half)] * 2,
        4 * rows * cols * width,
        light=True,
    )


def pair_kernel(places, normed_ref, x_ref, y_ref, w_ref, out_x_ref, out_y_ref):
    tall, width = out_x_ref.shape

    @pl.when(pl.program_id(0) == 0)
    def _():
        total = dot(normed_ref[tall:, :], columns(w_ref, places[1], width)) + x_ref[...].astype(F32)
        out_x_ref[...] = total.astype(BF16)

    @pl.when(pl.program_id(0) == 1)
    def _():
        total = dot(normed_ref[:tall, :], columns(w_ref, places[2], width)) + y_ref[...].astype(F32)
        out_y_ref[...] = total.astype(BF16)


def pair_call(places, normed, for_x, for_y, w_out, width):
    rows, cols = normed.shape
    quarter = (rows // 2, width)
    return call(
        pair_kernel,
        "sum_pair",
        2,
        places,
        (normed, for_x, for_y, w_out),
        [fixed((rows, cols)), fixed(quarter), fixed(quarter), WHOLE],
        (struct(quarter, BF16),) * 2,
        [fixed(quarter)] * 2,
        2 * rows * cols * width,
        light=True,
    )


def own_kernel(places, normed_ref, w_ref, *refs):
    out_ref = refs[-1]
    tall, width = out_ref.shape
    each = len(refs) // 2
    for p in range(2):
        rows = slice(p * tall, (p + 1) * tall)

        @pl.when(pl.program_id(0) == p)
        def _(p=p, rows=rows):
            total = dot(normed_ref[rows, :], columns(w_ref, places[0], width))
            for ref in refs[p * each : (p + 1) * each]:
                total = total + ref[...].astype(F32)
            out_ref[...] = total.astype(BF16)


def own_call(places, normed, first, second, w_out, width, height):
    rows, cols = normed.shape
    quarter = (rows // 2, width)
    return call(
        own_kernel,
        "own_block",
        2,
        places,
        (normed, w_out, *[a for a, _ in (*first, *second)]),
        [fixed((rows, cols)), WHOLE]
        + [pl.BlockSpec(quarter, lambda i, o, at=at: (at, 0)) for _, at in (*first, *second)],
        (struct((rows * height, width), BF16),),
        [pl.BlockSpec(quarter, lambda i, o: (i, 0))],
        2 * rows * cols * width,
        light=True,
    )[0]


def last_kernel(_, kept_ref, a_ref, b_ref, above_ref, out_ref):
    del above_ref

    @pl.when(pl.program_id(0) == 0)
    def _():
        out_ref[...] = (kept_ref[...].astype(F32) + a_ref[...].astype(F32)).astype(BF16)

    @pl.when(pl.program_id(0) == 1)
    def _():
        out_ref[...] = (kept_ref[...].astype(F32) + b_ref[...].astype(F32)).astype(BF16)


def last_call(kept, a, b, above):
    tall, width = a.shape
    return call(
        last_kernel,
        "last_add",
        2,
        jnp.zeros((1,), jnp.int32),
        (kept, a, b, above),
        [
            pl.BlockSpec((tall, width), lambda j, o: (j, 0)),
            fixed((tall, width)),
            fixed((tall, width)),
            pl.BlockSpec(memory_space=pl.ANY),
        ],
        (struct(above.shape, BF16),),
        [pl.BlockSpec((tall, width), lambda j, o: (2 + j, 0))],
        tall * width,
        aliases={4: 0},
    )[0]


def local(n_head, n_seq, tokens, w_qkv, w_out, decay_rate, prior_state):
    rows, width = tokens.shape
    heads, size = prior_state.shape[0], prior_state.shape[1]
    square = n_head == 4
    place = lax.axis_index("head").astype(jnp.int32)
    quarter = rows // 4
    group = 2 if heads % 2 == 0 else 1
    cols = group * size

    over_x = functools.partial(lax.ppermute, axis_name="head", perm=[(i, i ^ 1) for i in range(n_head)])
    over_y = functools.partial(lax.ppermute, axis_name="head", perm=[(i, i ^ 2) for i in range(n_head)])

    pos = lax.axis_index("seq").astype(jnp.int32)
    core, chip = pos % 2, pos // 2
    flips = (0, 1, 2, 3) if square else (0, 0, 0, 0)
    places = jnp.stack([*[place ^ f for f in flips], core, chip])

    along, inside, down, tail, to_end, half_fade = decay_call(decay_rate, quarter)
    n_chips = n_seq // 2
    swap = functools.partial(lax.ppermute, axis_name="seq", perm=[(i, i ^ 1) for i in range(n_seq)])

    def hop(x, *pairs):
        perm = [(2 * a + c, 2 * b + c) for a, b in pairs for c in range(2)]
        return lax.ppermute(x, "seq", perm=perm)

    def chip_tails(tail):
        other = swap(tail)
        return other, tail + other, hop(tail + other, (2, 3)) if n_chips == 4 else None

    if square:
        tokens, w_qkv = stay(tokens), stay(w_qkv)
        q0, q1 = cut_call(tokens, 0, 1)
        x0, y1 = over_x(q0), over_y(q1)
        x1, y0 = over_x(after(q1, tail)), over_y(after(q0, tail))
        acc = own_part_call(places, tokens, w_qkv, cols)
        q2, q3 = cut_call(stay(after(tokens, acc, x0, y1)), 1, 10**10)
        fy0, fx1 = over_y(x0), over_x(y1)
        tail_other, tail_chip, tail_below = chip_tails(after(tail, acc, x0, y1))
        x2 = over_x(after(q2, x1, y0, tail_chip))
        y3 = over_y(after(q3, x1, y0, tail_chip))
        acc_a = part_call(
            places,
            (1, 2),
            [(x0, x1), (y0, y1)],
            w_qkv,
            2 * quarter,
            cols,
            before=stay(after(acc, tail_chip)),
            at=0,
        )
        earlier = (fy0, fx1, acc_a) if tail_below is None else (fy0, fx1, acc_a, tail_below)
        x3, y2 = over_x(after(q3, *earlier)), over_y(after(q2, *earlier))
        query_a, within_a, state, w_far = first_call(
            places,
            (3,),
            [(fy0, fx1)],
            (acc_a,),
            w_qkv,
            along,
            inside,
            2 * quarter,
            quarter,
            size,
            group,
        )
        fy2, fx3 = over_y(after(x2, state)), over_x(after(y3, state))
        acc_b = part_call(
            places,
            (1, 2),
            [(x2, x3), (y2, y3)],
            w_qkv,
            2 * quarter,
            cols,
            before=stay(acc),
            at=1,
        )
        far = (fy2, fx3)
        middle = state
        k, v, state, sent = state_call(places, far, w_far, acc_b, to_end, half_fade, middle)
    else:
        tail_other, tail_chip, tail_below = chip_tails(tail)
        gathered = lax.all_gather(tokens, "head", axis=1, tiled=True)
        query, within, state = first_call(
            places, (), [(gathered,)], (), w_qkv, along, inside, rows, quarter, size, group
        )

    tails = (tail, tail_other)

    def scores_of_later(half, *earlier):
        start = after(middle, *earlier)
        return later_call(places, far, w_far, acc_b, k, v, along, inside, down, start, quarter, half)

    if square and n_chips == 4:
        leaving, alone, chip_state, first = chip_call(
            places, state, near(swap(sent)), tails, prior_state
        )
        alone = hop(alone, (2, 3))
        arriving = near(hop(leaving, (0, 1)))
        leaving = pass_call(places, arriving, chip_state, tails)
        to_third, to_second = hop(leaving, (1, 3)), hop(leaving, (1, 2))
        query_b, within_b = scores_of_later(0, leaving)
        alone, to_third, to_second, _ = lax.optimization_barrier((alone, to_third, to_second, query_b))
        here, passed = enter_call(
            places,
            arriving,
            near(alone),
            near(to_second),
            near(to_third),
            first,
            tails,
            tail_below,
            prior_state,
        )
    else:
        share = heads // 2

        def mine(x, core=core):
            return lax.dynamic_slice_in_dim(x, core * share, share, 0)

        def decay(tail):
            return jnp.exp(-mine(tail)[:, :1, None])

        ours = mine(state)
        other = swap(mine(state, 1 - core).astype(BF16)).astype(F32)
        first = jnp.where(core == 0, ours, other)
        second = jnp.where(core == 0, other, ours)
        chip_state = decay(jnp.where(core == 0, tail_other, tail)) * first + second
        chip_entering = mine(prior_state)
        for step in range(n_chips - 1):
            leaving = (decay(tail_chip) * chip_entering + chip_state).astype(BF16)
            arriving = hop(leaving, (step, step + 1))
            chip_entering = jnp.where(chip == step + 1, arriving.astype(F32), chip_entering)
        other = decay(jnp.where(core == 0, tail, tail_other)) * chip_entering + first
        here = jnp.where(core == 0, chip_entering, other).astype(BF16)
        passed = jnp.where(core == 0, other, chip_entering).astype(BF16)
    entering = (here, swap(passed))

    w_whole, w_out = w_out, near(w_out)
    if not square:
        halves = [
            head_call(
                places,
                (query[r * rows // 2 : (r + 1) * rows // 2],),
                (within[r * rows // 2 : (r + 1) * rows // 2],),
                entering,
                w_out,
                width,
                False,
            )[0]
            for r in range(2)
        ]
        partial = dot(jnp.concatenate(halves), w_whole).astype(BF16)
        return lax.psum_scatter(partial, "head", scatter_dimension=1, tiled=True)

    if n_chips != 4:
        query_b, within_b = scores_of_later(0)
    na, far0, far1 = head_call(places, (query_a,), (within_a,), entering, w_out, width, False)
    query_c, within_c = scores_of_later(1, na)
    far0, far1 = over_x(far0), over_y(far1)
    nb, by_x2, by_y2 = head_call(
        places, (query_b, query_c), (within_b, within_c), entering, w_out, width, True
    )
    by_x2, by_y2 = over_x(by_x2), over_y(by_y2)
    by_x, by_y = mixed_call(places, after(na, nb), far1, far0, w_out, width)
    by_x2, by_y2 = after(by_x2, by_x), after(by_y2, by_x)
    by_x, by_y = over_x(by_x), over_y(by_y)
    sum3, sum2 = pair_call(places, nb, by_y2, by_x2, w_out, width)
    sum3, sum2 = over_x(sum3), over_y(sum2)
    below = own_call(places, after(nb, by_x, by_y), ((by_x2, 1),), ((by_y2, 1),), w_out, width, 1)
    above = own_call(places, na, ((by_x, 1), (by_y, 0)), ((by_y, 1), (by_x, 0)), w_out, width, 2)
    return last_call(below, sum2, sum3, above)


def solution(mesh):
    in_specs = (
        P("seq", "head"),
        P(None, None, "head"),
        P("head", None),
        P("head", "seq"),
        P("head", None, None),
    )
    body = functools.partial(local, mesh.shape["head"], mesh.shape["seq"])
    return jax.shard_map(
        body, mesh=mesh, in_specs=in_specs, out_specs=P("seq", "head"), check_vma=False
    )
```

```python
import functools
import math

import jax
import jax.numpy as jnp
from jax import lax
from jax.experimental import pallas as pl
from jax.experimental.pallas import tpu as pltpu
from jax.sharding import PartitionSpec as P

BF16, F32 = jnp.bfloat16, jnp.float32
MIB = 1024 * 1024


def dot(a, b, contract=((1,), (0,))):
    return lax.dot_general(a, b, (contract, ((), ())), preferred_element_type=F32)


def after(x, *earlier):
    return lax.optimization_barrier((x, *earlier))[0]


def struct(shape, dtype):
    return jax.ShapeDtypeStruct(shape, dtype)


def stay(x):
    return pltpu.with_memory_space_constraint(x, pltpu.HBM)


def near(x):
    return pltpu.with_memory_space_constraint(x, pltpu.VMEM)


def fixed(shape):
    return pl.BlockSpec(shape, lambda j, o: (0,) * len(shape))


def call(kernel, name, steps, scalars, ins, in_specs, outs, out_specs, flops, scratch=(), aliases=None, light=False):
    moved = sum(a.size * a.dtype.itemsize for a in ins) + sum(
        math.prod(o.shape) * jnp.dtype(o.dtype).itemsize for o in outs
    )
    return pl.pallas_call(
        kernel,
        out_shape=tuple(outs),
        grid_spec=pltpu.PrefetchScalarGridSpec(
            num_scalar_prefetch=1,
            grid=(steps,),
            in_specs=in_specs,
            out_specs=out_specs,
            scratch_shapes=list(scratch),
        ),
        input_output_aliases=aliases or {},
        compiler_params=pltpu.CompilerParams(vmem_limit_bytes=(16 if light else 24) * MIB),
        cost_estimate=pl.CostEstimate(
            flops=1 if light else flops, bytes_accessed=1 if light else moved, transcendentals=0
        ),
        name=name,
    )(scalars, *ins)


def cut_kernel(_, x_ref, a_ref, b_ref):
    tall = a_ref.shape[0]
    a_ref[...] = x_ref[:tall, :]
    b_ref[...] = x_ref[tall:, :]


def cut_call(x, half, cost):
    rows, width = x.shape
    quarter = (rows // 4, width)
    return call(
        cut_kernel,
        "cut",
        1,
        jnp.zeros((1,), jnp.int32),
        (x,),
        [pl.BlockSpec((rows // 2, width), lambda j, o: (half, 0))],
        (struct(quarter, x.dtype),) * 2,
        [fixed(quarter)] * 2,
        cost,
    )


def decay_kernel(chunk, _, rate_ref, along_ref, inside_ref, down_ref, tail_ref, end_ref, half_ref):
    heads, rows = rate_ref.shape
    lane = lax.broadcasted_iota(jnp.int32, (heads, chunk), 1)
    base = jnp.zeros((heads, 1), F32)
    insides, wholes = [], []
    for c in range(rows // chunk):
        x = rate_ref[:, c * chunk : (c + 1) * chunk]
        step = 1
        while step < chunk:
            x = x + jnp.where(lane >= step, pltpu.roll(x, step, 1), 0.0)
            step *= 2
        insides.append(x)
        wholes.append(x + base)
        base = base + x[:, chunk - 1 :]
    inside, whole = jnp.concatenate(insides, axis=1), jnp.concatenate(wholes, axis=1)
    along_ref[...] = inside
    inside_ref[...] = inside.T
    down_ref[...] = whole.T
    tail_ref[...] = jnp.broadcast_to(base, tail_ref.shape)
    end_ref[...] = jnp.exp(whole - base)
    half_ref[...] = jnp.broadcast_to(jnp.exp(whole[:, rows // 2 - 1 : rows // 2] - base), half_ref.shape)


def decay_call(rate, chunk):
    heads, rows = rate.shape
    return call(
        functools.partial(decay_kernel, chunk),
        "decay",
        1,
        jnp.zeros((1,), jnp.int32),
        (rate,),
        [fixed((heads, rows))],
        (
            struct((heads, rows), F32),
            struct((rows, heads), F32),
            struct((rows, heads), F32),
            struct((heads, 128), F32),
            struct((heads, rows), F32),
            struct((heads, 128), F32),
        ),
        [
            fixed((heads, rows)),
            fixed((rows, heads)),
            fixed((rows, heads)),
            fixed((heads, 128)),
            fixed((heads, rows)),
            fixed((heads, 128)),
        ],
        heads * rows * 16,
    )


def by_core(places, body):
    for core in (0, 1):

        @pl.when(places[4] == core)
        def _(core=core):
            body(core)


def column(table, head):
    lane = lax.broadcasted_iota(jnp.int32, table.shape, 1)
    return jnp.sum(jnp.where(lane == head, table, 0.0), axis=1, keepdims=True)


def scores(q, k, v, along, down, state):
    rows = q.shape[0]
    causal = lax.broadcasted_iota(jnp.int32, (rows, rows), 0) >= lax.broadcasted_iota(
        jnp.int32, (rows, rows), 1
    )
    decay = jnp.exp(jnp.minimum(along - down, 0.0))
    weights = jnp.where(causal, dot(q, k, ((1,), (1,))) * decay, 0.0).astype(BF16)
    return dot(weights, v) + dot(q, state.astype(BF16)) * jnp.exp(-down)


def faded(q, down):
    return (q.astype(F32) * jnp.exp(-down)).astype(BF16)


def advance(k, v, down, state):
    last = down[down.shape[0] - 1 :, :]
    scaled = (k.astype(F32) * jnp.exp(down - last)).astype(BF16)
    return jnp.exp(-last) * state + dot(scaled, v, ((0,), (0,)))


def first_kernel(layout, added, chunk, group, size, _, *refs):
    count = sum(layout)
    x_refs, w_refs, refs = refs[:count], refs[count : count + len(layout)], refs[count + len(layout) :]
    passed_refs, held = refs[added + 5 : -1], refs[-1]
    along_ref, inside_ref, q_ref, within_ref, state_ref = refs[added : added + 5]
    for ref in passed_refs:
        ref[...] = w_refs[0][...]
    j = pl.program_id(0)
    rows = held.shape[1]

    @pl.when(j == 0)
    def _():
        at = 0
        for i, parts in enumerate(layout):
            tall = rows // parts
            for p in range(parts):
                held[i, p * tall : (p + 1) * tall, :] = x_refs[at][...]
                at += 1

    def project(c):
        total = dot(held[0], w_refs[0][c])
        for i in range(1, len(layout)):
            total = total + dot(held[i], w_refs[i][c])
        if added:
            total = total + refs[0][c]
        return total.astype(BF16)

    q_all, k_all, v_all = project(0), project(1), project(2)
    for a in range(group):
        head = j * group + a
        lanes = slice(a * size, (a + 1) * size)
        state, base = jnp.zeros((size, size), F32), jnp.zeros((1, 1), F32)
        for c in range(rows // chunk):
            here = slice(c * chunk, (c + 1) * chunk)
            q, k, v = q_all[here, lanes], k_all[here, lanes], v_all[here, lanes]
            down = column(inside_ref[here, :], head)
            along = along_ref[pl.ds(head, 1), here]
            q_ref[here, lanes] = faded(q, base + down)
            within_ref[here, lanes] = scores(q, k, v, along, down, state).astype(BF16)
            state, base = advance(k, v, down, state), base + down[chunk - 1 :, :]
        state_ref[a] = state


def first_call(places, blocks, pieces, before, w_qkv, along, inside, rows, chunk, size, group):
    heads = along.shape[0]
    cols = group * size
    flat = [p for piece in pieces for p in piece]
    depth = flat[0].shape[1]

    def block(i):
        return pl.BlockSpec((3, depth, cols), lambda j, o: (0, o[blocks[i]] if blocks else 0, j))

    wide = pl.BlockSpec((rows, cols), lambda j, o: (0, j))
    return call(
        functools.partial(
            first_kernel, tuple(len(p) for p in pieces), bool(before), chunk, group, size
        ),
        "first",
        heads // group,
        places,
        (*flat, *[w_qkv] * len(pieces), *before, along, inside),
        [
            pl.BlockSpec((rows // len(piece), depth), lambda j, o: (0, 0))
            for piece in pieces
            for _ in piece
        ]
        + [block(i) for i in range(len(pieces))]
        + [pl.BlockSpec((3, rows, cols), lambda j, o: (0, 0, j)) for _ in before]
        + [fixed((heads, rows)), fixed((rows, heads))],
        (
            struct((rows, heads * size), BF16),
            struct((rows, heads * size), BF16),
            struct((heads, size, size), F32),
            *[struct((3, depth, heads * size), BF16) for _ in before],
        ),
        [wide, wide, pl.BlockSpec((group, size, size), lambda j, o: (j, 0, 0))]
        + [pl.BlockSpec((3, depth, cols), lambda j, o: (0, 0, j)) for _ in before],
        2 * rows * 3 * heads * size * depth * len(pieces),
        scratch=[pltpu.VMEM((len(pieces), rows, depth), BF16)],
    )


def own_part_kernel(_, x_ref, w_ref, out_ref):
    for c in range(3):
        out_ref[c] = dot(x_ref[...], w_ref[c])


def own_part_call(places, tokens, w_qkv, cols):
    rows, depth = tokens.shape
    width = w_qkv.shape[2]
    return call(
        own_part_kernel,
        "own_part",
        width // cols,
        places,
        (tokens, w_qkv),
        [fixed((rows, depth)), pl.BlockSpec((3, depth, cols), lambda j, o: (0, o[0], j))],
        (pltpu.HBM((3, rows, width), F32),),
        [pl.BlockSpec((3, rows, cols), lambda j, o: (0, 0, j))],
        2 * rows * depth * width * 3,
    )[0]


def part_kernel(layout, _, *refs):
    count = sum(layout)
    x_refs, w_refs = refs[:count], refs[count : count + len(layout)]
    before_ref, out_ref, held = refs[-3:]
    rows = held.shape[1]

    @pl.when(pl.program_id(0) == 0)
    def _():
        at = 0
        for i, parts in enumerate(layout):
            tall = rows // parts
            for p in range(parts):
                held[i, p * tall : (p + 1) * tall, :] = x_refs[at][...]
                at += 1

    for c in range(3):
        total = dot(held[0], w_refs[0][c])
        for i in range(1, len(layout)):
            total = total + dot(held[i], w_refs[i][c])
        out_ref[c] = total + before_ref[c]


def part_call(places, blocks, pieces, w_qkv, rows, cols, before, at):
    flat = [p for piece in pieces for p in piece]
    depth = flat[0].shape[1]
    width = w_qkv.shape[2]

    def block(i):
        return pl.BlockSpec((3, depth, cols), lambda j, o: (0, o[blocks[i]], j))

    ins = [*flat, *[w_qkv] * len(pieces)]
    specs = [
        pl.BlockSpec((rows // len(piece), depth), lambda j, o: (0, 0)) for piece in pieces for _ in piece
    ] + [block(i) for i in range(len(pieces))]
    ins.append(before)
    specs.append(pl.BlockSpec((3, rows, cols), lambda j, o: (0, at, j)))
    return call(
        functools.partial(part_kernel, tuple(len(p) for p in pieces)),
        "part",
        width // cols,
        places,
        ins,
        specs,
        (struct((3, rows, width), F32),),
        [pl.BlockSpec((3, rows, cols), lambda j, o: (0, 0, j))],
        2 * rows * depth * len(pieces) * width * 3,
        scratch=[pltpu.VMEM((len(pieces), rows, depth), BF16)],
    )[0]


def state_kernel(own, places, xa, xb, w_ref, acc_ref, end_ref, half_ref, state_ref, k_ref, v_ref, out_ref, held):
    tall = xa.shape[0]
    share, size = out_ref.shape[0], out_ref.shape[1]
    held[:tall, :] = xa[...]
    held[tall:, :] = xb[...]

    def body(core):
        base = share * (core if own else 1 - core)
        for pair in range(0, share, 2):
            cols = slice((base + pair) * size, (base + pair + 2) * size)
            keys = (acc_ref[1, :, cols] + dot(held[...], w_ref[1, :, cols])).astype(BF16)
            values = (acc_ref[2, :, cols] + dot(held[...], w_ref[2, :, cols])).astype(BF16)
            k_ref[:, pair * size : (pair + 2) * size] = keys
            v_ref[:, pair * size : (pair + 2) * size] = values
            for a in range(2):
                head = slice(base + pair + a, base + pair + a + 1)
                lanes = slice(a * size, (a + 1) * size)
                scaled = (keys[:, lanes].T.astype(F32) * end_ref[head, 2 * tall :]).astype(BF16)
                end = half_ref[head, :] * state_ref[base + pair + a] + dot(scaled, values[:, lanes])
                out_ref[pair + a] = end.astype(out_ref.dtype)

    by_core(places, body)


def state_call(places, far, w_far, acc, to_end, half_fade, state, own):
    _, rows, width = acc.shape
    heads, size = state.shape[0], state.shape[1]
    ins = [near(x) for x in (*far, w_far, acc)] + [to_end, half_fade, near(state)]
    outs = (
        struct((rows, width // 2), BF16),
        struct((rows, width // 2), BF16),
        struct((heads // 2, size, size), F32 if own else BF16),
    )
    scratch = [pltpu.VMEM((rows, far[0].shape[1]), BF16)]
    kernel = functools.partial(state_kernel, own)
    return small_call(kernel, "states", places, ins, outs, 16, scratch)


def later_kernel(own, chunk, places, xa, xb, w_ref, acc_ref, k_ref, v_ref, *refs):
    along_ref, inside_ref, down_ref, state_ref, q_ref, within_ref, held = refs
    tall, rows = xa.shape[0], held.shape[0]
    share, size = state_ref.shape[0] // 2, state_ref.shape[1]
    held[:tall, :] = xa[...]
    held[tall:, :] = xb[...]

    def body(core):
        base = share * (core if own else 1 - core)
        for a in range(share):
            head, lanes = base + a, slice(a * size, (a + 1) * size)
            if a % 2 == 0:
                pair = slice(head * size, (head + 2) * size)
                queries = (acc_ref[0, :, pair] + dot(held[...], w_ref[0, :, pair])).astype(BF16)
            state = state_ref[head]
            for c in range(rows // chunk):
                here = slice(c * chunk, (c + 1) * chunk)
                there = slice(rows + c * chunk, rows + (c + 1) * chunk)
                q = queries[here, (a % 2) * size : (a % 2 + 1) * size]
                k, v = k_ref[here, lanes], v_ref[here, lanes]
                along, down = along_ref[head : head + 1, there], inside_ref[there, head : head + 1]
                q_ref[here, lanes] = faded(q, down_ref[there, head : head + 1])
                within_ref[here, lanes] = scores(q, k, v, along, down, state).astype(BF16)
                if c + 1 < rows // chunk:
                    state = advance(k, v, down, state)

    by_core(places, body)


def later_call(places, far, w_far, acc, k, v, along, inside, down, state, chunk, own):
    _, rows, width = acc.shape
    ins = [near(x) for x in (*far, w_far, acc, k, v)] + [along, inside, down, near(state)]
    outs = (struct((rows, width // 2), BF16),) * 2
    scratch = [pltpu.VMEM((rows, far[0].shape[1]), BF16)]
    kernel = functools.partial(later_kernel, own, chunk)
    return small_call(kernel, "later", places, ins, outs, 16, scratch)


def fades(tail_ref, other_ref, place, head):
    own, other = tail_ref[pl.ds(head, 1), :], other_ref[pl.ds(head, 1), :]
    first = jnp.where(place == 0, own, other)
    return jnp.exp(-first), jnp.exp(first - (own + other)), jnp.exp(-(own + other))


def chip_kernel(places, state_ref, come_ref, tail_ref, other_ref, prior_ref, *out_refs):
    leaving_ref, alone_ref, chip_ref, first_ref = out_refs
    core = places[4]
    share = come_ref.shape[0]
    for i in range(share):
        head = core * share + i
        _, second_fade, fade = fades(tail_ref, other_ref, core, head)
        ours, come = state_ref[i], come_ref[i].astype(F32)
        first, second = jnp.where(core == 0, ours, come), jnp.where(core == 0, come, ours)
        total = second_fade * first + second
        first_ref[i] = first
        chip_ref[i] = total
        alone_ref[i] = total.astype(BF16)
        leaving_ref[i] = (fade * prior_ref[head] + total).astype(BF16)


def pass_kernel(places, come_ref, chip_ref, tail_ref, other_ref, leaving_ref):
    share = come_ref.shape[0]
    for i in range(share):
        fade = fades(tail_ref, other_ref, places[4], places[4] * share + i)[2]
        leaving_ref[i] = (fade * come_ref[i].astype(F32) + chip_ref[i]).astype(BF16)


def enter_kernel(
    places, come_ref, alone_ref, second_ref, third_ref, first_ref, tail_ref, other_ref, below_ref, prior_ref, *out_refs
):
    here_ref, passed_ref = out_refs
    core, chip = places[4], places[5]
    share = come_ref.shape[0]
    for i in range(share):
        head = core * share + i
        below = jnp.exp(-below_ref[pl.ds(head, 1), :])
        through = below * third_ref[i].astype(F32) + alone_ref[i].astype(F32)
        state = jnp.where(chip == 0, prior_ref[head], come_ref[i].astype(F32))
        state = jnp.where(chip == 2, second_ref[i].astype(F32), state)
        state = jnp.where(chip == 3, through, state)
        later = fades(tail_ref, other_ref, core, head)[0] * state + first_ref[i]
        here_ref[i] = jnp.where(core == 0, state, later).astype(BF16)
        passed_ref[i] = jnp.where(core == 0, later, state).astype(BF16)


def small_call(kernel, name, places, ins, outs, limit=4, scratch=()):
    whole = pl.BlockSpec(memory_space=pltpu.VMEM)
    return pl.pallas_call(
        kernel,
        out_shape=tuple(outs),
        in_specs=[pl.BlockSpec(memory_space=pltpu.SMEM)] + [whole] * len(ins),
        out_specs=[whole] * len(outs),
        scratch_shapes=list(scratch),
        compiler_params=pltpu.CompilerParams(vmem_limit_bytes=limit * MIB),
        cost_estimate=pl.CostEstimate(flops=1, bytes_accessed=1, transcendentals=0),
        name=name,
    )(places, *ins)


def chip_call(places, state, come, tails, prior):
    outs = [struct(come.shape, kind) for kind in (BF16, BF16, F32, F32)]
    return small_call(chip_kernel, "chip_state", places, (state, come, *tails, prior), outs)


def pass_call(places, come, chip_state, tails):
    outs = (struct(come.shape, BF16),)
    return small_call(pass_kernel, "pass_on", places, (come, chip_state, *tails), outs)[0]


def enter_call(places, come, alone, second, third, first, tails, below, prior):
    outs = (struct(come.shape, BF16),) * 2
    ins = (come, alone, second, third, first, *tails, below, prior)
    return small_call(enter_kernel, "enter", places, ins, outs)


def columns(w_ref, block, width):
    return w_ref[:, pl.ds(pl.multiple_of(block * width, width), width)]


WHOLE = pl.BlockSpec(memory_space=pltpu.VMEM)


def normalise(places, q_refs, within_refs, here_ref, there_ref, rows, out_ref):
    share, size = here_ref.shape[0], here_ref.shape[1]
    ones = jnp.ones((size, size), BF16)

    def body(core):
        for a in range(2 * share):
            own, at = a // share == core, a % share
            part, column = (int(own), at) if len(q_refs) > 1 else (0, a)
            here = slice(column * size, (column + 1) * size)
            entering = here_ref[at] if own else there_ref[at]
            combined = within_refs[part][rows, here].astype(F32) + dot(q_refs[part][rows, here], entering)
            square = combined * combined
            high = square.astype(BF16)
            low = (square - high.astype(F32)).astype(BF16)
            power = (dot(high, ones) + dot(low, ones)) * (1.0 / size)
            out_ref[:, a * size : (a + 1) * size] = (combined * lax.rsqrt(power + 1e-06)).astype(BF16)

    by_core(places, body)


def head_kernel(count, places, *refs):
    q_refs, within_refs, refs = refs[:count], refs[count : 2 * count], refs[2 * count :]
    here_ref, there_ref, w_ref, normed_ref = refs[:4]
    out_refs = refs[4:]
    tall, width = normed_ref.shape[0] // 2, out_refs[0].shape[1]
    for p, out_ref in enumerate(out_refs):
        rows = slice(p * tall, (p + 1) * tall)
        normed = normed_ref.at[rows]
        normalise(places, q_refs, within_refs, here_ref, there_ref, rows, normed)
        out_ref[:tall, :] = dot(normed[...], columns(w_ref, places[3], width)).astype(BF16)
        if out_ref.shape[0] > tall:
            out_ref[tall:, :] = dot(normed[...], columns(w_ref, places[1 + p], width)).astype(BF16)


def head_call(places, q, within, entering, w_out, width, near_too):
    rows, cols = q[0].shape[0], w_out.shape[0]
    out = struct((rows if near_too else rows // 2, width), BF16)
    ins = [near(x) for x in (*q, *within, *entering)] + [w_out]
    outs = (struct((rows, cols), BF16), out, out)
    return small_call(functools.partial(head_kernel, len(q)), "heads", places, ins, outs, 12)


def mixed_kernel(places, normed_ref, x_ref, y_ref, w_ref, out_x_ref, out_y_ref):
    tall, width = x_ref.shape
    for p, (out_ref, come_ref) in enumerate(((out_x_ref, x_ref), (out_y_ref, y_ref))):

        @pl.when(pl.program_id(0) == p)
        def _(p=p, out_ref=out_ref, come_ref=come_ref):
            total = dot(normed_ref[...], columns(w_ref, places[1 + p], width))
            summed = total[(1 - p) * tall : (2 - p) * tall] + come_ref[...].astype(F32)
            out_ref[:tall, :] = summed.astype(BF16)
            out_ref[tall:, :] = total[p * tall : (p + 1) * tall].astype(BF16)


def mixed_call(places, normed, for_x, for_y, w_out, width):
    rows, cols = normed.shape
    quarter, half = (rows // 2, width), (rows, width)
    return call(
        mixed_kernel,
        "sum_and_near",
        2,
        places,
        (normed, for_x, for_y, w_out),
        [fixed((rows, cols)), fixed(quarter), fixed(quarter), WHOLE],
        (struct(half, BF16),) * 2,
        [fixed(half)] * 2,
        4 * rows * cols * width,
        light=True,
    )


def pair_kernel(places, normed_ref, x_ref, y_ref, w_ref, out_x_ref, out_y_ref):
    tall, width = out_x_ref.shape

    @pl.when(pl.program_id(0) == 0)
    def _():
        total = dot(normed_ref[tall:, :], columns(w_ref, places[1], width)) + x_ref[...].astype(F32)
        out_x_ref[...] = total.astype(BF16)

    @pl.when(pl.program_id(0) == 1)
    def _():
        total = dot(normed_ref[:tall, :], columns(w_ref, places[2], width)) + y_ref[...].astype(F32)
        out_y_ref[...] = total.astype(BF16)


def pair_call(places, normed, for_x, for_y, w_out, width):
    rows, cols = normed.shape
    quarter = (rows // 2, width)
    return call(
        pair_kernel,
        "sum_pair",
        2,
        places,
        (normed, for_x, for_y, w_out),
        [fixed((rows, cols)), fixed(quarter), fixed(quarter), WHOLE],
        (struct(quarter, BF16),) * 2,
        [fixed(quarter)] * 2,
        2 * rows * cols * width,
        light=True,
    )


def own_kernel(places, normed_ref, w_ref, *refs):
    out_ref = refs[-1]
    tall, width = out_ref.shape
    each = len(refs) // 2
    for p in range(2):
        rows = slice(p * tall, (p + 1) * tall)

        @pl.when(pl.program_id(0) == p)
        def _(p=p, rows=rows):
            total = dot(normed_ref[rows, :], columns(w_ref, places[0], width))
            for ref in refs[p * each : (p + 1) * each]:
                total = total + ref[...].astype(F32)
            out_ref[...] = total.astype(BF16)


def own_call(places, normed, first, second, w_out, width, height):
    rows, cols = normed.shape
    quarter = (rows // 2, width)
    return call(
        own_kernel,
        "own_block",
        2,
        places,
        (normed, w_out, *[a for a, _ in (*first, *second)]),
        [fixed((rows, cols)), WHOLE]
        + [pl.BlockSpec(quarter, lambda i, o, at=at: (at, 0)) for _, at in (*first, *second)],
        (struct((rows * height, width), BF16),),
        [pl.BlockSpec(quarter, lambda i, o: (i, 0))],
        2 * rows * cols * width,
        light=True,
    )[0]


def last_kernel(_, kept_ref, a_ref, b_ref, above_ref, out_ref):
    del above_ref

    @pl.when(pl.program_id(0) == 0)
    def _():
        out_ref[...] = (kept_ref[...].astype(F32) + a_ref[...].astype(F32)).astype(BF16)

    @pl.when(pl.program_id(0) == 1)
    def _():
        out_ref[...] = (kept_ref[...].astype(F32) + b_ref[...].astype(F32)).astype(BF16)


def last_call(kept, a, b, above):
    tall, width = a.shape
    return call(
        last_kernel,
        "last_add",
        2,
        jnp.zeros((1,), jnp.int32),
        (kept, a, b, above),
        [
            pl.BlockSpec((tall, width), lambda j, o: (j, 0)),
            fixed((tall, width)),
            fixed((tall, width)),
            pl.BlockSpec(memory_space=pl.ANY),
        ],
        (struct(above.shape, BF16),),
        [pl.BlockSpec((tall, width), lambda j, o: (2 + j, 0))],
        tall * width,
        aliases={4: 0},
    )[0]


def local(n_head, n_seq, tokens, w_qkv, w_out, decay_rate, prior_state):
    rows, width = tokens.shape
    heads, size = prior_state.shape[0], prior_state.shape[1]
    square = n_head == 4
    place = lax.axis_index("head").astype(jnp.int32)
    quarter = rows // 4
    group = 2 if heads % 2 == 0 else 1
    cols = group * size

    over_x = functools.partial(lax.ppermute, axis_name="head", perm=[(i, i ^ 1) for i in range(n_head)])
    over_y = functools.partial(lax.ppermute, axis_name="head", perm=[(i, i ^ 2) for i in range(n_head)])

    pos = lax.axis_index("seq").astype(jnp.int32)
    core, chip = pos % 2, pos // 2
    flips = (0, 1, 2, 3) if square else (0, 0, 0, 0)
    places = jnp.stack([*[place ^ f for f in flips], core, chip])

    along, inside, down, tail, to_end, half_fade = decay_call(decay_rate, quarter)
    n_chips = n_seq // 2
    swap = functools.partial(lax.ppermute, axis_name="seq", perm=[(i, i ^ 1) for i in range(n_seq)])

    def hop(x, *pairs):
        perm = [(2 * a + c, 2 * b + c) for a, b in pairs for c in range(2)]
        return lax.ppermute(x, "seq", perm=perm)

    def chip_tails(tail):
        other = swap(tail)
        return other, tail + other, hop(tail + other, (2, 3)) if n_chips == 4 else None

    if square:
        tokens, w_qkv = stay(tokens), stay(w_qkv)
        q0, q1 = cut_call(tokens, 0, 1)
        x0, y1 = over_x(q0), over_y(q1)
        x1, y0 = over_x(after(q1, tail)), over_y(after(q0, tail))
        acc = own_part_call(places, tokens, w_qkv, cols)
        q2, q3 = cut_call(stay(after(tokens, acc, x0, y1)), 1, 10**10)
        fy0, fx1 = over_y(x0), over_x(y1)
        tail_other, tail_chip, tail_below = chip_tails(after(tail, acc, x0, y1))
        x2 = over_x(after(q2, x1, y0, tail_chip))
        y3 = over_y(after(q3, x1, y0, tail_chip))
        acc_a = part_call(
            places,
            (1, 2),
            [(x0, x1), (y0, y1)],
            w_qkv,
            2 * quarter,
            cols,
            before=stay(after(acc, tail_chip)),
            at=0,
        )
        earlier = (fy0, fx1, acc_a) if tail_below is None else (fy0, fx1, acc_a, tail_below)
        x3, y2 = over_x(after(q3, *earlier)), over_y(after(q2, *earlier))
        query_a, within_a, state, w_far = first_call(
            places,
            (3,),
            [(fy0, fx1)],
            (acc_a,),
            w_qkv,
            along,
            inside,
            2 * quarter,
            quarter,
            size,
            group,
        )
        fy2, fx3 = over_y(after(x2, state)), over_x(after(y3, state))
        acc_b = part_call(
            places,
            (1, 2),
            [(x2, x3), (y2, y3)],
            w_qkv,
            2 * quarter,
            cols,
            before=stay(acc),
            at=1,
        )
        far = (fy2, fx3)
        middle = state
        k, v, sent = state_call(places, far, w_far, acc_b, to_end, half_fade, middle, False)
        k_own, v_own, state = state_call(
            places, far, w_far, acc_b, to_end, half_fade, after(middle, sent), True
        )
    else:
        tail_other, tail_chip, tail_below = chip_tails(tail)
        gathered = lax.all_gather(tokens, "head", axis=1, tiled=True)
        query, within, state = first_call(
            places, (), [(gathered,)], (), w_qkv, along, inside, rows, quarter, size, group
        )

    tails = (tail, tail_other)

    def scores_of_later(own, *earlier):
        start = after(middle, *earlier)
        keys, values = (k_own, v_own) if own else (k, v)
        tables = (along, inside, down, start)
        return later_call(places, far, w_far, acc_b, keys, values, *tables, quarter, own)

    if square and n_chips == 4:
        leaving, alone, chip_state, first = chip_call(
            places, near(state), near(swap(sent)), tails, prior_state
        )
        alone = hop(alone, (2, 3))
        arriving = near(hop(leaving, (0, 1)))
        leaving = pass_call(places, arriving, chip_state, tails)
        to_third, to_second = hop(leaving, (1, 3)), hop(leaving, (1, 2))
        query_b, within_b = scores_of_later(False, leaving)
        alone, to_third, to_second, _ = lax.optimization_barrier((alone, to_third, to_second, query_b))
        here, passed = enter_call(
            places,
            arriving,
            near(alone),
            near(to_second),
            near(to_third),
            first,
            tails,
            tail_below,
            prior_state,
        )
    else:
        share = heads // 2

        def mine(x, core=core):
            return lax.dynamic_slice_in_dim(x, core * share, share, 0)

        def decay(tail):
            return jnp.exp(-mine(tail)[:, :1, None])

        ours = state if square else mine(state)
        other = swap(sent if square else mine(state, 1 - core).astype(BF16)).astype(F32)
        first = jnp.where(core == 0, ours, other)
        second = jnp.where(core == 0, other, ours)
        chip_state = decay(jnp.where(core == 0, tail_other, tail)) * first + second
        chip_entering = mine(prior_state)
        for step in range(n_chips - 1):
            leaving = (decay(tail_chip) * chip_entering + chip_state).astype(BF16)
            arriving = hop(leaving, (step, step + 1))
            chip_entering = jnp.where(chip == step + 1, arriving.astype(F32), chip_entering)
        other = decay(jnp.where(core == 0, tail, tail_other)) * chip_entering + first
        here = jnp.where(core == 0, chip_entering, other).astype(BF16)
        passed = jnp.where(core == 0, other, chip_entering).astype(BF16)
    entering = (here, swap(passed))

    w_whole, w_out = w_out, near(w_out)
    if not square:
        halves = [
            head_call(
                places,
                (query[r * rows // 2 : (r + 1) * rows // 2],),
                (within[r * rows // 2 : (r + 1) * rows // 2],),
                entering,
                w_out,
                width,
                False,
            )[0]
            for r in range(2)
        ]
        partial = dot(jnp.concatenate(halves), w_whole).astype(BF16)
        return lax.psum_scatter(partial, "head", scatter_dimension=1, tiled=True)

    if n_chips != 4:
        query_b, within_b = scores_of_later(False)
    na, far0, far1 = head_call(places, (query_a,), (within_a,), entering, w_out, width, False)
    query_c, within_c = scores_of_later(True, na)
    far0, far1 = over_x(far0), over_y(far1)
    nb, by_x2, by_y2 = head_call(
        places, (query_b, query_c), (within_b, within_c), entering, w_out, width, True
    )
    by_x2, by_y2 = over_x(by_x2), over_y(by_y2)
    by_x, by_y = mixed_call(places, after(na, nb), far1, far0, w_out, width)
    by_x2, by_y2 = after(by_x2, by_x), after(by_y2, by_x)
    by_x, by_y = over_x(by_x), over_y(by_y)
    sum3, sum2 = pair_call(places, nb, by_y2, by_x2, w_out, width)
    sum3, sum2 = over_x(sum3), over_y(sum2)
    below = own_call(places, after(nb, by_x, by_y), ((by_x2, 1),), ((by_y2, 1),), w_out, width, 1)
    above = own_call(places, na, ((by_x, 1), (by_y, 0)), ((by_y, 1), (by_x, 0)), w_out, width, 2)
    return last_call(below, sum2, sum3, above)


def solution(mesh):
    in_specs = (
        P("seq", "head"),
        P(None, None, "head"),
        P("head", None),
        P("head", "seq"),
        P("head", None, None),
    )
    body = functools.partial(local, mesh.shape["head"], mesh.shape["seq"])
    return jax.shard_map(
        body, mesh=mesh, in_specs=in_specs, out_specs=P("seq", "head"), check_vma=False
    )
```

```python
import functools
import math

import jax
import jax.numpy as jnp
from jax import lax
from jax.experimental import pallas as pl
from jax.experimental.pallas import tpu as pltpu
from jax.sharding import PartitionSpec as P

BF16, F32 = jnp.bfloat16, jnp.float32
MIB = 1024 * 1024


def dot(a, b, contract=((1,), (0,))):
    return lax.dot_general(a, b, (contract, ((), ())), preferred_element_type=F32)


def after(x, *earlier):
    return lax.optimization_barrier((x, *earlier))[0]


def struct(shape, dtype):
    return jax.ShapeDtypeStruct(shape, dtype)


def stay(x):
    return pltpu.with_memory_space_constraint(x, pltpu.HBM)


def near(x):
    return pltpu.with_memory_space_constraint(x, pltpu.VMEM)


def fixed(shape):
    return pl.BlockSpec(shape, lambda j, o: (0,) * len(shape))


def call(kernel, name, steps, scalars, ins, in_specs, outs, out_specs, flops, scratch=(), aliases=None, light=False):
    moved = sum(a.size * a.dtype.itemsize for a in ins) + sum(
        math.prod(o.shape) * jnp.dtype(o.dtype).itemsize for o in outs
    )
    return pl.pallas_call(
        kernel,
        out_shape=tuple(outs),
        grid_spec=pltpu.PrefetchScalarGridSpec(
            num_scalar_prefetch=1,
            grid=(steps,),
            in_specs=in_specs,
            out_specs=out_specs,
            scratch_shapes=list(scratch),
        ),
        input_output_aliases=aliases or {},
        compiler_params=pltpu.CompilerParams(vmem_limit_bytes=(16 if light else 24) * MIB),
        cost_estimate=pl.CostEstimate(
            flops=1 if light else flops, bytes_accessed=1 if light else moved, transcendentals=0
        ),
        name=name,
    )(scalars, *ins)


def cut_kernel(_, x_ref, a_ref, b_ref):
    tall = a_ref.shape[0]
    a_ref[...] = x_ref[:tall, :]
    b_ref[...] = x_ref[tall:, :]


def cut_call(x, half, cost):
    rows, width = x.shape
    quarter = (rows // 4, width)
    return call(
        cut_kernel,
        "cut",
        1,
        jnp.zeros((1,), jnp.int32),
        (x,),
        [pl.BlockSpec((rows // 2, width), lambda j, o: (half, 0))],
        (struct(quarter, x.dtype),) * 2,
        [fixed(quarter)] * 2,
        cost,
    )


def decay_kernel(chunk, _, rate_ref, along_ref, inside_ref, down_ref, tail_ref, end_ref, half_ref):
    heads, rows = rate_ref.shape
    lane = lax.broadcasted_iota(jnp.int32, (heads, chunk), 1)
    base = jnp.zeros((heads, 1), F32)
    insides, wholes = [], []
    for c in range(rows // chunk):
        x = rate_ref[:, c * chunk : (c + 1) * chunk]
        step = 1
        while step < chunk:
            x = x + jnp.where(lane >= step, pltpu.roll(x, step, 1), 0.0)
            step *= 2
        insides.append(x)
        wholes.append(x + base)
        base = base + x[:, chunk - 1 :]
    inside, whole = jnp.concatenate(insides, axis=1), jnp.concatenate(wholes, axis=1)
    along_ref[...] = inside
    inside_ref[...] = inside.T
    down_ref[...] = whole.T
    tail_ref[...] = jnp.broadcast_to(base, tail_ref.shape)
    end_ref[...] = jnp.exp(whole - base)
    half_ref[...] = jnp.broadcast_to(jnp.exp(whole[:, rows // 2 - 1 : rows // 2] - base), half_ref.shape)


def decay_call(rate, chunk):
    heads, rows = rate.shape
    return call(
        functools.partial(decay_kernel, chunk),
        "decay",
        1,
        jnp.zeros((1,), jnp.int32),
        (rate,),
        [fixed((heads, rows))],
        (
            struct((heads, rows), F32),
            struct((rows, heads), F32),
            struct((rows, heads), F32),
            struct((heads, 128), F32),
            struct((heads, rows), F32),
            struct((heads, 128), F32),
        ),
        [
            fixed((heads, rows)),
            fixed((rows, heads)),
            fixed((rows, heads)),
            fixed((heads, 128)),
            fixed((heads, rows)),
            fixed((heads, 128)),
        ],
        heads * rows * 16,
    )


def by_core(places, body):
    for core in (0, 1):

        @pl.when(places[4] == core)
        def _(core=core):
            body(core)


def column(table, head):
    lane = lax.broadcasted_iota(jnp.int32, table.shape, 1)
    return jnp.sum(jnp.where(lane == head, table, 0.0), axis=1, keepdims=True)


def scores(q, k, v, along, down, state):
    rows = q.shape[0]
    causal = lax.broadcasted_iota(jnp.int32, (rows, rows), 0) >= lax.broadcasted_iota(
        jnp.int32, (rows, rows), 1
    )
    decay = jnp.exp(jnp.minimum(along - down, 0.0))
    weights = jnp.where(causal, dot(q, k, ((1,), (1,))) * decay, 0.0).astype(BF16)
    return dot(weights, v) + dot(q, state.astype(BF16)) * jnp.exp(-down)


def faded(q, down):
    return (q.astype(F32) * jnp.exp(-down)).astype(BF16)


def advance(k, v, down, state):
    last = down[down.shape[0] - 1 :, :]
    scaled = (k.astype(F32) * jnp.exp(down - last)).astype(BF16)
    return jnp.exp(-last) * state + dot(scaled, v, ((0,), (0,)))


def first_kernel(layout, added, chunk, group, size, _, *refs):
    count = sum(layout)
    x_refs, w_refs, refs = refs[:count], refs[count : count + len(layout)], refs[count + len(layout) :]
    passed_refs, held = refs[added + 5 : -1], refs[-1]
    along_ref, inside_ref, q_ref, within_ref, state_ref = refs[added : added + 5]
    for ref in passed_refs:
        ref[...] = w_refs[0][...]
    j = pl.program_id(0)
    rows = held.shape[1]

    @pl.when(j == 0)
    def _():
        at = 0
        for i, parts in enumerate(layout):
            tall = rows // parts
            for p in range(parts):
                held[i, p * tall : (p + 1) * tall, :] = x_refs[at][...]
                at += 1

    def project(c):
        total = dot(held[0], w_refs[0][c])
        for i in range(1, len(layout)):
            total = total + dot(held[i], w_refs[i][c])
        if added:
            total = total + refs[0][c]
        return total.astype(BF16)

    q_all, k_all, v_all = project(0), project(1), project(2)
    for a in range(group):
        head = j * group + a
        lanes = slice(a * size, (a + 1) * size)
        state, base = jnp.zeros((size, size), F32), jnp.zeros((1, 1), F32)
        for c in range(rows // chunk):
            here = slice(c * chunk, (c + 1) * chunk)
            q, k, v = q_all[here, lanes], k_all[here, lanes], v_all[here, lanes]
            down = column(inside_ref[here, :], head)
            along = along_ref[pl.ds(head, 1), here]
            q_ref[here, lanes] = faded(q, base + down)
            within_ref[here, lanes] = scores(q, k, v, along, down, state).astype(BF16)
            state, base = advance(k, v, down, state), base + down[chunk - 1 :, :]
        state_ref[a] = state


def first_call(places, blocks, pieces, before, w_qkv, along, inside, rows, chunk, size, group):
    heads = along.shape[0]
    cols = group * size
    flat = [p for piece in pieces for p in piece]
    depth = flat[0].shape[1]

    def block(i):
        return pl.BlockSpec((3, depth, cols), lambda j, o: (0, o[blocks[i]] if blocks else 0, j))

    wide = pl.BlockSpec((rows, cols), lambda j, o: (0, j))
    return call(
        functools.partial(
            first_kernel, tuple(len(p) for p in pieces), bool(before), chunk, group, size
        ),
        "first",
        heads // group,
        places,
        (*flat, *[w_qkv] * len(pieces), *before, along, inside),
        [
            pl.BlockSpec((rows // len(piece), depth), lambda j, o: (0, 0))
            for piece in pieces
            for _ in piece
        ]
        + [block(i) for i in range(len(pieces))]
        + [pl.BlockSpec((3, rows, cols), lambda j, o: (0, 0, j)) for _ in before]
        + [fixed((heads, rows)), fixed((rows, heads))],
        (
            struct((rows, heads * size), BF16),
            struct((rows, heads * size), BF16),
            struct((heads, size, size), F32),
            *[struct((3, depth, heads * size), BF16) for _ in before],
        ),
        [wide, wide, pl.BlockSpec((group, size, size), lambda j, o: (j, 0, 0))]
        + [pl.BlockSpec((3, depth, cols), lambda j, o: (0, 0, j)) for _ in before],
        2 * rows * 3 * heads * size * depth * len(pieces),
        scratch=[pltpu.VMEM((len(pieces), rows, depth), BF16)],
    )


def own_part_kernel(_, x_ref, w_ref, out_ref):
    for c in range(3):
        out_ref[c] = dot(x_ref[...], w_ref[c])


def own_part_call(places, tokens, w_qkv, cols):
    rows, depth = tokens.shape
    width = w_qkv.shape[2]
    return call(
        own_part_kernel,
        "own_part",
        width // cols,
        places,
        (tokens, w_qkv),
        [fixed((rows, depth)), pl.BlockSpec((3, depth, cols), lambda j, o: (0, o[0], j))],
        (pltpu.HBM((3, rows, width), F32),),
        [pl.BlockSpec((3, rows, cols), lambda j, o: (0, 0, j))],
        2 * rows * depth * width * 3,
    )[0]


def part_kernel(layout, _, *refs):
    count = sum(layout)
    x_refs, w_refs = refs[:count], refs[count : count + len(layout)]
    before_ref, out_ref, held = refs[-3:]
    rows = held.shape[1]

    @pl.when(pl.program_id(0) == 0)
    def _():
        at = 0
        for i, parts in enumerate(layout):
            tall = rows // parts
            for p in range(parts):
                held[i, p * tall : (p + 1) * tall, :] = x_refs[at][...]
                at += 1

    for c in range(3):
        total = dot(held[0], w_refs[0][c])
        for i in range(1, len(layout)):
            total = total + dot(held[i], w_refs[i][c])
        out_ref[c] = total + before_ref[c]


def part_call(places, blocks, pieces, w_qkv, rows, cols, before, at):
    flat = [p for piece in pieces for p in piece]
    depth = flat[0].shape[1]
    width = w_qkv.shape[2]

    def block(i):
        return pl.BlockSpec((3, depth, cols), lambda j, o: (0, o[blocks[i]], j))

    ins = [*flat, *[w_qkv] * len(pieces)]
    specs = [
        pl.BlockSpec((rows // len(piece), depth), lambda j, o: (0, 0)) for piece in pieces for _ in piece
    ] + [block(i) for i in range(len(pieces))]
    ins.append(before)
    specs.append(pl.BlockSpec((3, rows, cols), lambda j, o: (0, at, j)))
    return call(
        functools.partial(part_kernel, tuple(len(p) for p in pieces)),
        "part",
        width // cols,
        places,
        ins,
        specs,
        (struct((3, rows, width), F32),),
        [pl.BlockSpec((3, rows, cols), lambda j, o: (0, 0, j))],
        2 * rows * depth * len(pieces) * width * 3,
        scratch=[pltpu.VMEM((len(pieces), rows, depth), BF16)],
    )[0]


def state_kernel(own, places, xa, xb, w_ref, acc_ref, end_ref, half_ref, state_ref, k_ref, v_ref, out_ref, held):
    tall = xa.shape[0]
    share, size = out_ref.shape[0], out_ref.shape[1]
    held[:tall, :] = xa[...]
    held[tall:, :] = xb[...]

    def body(core):
        base = share * (core if own else 1 - core)
        for pair in range(0, share, 2):
            cols = slice((base + pair) * size, (base + pair + 2) * size)
            keys = (acc_ref[1, :, cols] + dot(held[...], w_ref[1, :, cols])).astype(BF16)
            values = (acc_ref[2, :, cols] + dot(held[...], w_ref[2, :, cols])).astype(BF16)
            k_ref[:, pair * size : (pair + 2) * size] = keys
            v_ref[:, pair * size : (pair + 2) * size] = values
            for a in range(2):
                head = slice(base + pair + a, base + pair + a + 1)
                lanes = slice(a * size, (a + 1) * size)
                scaled = (keys[:, lanes].T.astype(F32) * end_ref[head, 2 * tall :]).astype(BF16)
                end = half_ref[head, :] * state_ref[base + pair + a] + dot(scaled, values[:, lanes])
                out_ref[pair + a] = end.astype(out_ref.dtype)

    by_core(places, body)


def state_call(places, far, w_far, acc, to_end, half_fade, state, own):
    _, rows, width = acc.shape
    heads, size = state.shape[0], state.shape[1]
    ins = [near(x) for x in (*far, w_far, acc)] + [to_end, half_fade, near(state)]
    outs = (
        struct((rows, width // 2), BF16),
        struct((rows, width // 2), BF16),
        struct((heads // 2, size, size), F32 if own else BF16),
    )
    scratch = [pltpu.VMEM((rows, far[0].shape[1]), BF16)]
    kernel = functools.partial(state_kernel, own)
    return small_call(kernel, "states", places, ins, outs, 16, scratch)


def later_kernel(own, chunk, places, xa, xb, w_ref, acc_ref, k_ref, v_ref, *refs):
    along_ref, inside_ref, down_ref, state_ref, q_ref, within_ref, held = refs
    tall, rows = xa.shape[0], held.shape[0]
    share, size = state_ref.shape[0] // 2, state_ref.shape[1]
    held[:tall, :] = xa[...]
    held[tall:, :] = xb[...]

    def body(core):
        base = share * (core if own else 1 - core)
        for a in range(share):
            head, lanes = base + a, slice(a * size, (a + 1) * size)
            if a % 2 == 0:
                pair = slice(head * size, (head + 2) * size)
                queries = (acc_ref[0, :, pair] + dot(held[...], w_ref[0, :, pair])).astype(BF16)
            state = state_ref[head]
            for c in range(rows // chunk):
                here = slice(c * chunk, (c + 1) * chunk)
                there = slice(rows + c * chunk, rows + (c + 1) * chunk)
                q = queries[here, (a % 2) * size : (a % 2 + 1) * size]
                k, v = k_ref[here, lanes], v_ref[here, lanes]
                along, down = along_ref[head : head + 1, there], inside_ref[there, head : head + 1]
                q_ref[here, lanes] = faded(q, down_ref[there, head : head + 1])
                within_ref[here, lanes] = scores(q, k, v, along, down, state).astype(BF16)
                if c + 1 < rows // chunk:
                    state = advance(k, v, down, state)

    by_core(places, body)


def later_call(places, far, w_far, acc, k, v, along, inside, down, state, chunk, own):
    _, rows, width = acc.shape
    ins = [near(x) for x in (*far, w_far, acc, k, v)] + [along, inside, down, near(state)]
    outs = (struct((rows, width // 2), BF16),) * 2
    scratch = [pltpu.VMEM((rows, far[0].shape[1]), BF16)]
    kernel = functools.partial(later_kernel, own, chunk)
    return small_call(kernel, "later", places, ins, outs, 16, scratch)


def fades(tail_ref, other_ref, place, head):
    own, other = tail_ref[pl.ds(head, 1), :], other_ref[pl.ds(head, 1), :]
    first = jnp.where(place == 0, own, other)
    return jnp.exp(-first), jnp.exp(first - (own + other)), jnp.exp(-(own + other))


def chip_kernel(places, state_ref, come_ref, tail_ref, other_ref, prior_ref, *out_refs):
    leaving_ref, alone_ref, chip_ref, first_ref = out_refs
    core = places[4]
    share = come_ref.shape[0]
    for i in range(share):
        head = core * share + i
        _, second_fade, fade = fades(tail_ref, other_ref, core, head)
        ours, come = state_ref[i], come_ref[i].astype(F32)
        first, second = jnp.where(core == 0, ours, come), jnp.where(core == 0, come, ours)
        total = second_fade * first + second
        first_ref[i] = first
        chip_ref[i] = total
        alone_ref[i] = total.astype(BF16)
        leaving_ref[i] = (fade * prior_ref[head] + total).astype(BF16)


def pass_kernel(places, come_ref, chip_ref, tail_ref, other_ref, leaving_ref):
    share = come_ref.shape[0]
    for i in range(share):
        fade = fades(tail_ref, other_ref, places[4], places[4] * share + i)[2]
        leaving_ref[i] = (fade * come_ref[i].astype(F32) + chip_ref[i]).astype(BF16)


def enter_kernel(
    places, come_ref, alone_ref, second_ref, third_ref, first_ref, tail_ref, other_ref, below_ref, prior_ref, *out_refs
):
    here_ref, passed_ref = out_refs
    core, chip = places[4], places[5]
    share = come_ref.shape[0]
    for i in range(share):
        head = core * share + i
        below = jnp.exp(-below_ref[pl.ds(head, 1), :])
        through = below * third_ref[i].astype(F32) + alone_ref[i].astype(F32)
        state = jnp.where(chip == 0, prior_ref[head], come_ref[i].astype(F32))
        state = jnp.where(chip == 2, second_ref[i].astype(F32), state)
        state = jnp.where(chip == 3, through, state)
        later = fades(tail_ref, other_ref, core, head)[0] * state + first_ref[i]
        here_ref[i] = jnp.where(core == 0, state, later).astype(BF16)
        passed_ref[i] = jnp.where(core == 0, later, state).astype(BF16)


def small_call(kernel, name, places, ins, outs, limit=4, scratch=()):
    whole = pl.BlockSpec(memory_space=pltpu.VMEM)
    return pl.pallas_call(
        kernel,
        out_shape=tuple(outs),
        in_specs=[pl.BlockSpec(memory_space=pltpu.SMEM)] + [whole] * len(ins),
        out_specs=[whole] * len(outs),
        scratch_shapes=list(scratch),
        compiler_params=pltpu.CompilerParams(vmem_limit_bytes=limit * MIB),
        cost_estimate=pl.CostEstimate(flops=1, bytes_accessed=1, transcendentals=0),
        name=name,
    )(places, *ins)


def chip_call(places, state, come, tails, prior):
    outs = [struct(come.shape, kind) for kind in (BF16, BF16, F32, F32)]
    return small_call(chip_kernel, "chip_state", places, (state, come, *tails, prior), outs)


def pass_call(places, come, chip_state, tails):
    outs = (struct(come.shape, BF16),)
    return small_call(pass_kernel, "pass_on", places, (come, chip_state, *tails), outs)[0]


def enter_call(places, come, alone, second, third, first, tails, below, prior):
    outs = (struct(come.shape, BF16),) * 2
    ins = (come, alone, second, third, first, *tails, below, prior)
    return small_call(enter_kernel, "enter", places, ins, outs)


def columns(w_ref, block, width):
    return w_ref[:, pl.ds(pl.multiple_of(block * width, width), width)]


WHOLE = pl.BlockSpec(memory_space=pltpu.VMEM)


def normalise(q, within, entering):
    size = entering.shape[0]
    ones = jnp.ones((size, size), BF16)
    combined = within.astype(F32) + dot(q, entering)
    square = combined * combined
    high = square.astype(BF16)
    low = (square - high.astype(F32)).astype(BF16)
    power = (dot(high, ones) + dot(low, ones)) * (1.0 / size)
    return (combined * lax.rsqrt(power + 1e-06)).astype(BF16)


def normalise_all(places, q_refs, within_refs, here_ref, there_ref, rows, out_ref):
    share, size = here_ref.shape[0], here_ref.shape[1]

    def lanes(a):
        return slice(a * size, (a + 1) * size)

    if len(q_refs) == 1:
        for a in range(2 * share):
            entering = jnp.where(places[4] == a // share, here_ref[a % share], there_ref[a % share])
            q, within = q_refs[0][rows, lanes(a)], within_refs[0][rows, lanes(a)]
            out_ref[:, lanes(a)] = normalise(q, within, entering)
        return

    def body(core):
        for a in range(2 * share):
            own, at = a // share == core, a % share
            q, within = q_refs[int(own)][rows, lanes(at)], within_refs[int(own)][rows, lanes(at)]
            entering = here_ref[at] if own else there_ref[at]
            out_ref[:, lanes(a)] = normalise(q, within, entering)

    by_core(places, body)


def head_kernel(count, places, *refs):
    q_refs, within_refs, refs = refs[:count], refs[count : 2 * count], refs[2 * count :]
    here_ref, there_ref, w_ref, normed_ref = refs[:4]
    out_refs = refs[4:]
    tall, width = normed_ref.shape[0] // 2, out_refs[0].shape[1]
    for p, out_ref in enumerate(out_refs):
        rows = slice(p * tall, (p + 1) * tall)
        normed = normed_ref.at[rows]
        normalise_all(places, q_refs, within_refs, here_ref, there_ref, rows, normed)
        out_ref[:tall, :] = dot(normed[...], columns(w_ref, places[3], width)).astype(BF16)
        if out_ref.shape[0] > tall:
            out_ref[tall:, :] = dot(normed[...], columns(w_ref, places[1 + p], width)).astype(BF16)


def head_call(places, q, within, entering, w_out, width, near_too):
    rows, cols = q[0].shape[0], w_out.shape[0]
    out = struct((rows if near_too else rows // 2, width), BF16)
    ins = [near(x) for x in (*q, *within, *entering)] + [w_out]
    outs = (struct((rows, cols), BF16), out, out)
    return small_call(functools.partial(head_kernel, len(q)), "heads", places, ins, outs, 12)


def mixed_kernel(places, normed_ref, x_ref, y_ref, w_ref, out_x_ref, out_y_ref):
    tall, width = x_ref.shape
    for p, (out_ref, come_ref) in enumerate(((out_x_ref, x_ref), (out_y_ref, y_ref))):

        @pl.when(pl.program_id(0) == p)
        def _(p=p, out_ref=out_ref, come_ref=come_ref):
            total = dot(normed_ref[...], columns(w_ref, places[1 + p], width))
            summed = total[(1 - p) * tall : (2 - p) * tall] + come_ref[...].astype(F32)
            out_ref[:tall, :] = summed.astype(BF16)
            out_ref[tall:, :] = total[p * tall : (p + 1) * tall].astype(BF16)


def mixed_call(places, normed, for_x, for_y, w_out, width):
    rows, cols = normed.shape
    quarter, half = (rows // 2, width), (rows, width)
    return call(
        mixed_kernel,
        "sum_and_near",
        2,
        places,
        (normed, for_x, for_y, w_out),
        [fixed((rows, cols)), fixed(quarter), fixed(quarter), WHOLE],
        (struct(half, BF16),) * 2,
        [fixed(half)] * 2,
        4 * rows * cols * width,
        light=True,
    )


def pair_kernel(places, normed_ref, x_ref, y_ref, w_ref, out_x_ref, out_y_ref):
    tall, width = out_x_ref.shape

    @pl.when(pl.program_id(0) == 0)
    def _():
        total = dot(normed_ref[tall:, :], columns(w_ref, places[1], width)) + x_ref[...].astype(F32)
        out_x_ref[...] = total.astype(BF16)

    @pl.when(pl.program_id(0) == 1)
    def _():
        total = dot(normed_ref[:tall, :], columns(w_ref, places[2], width)) + y_ref[...].astype(F32)
        out_y_ref[...] = total.astype(BF16)


def pair_call(places, normed, for_x, for_y, w_out, width):
    rows, cols = normed.shape
    quarter = (rows // 2, width)
    return call(
        pair_kernel,
        "sum_pair",
        2,
        places,
        (normed, for_x, for_y, w_out),
        [fixed((rows, cols)), fixed(quarter), fixed(quarter), WHOLE],
        (struct(quarter, BF16),) * 2,
        [fixed(quarter)] * 2,
        2 * rows * cols * width,
        light=True,
    )


def own_kernel(places, normed_ref, w_ref, *refs):
    out_ref = refs[-1]
    tall, width = out_ref.shape
    each = len(refs) // 2
    for p in range(2):
        rows = slice(p * tall, (p + 1) * tall)

        @pl.when(pl.program_id(0) == p)
        def _(p=p, rows=rows):
            total = dot(normed_ref[rows, :], columns(w_ref, places[0], width))
            for ref in refs[p * each : (p + 1) * each]:
                total = total + ref[...].astype(F32)
            out_ref[...] = total.astype(BF16)


def own_call(places, normed, first, second, w_out, width, height):
    rows, cols = normed.shape
    quarter = (rows // 2, width)
    return call(
        own_kernel,
        "own_block",
        2,
        places,
        (normed, w_out, *[a for a, _ in (*first, *second)]),
        [fixed((rows, cols)), WHOLE]
        + [pl.BlockSpec(quarter, lambda i, o, at=at: (at, 0)) for _, at in (*first, *second)],
        (struct((rows * height, width), BF16),),
        [pl.BlockSpec(quarter, lambda i, o: (i, 0))],
        2 * rows * cols * width,
        light=True,
    )[0]


def last_kernel(_, kept_ref, a_ref, b_ref, above_ref, out_ref):
    del above_ref

    @pl.when(pl.program_id(0) == 0)
    def _():
        out_ref[...] = (kept_ref[...].astype(F32) + a_ref[...].astype(F32)).astype(BF16)

    @pl.when(pl.program_id(0) == 1)
    def _():
        out_ref[...] = (kept_ref[...].astype(F32) + b_ref[...].astype(F32)).astype(BF16)


def last_call(kept, a, b, above):
    tall, width = a.shape
    return call(
        last_kernel,
        "last_add",
        2,
        jnp.zeros((1,), jnp.int32),
        (kept, a, b, above),
        [
            pl.BlockSpec((tall, width), lambda j, o: (j, 0)),
            fixed((tall, width)),
            fixed((tall, width)),
            pl.BlockSpec(memory_space=pl.ANY),
        ],
        (struct(above.shape, BF16),),
        [pl.BlockSpec((tall, width), lambda j, o: (2 + j, 0))],
        tall * width,
        aliases={4: 0},
    )[0]


def local(n_head, n_seq, tokens, w_qkv, w_out, decay_rate, prior_state):
    rows, width = tokens.shape
    heads, size = prior_state.shape[0], prior_state.shape[1]
    square = n_head == 4
    place = lax.axis_index("head").astype(jnp.int32)
    quarter = rows // 4
    group = 2 if heads % 2 == 0 else 1
    cols = group * size

    over_x = functools.partial(lax.ppermute, axis_name="head", perm=[(i, i ^ 1) for i in range(n_head)])
    over_y = functools.partial(lax.ppermute, axis_name="head", perm=[(i, i ^ 2) for i in range(n_head)])

    pos = lax.axis_index("seq").astype(jnp.int32)
    core, chip = pos % 2, pos // 2
    flips = (0, 1, 2, 3) if square else (0, 0, 0, 0)
    places = jnp.stack([*[place ^ f for f in flips], core, chip])

    along, inside, down, tail, to_end, half_fade = decay_call(decay_rate, quarter)
    n_chips = n_seq // 2
    swap = functools.partial(lax.ppermute, axis_name="seq", perm=[(i, i ^ 1) for i in range(n_seq)])

    def hop(x, *pairs):
        perm = [(2 * a + c, 2 * b + c) for a, b in pairs for c in range(2)]
        return lax.ppermute(x, "seq", perm=perm)

    def chip_tails(tail):
        other = swap(tail)
        return other, tail + other, hop(tail + other, (2, 3)) if n_chips == 4 else None

    if square:
        tokens, w_qkv = stay(tokens), stay(w_qkv)
        q0, q1 = cut_call(tokens, 0, 1)
        x0, y1 = over_x(q0), over_y(q1)
        x1, y0 = over_x(after(q1, tail)), over_y(after(q0, tail))
        acc = own_part_call(places, tokens, w_qkv, cols)
        q2, q3 = cut_call(stay(after(tokens, acc, x0, y1)), 1, 10**10)
        fy0, fx1 = over_y(x0), over_x(y1)
        tail_other, tail_chip, tail_below = chip_tails(after(tail, acc, x0, y1))
        x2 = over_x(after(q2, x1, y0, tail_chip))
        y3 = over_y(after(q3, x1, y0, tail_chip))
        acc_a = part_call(
            places,
            (1, 2),
            [(x0, x1), (y0, y1)],
            w_qkv,
            2 * quarter,
            cols,
            before=stay(after(acc, tail_chip)),
            at=0,
        )
        earlier = (fy0, fx1, acc_a) if tail_below is None else (fy0, fx1, acc_a, tail_below)
        x3, y2 = over_x(after(q3, *earlier)), over_y(after(q2, *earlier))
        query_a, within_a, state, w_far = first_call(
            places,
            (3,),
            [(fy0, fx1)],
            (acc_a,),
            w_qkv,
            along,
            inside,
            2 * quarter,
            quarter,
            size,
            group,
        )
        fy2, fx3 = over_y(after(x2, state)), over_x(after(y3, state))
        acc_b = part_call(
            places,
            (1, 2),
            [(x2, x3), (y2, y3)],
            w_qkv,
            2 * quarter,
            cols,
            before=stay(acc),
            at=1,
        )
        far = (fy2, fx3)
        middle = state
        k, v, sent = state_call(places, far, w_far, acc_b, to_end, half_fade, middle, False)
        k_own, v_own, state = state_call(
            places, far, w_far, acc_b, to_end, half_fade, after(middle, sent), True
        )
    else:
        tail_other, tail_chip, tail_below = chip_tails(tail)
        gathered = lax.all_gather(tokens, "head", axis=1, tiled=True)
        query, within, state = first_call(
            places, (), [(gathered,)], (), w_qkv, along, inside, rows, quarter, size, group
        )

    tails = (tail, tail_other)

    def scores_of_later(own, *earlier):
        start = after(middle, *earlier)
        keys, values = (k_own, v_own) if own else (k, v)
        tables = (along, inside, down, start)
        return later_call(places, far, w_far, acc_b, keys, values, *tables, quarter, own)

    if square and n_chips == 4:
        leaving, alone, chip_state, first = chip_call(
            places, near(state), near(swap(sent)), tails, prior_state
        )
        alone = hop(alone, (2, 3))
        arriving = near(hop(leaving, (0, 1)))
        leaving = pass_call(places, arriving, chip_state, tails)
        to_third, to_second = hop(leaving, (1, 3)), hop(leaving, (1, 2))
        query_b, within_b = scores_of_later(False, leaving)
        alone, to_third, to_second, _ = lax.optimization_barrier((alone, to_third, to_second, query_b))
        here, passed = enter_call(
            places,
            arriving,
            near(alone),
            near(to_second),
            near(to_third),
            first,
            tails,
            tail_below,
            prior_state,
        )
    else:
        share = heads // 2

        def mine(x, core=core):
            return lax.dynamic_slice_in_dim(x, core * share, share, 0)

        def decay(tail):
            return jnp.exp(-mine(tail)[:, :1, None])

        ours = state if square else mine(state)
        other = swap(sent if square else mine(state, 1 - core).astype(BF16)).astype(F32)
        first = jnp.where(core == 0, ours, other)
        second = jnp.where(core == 0, other, ours)
        chip_state = decay(jnp.where(core == 0, tail_other, tail)) * first + second
        chip_entering = mine(prior_state)
        for step in range(n_chips - 1):
            leaving = (decay(tail_chip) * chip_entering + chip_state).astype(BF16)
            arriving = hop(leaving, (step, step + 1))
            chip_entering = jnp.where(chip == step + 1, arriving.astype(F32), chip_entering)
        other = decay(jnp.where(core == 0, tail, tail_other)) * chip_entering + first
        here = jnp.where(core == 0, chip_entering, other).astype(BF16)
        passed = jnp.where(core == 0, other, chip_entering).astype(BF16)
    entering = (here, swap(passed))

    w_whole, w_out = w_out, near(w_out)
    if not square:
        halves = [
            head_call(
                places,
                (query[r * rows // 2 : (r + 1) * rows // 2],),
                (within[r * rows // 2 : (r + 1) * rows // 2],),
                entering,
                w_out,
                width,
                False,
            )[0]
            for r in range(2)
        ]
        partial = dot(jnp.concatenate(halves), w_whole).astype(BF16)
        return lax.psum_scatter(partial, "head", scatter_dimension=1, tiled=True)

    if n_chips != 4:
        query_b, within_b = scores_of_later(False)
    na, far0, far1 = head_call(places, (query_a,), (within_a,), entering, w_out, width, False)
    query_c, within_c = scores_of_later(True, na)
    far0, far1 = over_x(far0), over_y(far1)
    nb, by_x2, by_y2 = head_call(
        places, (query_b, query_c), (within_b, within_c), entering, w_out, width, True
    )
    by_x2, by_y2 = over_x(by_x2), over_y(by_y2)
    by_x, by_y = mixed_call(places, after(na, nb), far1, far0, w_out, width)
    by_x2, by_y2 = after(by_x2, by_x), after(by_y2, by_x)
    by_x, by_y = over_x(by_x), over_y(by_y)
    sum3, sum2 = pair_call(places, nb, by_y2, by_x2, w_out, width)
    sum3, sum2 = over_x(sum3), over_y(sum2)
    below = own_call(places, after(nb, by_x, by_y), ((by_x2, 1),), ((by_y2, 1),), w_out, width, 1)
    above = own_call(places, na, ((by_x, 1), (by_y, 0)), ((by_y, 1), (by_x, 0)), w_out, width, 2)
    return last_call(below, sum2, sum3, above)


def solution(mesh):
    in_specs = (
        P("seq", "head"),
        P(None, None, "head"),
        P("head", None),
        P("head", "seq"),
        P("head", None, None),
    )
    body = functools.partial(local, mesh.shape["head"], mesh.shape["seq"])
    return jax.shard_map(
        body, mesh=mesh, in_specs=in_specs, out_specs=P("seq", "head"), check_vma=False
    )
```

```python
import functools
import math

import jax
import jax.numpy as jnp
from jax import lax
from jax.experimental import pallas as pl
from jax.experimental.pallas import tpu as pltpu
from jax.sharding import PartitionSpec as P

BF16, F32 = jnp.bfloat16, jnp.float32
MIB = 1024 * 1024


def dot(a, b, contract=((1,), (0,))):
    return lax.dot_general(a, b, (contract, ((), ())), preferred_element_type=F32)


def after(x, *earlier):
    return lax.optimization_barrier((x, *earlier))[0]


def struct(shape, dtype):
    return jax.ShapeDtypeStruct(shape, dtype)


def stay(x):
    return pltpu.with_memory_space_constraint(x, pltpu.HBM)


def near(x):
    return pltpu.with_memory_space_constraint(x, pltpu.VMEM)


def fixed(shape):
    return pl.BlockSpec(shape, lambda j, o: (0,) * len(shape))


def call(kernel, name, steps, scalars, ins, in_specs, outs, out_specs, flops, scratch=(), aliases=None, light=False):
    moved = sum(a.size * a.dtype.itemsize for a in ins) + sum(
        math.prod(o.shape) * jnp.dtype(o.dtype).itemsize for o in outs
    )
    return pl.pallas_call(
        kernel,
        out_shape=tuple(outs),
        grid_spec=pltpu.PrefetchScalarGridSpec(
            num_scalar_prefetch=1,
            grid=(steps,),
            in_specs=in_specs,
            out_specs=out_specs,
            scratch_shapes=list(scratch),
        ),
        input_output_aliases=aliases or {},
        compiler_params=pltpu.CompilerParams(vmem_limit_bytes=(16 if light else 24) * MIB),
        cost_estimate=pl.CostEstimate(
            flops=1 if light else flops, bytes_accessed=1 if light else moved, transcendentals=0
        ),
        name=name,
    )(scalars, *ins)


def cut_kernel(_, x_ref, a_ref, b_ref):
    tall = a_ref.shape[0]
    a_ref[...] = x_ref[:tall, :]
    b_ref[...] = x_ref[tall:, :]


def cut_call(x, half, cost):
    rows, width = x.shape
    quarter = (rows // 4, width)
    return call(
        cut_kernel,
        "cut",
        1,
        jnp.zeros((1,), jnp.int32),
        (x,),
        [pl.BlockSpec((rows // 2, width), lambda j, o: (half, 0))],
        (struct(quarter, x.dtype),) * 2,
        [fixed(quarter)] * 2,
        cost,
    )


def decay_kernel(chunk, _, rate_ref, along_ref, inside_ref, down_ref, tail_ref, end_ref, half_ref):
    heads, rows = rate_ref.shape
    lane = lax.broadcasted_iota(jnp.int32, (heads, chunk), 1)
    base = jnp.zeros((heads, 1), F32)
    insides, wholes = [], []
    for c in range(rows // chunk):
        x = rate_ref[:, c * chunk : (c + 1) * chunk]
        step = 1
        while step < chunk:
            x = x + jnp.where(lane >= step, pltpu.roll(x, step, 1), 0.0)
            step *= 2
        insides.append(x)
        wholes.append(x + base)
        base = base + x[:, chunk - 1 :]
    inside, whole = jnp.concatenate(insides, axis=1), jnp.concatenate(wholes, axis=1)
    along_ref[...] = inside
    inside_ref[...] = inside.T
    down_ref[...] = whole.T
    tail_ref[...] = jnp.broadcast_to(base, tail_ref.shape)
    end_ref[...] = jnp.exp(whole - base)
    half_ref[...] = jnp.broadcast_to(jnp.exp(whole[:, rows // 2 - 1 : rows // 2] - base), half_ref.shape)


def decay_call(rate, chunk):
    heads, rows = rate.shape
    return call(
        functools.partial(decay_kernel, chunk),
        "decay",
        1,
        jnp.zeros((1,), jnp.int32),
        (rate,),
        [fixed((heads, rows))],
        (
            struct((heads, rows), F32),
            struct((rows, heads), F32),
            struct((rows, heads), F32),
            struct((heads, 128), F32),
            struct((heads, rows), F32),
            struct((heads, 128), F32),
        ),
        [
            fixed((heads, rows)),
            fixed((rows, heads)),
            fixed((rows, heads)),
            fixed((heads, 128)),
            fixed((heads, rows)),
            fixed((heads, 128)),
        ],
        heads * rows * 16,
    )


def column(table, head):
    lane = lax.broadcasted_iota(jnp.int32, table.shape, 1)
    return jnp.sum(jnp.where(lane == head, table, 0.0), axis=1, keepdims=True)


def scores(q, k, v, along, down, state):
    rows = q.shape[0]
    causal = lax.broadcasted_iota(jnp.int32, (rows, rows), 0) >= lax.broadcasted_iota(
        jnp.int32, (rows, rows), 1
    )
    decay = jnp.exp(jnp.minimum(along - down, 0.0))
    weights = jnp.where(causal, dot(q, k, ((1,), (1,))) * decay, 0.0).astype(BF16)
    return dot(weights, v) + dot(q, state.astype(BF16)) * jnp.exp(-down)


def faded(q, down):
    return (q.astype(F32) * jnp.exp(-down)).astype(BF16)


def advance(k, v, down, state):
    last = down[down.shape[0] - 1 :, :]
    scaled = (k.astype(F32) * jnp.exp(down - last)).astype(BF16)
    return jnp.exp(-last) * state + dot(scaled, v, ((0,), (0,)))


def first_kernel(layout, added, chunk, group, size, _, *refs):
    count = sum(layout)
    x_refs, w_refs, refs = refs[:count], refs[count : count + len(layout)], refs[count + len(layout) :]
    passed_refs, held = refs[added + 5 : -1], refs[-1]
    along_ref, inside_ref, q_ref, within_ref, state_ref = refs[added : added + 5]
    for ref in passed_refs:
        ref[...] = w_refs[0][...]
    j = pl.program_id(0)
    rows = held.shape[1]

    @pl.when(j == 0)
    def _():
        at = 0
        for i, parts in enumerate(layout):
            tall = rows // parts
            for p in range(parts):
                held[i, p * tall : (p + 1) * tall, :] = x_refs[at][...]
                at += 1

    def project(c):
        total = dot(held[0], w_refs[0][c])
        for i in range(1, len(layout)):
            total = total + dot(held[i], w_refs[i][c])
        if added:
            total = total + refs[0][c]
        return total.astype(BF16)

    q_all, k_all, v_all = project(0), project(1), project(2)
    for a in range(group):
        head = j * group + a
        lanes = slice(a * size, (a + 1) * size)
        state, base = jnp.zeros((size, size), F32), jnp.zeros((1, 1), F32)
        for c in range(rows // chunk):
            here = slice(c * chunk, (c + 1) * chunk)
            q, k, v = q_all[here, lanes], k_all[here, lanes], v_all[here, lanes]
            down = column(inside_ref[here, :], head)
            along = along_ref[pl.ds(head, 1), here]
            q_ref[here, lanes] = faded(q, base + down)
            within_ref[here, lanes] = scores(q, k, v, along, down, state).astype(BF16)
            state, base = advance(k, v, down, state), base + down[chunk - 1 :, :]
        state_ref[a] = state


def first_call(places, blocks, pieces, before, w_qkv, along, inside, rows, chunk, size, group):
    heads = along.shape[0]
    cols = group * size
    flat = [p for piece in pieces for p in piece]
    depth = flat[0].shape[1]

    def block(i):
        return pl.BlockSpec((3, depth, cols), lambda j, o: (0, o[blocks[i]] if blocks else 0, j))

    wide = pl.BlockSpec((rows, cols), lambda j, o: (0, j))
    return call(
        functools.partial(
            first_kernel, tuple(len(p) for p in pieces), bool(before), chunk, group, size
        ),
        "first",
        heads // group,
        places,
        (*flat, *[w_qkv] * len(pieces), *before, along, inside),
        [
            pl.BlockSpec((rows // len(piece), depth), lambda j, o: (0, 0))
            for piece in pieces
            for _ in piece
        ]
        + [block(i) for i in range(len(pieces))]
        + [pl.BlockSpec((3, rows, cols), lambda j, o: (0, 0, j)) for _ in before]
        + [fixed((heads, rows)), fixed((rows, heads))],
        (
            struct((rows, heads * size), BF16),
            struct((rows, heads * size), BF16),
            struct((heads, size, size), F32),
            *[struct((3, depth, heads * size), BF16) for _ in before],
        ),
        [wide, wide, pl.BlockSpec((group, size, size), lambda j, o: (j, 0, 0))]
        + [pl.BlockSpec((3, depth, cols), lambda j, o: (0, 0, j)) for _ in before],
        2 * rows * 3 * heads * size * depth * len(pieces),
        scratch=[pltpu.VMEM((len(pieces), rows, depth), BF16)],
    )


def own_part_kernel(_, x_ref, w_ref, out_ref):
    for c in range(3):
        out_ref[c] = dot(x_ref[...], w_ref[c])


def own_part_call(places, tokens, w_qkv, cols):
    rows, depth = tokens.shape
    width = w_qkv.shape[2]
    return call(
        own_part_kernel,
        "own_part",
        width // cols,
        places,
        (tokens, w_qkv),
        [fixed((rows, depth)), pl.BlockSpec((3, depth, cols), lambda j, o: (0, o[0], j))],
        (pltpu.HBM((3, rows, width), F32),),
        [pl.BlockSpec((3, rows, cols), lambda j, o: (0, 0, j))],
        2 * rows * depth * width * 3,
    )[0]


def part_kernel(layout, _, *refs):
    count = sum(layout)
    x_refs, w_refs = refs[:count], refs[count : count + len(layout)]
    before_ref, out_ref, held = refs[-3:]
    rows = held.shape[1]

    @pl.when(pl.program_id(0) == 0)
    def _():
        at = 0
        for i, parts in enumerate(layout):
            tall = rows // parts
            for p in range(parts):
                held[i, p * tall : (p + 1) * tall, :] = x_refs[at][...]
                at += 1

    for c in range(3):
        total = dot(held[0], w_refs[0][c])
        for i in range(1, len(layout)):
            total = total + dot(held[i], w_refs[i][c])
        out_ref[c] = total + before_ref[c]


def part_call(places, blocks, pieces, w_qkv, rows, cols, before, at):
    flat = [p for piece in pieces for p in piece]
    depth = flat[0].shape[1]
    width = w_qkv.shape[2]

    def block(i):
        return pl.BlockSpec((3, depth, cols), lambda j, o: (0, o[blocks[i]], j))

    ins = [*flat, *[w_qkv] * len(pieces)]
    specs = [
        pl.BlockSpec((rows // len(piece), depth), lambda j, o: (0, 0)) for piece in pieces for _ in piece
    ] + [block(i) for i in range(len(pieces))]
    ins.append(before)
    specs.append(pl.BlockSpec((3, rows, cols), lambda j, o: (0, at, j)))
    return call(
        functools.partial(part_kernel, tuple(len(p) for p in pieces)),
        "part",
        width // cols,
        places,
        ins,
        specs,
        (struct((3, rows, width), F32),),
        [pl.BlockSpec((3, rows, cols), lambda j, o: (0, 0, j))],
        2 * rows * depth * len(pieces) * width * 3,
        scratch=[pltpu.VMEM((len(pieces), rows, depth), BF16)],
    )[0]


def state_kernel(own, places, xa, xb, w_ref, acc_ref, end_ref, half_ref, state_ref, k_ref, v_ref, out_ref, held):
    tall = xa.shape[0]
    share, size = out_ref.shape[0], out_ref.shape[1]
    held[:tall, :] = xa[...]
    held[tall:, :] = xb[...]
    base = share * (places[4] if own else 1 - places[4])
    for pair in range(0, share, 2):
        cols = pl.ds(pl.multiple_of((base + pair) * size, 2 * size), 2 * size)
        keys = (acc_ref[1, :, cols] + dot(held[...], w_ref[1, :, cols])).astype(BF16)
        values = (acc_ref[2, :, cols] + dot(held[...], w_ref[2, :, cols])).astype(BF16)
        k_ref[:, pair * size : (pair + 2) * size] = keys
        v_ref[:, pair * size : (pair + 2) * size] = values
        for a in range(2):
            head = pl.ds(base + pair + a, 1)
            lanes = slice(a * size, (a + 1) * size)
            scaled = (keys[:, lanes].T.astype(F32) * end_ref[head, 2 * tall :]).astype(BF16)
            end = half_ref[head, :] * state_ref[base + pair + a] + dot(scaled, values[:, lanes])
            out_ref[pair + a] = end.astype(out_ref.dtype)


def state_call(places, far, w_far, acc, to_end, half_fade, state, own):
    _, rows, width = acc.shape
    heads, size = state.shape[0], state.shape[1]
    ins = [near(x) for x in (*far, w_far, acc)] + [to_end, half_fade, near(state)]
    outs = (
        struct((rows, width // 2), BF16),
        struct((rows, width // 2), BF16),
        struct((heads // 2, size, size), F32 if own else BF16),
    )
    scratch = [pltpu.VMEM((rows, far[0].shape[1]), BF16)]
    kernel = functools.partial(state_kernel, own)
    return small_call(kernel, "states", places, ins, outs, 16, scratch)


def later_kernel(half, chunk, places, xa, xb, w_ref, acc_ref, *refs):
    k_ref, v_ref, k_own_ref, v_own_ref, refs = *refs[:4], refs[4:]
    own = places[4] == half
    along_ref, inside_ref, down_ref, state_ref, q_ref, within_ref, held = refs
    tall, rows = xa.shape[0], held.shape[0]
    heads, size = state_ref.shape[0], state_ref.shape[1]
    held[:tall, :] = xa[...]
    held[tall:, :] = xb[...]
    for a in range(heads // 2):
        head = half * heads // 2 + a
        out = slice(a * size, (a + 1) * size)
        if a % 2 == 0:
            pair = slice(head * size, (head + 2) * size)
            queries = (acc_ref[0, :, pair] + dot(held[...], w_ref[0, :, pair])).astype(BF16)
        state = state_ref[head]
        for c in range(rows // chunk):
            here, there = slice(c * chunk, (c + 1) * chunk), slice(rows + c * chunk, rows + (c + 1) * chunk)
            q = queries[here, (a % 2) * size : (a % 2 + 1) * size]
            k = jnp.where(own, k_own_ref[here, out], k_ref[here, out])
            v = jnp.where(own, v_own_ref[here, out], v_ref[here, out])
            along, down = along_ref[head : head + 1, there], inside_ref[there, head : head + 1]
            q_ref[here, out] = faded(q, down_ref[there, head : head + 1])
            within_ref[here, out] = scores(q, k, v, along, down, state).astype(BF16)
            if c + 1 < rows // chunk:
                state = advance(k, v, down, state)


def later_call(places, far, w_far, acc, keys_values, along, inside, down, state, chunk, half):
    _, rows, width = acc.shape
    ins = [near(x) for x in (*far, w_far, acc, *keys_values)] + [along, inside, down, near(state)]
    outs = (struct((rows, width // 2), BF16),) * 2
    scratch = [pltpu.VMEM((rows, far[0].shape[1]), BF16)]
    kernel = functools.partial(later_kernel, half, chunk)
    return small_call(kernel, "later", places, ins, outs, 16, scratch)


def fades(tail_ref, other_ref, place, head):
    own, other = tail_ref[pl.ds(head, 1), :], other_ref[pl.ds(head, 1), :]
    first = jnp.where(place == 0, own, other)
    return jnp.exp(-first), jnp.exp(first - (own + other)), jnp.exp(-(own + other))


def chip_kernel(places, state_ref, come_ref, tail_ref, other_ref, prior_ref, *out_refs):
    leaving_ref, alone_ref, chip_ref, first_ref = out_refs
    core = places[4]
    share = come_ref.shape[0]
    for i in range(share):
        head = core * share + i
        _, second_fade, fade = fades(tail_ref, other_ref, core, head)
        ours, come = state_ref[i], come_ref[i].astype(F32)
        first, second = jnp.where(core == 0, ours, come), jnp.where(core == 0, come, ours)
        total = second_fade * first + second
        first_ref[i] = first
        chip_ref[i] = total
        alone_ref[i] = total.astype(BF16)
        leaving_ref[i] = (fade * prior_ref[head] + total).astype(BF16)


def pass_kernel(places, come_ref, chip_ref, tail_ref, other_ref, leaving_ref):
    share = come_ref.shape[0]
    for i in range(share):
        fade = fades(tail_ref, other_ref, places[4], places[4] * share + i)[2]
        leaving_ref[i] = (fade * come_ref[i].astype(F32) + chip_ref[i]).astype(BF16)


def enter_kernel(
    places, come_ref, alone_ref, second_ref, third_ref, first_ref, tail_ref, other_ref, below_ref, prior_ref, *out_refs
):
    here_ref, passed_ref = out_refs
    core, chip = places[4], places[5]
    share = come_ref.shape[0]
    for i in range(share):
        head = core * share + i
        below = jnp.exp(-below_ref[pl.ds(head, 1), :])
        through = below * third_ref[i].astype(F32) + alone_ref[i].astype(F32)
        state = jnp.where(chip == 0, prior_ref[head], come_ref[i].astype(F32))
        state = jnp.where(chip == 2, second_ref[i].astype(F32), state)
        state = jnp.where(chip == 3, through, state)
        later = fades(tail_ref, other_ref, core, head)[0] * state + first_ref[i]
        here_ref[i] = jnp.where(core == 0, state, later).astype(BF16)
        passed_ref[i] = jnp.where(core == 0, later, state).astype(BF16)


def small_call(kernel, name, places, ins, outs, limit=4, scratch=()):
    whole = pl.BlockSpec(memory_space=pltpu.VMEM)
    return pl.pallas_call(
        kernel,
        out_shape=tuple(outs),
        in_specs=[pl.BlockSpec(memory_space=pltpu.SMEM)] + [whole] * len(ins),
        out_specs=[whole] * len(outs),
        scratch_shapes=list(scratch),
        compiler_params=pltpu.CompilerParams(vmem_limit_bytes=limit * MIB),
        cost_estimate=pl.CostEstimate(flops=1, bytes_accessed=1, transcendentals=0),
        name=name,
    )(places, *ins)


def chip_call(places, state, come, tails, prior):
    outs = [struct(come.shape, kind) for kind in (BF16, BF16, F32, F32)]
    return small_call(chip_kernel, "chip_state", places, (state, come, *tails, prior), outs)


def pass_call(places, come, chip_state, tails):
    outs = (struct(come.shape, BF16),)
    return small_call(pass_kernel, "pass_on", places, (come, chip_state, *tails), outs)[0]


def enter_call(places, come, alone, second, third, first, tails, below, prior):
    outs = (struct(come.shape, BF16),) * 2
    ins = (come, alone, second, third, first, *tails, below, prior)
    return small_call(enter_kernel, "enter", places, ins, outs)


def columns(w_ref, block, width):
    return w_ref[:, pl.ds(pl.multiple_of(block * width, width), width)]


WHOLE = pl.BlockSpec(memory_space=pltpu.VMEM)


def normalise(core, q_refs, within_refs, here_ref, there_ref, rows, out_ref):
    share, size = here_ref.shape[0], here_ref.shape[1]
    ones = jnp.ones((size, size), BF16)
    for a in range(2 * share):
        part, at = divmod(a, 2 * share // len(q_refs))
        here = slice(at * size, (at + 1) * size)
        entering = jnp.where(core == a // share, here_ref[a % share], there_ref[a % share])
        seen = dot(q_refs[part][rows, here], entering)
        combined = within_refs[part][rows, here].astype(F32) + seen
        square = combined * combined
        high = square.astype(BF16)
        low = (square - high.astype(F32)).astype(BF16)
        power = (dot(high, ones) + dot(low, ones)) * (1.0 / size)
        out_ref[:, a * size : (a + 1) * size] = (combined * lax.rsqrt(power + 1e-06)).astype(BF16)


def head_kernel(count, places, *refs):
    q_refs, within_refs, refs = refs[:count], refs[count : 2 * count], refs[2 * count :]
    here_ref, there_ref, w_ref, normed_ref = refs[:4]
    out_refs = refs[4:]
    tall, width = normed_ref.shape[0] // 2, out_refs[0].shape[1]
    for p, out_ref in enumerate(out_refs):
        rows = slice(p * tall, (p + 1) * tall)
        normed = normed_ref.at[rows]
        normalise(places[4], q_refs, within_refs, here_ref, there_ref, rows, normed)
        out_ref[:tall, :] = dot(normed[...], columns(w_ref, places[3], width)).astype(BF16)
        if out_ref.shape[0] > tall:
            out_ref[tall:, :] = dot(normed[...], columns(w_ref, places[1 + p], width)).astype(BF16)


def head_call(places, q, within, entering, w_out, width, near_too):
    rows, cols = q[0].shape[0], w_out.shape[0]
    out = struct((rows if near_too else rows // 2, width), BF16)
    ins = [near(x) for x in (*q, *within, *entering)] + [w_out]
    outs = (struct((rows, cols), BF16), out, out)
    return small_call(functools.partial(head_kernel, len(q)), "heads", places, ins, outs, 12)


def mixed_kernel(places, normed_ref, x_ref, y_ref, w_ref, out_x_ref, out_y_ref):
    tall, width = x_ref.shape
    for p, (out_ref, come_ref) in enumerate(((out_x_ref, x_ref), (out_y_ref, y_ref))):

        @pl.when(pl.program_id(0) == p)
        def _(p=p, out_ref=out_ref, come_ref=come_ref):
            total = dot(normed_ref[...], columns(w_ref, places[1 + p], width))
            summed = total[(1 - p) * tall : (2 - p) * tall] + come_ref[...].astype(F32)
            out_ref[:tall, :] = summed.astype(BF16)
            out_ref[tall:, :] = total[p * tall : (p + 1) * tall].astype(BF16)


def mixed_call(places, normed, for_x, for_y, w_out, width):
    rows, cols = normed.shape
    quarter, half = (rows // 2, width), (rows, width)
    return call(
        mixed_kernel,
        "sum_and_near",
        2,
        places,
        (normed, for_x, for_y, w_out),
        [fixed((rows, cols)), fixed(quarter), fixed(quarter), WHOLE],
        (struct(half, BF16),) * 2,
        [fixed(half)] * 2,
        4 * rows * cols * width,
        light=True,
    )


def pair_kernel(places, normed_ref, x_ref, y_ref, w_ref, out_x_ref, out_y_ref):
    tall, width = out_x_ref.shape

    @pl.when(pl.program_id(0) == 0)
    def _():
        total = dot(normed_ref[tall:, :], columns(w_ref, places[1], width)) + x_ref[...].astype(F32)
        out_x_ref[...] = total.astype(BF16)

    @pl.when(pl.program_id(0) == 1)
    def _():
        total = dot(normed_ref[:tall, :], columns(w_ref, places[2], width)) + y_ref[...].astype(F32)
        out_y_ref[...] = total.astype(BF16)


def pair_call(places, normed, for_x, for_y, w_out, width):
    rows, cols = normed.shape
    quarter = (rows // 2, width)
    return call(
        pair_kernel,
        "sum_pair",
        2,
        places,
        (normed, for_x, for_y, w_out),
        [fixed((rows, cols)), fixed(quarter), fixed(quarter), WHOLE],
        (struct(quarter, BF16),) * 2,
        [fixed(quarter)] * 2,
        2 * rows * cols * width,
        light=True,
    )


def own_kernel(places, normed_ref, w_ref, *refs):
    out_ref = refs[-1]
    tall, width = out_ref.shape
    each = len(refs) // 2
    for p in range(2):
        rows = slice(p * tall, (p + 1) * tall)

        @pl.when(pl.program_id(0) == p)
        def _(p=p, rows=rows):
            total = dot(normed_ref[rows, :], columns(w_ref, places[0], width))
            for ref in refs[p * each : (p + 1) * each]:
                total = total + ref[...].astype(F32)
            out_ref[...] = total.astype(BF16)


def own_call(places, normed, first, second, w_out, width, height):
    rows, cols = normed.shape
    quarter = (rows // 2, width)
    return call(
        own_kernel,
        "own_block",
        2,
        places,
        (normed, w_out, *[a for a, _ in (*first, *second)]),
        [fixed((rows, cols)), WHOLE]
        + [pl.BlockSpec(quarter, lambda i, o, at=at: (at, 0)) for _, at in (*first, *second)],
        (struct((rows * height, width), BF16),),
        [pl.BlockSpec(quarter, lambda i, o: (i, 0))],
        2 * rows * cols * width,
        light=True,
    )[0]


def last_kernel(_, kept_ref, a_ref, b_ref, above_ref, out_ref):
    del above_ref

    @pl.when(pl.program_id(0) == 0)
    def _():
        out_ref[...] = (kept_ref[...].astype(F32) + a_ref[...].astype(F32)).astype(BF16)

    @pl.when(pl.program_id(0) == 1)
    def _():
        out_ref[...] = (kept_ref[...].astype(F32) + b_ref[...].astype(F32)).astype(BF16)


def last_call(kept, a, b, above):
    tall, width = a.shape
    return call(
        last_kernel,
        "last_add",
        2,
        jnp.zeros((1,), jnp.int32),
        (kept, a, b, above),
        [
            pl.BlockSpec((tall, width), lambda j, o: (j, 0)),
            fixed((tall, width)),
            fixed((tall, width)),
            pl.BlockSpec(memory_space=pl.ANY),
        ],
        (struct(above.shape, BF16),),
        [pl.BlockSpec((tall, width), lambda j, o: (2 + j, 0))],
        tall * width,
        aliases={4: 0},
    )[0]


def local(n_head, n_seq, tokens, w_qkv, w_out, decay_rate, prior_state):
    rows, width = tokens.shape
    heads, size = prior_state.shape[0], prior_state.shape[1]
    square = n_head == 4
    place = lax.axis_index("head").astype(jnp.int32)
    quarter = rows // 4
    group = 2 if heads % 2 == 0 else 1
    cols = group * size

    over_x = functools.partial(lax.ppermute, axis_name="head", perm=[(i, i ^ 1) for i in range(n_head)])
    over_y = functools.partial(lax.ppermute, axis_name="head", perm=[(i, i ^ 2) for i in range(n_head)])

    pos = lax.axis_index("seq").astype(jnp.int32)
    core, chip = pos % 2, pos // 2
    flips = (0, 1, 2, 3) if square else (0, 0, 0, 0)
    places = jnp.stack([*[place ^ f for f in flips], core, chip])

    along, inside, down, tail, to_end, half_fade = decay_call(decay_rate, quarter)
    n_chips = n_seq // 2
    swap = functools.partial(lax.ppermute, axis_name="seq", perm=[(i, i ^ 1) for i in range(n_seq)])

    def hop(x, *pairs):
        perm = [(2 * a + c, 2 * b + c) for a, b in pairs for c in range(2)]
        return lax.ppermute(x, "seq", perm=perm)

    def chip_tails(tail):
        other = swap(tail)
        return other, tail + other, hop(tail + other, (2, 3)) if n_chips == 4 else None

    if square:
        tokens, w_qkv = stay(tokens), stay(w_qkv)
        q0, q1 = cut_call(tokens, 0, 1)
        x0, y1 = over_x(q0), over_y(q1)
        x1, y0 = over_x(after(q1, tail)), over_y(after(q0, tail))
        acc = own_part_call(places, tokens, w_qkv, cols)
        q2, q3 = cut_call(stay(after(tokens, acc, x0, y1)), 1, 10**10)
        fy0, fx1 = over_y(x0), over_x(y1)
        tail_other, tail_chip, tail_below = chip_tails(after(tail, acc, x0, y1))
        x2 = over_x(after(q2, x1, y0, tail_chip))
        y3 = over_y(after(q3, x1, y0, tail_chip))
        acc_a = part_call(
            places,
            (1, 2),
            [(x0, x1), (y0, y1)],
            w_qkv,
            2 * quarter,
            cols,
            before=stay(after(acc, tail_chip)),
            at=0,
        )
        earlier = (fy0, fx1, acc_a) if tail_below is None else (fy0, fx1, acc_a, tail_below)
        x3, y2 = over_x(after(q3, *earlier)), over_y(after(q2, *earlier))
        query_a, within_a, state, w_far = first_call(
            places,
            (3,),
            [(fy0, fx1)],
            (acc_a,),
            w_qkv,
            along,
            inside,
            2 * quarter,
            quarter,
            size,
            group,
        )
        fy2, fx3 = over_y(after(x2, state)), over_x(after(y3, state))
        acc_b = part_call(
            places,
            (1, 2),
            [(x2, x3), (y2, y3)],
            w_qkv,
            2 * quarter,
            cols,
            before=stay(acc),
            at=1,
        )
        far = (fy2, fx3)
        middle = state
        k, v, sent = state_call(places, far, w_far, acc_b, to_end, half_fade, middle, False)
        k_own, v_own, state = state_call(
            places, far, w_far, acc_b, to_end, half_fade, after(middle, sent), True
        )
        keys_values = (k, v, k_own, v_own)
    else:
        tail_other, tail_chip, tail_below = chip_tails(tail)
        gathered = lax.all_gather(tokens, "head", axis=1, tiled=True)
        query, within, state = first_call(
            places, (), [(gathered,)], (), w_qkv, along, inside, rows, quarter, size, group
        )

    tails = (tail, tail_other)

    def scores_of_later(half, *earlier):
        start = after(middle, *earlier)
        return later_call(
            places, far, w_far, acc_b, keys_values, along, inside, down, start, quarter, half
        )

    if square and n_chips == 4:
        leaving, alone, chip_state, first = chip_call(
            places, near(state), near(swap(sent)), tails, prior_state
        )
        alone = hop(alone, (2, 3))
        arriving = near(hop(leaving, (0, 1)))
        leaving = pass_call(places, arriving, chip_state, tails)
        to_third, to_second = hop(leaving, (1, 3)), hop(leaving, (1, 2))
        query_b, within_b = scores_of_later(0, leaving)
        alone, to_third, to_second, _ = lax.optimization_barrier((alone, to_third, to_second, query_b))
        here, passed = enter_call(
            places,
            arriving,
            near(alone),
            near(to_second),
            near(to_third),
            first,
            tails,
            tail_below,
            prior_state,
        )
    else:
        share = heads // 2

        def mine(x, core=core):
            return lax.dynamic_slice_in_dim(x, core * share, share, 0)

        def decay(tail):
            return jnp.exp(-mine(tail)[:, :1, None])

        ours = state if square else mine(state)
        other = swap(sent if square else mine(state, 1 - core).astype(BF16)).astype(F32)
        first = jnp.where(core == 0, ours, other)
        second = jnp.where(core == 0, other, ours)
        chip_state = decay(jnp.where(core == 0, tail_other, tail)) * first + second
        chip_entering = mine(prior_state)
        for step in range(n_chips - 1):
            leaving = (decay(tail_chip) * chip_entering + chip_state).astype(BF16)
            arriving = hop(leaving, (step, step + 1))
            chip_entering = jnp.where(chip == step + 1, arriving.astype(F32), chip_entering)
        other = decay(jnp.where(core == 0, tail, tail_other)) * chip_entering + first
        here = jnp.where(core == 0, chip_entering, other).astype(BF16)
        passed = jnp.where(core == 0, other, chip_entering).astype(BF16)
    entering = (here, swap(passed))

    w_whole, w_out = w_out, near(w_out)
    if not square:
        halves = [
            head_call(
                places,
                (query[r * rows // 2 : (r + 1) * rows // 2],),
                (within[r * rows // 2 : (r + 1) * rows // 2],),
                entering,
                w_out,
                width,
                False,
            )[0]
            for r in range(2)
        ]
        partial = dot(jnp.concatenate(halves), w_whole).astype(BF16)
        return lax.psum_scatter(partial, "head", scatter_dimension=1, tiled=True)

    if n_chips != 4:
        query_b, within_b = scores_of_later(0)
    na, far0, far1 = head_call(places, (query_a,), (within_a,), entering, w_out, width, False)
    query_c, within_c = scores_of_later(1, na)
    far0, far1 = over_x(far0), over_y(far1)
    nb, by_x2, by_y2 = head_call(
        places, (query_b, query_c), (within_b, within_c), entering, w_out, width, True
    )
    by_x2, by_y2 = over_x(by_x2), over_y(by_y2)
    by_x, by_y = mixed_call(places, after(na, nb), far1, far0, w_out, width)
    by_x2, by_y2 = after(by_x2, by_x), after(by_y2, by_x)
    by_x, by_y = over_x(by_x), over_y(by_y)
    sum3, sum2 = pair_call(places, nb, by_y2, by_x2, w_out, width)
    sum3, sum2 = over_x(sum3), over_y(sum2)
    below = own_call(places, after(nb, by_x, by_y), ((by_x2, 1),), ((by_y2, 1),), w_out, width, 1)
    above = own_call(places, na, ((by_x, 1), (by_y, 0)), ((by_y, 1), (by_x, 0)), w_out, width, 2)
    return last_call(below, sum2, sum3, above)


def solution(mesh):
    in_specs = (
        P("seq", "head"),
        P(None, None, "head"),
        P("head", None),
        P("head", "seq"),
        P("head", None, None),
    )
    body = functools.partial(local, mesh.shape["head"], mesh.shape["seq"])
    return jax.shard_map(
        body, mesh=mesh, in_specs=in_specs, out_specs=P("seq", "head"), check_vma=False
    )
```
